32 devices in a mesh: section: 2 (over core), dp: 4 (over y, x), tensor: 4 (over z).
Axes of the slice: x: 2, y: 2, z: 4, core: 2. Of those that a mesh axis runs over, the one named last changes fastest.
Arguments:
- token_ids: int32 [8, 1024], P('dp'), may hold values from 0 to 32767
- target_ids: int32 [8, 1024], P('dp'), may hold values from 0 to 32767
- lengths: int32 [8], replicated, may hold values from 204 to 1024, as said below
- embedding: bfloat16 [32768, 1024], P('tensor'), may hold values from -0.375 to 0.375
- outer_gain: float32 [2, 1024], P('section'), may hold values from 0.5 to 1.5
- outer_bias: float32 [2, 1024], P('section'), may hold values from -1.2 to 1.2
- norm_gain: float32 [2, 2, 1024], P('section'), may hold values from 0.5 to 1.5
- norm_bias: float32 [2, 2, 1024], P('section'), may hold values from -1.2 to 1.2
- qkv_weight: bfloat16 [2, 3, 1024, 1024], P('section', None, None, 'tensor'), may hold values from -0.1875 to 0.1875
- qv_bias: float32 [2, 2, 1024], P('section', None, 'tensor'), may hold values from -1.8 to 1.8
- out_weight: bfloat16 [2, 1024, 1024], P('section', 'tensor'), may hold values from -0.375 to 0.375
- up_weight: bfloat16 [2, 1024, 4096], P('section', None, 'tensor'), may hold values from -0.1875 to 0.1875
- up_bias: float32 [2, 4096], P('section', 'tensor'), may hold values from -1.8 to 1.8
- down_weight: bfloat16 [2, 4096, 1024], P('section', 'tensor'), may hold values from -0.09375 to 0.09375
- row_bias: float32 [2, 2, 1024], P('section'), may hold values from -1.2 to 1.2
Outputs:
- loss: float32 [], replicated
- grad_embedding: float32 [32768, 1024], P('tensor')
- grad_outer_gain: float32 [2, 1024], P('section')
- grad_outer_bias: float32 [2, 1024], P('section')
- grad_norm_gain: float32 [2, 2, 1024], P('section')
- grad_norm_bias: float32 [2, 2, 1024], P('section')
- grad_qkv_weight: float32 [2, 3, 1024, 1024], P('section', None, None, 'tensor')
- grad_qv_bias: float32 [2, 2, 1024], P('section', None, 'tensor')
- grad_out_weight: float32 [2, 1024, 1024], P('section', 'tensor')
- grad_up_weight: float32 [2, 1024, 4096], P('section', None, 'tensor')
- grad_up_bias: float32 [2, 4096], P('section', 'tensor')
- grad_down_weight: float32 [2, 4096, 1024], P('section', 'tensor')
- grad_row_bias: float32 [2, 2, 1024], P('section')
The draws below stay inside these ranges and needn't reach their ends.
Inputs may be any that keep to these rules, and one draw needn't show every extreme that they name: `lengths`: in each aligned block of 2 rows (one data group's rows) one row, drawn from the seed, has 1024 tokens.
All inputs are finite; a program needn't handle non-finite values.
Results may differ from the reference program's by a relative error of at most 0.005.
Values may be sent and summed in bfloat16 or wider, within the bound.
A program may use at most 704 MiB of HBM per device.

```python
import math
import jax
import jax.numpy as jnp
import numpy as np
from jax import lax

D = 1024
HEADS = 16
HEAD_DIM = 64
FF = 4096
SEQ = 1024
MICRO = 2
VOCAB = 32768
ROWS = 8


def draw_lengths(key, part):
    key = jax.random.fold_in(key, 7)
    drawn = jax.random.randint(jax.random.fold_in(key, 1), (ROWS,), SEQ // 5, SEQ + 1)
    chosen = jax.random.randint(jax.random.fold_in(key, 2), (ROWS // MICRO, 1), 0, MICRO)
    places = jnp.arange(MICRO)[None, :]
    longest = (places == chosen).reshape(ROWS)
    return jnp.where(longest, SEQ, drawn).astype(jnp.int32)


def place_ends(values, stream_key, low, largest):
    extent = values.shape
    place = [jax.random.randint(jax.random.fold_in(stream_key, axis), (), 0, extent[axis]) for axis in range(len(extent))]
    values = values.at[tuple(place)].set(low)
    longest = extent.index(max(extent))
    place[longest] = (place[longest] + 1) % extent[longest]
    return values.at[tuple(place)].set(largest)


def levels(stream_key, dims, cuts, low, high):
    factor_of, own = 1.0, jax.random.fold_in(stream_key, 6)
    for dim, shards_of in cuts:
        heights = jnp.exp(jax.random.uniform(jax.random.fold_in(own, dim), (shards_of,), jnp.float32, low / len(cuts), high / len(cuts)))
        factor_of = factor_of * jnp.repeat(heights, dims[dim] // shards_of).reshape([-1 if axis == dim else 1 for axis in range(len(dims))])
    return factor_of


def rank_table(amount, skew):
    portions = [(1 << 20) // math.isqrt(grade ** skew) + 1 for grade in range(1, amount + 1)]
    scale = 1 + sum(portions) // (1 << 30)
    return np.cumsum(np.array([max(1, weight // scale) for weight in portions]))


def skewed_ids(key, shape, amount, slope):
    table = rank_table(amount, slope)
    pick = jax.random.randint(jax.random.fold_in(key, 1), shape, 0, int(table[amount - 1]))
    standing = jnp.searchsorted(jnp.asarray(table, jnp.int32), pick, side="right")
    return jax.random.permutation(jax.random.fold_in(key, 2), amount)[standing].astype(jnp.int32)


def noise(stream_key, shape, deviation, most, shards=(), dtype=jnp.bfloat16):
    values = deviation * jax.random.normal(stream_key, shape, jnp.float32)
    if shards:
        values = values * levels(stream_key, shape, shards, -0.22, 0.18)
    return jnp.clip(values, -most, most).astype(dtype)


def setup_inputs(seed: int = 0) -> dict:
    seeds = jax.random.split(jax.random.key(seed), 16)
    return {
        "token_ids": place_ends(skewed_ids(seeds[0], (ROWS, SEQ), VOCAB, 2), jax.random.fold_in(seeds[0], 3), 0, VOCAB - 1).astype(jnp.int32),
        "target_ids": place_ends(jax.random.randint(seeds[1], (ROWS, SEQ), 0, VOCAB), jax.random.fold_in(seeds[1], 1), 0, VOCAB - 1).astype(jnp.int32),
        "lengths": draw_lengths(jax.random.fold_in(seeds[15], 71), 0),
        "embedding": noise(seeds[3], (VOCAB, D), (D // 4) ** -0.5, 0.375, ((0, 4),)),
        "outer_gain": jnp.clip(1.0 + 0.1 * jax.random.normal(seeds[4], (2, D), jnp.float32), 0.5, 1.5),
        "outer_bias": noise(seeds[5], (2, D), 0.2, 1.2, ((0, 2),), jnp.float32),
        "norm_gain": jnp.clip(1.0 + 0.1 * jax.random.normal(seeds[6], (2, 2, D), jnp.float32), 0.5, 1.5),
        "norm_bias": noise(seeds[7], (2, 2, D), 0.2, 1.2, ((0, 2),), jnp.float32),
        "qkv_weight": noise(seeds[8], (2, 3, D, D), D ** -0.5, 0.1875, ((0, 2), (3, 4))),
        "qv_bias": noise(seeds[9], (2, 2, D), 0.3, 1.8, ((0, 2), (2, 4)), jnp.float32),
        "out_weight": noise(seeds[10], (2, D, D), (D // 4) ** -0.5, 0.375, ((0, 2), (1, 4))),
        "up_weight": noise(seeds[11], (2, D, FF), D ** -0.5, 0.1875, ((0, 2), (2, 4))),
        "up_bias": noise(seeds[12], (2, FF), 0.3, 1.8, ((0, 2), (1, 4)), jnp.float32),
        "down_weight": noise(seeds[13], (2, FF, D), FF ** -0.5, 0.09375, ((0, 2), (1, 4))),
        "row_bias": noise(seeds[14], (2, 2, D), 0.2, 1.2, ((0, 2),), jnp.float32),
    }


EPS = 1e-05
NEG = -1e+30
HIGH = lax.Precision.HIGHEST

@jax.custom_vjp
def low(v):
    return lax.optimization_barrier(v.astype(jnp.bfloat16)).astype(jnp.float32)

@jax.custom_vjp
def low_back(v):
    return v

def low_keep(v):
    return (low(v), None)

def low_pass(kept, grad):
    return (grad,)

def back_keep(v):
    return (v, None)

def back_low(kept, grad):
    return (low(grad),)
low.defvjp(low_keep, low_pass)
low_back.defvjp(back_keep, back_low)

def layer_norm(inputs, weight, offset):
    centre = inputs - lax.optimization_barrier(jnp.mean(inputs, axis=-1, keepdims=True))
    spread = lax.optimization_barrier(jnp.mean(centre * centre, axis=-1, keepdims=True))
    return centre * lax.rsqrt(spread + EPS) * weight + offset

def gelu_tanh(inputs):
    return jax.nn.gelu(inputs, approximate=True)

def alibi_slopes(first_head, count_heads):
    number = (first_head + jnp.arange(count_heads) + 1).astype(jnp.float32)
    return jnp.exp2(-8.0 * number / HEADS)

def mask_scores(raw_scores, slopes, length):
    seq_len = raw_scores.shape[-1]
    places = jnp.arange(seq_len)
    distance = (places[:, None] - places[None, :]).astype(jnp.float32)
    scores = raw_scores * HEAD_DIM ** (-0.5) - slopes[:, None, None] * distance[None]
    allowed = (places[None, :] <= places[:, None]) & (places[None, :] < length)
    return jnp.where(allowed[None], scores, NEG)

def product(former, latter):
    return jnp.dot(former, latter, precision=HIGH, preferred_element_type=jnp.float32)

def product_t(former, latter):
    return lax.dot_general(former, latter, (((1,), (1,)), ((), ())), precision=HIGH, preferred_element_type=jnp.float32)

def split_heads(inputs):
    return inputs.reshape(inputs.shape[0], inputs.shape[1] // HEAD_DIM, HEAD_DIM)

def layer_apply(section_in, length, slopes, norm_gains, norm_offsets, qkv_mats, qv_offsets, out_mat, up_mat, up_offset, down_mat, row_offsets):
    seq_len = section_in.shape[0]
    normed = low(layer_norm(section_in, norm_gains[0], norm_offsets[0]))
    queries = low(low_back(product(normed, qkv_mats[0])) + qv_offsets[0])
    key_rows = low(low_back(product(normed, qkv_mats[1])))
    value_rows = low(low_back(product(normed, qkv_mats[2])) + qv_offsets[1])
    raw_scores = low_back(jnp.einsum('qhd,khd->hqk', split_heads(queries), split_heads(key_rows), precision=HIGH))
    scores = mask_scores(raw_scores, slopes, length)
    log_total = jax.nn.logsumexp(scores, axis=-1, keepdims=True)
    weights_low = low(jnp.exp(scores - log_total))
    attended = jnp.einsum('hqk,khd->qhd', weights_low, split_heads(value_rows), precision=HIGH).reshape(seq_len, -1)
    mixed_rows = low(low_back(attended))
    middle = section_in + low_back(product(mixed_rows, out_mat)) + row_offsets[0]
    second = low(layer_norm(middle, norm_gains[1], norm_offsets[1]))
    before = low_back(product(second, up_mat)) + up_offset
    active = low(gelu_tanh(before))
    return middle + low_back(product(active, down_mat)) + row_offsets[1]

def row_loss(params, row_ids, targets, length, token_count):
    table, outer_g, outer_b, norm_g, norm_b, qkv_mats, qv_offsets, out_mats, up_mats, up_offsets, down_mats, row_offsets = params
    seq_len = row_ids.shape[0]
    slopes = alibi_slopes(0, HEADS)
    hidden = layer_norm(jnp.take(table, row_ids, axis=0), outer_g[0], outer_b[0])
    for layer_index in range(2):
        hidden = layer_apply(hidden, length, slopes, norm_g[layer_index], norm_b[layer_index], qkv_mats[layer_index], qv_offsets[layer_index], out_mats[layer_index], up_mats[layer_index], up_offsets[layer_index], down_mats[layer_index], row_offsets[layer_index])
    final_rows = low(layer_norm(hidden, outer_g[1], outer_b[1]))
    logits = low_back(product_t(final_rows, table))
    log_norm = jax.nn.logsumexp(logits, axis=-1)
    picked = jnp.take_along_axis(logits, targets[:, None], axis=-1)[:, 0]
    valid_rows = jnp.arange(seq_len) < length
    return jnp.sum(jnp.where(valid_rows, log_norm - picked, 0.0)) / token_count

def reference(token_ids, target_ids, lengths, embedding, outer_gain, outer_bias, norm_gain, norm_bias, qkv_weight, qv_bias, out_weight, up_weight, up_bias, down_weight, row_bias):
    params = (embedding.astype(jnp.float32), outer_gain, outer_bias, norm_gain, norm_bias, qkv_weight.astype(jnp.float32), qv_bias, out_weight.astype(jnp.float32), up_weight.astype(jnp.float32), up_bias, down_weight.astype(jnp.float32), row_bias)
    token_count = jnp.sum(lengths).astype(jnp.float32)

    def total_loss(weights):

        def one_row(running_total, row_data):
            row_ids, targets, length = row_data
            return (running_total + row_loss(weights, row_ids, targets, length, token_count), None)
        summed, _ = lax.scan(jax.checkpoint(one_row), jnp.zeros((), jnp.float32), (token_ids, target_ids, lengths))
        return summed
    loss_value, pullback = jax.vjp(total_loss, params)
    gradients = pullback(jnp.ones((), jnp.float32))[0]
    return (loss_value, gradients[0], gradients[1], gradients[2], gradients[3], gradients[4], gradients[5], gradients[6], gradients[7], gradients[8], gradients[9], gradients[10], gradients[11])
```

```python
import functools
import math

import jax
import jax.numpy as jnp
from jax import lax
from jax.experimental import pallas as pl
from jax.experimental.pallas import tpu as pltpu
from jax.sharding import PartitionSpec as P

HEADS = 16
HEAD_DIM = 64
EPS = 1e-05
NEG = -1e30
MESH = pl.DeviceIdType.MESH
F32 = jnp.float32
BF16 = jnp.bfloat16


def matmul(former, latter):
    return jnp.dot(former, latter, preferred_element_type=F32)


def matmul_t(former, latter):
    return lax.dot_general(
        former, latter, (((1,), (1,)), ((), ())), preferred_element_type=F32
    )


def outer_sum(former, latter):
    return lax.dot_general(
        former, latter, (((0,), (0,)), ((), ())), preferred_element_type=F32
    )


def layer_norm(inputs, weight, offset):
    centre = inputs - jnp.mean(inputs, axis=-1, keepdims=True)
    spread = jnp.mean(centre * centre, axis=-1, keepdims=True)
    return centre * lax.rsqrt(spread + EPS) * weight + offset


def gelu_tanh(inputs):
    return jax.nn.gelu(inputs, approximate=True)


class Group:
    def __init__(self, axes, sizes):
        self.axes = axes
        self.sizes = sizes
        self.count = math.prod(sizes)

    def me(self):
        place = 0
        for axis, size in zip(self.axes, self.sizes):
            place = place * size + lax.axis_index(axis)
        return place

    def device(self, place):
        spot = {}
        for axis, size in reversed(list(zip(self.axes, self.sizes))):
            spot[axis] = lax.rem(place, size)
            place = lax.div(place, size)
        return spot

    def peers(self):
        me = self.me()
        return [lax.rem(me + step, self.count) for step in range(1, self.count)]


def greet(groups):
    barrier = pltpu.get_barrier_semaphore()
    total = 0
    for group in groups:
        for peer in group.peers():
            pl.semaphore_signal(
                barrier, inc=1, device_id=group.device(peer), device_id_type=MESH
            )
            total += 1
    pl.semaphore_wait(barrier, total)


def send(group, peer, step, src, dst, send_sem, recv_sem):
    copy = pltpu.make_async_remote_copy(
        src_ref=src,
        dst_ref=dst,
        send_sem=send_sem.at[step],
        recv_sem=recv_sem.at[step],
        device_id=group.device(peer),
        device_id_type=MESH,
    )
    copy.start()
    return copy


def gather_body(group, x_ref, out_ref, local_sem, send_sem, recv_sem):
    me = group.me()
    greet([group])
    copies = [
        send(group, peer, step, x_ref, out_ref.at[me], send_sem, recv_sem)
        for step, peer in enumerate(group.peers())
    ]
    own = pltpu.make_async_copy(x_ref, out_ref.at[me], local_sem)
    own.start()
    for copy in copies:
        copy.wait()
    own.wait()


def gather(group, x, ident):
    if group.count == 1:
        return x[None]
    others = group.count - 1
    return pl.pallas_call(
        functools.partial(gather_body, group),
        out_shape=jax.ShapeDtypeStruct((group.count,) + x.shape, x.dtype),
        in_specs=[pl.BlockSpec(memory_space=pl.ANY)],
        out_specs=pl.BlockSpec(memory_space=pl.ANY),
        scratch_shapes=[
            pltpu.SemaphoreType.DMA,
            pltpu.SemaphoreType.DMA((others,)),
            pltpu.SemaphoreType.DMA((others,)),
        ],
        compiler_params=pltpu.CompilerParams(collective_id=ident, has_side_effects=True),
    )(x)


def scatter_body(group, x_ref, out_ref, own, slots, local_sem, send_sem, recv_sem):
    me = group.me()
    greet([group])
    copies = [
        send(group, peer, step, x_ref.at[peer], slots.at[step], send_sem, recv_sem)
        for step, peer in enumerate(group.peers())
    ]
    kept = pltpu.make_async_copy(x_ref.at[me], own, local_sem)
    kept.start()
    kept.wait()
    for copy in copies:
        copy.wait()
    total = own[...].astype(F32)
    for step in range(group.count - 1):
        total = total + slots[step].astype(F32)
    out_ref[...] = total


def scatter_sum(group, x, ident):
    if group.count == 1:
        return x[0].astype(F32)
    others = group.count - 1
    block = x.shape[1:]
    return pl.pallas_call(
        functools.partial(scatter_body, group),
        out_shape=jax.ShapeDtypeStruct(block, F32),
        in_specs=[pl.BlockSpec(memory_space=pl.ANY)],
        out_specs=pl.BlockSpec(memory_space=pltpu.VMEM),
        scratch_shapes=[
            pltpu.VMEM(block, x.dtype),
            pltpu.VMEM((others,) + block, x.dtype),
            pltpu.SemaphoreType.DMA,
            pltpu.SemaphoreType.DMA((others,)),
            pltpu.SemaphoreType.DMA((others,)),
        ],
        compiler_params=pltpu.CompilerParams(
            collective_id=ident, has_side_effects=True, vmem_limit_bytes=32 * 2**20
        ),
    )(x)


def all_sum_body(groups, x_ref, out_ref, *scratch):
    greet(groups)
    out_ref[...] = x_ref[...]
    count = len(groups)
    for number, group in enumerate(groups):
        kept, slots, send_sem, recv_sem = scratch[4 * number : 4 * number + 4]
        kept[...] = out_ref[...]
        copies = [
            send(group, peer, step, kept, slots.at[step], send_sem, recv_sem)
            for step, peer in enumerate(group.peers())
        ]
        for copy in copies:
            copy.wait()
        me = group.me()
        total = jnp.zeros_like(out_ref)
        for place in range(group.count):
            step = lax.rem(me - place + group.count, group.count) - 1
            term = slots[jnp.maximum(step, 0)]
            total = total + jnp.where(place == me, kept[...], term)
        out_ref[...] = total


def all_sum(groups, x, ident):
    groups = [group for group in groups if group.count > 1]
    scratch = []
    for group in groups:
        others = group.count - 1
        scratch += [
            pltpu.VMEM(x.shape, x.dtype),
            pltpu.VMEM((others,) + x.shape, x.dtype),
            pltpu.SemaphoreType.DMA((others,)),
            pltpu.SemaphoreType.DMA((others,)),
        ]
    return pl.pallas_call(
        functools.partial(all_sum_body, groups),
        out_shape=jax.ShapeDtypeStruct(x.shape, x.dtype),
        in_specs=[pl.BlockSpec(memory_space=pltpu.VMEM)],
        out_specs=pl.BlockSpec(memory_space=pltpu.VMEM),
        scratch_shapes=scratch,
        compiler_params=pltpu.CompilerParams(
            collective_id=ident, has_side_effects=True, vmem_limit_bytes=32 * 2**20
        ),
    )(x)


BLOCK = 256


def masked_scores(queries, keys, slope, length, first):
    rows, cols = queries.shape[0], keys.shape[0]
    raw = matmul_t(queries, keys)
    i = first + lax.broadcasted_iota(jnp.int32, (rows, cols), 0)
    j = lax.broadcasted_iota(jnp.int32, (rows, cols), 1)
    scores = raw * HEAD_DIM ** (-0.5) - slope * (i - j).astype(F32)
    return jnp.where((j <= i) & (j < length), scores, NEG)


def attend_body(length_ref, slope_ref, q_ref, k_ref, v_ref, o_ref, lse_ref):
    seq, width = q_ref.shape
    for head in range(width // HEAD_DIM):
        lanes = slice(head * HEAD_DIM, (head + 1) * HEAD_DIM)
        slope = slope_ref[head]
        keys, values = k_ref[:, lanes], v_ref[:, lanes]
        for first in range(0, seq, BLOCK):
            upto = first + BLOCK
            scores = masked_scores(
                q_ref[first:upto, lanes], keys[:upto], slope, length_ref[0], first
            )
            highest = jnp.max(scores, axis=-1, keepdims=True)
            powers = jnp.exp(scores - highest)
            total = jnp.sum(powers, axis=-1, keepdims=True)
            probs = (powers * (1.0 / total)).astype(BF16)
            o_ref[first:upto, lanes] = matmul(probs, values[:upto]).astype(BF16)
            lse_ref[head, first:upto, :] = highest + jnp.log(total)


def attend(length, slopes, q, k, v):
    seq, width = q.shape
    heads = width // HEAD_DIM
    smem = pl.BlockSpec(memory_space=pltpu.SMEM)
    vmem = pl.BlockSpec(memory_space=pltpu.VMEM)
    return pl.pallas_call(
        attend_body,
        out_shape=(
            jax.ShapeDtypeStruct((seq, width), BF16),
            jax.ShapeDtypeStruct((heads, seq, 1), F32),
        ),
        in_specs=[smem, smem, vmem, vmem, vmem],
        out_specs=(vmem, vmem),
        compiler_params=pltpu.CompilerParams(vmem_limit_bytes=40 * 2**20),
    )(length, slopes, q, k, v)


def attend_back_body(
    length_ref, slope_ref, q_ref, k_ref, v_ref, go_ref, lse_ref, gq_ref, gk_ref, gv_ref
):
    seq, width = q_ref.shape
    gk_ref[...] = jnp.zeros_like(gk_ref)
    gv_ref[...] = jnp.zeros_like(gv_ref)
    for head in range(width // HEAD_DIM):
        lanes = slice(head * HEAD_DIM, (head + 1) * HEAD_DIM)
        slope = slope_ref[head]
        keys, values = k_ref[:, lanes], v_ref[:, lanes]
        for first in range(0, seq, BLOCK):
            upto = first + BLOCK
            queries = q_ref[first:upto, lanes]
            grads = go_ref[first:upto, lanes]
            scores = masked_scores(queries, keys[:upto], slope, length_ref[0], first)
            probs = jnp.exp(scores - lse_ref[head, first:upto, :])
            grad_probs = matmul_t(grads, values[:upto])
            inner = jnp.sum(probs * grad_probs, axis=-1, keepdims=True)
            grad_scores = (probs * (grad_probs - inner) * HEAD_DIM ** (-0.5)).astype(BF16)
            gq_ref[first:upto, lanes] = matmul(grad_scores, keys[:upto])
            gk_ref[:upto, lanes] += outer_sum(grad_scores, queries)
            gv_ref[:upto, lanes] += outer_sum(probs.astype(BF16), grads)


def attend_back(length, slopes, q, k, v, go, lse):
    smem = pl.BlockSpec(memory_space=pltpu.SMEM)
    vmem = pl.BlockSpec(memory_space=pltpu.VMEM)
    return pl.pallas_call(
        attend_back_body,
        out_shape=(jax.ShapeDtypeStruct(q.shape, F32),) * 3,
        in_specs=[smem, smem] + [vmem] * 5,
        out_specs=(vmem,) * 3,
        compiler_params=pltpu.CompilerParams(vmem_limit_bytes=40 * 2**20),
    )(length, slopes, q, k, v, go, lse)


def per_device(
    mesh_shape,
    token_ids,
    target_ids,
    lengths,
    embedding,
    outer_gain,
    outer_bias,
    norm_gain,
    norm_bias,
    qkv_weight,
    qv_bias,
    out_weight,
    up_weight,
    up_bias,
    down_weight,
    row_bias,
):
    sections, groups, shards = (mesh_shape[name] for name in ("section", "dp", "tensor"))
    s, j, z = (lax.axis_index(name) for name in ("section", "dp", "tensor"))
    by_section = Group(("section",), (sections,))
    by_dp = Group(("dp",), (groups,))
    by_tensor = Group(("tensor",), (shards,))
    layers = sections
    vocab, width = embedding.shape
    seq = token_ids.shape[1]
    rows = token_ids.shape[0] * groups
    local_cols = qkv_weight.shape[-1]
    planes = rows == sections * shards and local_cols % (groups * HEAD_DIM) == 0
    team = by_dp if planes else by_tensor
    cut = groups if planes else 1
    part = seq // team.count
    cols = local_cols // cut
    hidden = up_weight.shape[-1] // cut
    cut_index = j if planes else 0
    my_part = j if planes else z
    my_row = z * sections + s if planes else j * sections + s

    if planes:
        both = gather(by_dp, jnp.stack([token_ids, target_ids]), 1)
        both = jnp.swapaxes(both, 0, 1).reshape(2, shards, sections, groups, part)
        both = lax.dynamic_index_in_dim(
            lax.dynamic_index_in_dim(both, s, 2, keepdims=False), j, 2, keepdims=False
        )
        ids, targets = both[0].reshape(-1), both[1].reshape(-1)
        group_lengths = lax.dynamic_index_in_dim(
            lengths.reshape(shards, sections), s, 1, keepdims=False
        )
        places = jnp.broadcast_to(j * part + jnp.arange(part), (shards, part))
        valid = (places < group_lengths[:, None]).reshape(-1)
    else:
        ids, targets = token_ids[s], target_ids[s]
        valid = jnp.arange(seq) < lengths[my_row]
    length = lax.dynamic_slice(lengths, (my_row,), (1,))
    token_count = jnp.sum(lengths).astype(F32)
    vocab_start = z * vocab

    def chosen_cols(array, size):
        piece = lax.dynamic_slice_in_dim(array, cut_index * size, size, array.ndim - 1)
        return jnp.swapaxes(piece, -1, -2)

    def chosen_rows(array, size):
        return lax.dynamic_slice_in_dim(array, cut_index * size, size, 0)

    def spread_weights(piece):
        if planes:
            piece = lax.all_gather(piece, "tensor", axis=0)
        else:
            piece = piece[None]
        return lax.all_gather(piece, "section", axis=0)

    attn_piece = jnp.concatenate(
        [chosen_cols(qkv_weight[0], cols), chosen_rows(out_weight[0], cols)[None]]
    )
    feed_piece = jnp.stack(
        [chosen_cols(up_weight[0], hidden), chosen_rows(down_weight[0], hidden)]
    )
    attn_all = spread_weights(attn_piece)
    feed_all = spread_weights(feed_piece)
    fan = attn_all.shape[1]

    def pad_rows(array, count):
        return jnp.pad(array, ((0, count - array.shape[0]), (0, width - array.shape[1])))

    qv_piece = lax.dynamic_slice_in_dim(qv_bias[0], cut_index * cols, cols, 1)
    up_piece = lax.dynamic_slice_in_dim(up_bias[0], cut_index * hidden, hidden, 0)
    small = jnp.concatenate(
        [
            outer_gain,
            outer_bias,
            norm_gain[0],
            norm_bias[0],
            row_bias[0],
            pad_rows(qv_piece, 2),
            pad_rows(up_piece[None], 6),
        ]
    )
    if planes:
        small_all = gather(Group(("section", "tensor"), (sections, shards)), small, 2)
        small_all = small_all.reshape((sections, shards) + small.shape)
    else:
        small_all = gather(by_section, small, 2)[:, None]
    outer_gains = [small_all[l, 0, 0] for l in range(layers)]
    outer_offsets = [small_all[l, 0, 1] for l in range(layers)]
    params = []
    for l in range(layers):
        attn = jnp.swapaxes(attn_all[l], 0, 1).reshape(4, fan * cols, width)
        feed = jnp.swapaxes(feed_all[l], 0, 1).reshape(2, fan * hidden, width)
        params.append(
            dict(
                gains=small_all[l, 0, 2:4],
                offsets=small_all[l, 0, 4:6],
                row_bias=small_all[l, 0, 6:8],
                q=attn[0],
                k=attn[1],
                v=attn[2],
                o=attn[3],
                up=feed[0],
                down=feed[1],
                q_bias=small_all[l, :, 8, :cols].reshape(-1),
                v_bias=small_all[l, :, 9, :cols].reshape(-1),
                up_bias=small_all[l, :, 10, :hidden].reshape(-1),
            )
        )
    head_number = (
        (jnp.arange(fan)[:, None] if planes else z) * (local_cols // HEAD_DIM)
        + cut_index * (cols // HEAD_DIM)
        + jnp.arange(cols // HEAD_DIM)
    ).reshape(-1)
    slopes = jnp.exp2(-8.0 * (head_number + 1).astype(F32) / HEADS)

    def whole(block):
        return gather(team, block.astype(BF16), 3).reshape(seq, width)

    def summed(terms):
        return scatter_sum(team, terms.astype(BF16).reshape(team.count, part, width), 4)

    local_ids = ids - vocab_start
    inside = (local_ids >= 0) & (local_ids < vocab)
    looked = jnp.where(
        inside[:, None], jnp.take(embedding, jnp.clip(local_ids, 0, vocab - 1), axis=0), 0
    )
    group_part = looked.shape[0] // shards
    x = scatter_sum(by_tensor, looked.reshape(shards, group_part, width), 5)
    h = layer_norm(x, outer_gains[0], outer_offsets[0])

    kept = []
    for p in params:
        normed = whole(layer_norm(h, p["gains"][0], p["offsets"][0]))
        q = (matmul_t(normed, p["q"]) + p["q_bias"]).astype(BF16)
        k = matmul_t(normed, p["k"]).astype(BF16)
        v = (matmul_t(normed, p["v"]) + p["v_bias"]).astype(BF16)
        mixed, lse = attend(length, slopes, q, k, v)
        middle = h + summed(matmul(mixed, p["o"])) + p["row_bias"][0]
        second = whole(layer_norm(middle, p["gains"][1], p["offsets"][1]))
        before = matmul_t(second, p["up"]) + p["up_bias"]
        active = gelu_tanh(before).astype(BF16)
        kept.append((h, normed, q, k, v, mixed, lse, middle, second, before, active))
        h = middle + summed(matmul(active, p["down"])) + p["row_bias"][1]

    final = gather(by_tensor, layer_norm(h, outer_gains[-1], outer_offsets[-1]).astype(BF16), 6)
    final = final.reshape(-1, width)
    tokens = final.shape[0]
    hits = jnp.arange(vocab)[None, :] == (targets - vocab_start)[:, None]
    logits = matmul_t(final, embedding)
    top = jnp.max(logits, axis=-1)
    total = jnp.sum(jnp.exp(logits - top[:, None]), axis=-1)
    pick = jnp.sum(jnp.where(hits, logits, 0.0), axis=-1)
    stats = gather(by_tensor, pad_rows(jnp.stack([top, total, pick]), 8), 7)
    top_all = jnp.max(stats[:, 0], axis=0)
    log_norm = top_all + jnp.log(jnp.sum(stats[:, 1] * jnp.exp(stats[:, 0] - top_all), axis=0))
    terms = jnp.where(valid, log_norm - jnp.sum(stats[:, 2], axis=0), 0.0)
    loss_part = jnp.sum(
        lax.dynamic_index_in_dim(terms.reshape(shards, -1), z, 0, keepdims=False)
    )
    row_weight = jnp.where(valid, 1.0 / token_count, 0.0)
    grad_logits = (
        (jnp.exp(logits - log_norm[:, None]) - hits.astype(F32)) * row_weight[:, None]
    ).astype(BF16)
    grad_final = scatter_sum(
        by_tensor,
        matmul(grad_logits, embedding).astype(BF16).reshape(shards, group_part, width),
        5,
    )
    table = outer_sum(grad_logits, final)
    _, final_back = jax.vjp(layer_norm, h, outer_gains[-1], outer_offsets[-1])
    grad, final_gain, final_offset = final_back(grad_final)

    layer_grads, small_rows = [None] * layers, [None] * layers
    for l in reversed(range(layers)):
        p = params[l]
        section_in, normed, q, k, v, mixed, lse, middle, second, before, active = kept[l]
        grad_down_full = whole(grad)
        g_down = outer_sum(active, grad_down_full)
        _, gelu_back = jax.vjp(gelu_tanh, before)
        grad_before = gelu_back(matmul_t(grad_down_full, p["down"]))[0]
        before_low = grad_before.astype(BF16)
        g_up = outer_sum(before_low, second)
        _, norm_back = jax.vjp(layer_norm, middle, p["gains"][1], p["offsets"][1])
        grad_mid, gain_two, offset_two = norm_back(summed(matmul(before_low, p["up"])))
        grad_mid = grad_mid + grad
        grad_mid_full = whole(grad_mid)
        g_out = outer_sum(mixed, grad_mid_full)
        grad_mixed = matmul_t(grad_mid_full, p["o"]).astype(BF16)
        gq, gk, gv = attend_back(length, slopes, q, k, v, grad_mixed, lse)
        gq_sum, gv_sum = jnp.sum(gq, axis=0), jnp.sum(gv, axis=0)
        gq, gk, gv = gq.astype(BF16), gk.astype(BF16), gv.astype(BF16)
        g_qkvo = [outer_sum(gq, normed), outer_sum(gk, normed), outer_sum(gv, normed), g_out]
        back = matmul(gq, p["q"]) + matmul(gk, p["k"]) + matmul(gv, p["v"])
        _, norm_back = jax.vjp(layer_norm, section_in, p["gains"][0], p["offsets"][0])
        grad_in, gain_one, offset_one = norm_back(summed(back))
        bias_two = jnp.sum(grad, axis=0)
        grad = grad_in + grad_mid
        layer_grads[l] = jnp.concatenate(
            [g.reshape(fan, cols, width) for g in g_qkvo]
            + [g_up.reshape(fan, hidden, width), g_down.reshape(fan, hidden, width)],
            axis=1,
        )

        def placed(values, size, full):
            out = jnp.zeros((fan if planes else shards, cut, size), F32)
            if planes:
                return lax.dynamic_update_slice(
                    out, values.reshape(fan, 1, size), (0, j, 0)
                ).reshape(-1)
            return lax.dynamic_update_slice(
                out, values.reshape(1, 1, size), (z, 0, 0)
            ).reshape(-1)

        small_rows[l] = [
            gain_one[None],
            gain_two[None],
            offset_one[None],
            offset_two[None],
            jnp.sum(grad_mid, axis=0)[None],
            bias_two[None],
            placed(gq_sum, cols, width).reshape(-1, width),
            placed(gv_sum, cols, width).reshape(-1, width),
            placed(jnp.sum(grad_before, axis=0), hidden, width).reshape(-1, width),
        ]

    _, embed_back = jax.vjp(layer_norm, x, outer_gains[0], outer_offsets[0])
    grad_rows, embed_gain, embed_offset = embed_back(grad)
    grad_rows = gather(by_tensor, grad_rows.astype(BF16), 6).reshape(tokens, width)
    table = table.at[jnp.clip(local_ids, 0, vocab - 1)].add(
        jnp.where(inside[:, None], grad_rows.astype(F32), 0.0)
    )

    packed = jnp.concatenate(
        [row for l in range(layers) for row in small_rows[l]]
        + [embed_gain[None], final_gain[None], embed_offset[None], final_offset[None]]
        + [jnp.broadcast_to(loss_part, (1, width))]
    )
    used = packed.shape[0]
    packed = jnp.pad(packed, ((0, -used % 8), (0, 0)))
    packed = all_sum([by_section, by_dp, by_tensor], packed, 8)
    per_layer = (used - 5) // layers
    mine = lax.dynamic_slice_in_dim(packed, s * per_layer, per_layer, 0)
    qv_rows = mine[6:8].reshape(2, -1)
    ff_row = mine[8:].reshape(-1)
    grad_qv = lax.dynamic_slice_in_dim(qv_rows, z * local_cols, local_cols, 1)
    grad_up_bias = lax.dynamic_slice_in_dim(ff_row, z * hidden * cut, hidden * cut, 0)
    base = per_layer * layers
    grad_outer_gain = lax.dynamic_slice_in_dim(packed, base + s, 1, 0)
    grad_outer_bias = lax.dynamic_slice_in_dim(packed, base + 2 + s, 1, 0)
    loss = packed[base + 4, 0] / token_count

    layer_sum = lax.psum_scatter(
        jnp.stack(layer_grads), "section", scatter_dimension=0, tiled=False
    )
    if planes:
        layer_sum = lax.psum_scatter(
            layer_sum.astype(BF16), "tensor", scatter_dimension=0, tiled=False
        )
        layer_sum = lax.all_gather(layer_sum, "dp", axis=0)
    else:
        layer_sum = lax.psum(layer_sum.astype(BF16), "dp")
    layer_sum = layer_sum.astype(F32)

    def as_cols(array):
        return jnp.moveaxis(array, 0, -2).swapaxes(-1, -3).swapaxes(-1, -2)

    def columns(array):
        return array.reshape(-1, width).T

    grad_qkv = jnp.stack(
        [columns(layer_sum[:, i * cols : (i + 1) * cols]) for i in range(3)]
    )
    grad_out_mat = layer_sum[:, 3 * cols : 4 * cols].reshape(-1, width)
    grad_up = columns(layer_sum[:, 4 * cols : 4 * cols + hidden])
    grad_down = layer_sum[:, 4 * cols + hidden :].reshape(-1, width)
    embed_sum = lax.psum(table.astype(BF16), ("section", "dp")).astype(F32)
    return (
        loss,
        embed_sum,
        grad_outer_gain,
        grad_outer_bias,
        mine[0:2][None],
        mine[2:4][None],
        grad_qkv[None],
        grad_qv[None],
        grad_out_mat[None],
        grad_up[None],
        grad_up_bias[None],
        grad_down[None],
        mine[4:6][None],
    )


def solution(mesh):
    return jax.shard_map(
        functools.partial(per_device, dict(mesh.shape)),
        mesh=mesh,
        in_specs=(
            P("dp", None),
            P("dp", None),
            P(),
            P("tensor", None),
            P("section", None),
            P("section", None),
            P("section", None, None),
            P("section", None, None),
            P("section", None, None, "tensor"),
            P("section", None, "tensor"),
            P("section", "tensor", None),
            P("section", None, "tensor"),
            P("section", "tensor"),
            P("section", "tensor", None),
            P("section", None, None),
        ),
        out_specs=(
            P(),
            P("tensor", None),
            P("section", None),
            P("section", None),
            P("section", None, None),
            P("section", None, None),
            P("section", None, None, "tensor"),
            P("section", None, "tensor"),
            P("section", "tensor", None),
            P("section", None, "tensor"),
            P("section", "tensor"),
            P("section", "tensor", None),
            P("section", None, None),
        ),
        check_vma=False,
    )
```

```python
import functools
import math

import jax
import jax.numpy as jnp
from jax import lax
from jax.experimental import pallas as pl
from jax.experimental.pallas import tpu as pltpu
from jax.sharding import PartitionSpec as P

HEADS = 16
HEAD_DIM = 64
EPS = 1e-05
NEG = -1e30
MESH = pl.DeviceIdType.MESH
F32 = jnp.float32
BF16 = jnp.bfloat16


def matmul(former, latter):
    return jnp.dot(former, latter, preferred_element_type=F32)


def matmul_t(former, latter):
    return lax.dot_general(
        former, latter, (((1,), (1,)), ((), ())), preferred_element_type=F32
    )


def outer_sum(former, latter):
    return lax.dot_general(
        former, latter, (((0,), (0,)), ((), ())), preferred_element_type=F32
    )


def layer_norm(inputs, weight, offset):
    centre = inputs - jnp.mean(inputs, axis=-1, keepdims=True)
    spread = jnp.mean(centre * centre, axis=-1, keepdims=True)
    return centre * lax.rsqrt(spread + EPS) * weight + offset


def gelu_tanh(inputs):
    return jax.nn.gelu(inputs, approximate=True)


class Group:
    def __init__(self, axes, sizes):
        self.axes = axes
        self.sizes = sizes
        self.count = math.prod(sizes)

    def me(self):
        place = 0
        for axis, size in zip(self.axes, self.sizes):
            place = place * size + lax.axis_index(axis)
        return place

    def device(self, place):
        spot = {}
        for axis, size in reversed(list(zip(self.axes, self.sizes))):
            spot[axis] = lax.rem(place, size)
            place = lax.div(place, size)
        return spot

    def peers(self):
        me = self.me()
        return [lax.rem(me + step, self.count) for step in range(1, self.count)]


def greet(groups):
    barrier = pltpu.get_barrier_semaphore()
    total = 0
    for group in groups:
        for peer in group.peers():
            pl.semaphore_signal(
                barrier, inc=1, device_id=group.device(peer), device_id_type=MESH
            )
            total += 1
    pl.semaphore_wait(barrier, total)


def send(group, peer, step, src, dst, send_sem, recv_sem):
    copy = pltpu.make_async_remote_copy(
        src_ref=src,
        dst_ref=dst,
        send_sem=send_sem.at[step],
        recv_sem=recv_sem.at[step],
        device_id=group.device(peer),
        device_id_type=MESH,
    )
    copy.start()
    return copy


def tie(*arrays):
    return lax.optimization_barrier(arrays)


class Job:
    def __init__(self, kind, groups, x, axis=0):
        self.kind, self.groups, self.x, self.axis = kind, groups, x, axis
        count = groups[0].count
        rest = x.shape[:axis] + x.shape[axis + 1 :]
        dma = pltpu.SemaphoreType.DMA
        self.in_spec = pl.BlockSpec(memory_space=pl.ANY)
        self.out_spec = pl.BlockSpec(memory_space=pl.ANY)
        self.scratch = [dma((count - 1,)), dma((count - 1,)), dma]
        if kind in ("gather", "spread"):
            self.in_spec = pl.BlockSpec(memory_space=pltpu.VMEM)
        if kind == "gather":
            self.out = jax.ShapeDtypeStruct((count,) + x.shape, x.dtype)
        elif kind == "spread":
            self.out = jax.ShapeDtypeStruct((groups[1].count, count) + x.shape, x.dtype)
            self.scratch += [dma((count,)), dma((count,))]
        elif kind == "deal":
            self.out = jax.ShapeDtypeStruct((count - 1,) + rest, x.dtype)
        else:
            self.out = jax.ShapeDtypeStruct(rest, F32)
            self.out_spec = pl.BlockSpec(memory_space=pltpu.VMEM)
            self.scratch += [pltpu.VMEM(rest, x.dtype), pltpu.VMEM((count - 1,) + rest, x.dtype)]

    def key(self):
        return (self.kind, tuple(g.axes for g in self.groups), self.x.shape, str(self.x.dtype), self.axis)

    def start(self, x, out, send_sem, recv_sem, own_sem, *more):
        group = self.groups[0]
        me = group.me()
        peers = list(enumerate(group.peers()))

        def block(place):
            return x.at[(slice(None),) * self.axis + (place,)]

        if self.kind == "gather":
            copies = [send(group, p, k, x, out.at[me], send_sem, recv_sem) for k, p in peers]
            own = pltpu.make_async_copy(x, out.at[me], own_sem)
            own.start()

            def finish():
                for copy in copies + [own]:
                    copy.wait()

        elif self.kind == "spread":
            pair = self.groups[1]
            side = pair.me()
            fw_send, fw_recv = more
            home = out.at[side, me]
            copies = [send(group, p, k, x, home, send_sem, recv_sem) for k, p in peers]
            last = group.count - 1
            passed = [send(pair, 1 - side, last, x, home, fw_send, fw_recv)]
            own = pltpu.make_async_copy(x, home, own_sem)
            own.start()

            def finish():
                for k, copy in enumerate(copies):
                    copy.wait_recv()
                    place = out.at[side, lax.rem(me + group.count - 1 - k, group.count)]
                    passed.append(send(pair, 1 - side, k, place, place, fw_send, fw_recv))
                for copy in passed:
                    copy.wait()
                for copy in copies:
                    copy.wait_send()
                own.wait()

        elif self.kind == "deal":
            copies = [send(group, p, k, block(p), out.at[k], send_sem, recv_sem) for k, p in peers]

            def finish():
                for copy in copies:
                    copy.wait()

        else:
            kept, slots = more
            copies = [send(group, p, k, block(p), slots.at[k], send_sem, recv_sem) for k, p in peers]
            own = pltpu.make_async_copy(block(me), kept, own_sem)
            own.start()

            def finish():
                own.wait()
                for copy in copies:
                    copy.wait()
                total = kept[...].astype(F32)
                for k in range(group.count - 1):
                    total = total + slots[k].astype(F32)
                out[...] = total

        return finish


def job_groups(jobs):
    return [group for job in jobs for group in job.groups]


def split_scratch(jobs, scratch):
    parts, at = [], 0
    for job in jobs:
        parts.append(scratch[at : at + len(job.scratch)])
        at += len(job.scratch)
    return parts


def exchange_body(jobs, *refs):
    count = len(jobs)
    greet(job_groups(jobs))
    parts = split_scratch(jobs, refs[2 * count :])
    ends = [
        job.start(refs[n], refs[count + n], *parts[n]) for n, job in enumerate(jobs)
    ]
    for end in ends:
        end()


class Exchanges:
    def __init__(self):
        self.idents = {}

    def ident(self, key):
        return self.idents.setdefault(key, len(self.idents))

    def __call__(self, *jobs):
        jobs = list(jobs)
        return pl.pallas_call(
            functools.partial(exchange_body, jobs),
            out_shape=tuple(job.out for job in jobs),
            in_specs=[job.in_spec for job in jobs],
            out_specs=tuple(job.out_spec for job in jobs),
            scratch_shapes=[one for job in jobs for one in job.scratch],
            compiler_params=pltpu.CompilerParams(
                collective_id=self.ident(tuple(job.key() for job in jobs)),
                has_side_effects=True,
                vmem_limit_bytes=32 * 2**20,
            ),
        )(*[job.x for job in jobs])


def all_sum_body(groups, x_ref, out_ref, *scratch):
    greet(groups)
    out_ref[...] = x_ref[...]
    count = len(groups)
    for number, group in enumerate(groups):
        kept, slots, send_sem, recv_sem = scratch[4 * number : 4 * number + 4]
        kept[...] = out_ref[...]
        copies = [
            send(group, peer, step, kept, slots.at[step], send_sem, recv_sem)
            for step, peer in enumerate(group.peers())
        ]
        for copy in copies:
            copy.wait()
        me = group.me()
        total = jnp.zeros_like(out_ref)
        for place in range(group.count):
            step = lax.rem(me - place + group.count, group.count) - 1
            term = slots[jnp.maximum(step, 0)]
            total = total + jnp.where(place == me, kept[...], term)
        out_ref[...] = total


def all_sum(groups, x, ident):
    groups = [group for group in groups if group.count > 1]
    scratch = []
    for group in groups:
        others = group.count - 1
        scratch += [
            pltpu.VMEM(x.shape, x.dtype),
            pltpu.VMEM((others,) + x.shape, x.dtype),
            pltpu.SemaphoreType.DMA((others,)),
            pltpu.SemaphoreType.DMA((others,)),
        ]
    return pl.pallas_call(
        functools.partial(all_sum_body, groups),
        out_shape=jax.ShapeDtypeStruct(x.shape, x.dtype),
        in_specs=[pl.BlockSpec(memory_space=pltpu.VMEM)],
        out_specs=pl.BlockSpec(memory_space=pltpu.VMEM),
        scratch_shapes=scratch,
        compiler_params=pltpu.CompilerParams(
            collective_id=ident, has_side_effects=True, vmem_limit_bytes=32 * 2**20
        ),
    )(x)


CHUNK = 256


def table_body(
    by_section, by_dp, jobs, g_ref, ids_ref, u_ref, gx_ref, *refs
):
    riders = len(jobs)
    xs, (out_ref, *outs), refs = refs[:riders], refs[riders : 2 * riders + 1], refs[2 * riders + 1 :]
    (g_buf, to_partner, from_partner, to_dp, from_dp, own, result,
    g_sem, ps_send, ps_recv, dp_send, dp_recv, ag_send, ag_recv, fw_send, fw_recv, own_sem,
    ) = refs[:17]
    s, j = by_section.me(), by_dp.me()
    partner = 1 - s
    peers = by_dp.peers() + [j]
    count = by_dp.count
    block = own.shape[0]
    subs = block // CHUNK
    tokens = u_ref.shape[0]
    greet([by_section, by_dp] + job_groups(jobs))
    parts = split_scratch(jobs, refs[17:])
    ends = [job.start(xs[n], outs[n], *parts[n]) for n, job in enumerate(jobs)]

    def chunk(half, place, sub):
        return (half * count + place) * subs + sub

    order = [(number, half) for number in range(count) for half in (0, 1)]

    def fetch(index, sub, slot):
        number, away = order[index]
        half = partner if away == 0 else s
        return pltpu.make_async_copy(
            g_ref.at[chunk(half, peers[number], sub)], g_buf.at[slot], g_sem.at[slot]
        )

    def remote(group, peer, number, sub, src, dst, send_sem, recv_sem):
        return pltpu.make_async_remote_copy(
            src_ref=src,
            dst_ref=dst,
            send_sem=send_sem.at[number, sub],
            recv_sem=recv_sem.at[number, sub],
            device_id=group.device(peer),
            device_id_type=MESH,
        )

    def rows(sub):
        return pl.ds(pl.multiple_of(sub * CHUNK, CHUNK), CHUNK)

    def partner_copy(number, sub):
        return remote(
            by_section, partner, number, sub,
            to_partner.at[number, rows(sub)], from_partner.at[number, rows(sub)],
            ps_send, ps_recv,
        )

    def chip_copy(number, sub):
        return remote(
            by_dp, peers[number], number, sub,
            to_dp.at[number, rows(sub)], from_dp.at[number, rows(sub)], dp_send, dp_recv,
        )

    def spread_copy(number, sub):
        return remote(
            by_dp, peers[number], number, sub,
            result.at[rows(sub)], out_ref.at[chunk(s, j, sub)], ag_send, ag_recv,
        )

    sources = [lax.rem(j + count - 1 - number, count) for number in range(count - 1)] + [j]

    def forward_copy(number, sub):
        target = out_ref.at[chunk(s, sources[number], sub)]
        origin = result.at[rows(sub)] if number == count - 1 else target
        return remote(by_section, partner, number, sub, origin, target, fw_send, fw_recv)

    def own_copy(sub):
        return pltpu.make_async_copy(
            result.at[rows(sub)], out_ref.at[chunk(s, j, sub)], own_sem.at[sub]
        )

    fetch(0, 0, 0).start()
    for index, (number, away) in enumerate(order):
        half = partner if away == 0 else s

        def one(sub, carry, index=index, number=number, away=away, half=half):
            slot = lax.rem(sub, 2)
            fetch(index, sub, slot).wait()

            @pl.when(sub + 1 < subs)
            def _():
                fetch(index, sub + 1, 1 - slot).start()

            if index + 1 < len(order):

                @pl.when(sub + 1 == subs)
                def _():
                    fetch(index + 1, 0, 1 - slot).start()

            base = chunk(half, peers[number], sub) * CHUNK
            place = base + lax.broadcasted_iota(jnp.int32, (tokens, CHUNK), 1)
            chosen = jnp.where(place == ids_ref[...], 1.0, 0.0).astype(BF16)
            term = outer_sum(g_buf[slot], u_ref[...]) + outer_sum(chosen, gx_ref[...])
            if away == 0:
                to_partner[number, rows(sub), :] = term.astype(BF16)
                partner_copy(number, sub).start()
            else:
                partner_copy(number, sub).wait_recv()
                term = term + from_partner[number, rows(sub), :].astype(F32)
                if number < count - 1:
                    to_dp[number, rows(sub), :] = term.astype(BF16)
                    chip_copy(number, sub).start()
                else:
                    own[rows(sub), :] = term
            return carry

        lax.fori_loop(0, subs, one, 0)

    def finish(sub, carry):
        term = own[rows(sub), :]
        for number in range(count - 1):
            chip_copy(number, sub).wait_recv()
            term = term + from_dp[number, rows(sub), :].astype(F32)
        result[rows(sub), :] = term.astype(BF16)
        for number in range(count - 1):
            spread_copy(number, sub).start()
        forward_copy(count - 1, sub).start()
        own_copy(sub).start()
        return carry

    lax.fori_loop(0, subs, finish, 0)

    def take(sub, carry):
        for number in range(count - 1):
            spread_copy(number, sub).wait_recv()
            forward_copy(number, sub).start()
        return carry

    lax.fori_loop(0, subs, take, 0)

    def drain(sub, carry):
        own_copy(sub).wait()
        for number in range(count):
            partner_copy(number, sub).wait_send()
            forward_copy(number, sub).wait()
        for number in range(count - 1):
            chip_copy(number, sub).wait_send()
            spread_copy(number, sub).wait_send()
        return carry

    lax.fori_loop(0, subs, drain, 0)
    for end in ends:
        end()


def table_sum(by_section, by_dp, jobs, grads, ids, final, grad_rows, ident):
    chunks, tokens, _ = grads.shape
    width = final.shape[1]
    count = by_dp.count
    subs = chunks // (2 * count)
    block = subs * CHUNK
    assert subs % 2 == 0
    vmem = pl.BlockSpec(memory_space=pltpu.VMEM)
    hbm = pl.BlockSpec(memory_space=pl.ANY)
    dma = pltpu.SemaphoreType.DMA
    return pl.pallas_call(
        functools.partial(table_body, by_section, by_dp, jobs),
        out_shape=(jax.ShapeDtypeStruct((chunks, CHUNK, width), BF16),)
        + tuple(job.out for job in jobs),
        in_specs=[hbm, vmem, vmem, vmem] + [job.in_spec for job in jobs],
        out_specs=(hbm,) + tuple(job.out_spec for job in jobs),
        scratch_shapes=[
            pltpu.VMEM((2, tokens, CHUNK), BF16),
            pltpu.VMEM((count, block, width), BF16),
            pltpu.VMEM((count, block, width), BF16),
            pltpu.VMEM((count - 1, block, width), BF16),
            pltpu.VMEM((count - 1, block, width), BF16),
            pltpu.VMEM((block, width), F32),
            pltpu.VMEM((block, width), BF16),
            dma((2,)),
            dma((count, subs)),
            dma((count, subs)),
            dma((count - 1, subs)),
            dma((count - 1, subs)),
            dma((count - 1, subs)),
            dma((count - 1, subs)),
            dma((count, subs)),
            dma((count, subs)),
            dma((subs,)),
        ]
        + [one for job in jobs for one in job.scratch],
        compiler_params=pltpu.CompilerParams(
            collective_id=ident, has_side_effects=True, vmem_limit_bytes=56 * 2**20
        ),
    )(grads, ids, final, grad_rows, *[job.x for job in jobs])


LANES = 128


def head_logits_body(u_ref, e_ref, ids_ref, logits_ref, top_ref, total_ref, pick_ref):
    step = pl.program_id(0)
    tokens, tile = logits_ref.shape[1:]

    @pl.when(step == 0)
    def _():
        top_ref[...] = jnp.full_like(top_ref, NEG)
        total_ref[...] = jnp.zeros_like(total_ref)
        pick_ref[...] = jnp.zeros_like(pick_ref)

    logits = matmul_t(u_ref[...], e_ref[...])
    logits_ref[0] = logits
    place = step * tile + lax.broadcasted_iota(jnp.int32, (tokens, tile), 1)
    picked = jnp.where(place == ids_ref[...], logits, 0.0)
    pieces = [logits[:, at : at + LANES] for at in range(0, tile, LANES)]
    before = top_ref[...]
    top = functools.reduce(jnp.maximum, pieces, before)
    total = total_ref[...] * jnp.exp(before - top)
    pick = pick_ref[...]
    for number, piece in enumerate(pieces):
        total = total + jnp.exp(piece - top)
        pick = pick + picked[:, number * LANES : (number + 1) * LANES]
    top_ref[...] = top
    total_ref[...] = total
    pick_ref[...] = pick


def head_logits(final, embedding, ids):
    tokens, width = final.shape
    vocab = embedding.shape[0]
    fixed = pl.BlockSpec((tokens, LANES), lambda step: (0, 0))
    stat = jax.ShapeDtypeStruct((tokens, LANES), F32)
    return pl.pallas_call(
        head_logits_body,
        grid=(vocab // CHUNK,),
        out_shape=(
            jax.ShapeDtypeStruct((vocab // CHUNK, tokens, CHUNK), F32), stat, stat, stat
        ),
        in_specs=[
            pl.BlockSpec((tokens, width), lambda step: (0, 0)),
            pl.BlockSpec((CHUNK, width), lambda step: (step, 0)),
            pl.BlockSpec((tokens, 1), lambda step: (0, 0)),
        ],
        out_specs=(
            pl.BlockSpec((1, tokens, CHUNK), lambda step: (step, 0, 0)), fixed, fixed, fixed
        ),
        compiler_params=pltpu.CompilerParams(vmem_limit_bytes=40 * 2**20),
        cost_estimate=pl.CostEstimate(
            flops=2 * tokens * vocab * width,
            bytes_accessed=4 * tokens * vocab + 2 * vocab * width,
            transcendentals=tokens * vocab,
        ),
    )(final, embedding, ids)


def head_grads_body(logits_ref, e_ref, ids_ref, norm_ref, weight_ref, grads_ref, back_ref, acc):
    step = pl.program_id(0)
    tokens, tile = grads_ref.shape[1:]

    @pl.when(step == 0)
    def _():
        acc[...] = jnp.zeros_like(acc)

    place = step * tile + lax.broadcasted_iota(jnp.int32, (tokens, tile), 1)
    probs = jnp.exp(logits_ref[0] - norm_ref[...])
    grads = (jnp.where(place == ids_ref[...], probs - 1.0, probs) * weight_ref[...]).astype(BF16)
    grads_ref[0] = grads
    acc[...] += matmul(grads, e_ref[...])

    @pl.when(step == pl.num_programs(0) - 1)
    def _():
        back_ref[...] = acc[...].astype(BF16)


def head_grads(logits, embedding, ids, norm, weight):
    chunks, tokens, _ = logits.shape
    vocab, width = embedding.shape
    column = pl.BlockSpec((tokens, 1), lambda step: (0, 0))
    tile = pl.BlockSpec((1, tokens, CHUNK), lambda step: (step, 0, 0))
    return pl.pallas_call(
        head_grads_body,
        grid=(chunks,),
        out_shape=(
            jax.ShapeDtypeStruct(logits.shape, BF16),
            jax.ShapeDtypeStruct((tokens, width), BF16),
        ),
        in_specs=[
            tile, pl.BlockSpec((CHUNK, width), lambda step: (step, 0)), column, column, column
        ],
        out_specs=(tile, pl.BlockSpec((tokens, width), lambda step: (0, 0))),
        scratch_shapes=[pltpu.VMEM((tokens, width), F32)],
        compiler_params=pltpu.CompilerParams(vmem_limit_bytes=40 * 2**20),
        cost_estimate=pl.CostEstimate(
            flops=2 * tokens * vocab * width,
            bytes_accessed=6 * tokens * vocab + 2 * vocab * width,
            transcendentals=tokens * vocab,
        ),
    )(logits, embedding, ids, norm, weight)


BLOCK = 256


def masked_scores(queries, keys, slope, length, first):
    rows, cols = queries.shape[0], keys.shape[0]
    raw = matmul_t(queries, keys)
    i = first + lax.broadcasted_iota(jnp.int32, (rows, cols), 0)
    j = lax.broadcasted_iota(jnp.int32, (rows, cols), 1)
    scores = raw * HEAD_DIM ** (-0.5) - slope * (i - j).astype(F32)
    return jnp.where((j <= i) & (j < length), scores, NEG)


SMEM = pl.BlockSpec(memory_space=pltpu.SMEM)
VMEM = pl.BlockSpec(memory_space=pltpu.VMEM)


def attend_body(
    length_ref, slope_ref, a_ref, qk_ref, vo_ref, bias_ref,
    q_ref, k_ref, v_ref, mixed_ref, lse_ref, part_ref,
):
    seq, width = q_ref.shape

    def project(step, carry):
        rows = pl.ds(pl.multiple_of(step * BLOCK, BLOCK), BLOCK)
        block = a_ref[rows, :]
        q_ref[rows, :] = (matmul_t(block, qk_ref[0]) + bias_ref[0:1, :]).astype(BF16)
        k_ref[rows, :] = matmul_t(block, qk_ref[1]).astype(BF16)
        v_ref[rows, :] = (matmul_t(block, vo_ref[0]) + bias_ref[1:2, :]).astype(BF16)
        return carry

    lax.fori_loop(0, seq // BLOCK, project, 0)
    for first in range(0, seq, BLOCK):
        upto = first + BLOCK
        for head in range(width // HEAD_DIM):
            lanes = slice(head * HEAD_DIM, (head + 1) * HEAD_DIM)
            scores = masked_scores(
                q_ref[first:upto, lanes], k_ref[:upto, lanes], slope_ref[head], length_ref[0], first
            )
            highest = jnp.max(scores, axis=-1, keepdims=True)
            powers = jnp.exp(scores - highest)
            total = jnp.sum(powers, axis=-1, keepdims=True)
            probs = (powers * (1.0 / total)).astype(BF16)
            mixed_ref[first:upto, lanes] = matmul(probs, v_ref[:upto, lanes]).astype(BF16)
            lse_ref[head, first:upto, :] = highest + jnp.log(total)
        part_ref[first:upto, :] = matmul(mixed_ref[first:upto, :], vo_ref[1]).astype(BF16)


def attend(length, slopes, a, qk, vo, bias):
    seq, model = a.shape
    width = qk.shape[1]
    low = jax.ShapeDtypeStruct((seq, width), BF16)
    return pl.pallas_call(
        attend_body,
        out_shape=(
            low, low, low, low,
            jax.ShapeDtypeStruct((width // HEAD_DIM, seq, 1), F32),
            jax.ShapeDtypeStruct((seq, model), BF16),
        ),
        in_specs=[SMEM, SMEM, VMEM, VMEM, VMEM, VMEM],
        out_specs=(VMEM,) * 6,
        compiler_params=pltpu.CompilerParams(vmem_limit_bytes=48 * 2**20),
    )(length, slopes, a, qk, vo, bias)


def attend_back_body(
    length_ref, slope_ref, gy_ref, a_ref, qk_ref, vo_ref, q_ref, k_ref, v_ref, mixed_ref, lse_ref,
    part_ref, grads_ref, sums_ref, go, gq, gk, gv, gk_sum, gv_sum,
):
    seq, width = q_ref.shape
    heads = width // HEAD_DIM
    gk_sum[...] = jnp.zeros_like(gk_sum)
    gv_sum[...] = jnp.zeros_like(gv_sum)

    def open_block(step, carry):
        rows = pl.ds(pl.multiple_of(step * BLOCK, BLOCK), BLOCK)
        go[rows, :] = matmul_t(gy_ref[rows, :], vo_ref[1]).astype(BF16)
        return carry

    lax.fori_loop(0, seq // BLOCK, open_block, 0)
    grads_ref[3] = outer_sum(mixed_ref[...], gy_ref[...])
    for head in range(heads):
        lanes = slice(head * HEAD_DIM, (head + 1) * HEAD_DIM)
        gq_total = jnp.zeros((1, HEAD_DIM), F32)
        for first in range(0, seq, BLOCK):
            upto = first + BLOCK
            queries, grads = q_ref[first:upto, lanes], go[first:upto, lanes]
            keys, values = k_ref[:upto, lanes], v_ref[:upto, lanes]
            scores = masked_scores(queries, keys, slope_ref[head], length_ref[0], first)
            probs = jnp.exp(scores - lse_ref[head, first:upto, :])
            grad_probs = matmul_t(grads, values)
            inner = jnp.sum(probs * grad_probs, axis=-1, keepdims=True)
            grad_scores = (probs * (grad_probs - inner) * HEAD_DIM ** (-0.5)).astype(BF16)
            block = matmul(grad_scores, keys)
            gq_total = gq_total + jnp.sum(block, axis=0, keepdims=True)
            gq[first:upto, lanes] = block.astype(BF16)
            gk_sum[:upto, lanes] += outer_sum(grad_scores, queries)
            gv_sum[:upto, lanes] += outer_sum(probs.astype(BF16), grads)
        sums_ref[0:1, lanes] = gq_total
    sums_ref[1:2, :] = jnp.sum(gv_sum[...], axis=0, keepdims=True)
    gk[...] = gk_sum[...].astype(BF16)
    gv[...] = gv_sum[...].astype(BF16)
    grads_ref[0] = outer_sum(gq[...], a_ref[...])
    grads_ref[1] = outer_sum(gv[...], a_ref[...])
    grads_ref[2] = outer_sum(gk[...], a_ref[...])

    def close_block(step, carry):
        rows = pl.ds(pl.multiple_of(step * BLOCK, BLOCK), BLOCK)
        part_ref[rows, :] = (
            matmul(gq[rows, :], qk_ref[0]) + matmul(gk[rows, :], qk_ref[1])
            + matmul(gv[rows, :], vo_ref[0])
        ).astype(BF16)
        return carry

    lax.fori_loop(0, seq // BLOCK, close_block, 0)


def attend_back(length, slopes, gy, a, qk, vo, q, k, v, mixed, lse):
    seq, model = a.shape
    width = qk.shape[1]
    return pl.pallas_call(
        attend_back_body,
        out_shape=(
            jax.ShapeDtypeStruct((seq, model), BF16),
            jax.ShapeDtypeStruct((4, width, model), F32),
            jax.ShapeDtypeStruct((2, width), F32),
        ),
        in_specs=[SMEM, SMEM] + [VMEM] * 9,
        out_specs=(VMEM,) * 3,
        scratch_shapes=[pltpu.VMEM((seq, width), BF16)] * 4 + [pltpu.VMEM((seq, width), F32)] * 2,
        compiler_params=pltpu.CompilerParams(vmem_limit_bytes=52 * 2**20),
    )(length, slopes, gy, a, qk, vo, q, k, v, mixed, lse)


GELU_A = 0.7978845608028654
GELU_B = 0.044715


def feed_body(c_ref, up_ref, down_ref, bias_ref, before_ref, part_ref, total):
    seq = c_ref.shape[0]
    units = up_ref.shape[0]
    tile = min(units, BLOCK)

    def one(step, carry):
        rows = pl.ds(pl.multiple_of(step * BLOCK, BLOCK), BLOCK)
        block = c_ref[rows, :]
        for first in range(0, units, tile):
            lanes = slice(first, first + tile)
            before = matmul_t(block, up_ref[lanes, :]) + bias_ref[:, lanes]
            before_ref[rows, lanes] = before
            bend = jnp.tanh(GELU_A * (before + GELU_B * before * before * before))
            active = (0.5 * before * (1.0 + bend)).astype(BF16)
            term = matmul(active, down_ref[lanes, :])
            if first == 0:
                total[...] = term
            else:
                total[...] += term
        part_ref[rows, :] = total[...].astype(BF16)
        return carry

    lax.fori_loop(0, seq // BLOCK, one, 0)


def feed(c, up, down, bias):
    seq, model = c.shape
    units = up.shape[0]
    return pl.pallas_call(
        feed_body,
        out_shape=(
            jax.ShapeDtypeStruct((seq, units), F32),
            jax.ShapeDtypeStruct((seq, model), BF16),
        ),
        in_specs=[VMEM] * 4,
        out_specs=(VMEM, VMEM),
        scratch_shapes=[pltpu.VMEM((BLOCK, model), F32)],
        compiler_params=pltpu.CompilerParams(vmem_limit_bytes=48 * 2**20),
    )(c, up, down, bias)


def feed_back_body(
    gz_ref, c_ref, before_ref, up_ref, down_ref, part_ref, grads_ref, sums_ref, active, low
):
    seq = c_ref.shape[0]
    units = up_ref.shape[0]
    tile = min(units, BLOCK)
    sums_ref[...] = jnp.zeros_like(sums_ref)

    def one(step, carry):
        rows = pl.ds(pl.multiple_of(step * BLOCK, BLOCK), BLOCK)
        gz = gz_ref[rows, :]
        for first in range(0, units, tile):
            lanes = slice(first, first + tile)
            before = before_ref[rows, lanes]
            square = before * before
            bend = jnp.tanh(GELU_A * before * (1.0 + GELU_B * square))
            half = 0.5 * (1.0 + bend)
            slope = half + 0.5 * before * (1.0 - bend * bend) * (
                GELU_A * (1.0 + 3.0 * GELU_B * square)
            )
            grad = matmul_t(gz, down_ref[lanes, :]) * slope
            sums_ref[:, lanes] += jnp.sum(grad, axis=0, keepdims=True)
            active[rows, lanes] = (before * half).astype(BF16)
            low[rows, lanes] = grad.astype(BF16)
        part_ref[rows, :] = matmul(low[rows, :], up_ref[...]).astype(BF16)
        return carry

    lax.fori_loop(0, seq // BLOCK, one, 0)
    for first in range(0, units, tile):
        lanes = slice(first, first + tile)
        grads_ref[0, lanes, :] = outer_sum(low[:, lanes], c_ref[...])
        grads_ref[1, lanes, :] = outer_sum(active[:, lanes], gz_ref[...])


def feed_back(gz, c, before, up, down):
    seq, model = c.shape
    units = up.shape[0]
    return pl.pallas_call(
        feed_back_body,
        out_shape=(
            jax.ShapeDtypeStruct((seq, model), BF16),
            jax.ShapeDtypeStruct((2, units, model), F32),
            jax.ShapeDtypeStruct((1, units), F32),
        ),
        in_specs=[VMEM] * 5,
        out_specs=(VMEM,) * 3,
        scratch_shapes=[pltpu.VMEM((seq, units), BF16)] * 2,
        compiler_params=pltpu.CompilerParams(vmem_limit_bytes=52 * 2**20),
    )(gz, c, before, up, down)


def per_device(
    mesh_shape,
    token_ids,
    target_ids,
    lengths,
    embedding,
    outer_gain,
    outer_bias,
    norm_gain,
    norm_bias,
    qkv_weight,
    qv_bias,
    out_weight,
    up_weight,
    up_bias,
    down_weight,
    row_bias,
):
    sections, groups, shards = (mesh_shape[name] for name in ("section", "dp", "tensor"))
    s, j, z = (lax.axis_index(name) for name in ("section", "dp", "tensor"))
    by_section = Group(("section",), (sections,))
    by_dp = Group(("dp",), (groups,))
    by_tensor = Group(("tensor",), (shards,))
    exchange = Exchanges()
    layers = sections
    vocab, width = embedding.shape
    seq = token_ids.shape[1]
    rows = token_ids.shape[0] * groups
    local_cols = qkv_weight.shape[-1]
    planes = rows == sections * shards and local_cols % (groups * HEAD_DIM) == 0
    team = by_dp if planes else by_tensor
    cut = groups if planes else 1
    fan = shards if planes else 1
    halves = 2 if planes else 1
    part = seq // team.count
    cols = local_cols // cut
    hidden = up_weight.shape[-1] // cut
    strip = hidden // halves
    cut_index = j if planes else 0
    my_row = z * sections + s if planes else j * sections + s
    length = lax.dynamic_slice(lengths, (my_row,), (1,))
    token_count = jnp.sum(lengths).astype(F32)
    vocab_start = z * vocab

    def chosen_cols(array, size):
        return lax.dynamic_slice_in_dim(array, cut_index * size, size, array.ndim - 1).T

    def chosen_rows(array, size):
        return lax.dynamic_slice_in_dim(array, cut_index * size, size, 0)

    def pad_rows(array, count):
        return jnp.pad(array, ((0, count - array.shape[0]), (0, width - array.shape[1])))

    sides = jnp.stack(
        [
            jnp.concatenate(
                [
                    chosen_cols(qkv_weight[0, 0], cols),
                    chosen_cols(qkv_weight[0, 2], cols),
                    chosen_cols(up_weight[0], hidden),
                ]
            ),
            jnp.concatenate(
                [
                    chosen_cols(qkv_weight[0, 1], cols),
                    chosen_rows(out_weight[0], cols),
                    chosen_rows(down_weight[0], hidden),
                ]
            ),
        ]
    )
    qv_piece = lax.dynamic_slice_in_dim(qv_bias[0], cut_index * cols, cols, 1)
    up_piece = lax.dynamic_slice_in_dim(up_bias[0], cut_index * hidden, hidden, 0)
    small = jnp.concatenate(
        [
            outer_gain,
            outer_bias,
            norm_gain[0],
            norm_bias[0],
            row_bias[0],
            pad_rows(qv_piece, 2),
            pad_rows(up_piece[None], 6),
        ]
    )

    def gather(group, x):
        return Job("gather", [group], x)

    def deal(group, x, axis=0):
        return Job("deal", [group], x, axis)

    def own_and_dealt(x, dealt, place, axis=0):
        own = lax.dynamic_index_in_dim(x, place, axis, keepdims=False).astype(F32)
        return own + jnp.sum(dealt.astype(F32), axis=0)

    if planes:
        other, both, small_all = exchange(
            deal(by_section, sides),
            gather(by_dp, jnp.stack([token_ids, target_ids])),
            gather(Group(("section", "tensor"), (sections, shards)), small),
        )
        small_all = small_all.reshape((sections, shards) + small.shape)
        own_side = lax.dynamic_index_in_dim(sides, s, 0, keepdims=False)
        side = [jnp.where(s == l, own_side, other[0]) for l in range(layers)]
        both = jnp.swapaxes(both, 0, 1).reshape(2, shards, sections, groups, part)
        both = lax.dynamic_index_in_dim(
            lax.dynamic_index_in_dim(both, s, 2, keepdims=False), j, 2, keepdims=False
        )
        ids, targets = both[0].reshape(-1), both[1].reshape(-1)
        group_lengths = lax.dynamic_index_in_dim(
            lengths.reshape(shards, sections), s, 1, keepdims=False
        )
        places = jnp.broadcast_to(j * part + jnp.arange(part), (shards, part))
        valid = (places < group_lengths[:, None]).reshape(-1)
    else:
        sides_all, small_all = exchange(gather(by_section, sides), gather(by_section, small))
        small_all = small_all[:, None]
        ids, targets = token_ids[s], target_ids[s]
        valid = jnp.arange(seq) < lengths[my_row]

    outer_gains = [small_all[l, 0, 0] for l in range(layers)]
    outer_offsets = [small_all[l, 0, 1] for l in range(layers)]
    params = []
    for l in range(layers):
        biases = [small_all[l, :, 8 + n, :cols].reshape(-1) for n in range(2)]
        units = small_all[l, :, 10, :hidden].reshape(fan, halves, strip)
        params.append(
            dict(
                gains=small_all[l, 0, 2:4],
                offsets=small_all[l, 0, 4:6],
                row_bias=small_all[l, 0, 6:8],
                bias=jnp.stack(biases),
                up_bias=jnp.swapaxes(units, 0, 1).reshape(1, -1),
            )
        )
        if not planes:
            block = sides_all[l]
            params[l].update(
                qk=block[:, :cols],
                vo=block[:, cols : 2 * cols],
                up=block[0, 2 * cols :],
                down=block[1, 2 * cols :],
            )
    head_number = (
        (jnp.arange(fan)[:, None] if planes else z) * (local_cols // HEAD_DIM)
        + cut_index * (cols // HEAD_DIM)
        + jnp.arange(cols // HEAD_DIM)
    ).reshape(-1)
    slopes = jnp.exp2(-8.0 * (head_number + 1).astype(F32) / HEADS)

    def attn_jobs(l):
        if not planes or l >= layers:
            return []
        return [
            Job("spread", [by_tensor, by_section], side[l][first : first + cols])
            for first in (0, cols)
        ]

    def feed_jobs(l, n):
        if not planes or l >= layers:
            return []
        first = 2 * cols + n * strip
        return [Job("spread", [by_tensor, by_section], side[l][first : first + strip])]

    def take_attn(l, got):
        if got:
            params[l]["qk"], params[l]["vo"] = (
                one.reshape(2, fan * cols, width) for one in got
            )

    def take_feed(l, got):
        if got:
            strips = [one.reshape(2, fan * strip, width) for one in got]
            params[l]["up"], params[l]["down"] = (
                jnp.concatenate([one[n] for one in strips]) for n in range(2)
            )

    def whole(block, *jobs):
        first, *got = exchange(gather(team, block.astype(BF16)), *jobs)
        return first.reshape(seq, width), got

    def summed(terms, *jobs):
        first, *got = exchange(
            Job("reduce", [team], terms.reshape(team.count, part, width)), *jobs
        )
        return first, got

    local_ids = ids - vocab_start
    inside = (local_ids >= 0) & (local_ids < vocab)
    looked = jnp.where(
        inside[:, None], jnp.take(embedding, jnp.clip(local_ids, 0, vocab - 1), axis=0), 0
    )
    group_part = looked.shape[0] // shards
    x, *got = exchange(
        Job("reduce", [by_tensor], looked.reshape(shards, group_part, width)), *attn_jobs(0)
    )
    take_attn(0, got)
    h = layer_norm(x, outer_gains[0], outer_offsets[0])

    kept = []
    strips = []
    for l, p in enumerate(params):
        normed, got = whole(
            layer_norm(h, p["gains"][0], p["offsets"][0]),
            *feed_jobs(l, 0 if l == 0 else 1),
        )
        strips += got
        q, k, v, mixed, lse, back = attend(length, slopes, normed, p["qk"], p["vo"], p["bias"])
        if l > 0:
            take_feed(l, strips)
        total, got = summed(back, *(feed_jobs(l, 1) if l == 0 else []))
        if l == 0:
            take_feed(l, strips + got)
        middle = h + total + p["row_bias"][0]
        second, got = whole(
            layer_norm(middle, p["gains"][1], p["offsets"][1]), *attn_jobs(l + 1)
        )
        take_attn(l + 1, got)
        before, back = feed(second, p["up"], p["down"], p["up_bias"])
        kept.append((h, normed, q, k, v, mixed, lse, middle, second, before))
        total, strips = summed(back, *feed_jobs(l + 1, 0))
        h = middle + total + p["row_bias"][1]

    (final,) = exchange(
        gather(by_tensor, layer_norm(h, outer_gains[-1], outer_offsets[-1]).astype(BF16))
    )
    final = final.reshape(-1, width)
    tokens = final.shape[0]
    columns_of = (targets - vocab_start)[:, None]
    logits, tops, totals, picks = head_logits(final, embedding, columns_of)
    top = jnp.max(tops, axis=1)
    total = jnp.sum(totals * jnp.exp(tops - top[:, None]), axis=1)
    pick = jnp.sum(picks, axis=1)
    (stats,) = exchange(
        gather(by_tensor, jnp.pad(jnp.stack([top, total, pick]), ((0, 5), (0, 0))))
    )
    top_all = jnp.max(stats[:, 0], axis=0)
    log_norm = top_all + jnp.log(jnp.sum(stats[:, 1] * jnp.exp(stats[:, 0] - top_all), axis=0))
    terms = jnp.where(valid, log_norm - jnp.sum(stats[:, 2], axis=0), 0.0)
    loss_part = jnp.sum(
        lax.dynamic_index_in_dim(terms.reshape(shards, -1), z, 0, keepdims=False)
    )
    row_weight = jnp.where(valid, 1.0 / token_count, 0.0)
    grad_logits, back = head_grads(
        logits, embedding, columns_of, log_norm[:, None], row_weight[:, None]
    )
    (grad_final,) = exchange(
        Job("reduce", [by_tensor], back.reshape(shards, group_part, width))
    )
    _, final_back = jax.vjp(layer_norm, h, outer_gains[-1], outer_offsets[-1])
    grad, final_gain, final_offset = final_back(grad_final)

    def section_jobs(pair):
        return [deal(by_section, one) for one in pair] if planes else []

    def section_sums(pair, got):
        out = []
        for one, dealt in zip(pair, got):
            low = own_and_dealt(one, dealt, s).astype(BF16)
            if one.ndim == 4:
                out.append(low.reshape(low.shape[0], fan, cols, width))
            else:
                out.append(low.reshape(halves, fan, strip, width))
        return out

    def tensor_jobs(lows):
        return [deal(by_tensor, low, 1) for low in lows]

    def tensor_sums(lows, got):
        return [
            own_and_dealt(low, dealt, z, 1).astype(BF16) for low, dealt in zip(lows, got)
        ]

    def spread_jobs(pieces):
        return [Job("spread", [by_dp, by_section], piece) for piece in pieces]

    small_rows = [None] * layers
    pairs = [None] * layers
    done = [None] * layers
    lows = None
    for l in reversed(range(layers)):
        p = params[l]
        section_in, normed, q, k, v, mixed, lse, middle, second, before = kept[l]
        late = planes and l + 1 < layers
        gz, got = whole(grad, *(section_jobs(pairs[l + 1]) if late else []))
        if late:
            lows = section_sums(pairs[l + 1], got)
        back, g_feed, up_sum = feed_back(gz, second, before, p["up"], p["down"])
        _, norm_back = jax.vjp(layer_norm, middle, p["gains"][1], p["offsets"][1])
        total, got_a = summed(back, *(tensor_jobs(lows[:1]) if late else []))
        grad_mid, gain_two, offset_two = norm_back(total)
        grad_mid = grad_mid + grad
        gy, got_b = whole(grad_mid, *(tensor_jobs(lows[1:]) if late else []))
        back, g_attn, qv_sum = attend_back(
            length, slopes, gy, normed, p["qk"], p["vo"], q, k, v, mixed, lse
        )
        if late:
            done[l + 1] = tensor_sums(lows, got_a + got_b)
        _, norm_back = jax.vjp(layer_norm, section_in, p["gains"][0], p["offsets"][0])
        total, got = summed(back)
        grad_in, gain_one, offset_one = norm_back(total)
        bias_two = jnp.sum(grad, axis=0)
        grad = grad_in + grad_mid
        pairs[l] = (g_attn.reshape((2, 2) + g_attn.shape[1:]), g_feed)

        def placed(values, size):
            out = jnp.zeros((fan if planes else shards, cut, size), F32)
            at = (0, j, 0) if planes else (z, 0, 0)
            return lax.dynamic_update_slice(out, values.reshape(fan, 1, size), at).reshape(
                -1, width
            )

        units = jnp.swapaxes(up_sum.reshape(halves, fan, strip), 0, 1)
        small_rows[l] = [
            gain_one[None],
            gain_two[None],
            offset_one[None],
            offset_two[None],
            jnp.sum(grad_mid, axis=0)[None],
            bias_two[None],
            placed(qv_sum[0], cols),
            placed(qv_sum[1], cols),
            placed(units, hidden),
        ]

    _, embed_back = jax.vjp(layer_norm, x, outer_gains[0], outer_offsets[0])
    grad_rows, embed_gain, embed_offset = embed_back(grad)
    jobs = [gather(by_tensor, grad_rows.astype(BF16))]
    if planes:
        jobs += section_jobs(pairs[0]) + spread_jobs(done[1])
    grad_rows, *got = exchange(*jobs)
    grad_rows = grad_rows.reshape(tokens, width)

    packed = jnp.concatenate(
        [row for l in range(layers) for row in small_rows[l]]
        + [embed_gain[None], final_gain[None], embed_offset[None], final_offset[None]]
        + [jnp.broadcast_to(loss_part, (1, width))]
    )
    used = packed.shape[0]
    packed = jnp.pad(packed, ((0, -used % 8), (0, 0)))
    packed = all_sum([by_section, by_dp, by_tensor], packed, exchange.ident("small"))
    jobs = []
    if planes:
        lows = section_sums(pairs[0], got[:2])
        spread_one = got[2:]
        jobs = tensor_jobs(lows)
    packed, grad_rows = tie(packed, grad_rows)
    embed_sum, *got = table_sum(
        by_section, by_dp, jobs, grad_logits, ids[:, None] - vocab_start, final, grad_rows,
        exchange.ident("table"),
    )
    if planes:
        spread_zero = exchange(*spread_jobs(tensor_sums(lows, got)))
        attn_sum, feed_sum = (
            jnp.where(s == 0, zero, one) for zero, one in zip(spread_zero, spread_one)
        )
    else:
        chosen = [
            lax.dynamic_index_in_dim(
                lax.psum(jnp.stack([pair[n] for pair in pairs]), ("section", "dp")),
                s, 0, keepdims=False,
            )
            for n in range(2)
        ]
        attn_sum = chosen[0][:, None]
        feed_sum = chosen[1][:, None, None]
    embed_sum = embed_sum.reshape(vocab, width).astype(F32)
    per_layer = (used - 5) // layers
    mine = lax.dynamic_slice_in_dim(packed, s * per_layer, per_layer, 0)
    qv_rows = mine[6:8].reshape(2, -1)
    ff_row = mine[8:].reshape(-1)
    grad_qv = lax.dynamic_slice_in_dim(qv_rows, z * local_cols, local_cols, 1)
    grad_up_bias = lax.dynamic_slice_in_dim(ff_row, z * hidden * cut, hidden * cut, 0)
    base = per_layer * layers
    grad_outer_gain = lax.dynamic_slice_in_dim(packed, base + s, 1, 0)
    grad_outer_bias = lax.dynamic_slice_in_dim(packed, base + 2 + s, 1, 0)
    loss = packed[base + 4, 0] / token_count

    def columns(array):
        return array.astype(F32).reshape(-1, width).T

    grad_qkv = jnp.stack(
        [columns(attn_sum[0, :, 0]), columns(attn_sum[1, :, 0]), columns(attn_sum[0, :, 1])]
    )
    grad_out_mat = attn_sum[1, :, 1].astype(F32).reshape(-1, width)
    grad_up = columns(feed_sum[0])
    grad_down = feed_sum[1].astype(F32).reshape(-1, width)
    return (
        loss,
        embed_sum,
        grad_outer_gain,
        grad_outer_bias,
        mine[0:2][None],
        mine[2:4][None],
        grad_qkv[None],
        grad_qv[None],
        grad_out_mat[None],
        grad_up[None],
        grad_up_bias[None],
        grad_down[None],
        mine[4:6][None],
    )


def solution(mesh):
    return jax.shard_map(
        functools.partial(per_device, dict(mesh.shape)),
        mesh=mesh,
        in_specs=(
            P("dp", None),
            P("dp", None),
            P(),
            P("tensor", None),
            P("section", None),
            P("section", None),
            P("section", None, None),
            P("section", None, None),
            P("section", None, None, "tensor"),
            P("section", None, "tensor"),
            P("section", "tensor", None),
            P("section", None, "tensor"),
            P("section", "tensor"),
            P("section", "tensor", None),
            P("section", None, None),
        ),
        out_specs=(
            P(),
            P("tensor", None),
            P("section", None),
            P("section", None),
            P("section", None, None),
            P("section", None, None),
            P("section", None, None, "tensor"),
            P("section", None, "tensor"),
            P("section", "tensor", None),
            P("section", None, "tensor"),
            P("section", "tensor"),
            P("section", "tensor", None),
            P("section", None, None),
        ),
        check_vma=False,
    )
```

```python
import functools
import math

import jax
import jax.numpy as jnp
from jax import lax
from jax.experimental import pallas as pl
from jax.experimental.pallas import tpu as pltpu
from jax.sharding import PartitionSpec as P

HEADS = 16
HEAD_DIM = 64
EPS = 1e-05
NEG = -1e30
MESH = pl.DeviceIdType.MESH
F32 = jnp.float32
BF16 = jnp.bfloat16


def matmul(former, latter):
    return jnp.dot(former, latter, preferred_element_type=F32)


def matmul_t(former, latter):
    return lax.dot_general(
        former, latter, (((1,), (1,)), ((), ())), preferred_element_type=F32
    )


def outer_sum(former, latter):
    return lax.dot_general(
        former, latter, (((0,), (0,)), ((), ())), preferred_element_type=F32
    )


def layer_norm(inputs, weight, offset):
    centre = inputs - jnp.mean(inputs, axis=-1, keepdims=True)
    spread = jnp.mean(centre * centre, axis=-1, keepdims=True)
    return centre * lax.rsqrt(spread + EPS) * weight + offset


def gelu_tanh(inputs):
    return jax.nn.gelu(inputs, approximate=True)


class Group:
    def __init__(self, axes, sizes):
        self.axes = axes
        self.sizes = sizes
        self.count = math.prod(sizes)

    def me(self):
        place = 0
        for axis, size in zip(self.axes, self.sizes):
            place = place * size + lax.axis_index(axis)
        return place

    def device(self, place):
        spot = {}
        for axis, size in reversed(list(zip(self.axes, self.sizes))):
            spot[axis] = lax.rem(place, size)
            place = lax.div(place, size)
        return spot

    def peers(self):
        me = self.me()
        return [lax.rem(me + step, self.count) for step in range(1, self.count)]


def greet(groups):
    barrier = pltpu.get_barrier_semaphore()
    total = 0
    for group in groups:
        for peer in group.peers():
            pl.semaphore_signal(
                barrier, inc=1, device_id=group.device(peer), device_id_type=MESH
            )
            total += 1
    pl.semaphore_wait(barrier, total)


def send(group, peer, step, src, dst, send_sem, recv_sem):
    copy = pltpu.make_async_remote_copy(
        src_ref=src,
        dst_ref=dst,
        send_sem=send_sem.at[step],
        recv_sem=recv_sem.at[step],
        device_id=group.device(peer),
        device_id_type=MESH,
    )
    copy.start()
    return copy


def tie(*arrays):
    return lax.optimization_barrier(arrays)


class Job:
    def __init__(self, kind, groups, x, axis=0):
        self.kind, self.groups, self.x, self.axis = kind, groups, x, axis
        count = groups[0].count
        rest = x.shape[:axis] + x.shape[axis + 1 :]
        dma = pltpu.SemaphoreType.DMA
        self.in_spec = pl.BlockSpec(memory_space=pl.ANY)
        self.out_spec = pl.BlockSpec(memory_space=pl.ANY)
        self.scratch = [dma((count - 1,)), dma((count - 1,)), dma]
        if kind in ("gather", "spread"):
            self.in_spec = pl.BlockSpec(memory_space=pltpu.VMEM)
        if kind == "gather":
            self.out = jax.ShapeDtypeStruct((count,) + x.shape, x.dtype)
        elif kind == "spread":
            self.out = jax.ShapeDtypeStruct((groups[1].count, count) + x.shape, x.dtype)
            self.scratch += [dma((count,)), dma((count,))]
        elif kind == "deal":
            self.out = jax.ShapeDtypeStruct((count - 1,) + rest, x.dtype)
        else:
            self.out = jax.ShapeDtypeStruct(rest, F32)
            self.out_spec = pl.BlockSpec(memory_space=pltpu.VMEM)
            self.scratch += [pltpu.VMEM(rest, x.dtype), pltpu.VMEM((count - 1,) + rest, x.dtype)]

    def key(self):
        return (self.kind, tuple(g.axes for g in self.groups), self.x.shape, str(self.x.dtype), self.axis)

    def start(self, x, out, send_sem, recv_sem, own_sem, *more):
        group = self.groups[0]
        me = group.me()
        peers = list(enumerate(group.peers()))

        def block(place):
            return x.at[(slice(None),) * self.axis + (place,)]

        if self.kind == "gather":
            copies = [send(group, p, k, x, out.at[me], send_sem, recv_sem) for k, p in peers]
            own = pltpu.make_async_copy(x, out.at[me], own_sem)
            own.start()

            def finish():
                for copy in copies + [own]:
                    copy.wait()

        elif self.kind == "spread":
            pair = self.groups[1]
            side = pair.me()
            fw_send, fw_recv = more
            home = out.at[side, me]
            copies = [send(group, p, k, x, home, send_sem, recv_sem) for k, p in peers]
            last = group.count - 1
            passed = [send(pair, 1 - side, last, x, home, fw_send, fw_recv)]
            own = pltpu.make_async_copy(x, home, own_sem)
            own.start()

            def finish():
                for k, copy in enumerate(copies):
                    copy.wait_recv()
                    place = out.at[side, lax.rem(me + group.count - 1 - k, group.count)]
                    passed.append(send(pair, 1 - side, k, place, place, fw_send, fw_recv))
                for copy in passed:
                    copy.wait()
                for copy in copies:
                    copy.wait_send()
                own.wait()

        elif self.kind == "deal":
            copies = [send(group, p, k, block(p), out.at[k], send_sem, recv_sem) for k, p in peers]

            def finish():
                for copy in copies:
                    copy.wait()

        else:
            kept, slots = more
            copies = [send(group, p, k, block(p), slots.at[k], send_sem, recv_sem) for k, p in peers]
            own = pltpu.make_async_copy(block(me), kept, own_sem)
            own.start()

            def finish():
                own.wait()
                for copy in copies:
                    copy.wait()
                total = kept[...].astype(F32)
                for k in range(group.count - 1):
                    total = total + slots[k].astype(F32)
                out[...] = total

        return finish


def job_groups(jobs):
    return [group for job in jobs for group in job.groups]


def split_scratch(jobs, scratch):
    parts, at = [], 0
    for job in jobs:
        parts.append(scratch[at : at + len(job.scratch)])
        at += len(job.scratch)
    return parts


def exchange_body(jobs, *refs):
    count = len(jobs)
    greet(job_groups(jobs))
    parts = split_scratch(jobs, refs[2 * count :])
    ends = [
        job.start(refs[n], refs[count + n], *parts[n]) for n, job in enumerate(jobs)
    ]
    for end in ends:
        end()


class Exchanges:
    def __init__(self):
        self.idents = {}

    def ident(self, key):
        return self.idents.setdefault(key, len(self.idents))

    def __call__(self, *jobs):
        jobs = list(jobs)
        return pl.pallas_call(
            functools.partial(exchange_body, jobs),
            out_shape=tuple(job.out for job in jobs),
            in_specs=[job.in_spec for job in jobs],
            out_specs=tuple(job.out_spec for job in jobs),
            scratch_shapes=[one for job in jobs for one in job.scratch],
            compiler_params=pltpu.CompilerParams(
                collective_id=self.ident(tuple(job.key() for job in jobs)),
                has_side_effects=True,
                vmem_limit_bytes=32 * 2**20,
            ),
        )(*[job.x for job in jobs])


CHUNK = 256


def table_body(
    by_section, by_dp, jobs, g_ref, ids_ref, u_ref, gx_ref, *refs
):
    riders = len(jobs)
    xs, (out_ref, *outs), refs = refs[:riders], refs[riders : 2 * riders + 1], refs[2 * riders + 1 :]
    (g_buf, to_partner, from_partner, to_dp, from_dp, own, result,
    g_sem, ps_send, ps_recv, dp_send, dp_recv, ag_send, ag_recv, fw_send, fw_recv, own_sem,
    ) = refs[:17]
    s, j = by_section.me(), by_dp.me()
    partner = 1 - s
    peers = by_dp.peers() + [j]
    count = by_dp.count
    block = own.shape[0]
    subs = block // CHUNK
    tokens = u_ref.shape[0]
    greet([by_section, by_dp] + job_groups(jobs))
    parts = split_scratch(jobs, refs[17:])
    ends = [job.start(xs[n], outs[n], *parts[n]) for n, job in enumerate(jobs)]

    def chunk(half, place, sub):
        return (half * count + place) * subs + sub

    order = [(number, half) for number in range(count) for half in (0, 1)]

    def fetch(index, sub, slot):
        number, away = order[index]
        half = partner if away == 0 else s
        return pltpu.make_async_copy(
            g_ref.at[chunk(half, peers[number], sub)], g_buf.at[slot], g_sem.at[slot]
        )

    def remote(group, peer, number, sub, src, dst, send_sem, recv_sem):
        return pltpu.make_async_remote_copy(
            src_ref=src,
            dst_ref=dst,
            send_sem=send_sem.at[number, sub],
            recv_sem=recv_sem.at[number, sub],
            device_id=group.device(peer),
            device_id_type=MESH,
        )

    def rows(sub):
        return pl.ds(pl.multiple_of(sub * CHUNK, CHUNK), CHUNK)

    def partner_copy(number, sub):
        return remote(
            by_section, partner, number, sub,
            to_partner.at[number, rows(sub)], from_partner.at[number, rows(sub)],
            ps_send, ps_recv,
        )

    def chip_copy(number, sub):
        return remote(
            by_dp, peers[number], number, sub,
            to_dp.at[number, rows(sub)], from_dp.at[number, rows(sub)], dp_send, dp_recv,
        )

    def spread_copy(number, sub):
        return remote(
            by_dp, peers[number], number, sub,
            result.at[rows(sub)], out_ref.at[chunk(s, j, sub)], ag_send, ag_recv,
        )

    sources = [lax.rem(j + count - 1 - number, count) for number in range(count - 1)] + [j]

    def forward_copy(number, sub):
        target = out_ref.at[chunk(s, sources[number], sub)]
        origin = result.at[rows(sub)] if number == count - 1 else target
        return remote(by_section, partner, number, sub, origin, target, fw_send, fw_recv)

    def own_copy(sub):
        return pltpu.make_async_copy(
            result.at[rows(sub)], out_ref.at[chunk(s, j, sub)], own_sem.at[sub]
        )

    fetch(0, 0, 0).start()
    for index, (number, away) in enumerate(order):
        half = partner if away == 0 else s

        def one(sub, carry, index=index, number=number, away=away, half=half):
            slot = lax.rem(sub, 2)
            fetch(index, sub, slot).wait()

            @pl.when(sub + 1 < subs)
            def _():
                fetch(index, sub + 1, 1 - slot).start()

            if index + 1 < len(order):

                @pl.when(sub + 1 == subs)
                def _():
                    fetch(index + 1, 0, 1 - slot).start()

            base = chunk(half, peers[number], sub) * CHUNK
            place = base + lax.broadcasted_iota(jnp.int32, (tokens, CHUNK), 1)
            chosen = jnp.where(place == ids_ref[...], 1.0, 0.0).astype(BF16)
            term = outer_sum(g_buf[slot], u_ref[...]) + outer_sum(chosen, gx_ref[...])
            if away == 0:
                to_partner[number, rows(sub), :] = term.astype(BF16)
                partner_copy(number, sub).start()
            else:
                partner_copy(number, sub).wait_recv()
                term = term + from_partner[number, rows(sub), :].astype(F32)
                if number < count - 1:
                    to_dp[number, rows(sub), :] = term.astype(BF16)
                    chip_copy(number, sub).start()
                else:
                    own[rows(sub), :] = term
            return carry

        lax.fori_loop(0, subs, one, 0)

    def finish(sub, carry):
        term = own[rows(sub), :]
        for number in range(count - 1):
            chip_copy(number, sub).wait_recv()
            term = term + from_dp[number, rows(sub), :].astype(F32)
        result[rows(sub), :] = term.astype(BF16)
        for number in range(count - 1):
            spread_copy(number, sub).start()
        forward_copy(count - 1, sub).start()
        own_copy(sub).start()
        return carry

    lax.fori_loop(0, subs, finish, 0)

    def take(sub, carry):
        for number in range(count - 1):
            spread_copy(number, sub).wait_recv()
            forward_copy(number, sub).start()
        return carry

    lax.fori_loop(0, subs, take, 0)

    def drain(sub, carry):
        own_copy(sub).wait()
        for number in range(count):
            partner_copy(number, sub).wait_send()
            forward_copy(number, sub).wait()
        for number in range(count - 1):
            chip_copy(number, sub).wait_send()
            spread_copy(number, sub).wait_send()
        return carry

    lax.fori_loop(0, subs, drain, 0)
    for end in ends:
        end()


def table_sum(by_section, by_dp, jobs, grads, ids, final, grad_rows, ident):
    chunks, tokens, _ = grads.shape
    width = final.shape[1]
    count = by_dp.count
    subs = chunks // (2 * count)
    block = subs * CHUNK
    assert subs % 2 == 0
    vmem = pl.BlockSpec(memory_space=pltpu.VMEM)
    hbm = pl.BlockSpec(memory_space=pl.ANY)
    dma = pltpu.SemaphoreType.DMA
    return pl.pallas_call(
        functools.partial(table_body, by_section, by_dp, jobs),
        out_shape=(jax.ShapeDtypeStruct((chunks, CHUNK, width), BF16),)
        + tuple(job.out for job in jobs),
        in_specs=[hbm, vmem, vmem, vmem] + [job.in_spec for job in jobs],
        out_specs=(hbm,) + tuple(job.out_spec for job in jobs),
        scratch_shapes=[
            pltpu.VMEM((2, tokens, CHUNK), BF16),
            pltpu.VMEM((count, block, width), BF16),
            pltpu.VMEM((count, block, width), BF16),
            pltpu.VMEM((count - 1, block, width), BF16),
            pltpu.VMEM((count - 1, block, width), BF16),
            pltpu.VMEM((block, width), F32),
            pltpu.VMEM((block, width), BF16),
            dma((2,)),
            dma((count, subs)),
            dma((count, subs)),
            dma((count - 1, subs)),
            dma((count - 1, subs)),
            dma((count - 1, subs)),
            dma((count - 1, subs)),
            dma((count, subs)),
            dma((count, subs)),
            dma((subs,)),
        ]
        + [one for job in jobs for one in job.scratch],
        compiler_params=pltpu.CompilerParams(
            collective_id=ident, has_side_effects=True, vmem_limit_bytes=56 * 2**20
        ),
    )(grads, ids, final, grad_rows, *[job.x for job in jobs])


LANES = 128


def head_logits_body(u_ref, e_ref, ids_ref, logits_ref, top_ref, total_ref, pick_ref):
    step = pl.program_id(0)
    tokens, tile = logits_ref.shape[1:]

    @pl.when(step == 0)
    def _():
        top_ref[...] = jnp.full_like(top_ref, NEG)
        total_ref[...] = jnp.zeros_like(total_ref)
        pick_ref[...] = jnp.zeros_like(pick_ref)

    logits = matmul_t(u_ref[...], e_ref[...])
    logits_ref[0] = logits
    place = step * tile + lax.broadcasted_iota(jnp.int32, (tokens, tile), 1)
    picked = jnp.where(place == ids_ref[...], logits, 0.0)
    pieces = [logits[:, at : at + LANES] for at in range(0, tile, LANES)]
    before = top_ref[...]
    top = functools.reduce(jnp.maximum, pieces, before)
    total = total_ref[...] * jnp.exp(before - top)
    pick = pick_ref[...]
    for number, piece in enumerate(pieces):
        total = total + jnp.exp(piece - top)
        pick = pick + picked[:, number * LANES : (number + 1) * LANES]
    top_ref[...] = top
    total_ref[...] = total
    pick_ref[...] = pick


def head_logits(final, embedding, ids):
    tokens, width = final.shape
    vocab = embedding.shape[0]
    fixed = pl.BlockSpec((tokens, LANES), lambda step: (0, 0))
    stat = jax.ShapeDtypeStruct((tokens, LANES), F32)
    return pl.pallas_call(
        head_logits_body,
        grid=(vocab // CHUNK,),
        out_shape=(
            jax.ShapeDtypeStruct((vocab // CHUNK, tokens, CHUNK), F32), stat, stat, stat
        ),
        in_specs=[
            pl.BlockSpec((tokens, width), lambda step: (0, 0)),
            pl.BlockSpec((CHUNK, width), lambda step: (step, 0)),
            pl.BlockSpec((tokens, 1), lambda step: (0, 0)),
        ],
        out_specs=(
            pl.BlockSpec((1, tokens, CHUNK), lambda step: (step, 0, 0)), fixed, fixed, fixed
        ),
        compiler_params=pltpu.CompilerParams(vmem_limit_bytes=40 * 2**20),
        cost_estimate=pl.CostEstimate(
            flops=2 * tokens * vocab * width,
            bytes_accessed=4 * tokens * vocab + 2 * vocab * width,
            transcendentals=tokens * vocab,
        ),
    )(final, embedding, ids)


def head_grads_body(logits_ref, e_ref, ids_ref, norm_ref, weight_ref, grads_ref, back_ref, acc):
    step = pl.program_id(0)
    tokens, tile = grads_ref.shape[1:]

    @pl.when(step == 0)
    def _():
        acc[...] = jnp.zeros_like(acc)

    place = step * tile + lax.broadcasted_iota(jnp.int32, (tokens, tile), 1)
    probs = jnp.exp(logits_ref[0] - norm_ref[...])
    grads = (jnp.where(place == ids_ref[...], probs - 1.0, probs) * weight_ref[...]).astype(BF16)
    grads_ref[0] = grads
    acc[...] += matmul(grads, e_ref[...])

    @pl.when(step == pl.num_programs(0) - 1)
    def _():
        back_ref[...] = acc[...].astype(BF16)


def head_grads(logits, embedding, ids, norm, weight):
    chunks, tokens, _ = logits.shape
    vocab, width = embedding.shape
    column = pl.BlockSpec((tokens, 1), lambda step: (0, 0))
    tile = pl.BlockSpec((1, tokens, CHUNK), lambda step: (step, 0, 0))
    return pl.pallas_call(
        head_grads_body,
        grid=(chunks,),
        out_shape=(
            jax.ShapeDtypeStruct(logits.shape, BF16),
            jax.ShapeDtypeStruct((tokens, width), BF16),
        ),
        in_specs=[
            tile, pl.BlockSpec((CHUNK, width), lambda step: (step, 0)), column, column, column
        ],
        out_specs=(tile, pl.BlockSpec((tokens, width), lambda step: (0, 0))),
        scratch_shapes=[pltpu.VMEM((tokens, width), F32)],
        compiler_params=pltpu.CompilerParams(vmem_limit_bytes=40 * 2**20),
        cost_estimate=pl.CostEstimate(
            flops=2 * tokens * vocab * width,
            bytes_accessed=6 * tokens * vocab + 2 * vocab * width,
            transcendentals=tokens * vocab,
        ),
    )(logits, embedding, ids, norm, weight)


BLOCK = 256


def masked_scores(queries, keys, slope, length, first):
    rows, cols = queries.shape[0], keys.shape[0]
    raw = matmul_t(queries, keys)
    i = first + lax.broadcasted_iota(jnp.int32, (rows, cols), 0)
    j = lax.broadcasted_iota(jnp.int32, (rows, cols), 1)
    scores = raw * HEAD_DIM ** (-0.5) - slope * (i - j).astype(F32)
    return jnp.where((j <= i) & (j < length), scores, NEG)


SMEM = pl.BlockSpec(memory_space=pltpu.SMEM)
VMEM = pl.BlockSpec(memory_space=pltpu.VMEM)


class TeamRows:
    def __init__(self, team, full, stage, slots, own, ag_send, ag_recv, rs_send, rs_recv):
        self.team, self.count, self.me = team, team.count, team.me()
        self.full, self.stage, self.slots, self.own = full, stage, slots, own
        self.sems = (ag_send, ag_recv, rs_send, rs_recv)

    def peer(self, step):
        return lax.rem(self.me + 1 + step, self.count)

    def source(self, step):
        return lax.rem(self.me + self.count - 1 - step, self.count)

    def remote(self, step, src, dst, send_sem, recv_sem):
        return pltpu.make_async_remote_copy(
            src_ref=src,
            dst_ref=dst,
            send_sem=send_sem.at[step],
            recv_sem=recv_sem.at[step],
            device_id=self.team.device(self.peer(step)),
            device_id_type=MESH,
        )

    def ag(self, step, x_ref):
        return self.remote(step, x_ref, self.full.at[self.me], self.sems[0], self.sems[1])

    def rs(self, step):
        return self.remote(
            step, self.stage.at[self.peer(step)], self.slots.at[step], self.sems[2], self.sems[3]
        )

    def send_rows(self, x_ref):
        for step in range(self.count - 1):
            self.ag(step, x_ref).start()
        self.full[self.me] = x_ref[...]

    def each_arrival(self, x_ref, work):
        work(self.me)

        def one(step, carry):
            self.ag(step, x_ref).wait_recv()
            work(self.source(step))
            return carry

        lax.fori_loop(0, self.count - 1, one, 0)

    def each_arrival_and_back(self, x_ref, term):
        self.own[...] = term(self.me)

        def one(step, carry):
            self.ag(step, x_ref).wait_recv()
            place = self.source(step)
            self.stage[place] = term(place).astype(BF16)
            self.rs(self.count - 2 - step).start()
            return carry

        lax.fori_loop(0, self.count - 1, one, 0)

    def finish(self, x_ref, total_ref):
        for step in range(self.count - 1):
            self.rs(step).wait()
        total = self.own[...]
        for step in range(self.count - 1):
            total = total + self.slots[step].astype(F32)
        total_ref[...] = total
        for step in range(self.count - 1):
            self.ag(step, x_ref).wait_send()


def team_scratch(team, part, model):
    count = team.count
    dma = pltpu.SemaphoreType.DMA
    return [
        pltpu.VMEM((count, part, model), BF16),
        pltpu.VMEM((count, part, model), BF16),
        pltpu.VMEM((count - 1, part, model), BF16),
        pltpu.VMEM((part, model), F32),
    ] + [dma((count - 1,))] * 4


def team_call(body, team, ident, jobs, arrays, specs, outs, out_specs, scratch):
    part, model = arrays[0].shape
    count_in, count_out, riders = len(arrays), len(outs), len(jobs)
    own_scratch = team_scratch(team, part, model)

    def kernel(*refs):
        ins, refs = refs[:count_in], refs[count_in:]
        xs, refs = refs[:riders], refs[riders:]
        results, refs = refs[:count_out], refs[count_out:]
        landings, refs = refs[:riders], refs[riders:]
        rows = TeamRows(team, *refs[: len(own_scratch)])
        refs = refs[len(own_scratch) :]
        mine, refs = refs[: len(scratch)], refs[len(scratch) :]
        greet([team] + job_groups(jobs))
        rows.send_rows(ins[0])
        parts = split_scratch(jobs, refs)
        ends = [job.start(xs[n], landings[n], *parts[n]) for n, job in enumerate(jobs)]
        body(rows, ins, results, mine)
        for end in ends:
            end()

    out = pl.pallas_call(
        kernel,
        out_shape=tuple(outs) + tuple(job.out for job in jobs),
        in_specs=list(specs) + [job.in_spec for job in jobs],
        out_specs=tuple(out_specs) + tuple(job.out_spec for job in jobs),
        scratch_shapes=own_scratch + list(scratch) + [one for job in jobs for one in job.scratch],
        compiler_params=pltpu.CompilerParams(
            collective_id=ident, has_side_effects=True, vmem_limit_bytes=58 * 2**20
        ),
    )(*arrays, *[job.x for job in jobs])
    return out[:count_out], list(out[count_out:])


def part_rows(place, part):
    return pl.ds(pl.multiple_of(place * part, part), part)


def attend_body(rows, ins, outs, scratch):
    x_ref, length_ref, slope_ref, qk_ref, vo_ref, bias_ref = ins
    total_ref, full_out, q_ref, k_ref, v_ref, mixed_ref, lse_ref = outs
    (full_sem,) = scratch
    part = x_ref.shape[0]
    width = q_ref.shape[1]

    def project(place):
        at = part_rows(place, part)
        block = rows.full[place]
        q_ref[at, :] = (matmul_t(block, qk_ref[0]) + bias_ref[0:1, :]).astype(BF16)
        k_ref[at, :] = matmul_t(block, qk_ref[1]).astype(BF16)
        v_ref[at, :] = (matmul_t(block, vo_ref[0]) + bias_ref[1:2, :]).astype(BF16)

    rows.each_arrival(x_ref, project)
    keep = pltpu.make_async_copy(rows.full, full_out, full_sem)
    keep.start()

    def one(step, carry):
        place = rows.peer(step)
        for block in range(rows.count):

            @pl.when(place == block)
            def _(first=block * part, upto=(block + 1) * part):
                for head in range(width // HEAD_DIM):
                    lanes = slice(head * HEAD_DIM, (head + 1) * HEAD_DIM)
                    scores = masked_scores(
                        q_ref[first:upto, lanes], k_ref[:upto, lanes], slope_ref[head],
                        length_ref[0], first,
                    )
                    highest = jnp.max(scores, axis=-1, keepdims=True)
                    powers = jnp.exp(scores - highest)
                    total = jnp.sum(powers, axis=-1, keepdims=True)
                    probs = (powers * (1.0 / total)).astype(BF16)
                    mixed_ref[first:upto, lanes] = matmul(probs, v_ref[:upto, lanes]).astype(BF16)
                    lse_ref[head, first:upto, :] = highest + jnp.log(total)

        term = matmul(mixed_ref[part_rows(place, part), :], vo_ref[1])

        @pl.when(step < rows.count - 1)
        def _():
            rows.stage[place] = term.astype(BF16)
            rows.rs(step).start()

        @pl.when(step == rows.count - 1)
        def _():
            rows.own[...] = term

        return carry

    lax.fori_loop(0, rows.count, one, 0)
    rows.finish(x_ref, total_ref)
    keep.wait()


HBM = pl.BlockSpec(memory_space=pl.ANY)


def attend(team, ident, jobs, x, length, slopes, qk, vo, bias):
    part, model = x.shape
    seq = part * team.count
    width = qk.shape[1]
    low = jax.ShapeDtypeStruct((seq, width), BF16)
    return team_call(
        attend_body, team, ident, jobs,
        [x, length, slopes, qk, vo, bias],
        [VMEM, SMEM, SMEM, VMEM, VMEM, VMEM],
        (
            jax.ShapeDtypeStruct((part, model), F32),
            jax.ShapeDtypeStruct((team.count, part, model), BF16),
            low, low, low, low,
            jax.ShapeDtypeStruct((width // HEAD_DIM, seq, 1), F32),
        ),
        (VMEM, HBM, VMEM, VMEM, VMEM, VMEM, VMEM),
        [pltpu.SemaphoreType.DMA],
    )


def attend_back_body(rows, ins, outs, scratch):
    gy_ref, length_ref, slope_ref, a_ref, qk_ref, vo_ref, q_ref, k_ref, v_ref, mixed_ref, lse_ref = ins
    total_ref, grads_ref, sums_ref = outs
    go, gq, gk, gv, gk_sum, gv_sum = scratch
    part = gy_ref.shape[0]
    seq, width = q_ref.shape
    heads = width // HEAD_DIM
    gk_sum[...] = jnp.zeros_like(gk_sum)
    gv_sum[...] = jnp.zeros_like(gv_sum)
    sums_ref[...] = jnp.zeros_like(sums_ref)

    def open_block(place):
        go[part_rows(place, part), :] = matmul_t(rows.full[place], vo_ref[1]).astype(BF16)

    rows.each_arrival(gy_ref, open_block)
    for block in reversed(range(rows.count)):
        first, upto = block * part, (block + 1) * part
        for head in range(heads):
            lanes = slice(head * HEAD_DIM, (head + 1) * HEAD_DIM)
            queries, grads = q_ref[first:upto, lanes], go[first:upto, lanes]
            keys, values = k_ref[:upto, lanes], v_ref[:upto, lanes]
            scores = masked_scores(queries, keys, slope_ref[head], length_ref[0], first)
            probs = jnp.exp(scores - lse_ref[head, first:upto, :])
            grad_probs = matmul_t(grads, values)
            inner = jnp.sum(probs * grad_probs, axis=-1, keepdims=True)
            grad_scores = (probs * (grad_probs - inner) * HEAD_DIM ** (-0.5)).astype(BF16)
            piece = matmul(grad_scores, keys)
            sums_ref[0:1, lanes] += jnp.sum(piece, axis=0, keepdims=True)
            gq[first:upto, lanes] = piece.astype(BF16)
            gk_sum[:upto, lanes] += outer_sum(grad_scores, queries)
            gv_sum[:upto, lanes] += outer_sum(probs.astype(BF16), grads)
        gk[first:upto, :] = gk_sum[first:upto, :].astype(BF16)
        gv[first:upto, :] = gv_sum[first:upto, :].astype(BF16)
        term = (
            matmul(gq[first:upto, :], qk_ref[0]) + matmul(gk[first:upto, :], qk_ref[1])
            + matmul(gv[first:upto, :], vo_ref[0])
        )

        @pl.when(rows.me != block)
        def _(block=block, term=term):
            rows.stage[block] = term.astype(BF16)
            rows.rs(lax.rem(block + rows.count - 1 - rows.me, rows.count)).start()

        @pl.when(rows.me == block)
        def _(term=term):
            rows.own[...] = term

    sums_ref[1:2, :] = jnp.sum(gv_sum[...], axis=0, keepdims=True)
    model = gy_ref.shape[1]
    grads_ref[3] = outer_sum(mixed_ref[...], rows.full[...].reshape(seq, model))
    grads_ref[0] = outer_sum(gq[...], a_ref[...])
    grads_ref[1] = outer_sum(gv[...], a_ref[...])
    grads_ref[2] = outer_sum(gk[...], a_ref[...])
    rows.finish(gy_ref, total_ref)


def attend_back(team, ident, jobs, gy, length, slopes, a, qk, vo, q, k, v, mixed, lse):
    part, model = gy.shape
    seq, width = q.shape
    return team_call(
        attend_back_body, team, ident, jobs,
        [gy, length, slopes, a, qk, vo, q, k, v, mixed, lse],
        [VMEM, SMEM, SMEM] + [VMEM] * 8,
        (
            jax.ShapeDtypeStruct((part, model), F32),
            jax.ShapeDtypeStruct((4, width, model), F32),
            jax.ShapeDtypeStruct((2, width), F32),
        ),
        (VMEM,) * 3,
        [pltpu.VMEM((seq, width), BF16)] * 4 + [pltpu.VMEM((seq, width), F32)] * 2,
    )


GELU_A = 0.7978845608028654
GELU_B = 0.044715


def feed_body(rows, ins, outs, scratch):
    x_ref, up_ref, down_ref, bias_ref = ins
    total_ref, full_out, before_ref = outs
    (full_sem,) = scratch
    part = x_ref.shape[0]
    units = up_ref.shape[0]
    tile = min(units, BLOCK)

    def term(place):
        at = part_rows(place, part)
        block = rows.full[place]
        total = None
        for first in range(0, units, tile):
            lanes = slice(first, first + tile)
            before = matmul_t(block, up_ref[lanes, :]) + bias_ref[:, lanes]
            before_ref[at, lanes] = before
            bend = jnp.tanh(GELU_A * (before + GELU_B * before * before * before))
            active = (0.5 * before * (1.0 + bend)).astype(BF16)
            piece = matmul(active, down_ref[lanes, :])
            total = piece if total is None else total + piece
        return total

    rows.each_arrival_and_back(x_ref, term)
    keep = pltpu.make_async_copy(rows.full, full_out, full_sem)
    keep.start()
    rows.finish(x_ref, total_ref)
    keep.wait()


def feed(team, ident, jobs, x, up, down, bias):
    part, model = x.shape
    units = up.shape[0]
    return team_call(
        feed_body, team, ident, jobs,
        [x, up, down, bias],
        [VMEM] * 4,
        (
            jax.ShapeDtypeStruct((part, model), F32),
            jax.ShapeDtypeStruct((team.count, part, model), BF16),
            jax.ShapeDtypeStruct((part * team.count, units), F32),
        ),
        (VMEM, HBM, VMEM),
        [pltpu.SemaphoreType.DMA],
    )


def feed_back_body(rows, ins, outs, scratch):
    gz_ref, c_ref, before_ref, up_ref, down_ref = ins
    total_ref, grads_ref, sums_ref = outs
    active, low = scratch
    part, model = gz_ref.shape
    seq = part * rows.count
    units = up_ref.shape[0]
    tile = min(units, BLOCK)
    sums_ref[...] = jnp.zeros_like(sums_ref)

    def term(place):
        at = part_rows(place, part)
        gz = rows.full[place]
        for first in range(0, units, tile):
            lanes = slice(first, first + tile)
            before = before_ref[at, lanes]
            square = before * before
            bend = jnp.tanh(GELU_A * before * (1.0 + GELU_B * square))
            half = 0.5 * (1.0 + bend)
            slope = half + 0.5 * before * (1.0 - bend * bend) * (
                GELU_A * (1.0 + 3.0 * GELU_B * square)
            )
            grad = matmul_t(gz, down_ref[lanes, :]) * slope
            sums_ref[:, lanes] += jnp.sum(grad, axis=0, keepdims=True)
            active[at, lanes] = (before * half).astype(BF16)
            low[at, lanes] = grad.astype(BF16)
        return matmul(low[at, :], up_ref[...])

    rows.each_arrival_and_back(gz_ref, term)
    for first in range(0, units, tile):
        lanes = slice(first, first + tile)
        grads_ref[0, lanes, :] = outer_sum(low[:, lanes], c_ref[...])
        grads_ref[1, lanes, :] = outer_sum(active[:, lanes], rows.full[...].reshape(seq, model))
    rows.finish(gz_ref, total_ref)


def feed_back(team, ident, jobs, gz, c, before, up, down):
    part, model = gz.shape
    seq = part * team.count
    units = up.shape[0]
    return team_call(
        feed_back_body, team, ident, jobs,
        [gz, c, before, up, down],
        [VMEM] * 5,
        (
            jax.ShapeDtypeStruct((part, model), F32),
            jax.ShapeDtypeStruct((2, units, model), F32),
            jax.ShapeDtypeStruct((1, units), F32),
        ),
        (VMEM,) * 3,
        [pltpu.VMEM((seq, units), BF16)] * 2,
    )


def per_device(
    mesh_shape,
    token_ids,
    target_ids,
    lengths,
    embedding,
    outer_gain,
    outer_bias,
    norm_gain,
    norm_bias,
    qkv_weight,
    qv_bias,
    out_weight,
    up_weight,
    up_bias,
    down_weight,
    row_bias,
):
    sections, groups, shards = (mesh_shape[name] for name in ("section", "dp", "tensor"))
    s, j, z = (lax.axis_index(name) for name in ("section", "dp", "tensor"))
    by_section = Group(("section",), (sections,))
    by_dp = Group(("dp",), (groups,))
    by_tensor = Group(("tensor",), (shards,))
    exchange = Exchanges()
    layers = sections
    vocab, width = embedding.shape
    seq = token_ids.shape[1]
    rows = token_ids.shape[0] * groups
    local_cols = qkv_weight.shape[-1]
    planes = rows == sections * shards and local_cols % (groups * HEAD_DIM) == 0
    team = by_dp if planes else by_tensor
    cut = groups if planes else 1
    fan = shards if planes else 1
    halves = 2 if planes else 1
    part = seq // team.count
    cols = local_cols // cut
    hidden = up_weight.shape[-1] // cut
    strip = hidden // halves
    cut_index = j if planes else 0
    my_row = z * sections + s if planes else j * sections + s
    length = lax.dynamic_slice(lengths, (my_row,), (1,))
    token_count = jnp.sum(lengths).astype(F32)
    vocab_start = z * vocab

    def chosen_cols(array, size):
        return lax.dynamic_slice_in_dim(array, cut_index * size, size, array.ndim - 1).T

    def chosen_rows(array, size):
        return lax.dynamic_slice_in_dim(array, cut_index * size, size, 0)

    def pad_rows(array, count):
        return jnp.pad(array, ((0, count - array.shape[0]), (0, width - array.shape[1])))

    sides = jnp.stack(
        [
            jnp.concatenate(
                [
                    chosen_cols(qkv_weight[0, 0], cols),
                    chosen_cols(qkv_weight[0, 2], cols),
                    chosen_cols(up_weight[0], hidden),
                ]
            ),
            jnp.concatenate(
                [
                    chosen_cols(qkv_weight[0, 1], cols),
                    chosen_rows(out_weight[0], cols),
                    chosen_rows(down_weight[0], hidden),
                ]
            ),
        ]
    )
    qv_piece = lax.dynamic_slice_in_dim(qv_bias[0], cut_index * cols, cols, 1)
    up_piece = lax.dynamic_slice_in_dim(up_bias[0], cut_index * hidden, hidden, 0)
    small = jnp.concatenate(
        [
            outer_gain,
            outer_bias,
            norm_gain[0],
            norm_bias[0],
            row_bias[0],
            pad_rows(qv_piece, 2),
            pad_rows(up_piece[None], 6),
        ]
    )

    def gather(group, x):
        return Job("gather", [group], x)

    def deal(group, x, axis=0):
        return Job("deal", [group], x, axis)

    def own_and_dealt(x, dealt, place, axis=0):
        own = lax.dynamic_index_in_dim(x, place, axis, keepdims=False).astype(F32)
        return own + jnp.sum(dealt.astype(F32), axis=0)

    if planes:
        other, both, small_all = exchange(
            deal(by_section, sides),
            gather(by_dp, jnp.stack([token_ids, target_ids])),
            gather(Group(("section", "tensor"), (sections, shards)), small),
        )
        small_all = small_all.reshape((sections, shards) + small.shape)
        own_side = lax.dynamic_index_in_dim(sides, s, 0, keepdims=False)
        side = [jnp.where(s == l, own_side, other[0]) for l in range(layers)]
        both = jnp.swapaxes(both, 0, 1).reshape(2, shards, sections, groups, part)
        both = lax.dynamic_index_in_dim(
            lax.dynamic_index_in_dim(both, s, 2, keepdims=False), j, 2, keepdims=False
        )
        ids, targets = both[0].reshape(-1), both[1].reshape(-1)
        group_lengths = lax.dynamic_index_in_dim(
            lengths.reshape(shards, sections), s, 1, keepdims=False
        )
        places = jnp.broadcast_to(j * part + jnp.arange(part), (shards, part))
        valid = (places < group_lengths[:, None]).reshape(-1)
    else:
        sides_all, small_all = exchange(gather(by_section, sides), gather(by_section, small))
        small_all = small_all[:, None]
        ids, targets = token_ids[s], target_ids[s]
        valid = jnp.arange(seq) < lengths[my_row]

    outer_gains = [small_all[l, 0, 0] for l in range(layers)]
    outer_offsets = [small_all[l, 0, 1] for l in range(layers)]
    params = []
    for l in range(layers):
        biases = [small_all[l, :, 8 + n, :cols].reshape(-1) for n in range(2)]
        units = small_all[l, :, 10, :hidden].reshape(fan, halves, strip)
        params.append(
            dict(
                gains=small_all[l, 0, 2:4],
                offsets=small_all[l, 0, 4:6],
                row_bias=small_all[l, 0, 6:8],
                bias=jnp.stack(biases),
                up_bias=jnp.swapaxes(units, 0, 1).reshape(1, -1),
            )
        )
        if not planes:
            block = sides_all[l]
            params[l].update(
                qk=block[:, :cols],
                vo=block[:, cols : 2 * cols],
                up=block[0, 2 * cols :],
                down=block[1, 2 * cols :],
            )
    head_number = (
        (jnp.arange(fan)[:, None] if planes else z) * (local_cols // HEAD_DIM)
        + cut_index * (cols // HEAD_DIM)
        + jnp.arange(cols // HEAD_DIM)
    ).reshape(-1)
    slopes = jnp.exp2(-8.0 * (head_number + 1).astype(F32) / HEADS)

    def attn_jobs(l):
        if not planes or l >= layers:
            return []
        return [
            Job("spread", [by_tensor, by_section], side[l][first : first + cols])
            for first in (0, cols)
        ]

    def feed_jobs(l, n):
        if not planes or l >= layers:
            return []
        first = 2 * cols + n * strip
        return [Job("spread", [by_tensor, by_section], side[l][first : first + strip])]

    def take_attn(l, got):
        if got:
            params[l]["qk"], params[l]["vo"] = (
                one.reshape(2, fan * cols, width) for one in got
            )

    def take_feed(l, got):
        if got:
            strips = [one.reshape(2, fan * strip, width) for one in got]
            params[l]["up"], params[l]["down"] = (
                jnp.concatenate([one[n] for one in strips]) for n in range(2)
            )

    def ident(kind, jobs):
        return exchange.ident((kind,) + tuple(job.key() for job in jobs))

    local_ids = ids - vocab_start
    inside = (local_ids >= 0) & (local_ids < vocab)
    looked = jnp.where(
        inside[:, None], jnp.take(embedding, jnp.clip(local_ids, 0, vocab - 1), axis=0), 0
    )
    group_part = looked.shape[0] // shards
    x, *got = exchange(
        Job("reduce", [by_tensor], looked.reshape(shards, group_part, width)), *attn_jobs(0)
    )
    take_attn(0, got)
    h = layer_norm(x, outer_gains[0], outer_offsets[0])

    kept = []
    strips = []
    for l, p in enumerate(params):
        jobs = (feed_jobs(l, 0) if l == 0 else []) + feed_jobs(l, 1)
        normed = layer_norm(h, p["gains"][0], p["offsets"][0]).astype(BF16)
        (total, normed, q, k, v, mixed, lse), got = attend(
            team, ident("attend", jobs), jobs, normed, length, slopes, p["qk"], p["vo"], p["bias"]
        )
        take_feed(l, strips + got)
        middle = h + total + p["row_bias"][0]
        jobs = attn_jobs(l + 1) + feed_jobs(l + 1, 0)
        second = layer_norm(middle, p["gains"][1], p["offsets"][1]).astype(BF16)
        (total, second, before), got = feed(
            team, ident("feed", jobs), jobs, second, p["up"], p["down"], p["up_bias"]
        )
        take_attn(l + 1, got[:2])
        strips = got[2:]
        kept.append((h, normed.reshape(seq, width), q, k, v, mixed, lse, middle, second, before))
        h = middle + total + p["row_bias"][1]

    (final,) = exchange(
        gather(by_tensor, layer_norm(h, outer_gains[-1], outer_offsets[-1]).astype(BF16))
    )
    final = final.reshape(-1, width)
    tokens = final.shape[0]
    columns_of = (targets - vocab_start)[:, None]
    logits, tops, totals, picks = head_logits(final, embedding, columns_of)
    top = jnp.max(tops, axis=1)
    total = jnp.sum(totals * jnp.exp(tops - top[:, None]), axis=1)
    pick = jnp.sum(picks, axis=1)
    (stats,) = exchange(
        gather(by_tensor, jnp.pad(jnp.stack([top, total, pick]), ((0, 5), (0, 0))))
    )
    top_all = jnp.max(stats[:, 0], axis=0)
    log_norm = top_all + jnp.log(jnp.sum(stats[:, 1] * jnp.exp(stats[:, 0] - top_all), axis=0))
    terms = jnp.where(valid, log_norm - jnp.sum(stats[:, 2], axis=0), 0.0)
    loss_part = jnp.sum(
        lax.dynamic_index_in_dim(terms.reshape(shards, -1), z, 0, keepdims=False)
    )
    row_weight = jnp.where(valid, 1.0 / token_count, 0.0)
    grad_logits, back = head_grads(
        logits, embedding, columns_of, log_norm[:, None], row_weight[:, None]
    )
    (grad_final,) = exchange(
        Job("reduce", [by_tensor], back.reshape(shards, group_part, width))
    )
    _, final_back = jax.vjp(layer_norm, h, outer_gains[-1], outer_offsets[-1])
    grad, final_gain, final_offset = final_back(grad_final)

    def section_jobs(pair):
        return [deal(by_section, one) for one in pair] if planes else []

    def section_sums(pair, got):
        out = []
        for one, dealt in zip(pair, got):
            low = own_and_dealt(one, dealt, s).astype(BF16)
            if one.ndim == 4:
                out.append(low.reshape(low.shape[0], fan, cols, width))
            else:
                out.append(low.reshape(halves, fan, strip, width))
        return out

    def tensor_jobs(lows):
        return [deal(by_tensor, low, 1) for low in lows]

    def tensor_sums(lows, got):
        return [
            own_and_dealt(low, dealt, z, 1).astype(BF16) for low, dealt in zip(lows, got)
        ]

    def spread_jobs(pieces):
        return [Job("spread", [by_dp, by_section], piece) for piece in pieces]

    small_rows = [None] * layers
    pairs = [None] * layers
    done = [None] * layers
    lows = None
    for l in reversed(range(layers)):
        p = params[l]
        section_in, normed, q, k, v, mixed, lse, middle, second, before = kept[l]
        late = planes and l + 1 < layers
        jobs = section_jobs(pairs[l + 1]) if late else []
        (total, g_feed, up_sum), got = feed_back(
            team, ident("feed back", jobs), jobs, grad.astype(BF16), second.reshape(seq, width),
            before, p["up"], p["down"],
        )
        if late:
            lows = section_sums(pairs[l + 1], got)
        _, norm_back = jax.vjp(layer_norm, middle, p["gains"][1], p["offsets"][1])
        grad_mid, gain_two, offset_two = norm_back(total)
        grad_mid = grad_mid + grad
        jobs = tensor_jobs(lows) if late else []
        (total, g_attn, qv_sum), got = attend_back(
            team, ident("attend back", jobs), jobs, grad_mid.astype(BF16), length, slopes, normed,
            p["qk"], p["vo"], q, k, v, mixed, lse,
        )
        if late:
            done[l + 1] = tensor_sums(lows, got)
        _, norm_back = jax.vjp(layer_norm, section_in, p["gains"][0], p["offsets"][0])
        grad_in, gain_one, offset_one = norm_back(total)
        bias_two = jnp.sum(grad, axis=0)
        grad = grad_in + grad_mid
        pairs[l] = (g_attn.reshape((2, 2) + g_attn.shape[1:]), g_feed)

        def placed(values, size):
            out = jnp.zeros((fan if planes else shards, cut, size), F32)
            at = (0, j, 0) if planes else (z, 0, 0)
            return lax.dynamic_update_slice(out, values.reshape(fan, 1, size), at).reshape(
                -1, width
            )

        units = jnp.swapaxes(up_sum.reshape(halves, fan, strip), 0, 1)
        small_rows[l] = [
            gain_one[None],
            gain_two[None],
            offset_one[None],
            offset_two[None],
            jnp.sum(grad_mid, axis=0)[None],
            bias_two[None],
            placed(qv_sum[0], cols),
            placed(qv_sum[1], cols),
            placed(units, hidden),
        ]

    _, embed_back = jax.vjp(layer_norm, x, outer_gains[0], outer_offsets[0])
    grad_rows, embed_gain, embed_offset = embed_back(grad)
    packed = jnp.concatenate(
        [row for l in range(layers) for row in small_rows[l]]
        + [embed_gain[None], final_gain[None], embed_offset[None], final_offset[None]]
        + [jnp.broadcast_to(loss_part, (1, width))]
    )
    used = packed.shape[0]
    packed = jnp.pad(packed, ((0, -used % 8), (0, 0)))
    jobs = [gather(by_tensor, grad_rows.astype(BF16)), gather(by_dp, packed)]
    if planes:
        jobs += section_jobs(pairs[0]) + spread_jobs(done[1])
    grad_rows, packed, *got = exchange(*jobs)
    grad_rows = grad_rows.reshape(tokens, width)
    packed = jnp.sum(packed, axis=0)
    jobs = [gather(Group(("section", "tensor"), (sections, shards)), packed)]
    if planes:
        lows = section_sums(pairs[0], got[:2])
        spread_one = got[2:]
        jobs += tensor_jobs(lows)
    embed_sum, packed, *got = table_sum(
        by_section, by_dp, jobs, grad_logits, ids[:, None] - vocab_start, final, grad_rows,
        exchange.ident("table"),
    )
    packed = jnp.sum(packed, axis=0)
    if planes:
        spread_zero = exchange(*spread_jobs(tensor_sums(lows, got)))
        attn_sum, feed_sum = (
            jnp.where(s == 0, zero, one) for zero, one in zip(spread_zero, spread_one)
        )
    else:
        chosen = [
            lax.dynamic_index_in_dim(
                lax.psum(jnp.stack([pair[n] for pair in pairs]), ("section", "dp")),
                s, 0, keepdims=False,
            )
            for n in range(2)
        ]
        attn_sum = chosen[0][:, None]
        feed_sum = chosen[1][:, None, None]
    embed_sum = embed_sum.reshape(vocab, width).astype(F32)
    per_layer = (used - 5) // layers
    mine = lax.dynamic_slice_in_dim(packed, s * per_layer, per_layer, 0)
    qv_rows = mine[6:8].reshape(2, -1)
    ff_row = mine[8:].reshape(-1)
    grad_qv = lax.dynamic_slice_in_dim(qv_rows, z * local_cols, local_cols, 1)
    grad_up_bias = lax.dynamic_slice_in_dim(ff_row, z * hidden * cut, hidden * cut, 0)
    base = per_layer * layers
    grad_outer_gain = lax.dynamic_slice_in_dim(packed, base + s, 1, 0)
    grad_outer_bias = lax.dynamic_slice_in_dim(packed, base + 2 + s, 1, 0)
    loss = packed[base + 4, 0] / token_count

    def columns(array):
        return array.astype(F32).reshape(-1, width).T

    grad_qkv = jnp.stack(
        [columns(attn_sum[0, :, 0]), columns(attn_sum[1, :, 0]), columns(attn_sum[0, :, 1])]
    )
    grad_out_mat = attn_sum[1, :, 1].astype(F32).reshape(-1, width)
    grad_up = columns(feed_sum[0])
    grad_down = feed_sum[1].astype(F32).reshape(-1, width)
    return (
        loss,
        embed_sum,
        grad_outer_gain,
        grad_outer_bias,
        mine[0:2][None],
        mine[2:4][None],
        grad_qkv[None],
        grad_qv[None],
        grad_out_mat[None],
        grad_up[None],
        grad_up_bias[None],
        grad_down[None],
        mine[4:6][None],
    )


def solution(mesh):
    return jax.shard_map(
        functools.partial(per_device, dict(mesh.shape)),
        mesh=mesh,
        in_specs=(
            P("dp", None),
            P("dp", None),
            P(),
            P("tensor", None),
            P("section", None),
            P("section", None),
            P("section", None, None),
            P("section", None, None),
            P("section", None, None, "tensor"),
            P("section", None, "tensor"),
            P("section", "tensor", None),
            P("section", None, "tensor"),
            P("section", "tensor"),
            P("section", "tensor", None),
            P("section", None, None),
        ),
        out_specs=(
            P(),
            P("tensor", None),
            P("section", None),
            P("section", None),
            P("section", None, None),
            P("section", None, None),
            P("section", None, None, "tensor"),
            P("section", None, "tensor"),
            P("section", "tensor", None),
            P("section", None, "tensor"),
            P("section", "tensor"),
            P("section", "tensor", None),
            P("section", None, None),
        ),
        check_vma=False,
    )
```

```python
import functools
import math

import jax
import jax.numpy as jnp
from jax import lax
from jax.experimental import pallas as pl
from jax.experimental.pallas import tpu as pltpu
from jax.sharding import PartitionSpec as P

HEADS = 16
HEAD_DIM = 64
EPS = 1e-05
NEG = -1e30
MESH = pl.DeviceIdType.MESH
F32 = jnp.float32
BF16 = jnp.bfloat16


def matmul(former, latter):
    return jnp.dot(former, latter, preferred_element_type=F32)


def matmul_t(former, latter):
    return lax.dot_general(
        former, latter, (((1,), (1,)), ((), ())), preferred_element_type=F32
    )


def outer_sum(former, latter):
    return lax.dot_general(
        former, latter, (((0,), (0,)), ((), ())), preferred_element_type=F32
    )


def layer_norm(inputs, weight, offset):
    centre = inputs - jnp.mean(inputs, axis=-1, keepdims=True)
    spread = jnp.mean(centre * centre, axis=-1, keepdims=True)
    return centre * lax.rsqrt(spread + EPS) * weight + offset


def gelu_tanh(inputs):
    return jax.nn.gelu(inputs, approximate=True)


class Group:
    def __init__(self, axes, sizes, square=False):
        self.square = square
        self.axes = axes
        self.sizes = sizes
        self.count = math.prod(sizes)

    def me(self):
        place = 0
        for axis, size in zip(self.axes, self.sizes):
            place = place * size + lax.axis_index(axis)
        return place

    def device(self, place):
        spot = {}
        for axis, size in reversed(list(zip(self.axes, self.sizes))):
            spot[axis] = lax.rem(place, size)
            place = lax.div(place, size)
        return spot

    def peers(self):
        me = self.me()
        return [lax.rem(me + step, self.count) for step in range(1, self.count)]


def greet(groups):
    barrier = pltpu.get_barrier_semaphore()
    total = 0
    for group in groups:
        for peer in group.peers():
            pl.semaphore_signal(
                barrier, inc=1, device_id=group.device(peer), device_id_type=MESH
            )
            total += 1
    pl.semaphore_wait(barrier, total)


def send(group, peer, step, src, dst, send_sem, recv_sem):
    copy = pltpu.make_async_remote_copy(
        src_ref=src,
        dst_ref=dst,
        send_sem=send_sem.at[step],
        recv_sem=recv_sem.at[step],
        device_id=group.device(peer),
        device_id_type=MESH,
    )
    copy.start()
    return copy


def tie(*arrays):
    return lax.optimization_barrier(arrays)


class Job:
    def __init__(self, kind, groups, x, axis=0):
        self.kind, self.groups, self.x, self.axis = kind, groups, x, axis
        count = groups[0].count
        rest = x.shape[:axis] + x.shape[axis + 1 :]
        dma = pltpu.SemaphoreType.DMA
        self.in_spec = pl.BlockSpec(memory_space=pl.ANY)
        self.out_spec = pl.BlockSpec(memory_space=pl.ANY)
        self.scratch = [dma((count - 1,)), dma((count - 1,)), dma]
        if kind in ("gather", "spread"):
            self.in_spec = pl.BlockSpec(memory_space=pltpu.VMEM)
        if kind == "gather":
            self.out = jax.ShapeDtypeStruct((count,) + x.shape, x.dtype)
        elif kind == "spread":
            self.out = jax.ShapeDtypeStruct((groups[1].count, count) + x.shape, x.dtype)
            copies = 7 if groups[0].square else count
            if groups[0].square:
                self.scratch = [dma((6,)), dma((6,)), dma]
            self.scratch += [dma((copies,)), dma((copies,))]
        elif kind == "deal":
            self.out = jax.ShapeDtypeStruct((count - 1,) + rest, x.dtype)
        else:
            self.out = jax.ShapeDtypeStruct(rest, F32)
            self.out_spec = pl.BlockSpec(memory_space=pltpu.VMEM)
            self.scratch += [pltpu.VMEM(rest, x.dtype), pltpu.VMEM((count - 1,) + rest, x.dtype)]

    def key(self):
        return (self.kind, tuple(g.axes for g in self.groups), self.x.shape, str(self.x.dtype), self.axis)

    def start(self, x, out, send_sem, recv_sem, own_sem, *more):
        group = self.groups[0]
        me = group.me()
        peers = list(enumerate(group.peers()))

        def block(place):
            return x.at[(slice(None),) * self.axis + (place,)]

        if self.kind == "gather":
            copies = [send(group, p, k, x, out.at[me], send_sem, recv_sem) for k, p in peers]
            own = pltpu.make_async_copy(x, out.at[me], own_sem)
            own.start()

            def finish():
                for copy in copies + [own]:
                    copy.wait()

        elif self.kind == "spread" and group.square:
            pair = self.groups[1]
            side = pair.me()
            fw_send, fw_recv = more
            size = self.x.shape[0] // 2
            near = [across(me, 0), across(me, 1)]

            def copy_of(number):
                at = pl.ds(SQUARE_HALF[number] * size, size)
                place = me if number < 4 else near[number - 4]
                dst = out.at[side, place, at]
                src = x.at[at] if number < 4 else dst
                copy = pltpu.make_async_remote_copy(
                    src_ref=src, dst_ref=dst, send_sem=send_sem.at[number],
                    recv_sem=recv_sem.at[number], device_id=group.device(near[SQUARE_STEP[number]]),
                    device_id_type=MESH,
                )
                origin = near[SQUARE_STEP[number]] if number < 4 else across(me, 2)
                return copy, out.at[side, origin, at]

            copies = [copy_of(number) for number in range(6)]
            for number in (0, 2, 1, 3):
                copies[number][0].start()
            passed = [send(pair, 1 - side, 6, x, out.at[side, me], fw_send, fw_recv)]
            own = pltpu.make_async_copy(x, out.at[side, me], own_sem)
            own.start()

            def arrived(number):
                copy, landed = copies[number]
                copy.wait_recv()
                passed.append(send(pair, 1 - side, number, landed, landed, fw_send, fw_recv))

            def finish():
                for number in (0, 2):
                    copies[number][0].wait_recv()
                    copies[4 + number // 2][0].start()
                    landed = copies[number][1]
                    passed.append(send(pair, 1 - side, number, landed, landed, fw_send, fw_recv))
                for number in (1, 3, 4, 5):
                    arrived(number)
                for copy in passed:
                    copy.wait()
                for copy, _ in copies:
                    copy.wait_send()
                own.wait()

        elif self.kind == "spread":
            pair = self.groups[1]
            side = pair.me()
            fw_send, fw_recv = more
            home = out.at[side, me]
            copies = [send(group, p, k, x, home, send_sem, recv_sem) for k, p in peers]
            last = group.count - 1
            passed = [send(pair, 1 - side, last, x, home, fw_send, fw_recv)]
            own = pltpu.make_async_copy(x, home, own_sem)
            own.start()

            def finish():
                for k, copy in enumerate(copies):
                    copy.wait_recv()
                    place = out.at[side, lax.rem(me + group.count - 1 - k, group.count)]
                    passed.append(send(pair, 1 - side, k, place, place, fw_send, fw_recv))
                for copy in passed:
                    copy.wait()
                for copy in copies:
                    copy.wait_send()
                own.wait()

        elif self.kind == "deal":
            copies = [send(group, p, k, block(p), out.at[k], send_sem, recv_sem) for k, p in peers]

            def finish():
                for copy in copies:
                    copy.wait()

        else:
            kept, slots = more
            copies = [send(group, p, k, block(p), slots.at[k], send_sem, recv_sem) for k, p in peers]
            own = pltpu.make_async_copy(block(me), kept, own_sem)
            own.start()

            def finish():
                own.wait()
                for copy in copies:
                    copy.wait()
                total = kept[...].astype(F32)
                for k in range(group.count - 1):
                    total = total + slots[k].astype(F32)
                out[...] = total

        return finish


def job_groups(jobs):
    return [group for job in jobs for group in job.groups]


def split_scratch(jobs, scratch):
    parts, at = [], 0
    for job in jobs:
        parts.append(scratch[at : at + len(job.scratch)])
        at += len(job.scratch)
    return parts


def exchange_body(jobs, *refs):
    count = len(jobs)
    greet(job_groups(jobs))
    parts = split_scratch(jobs, refs[2 * count :])
    ends = [
        job.start(refs[n], refs[count + n], *parts[n]) for n, job in enumerate(jobs)
    ]
    for end in ends:
        end()


class Exchanges:
    def __init__(self):
        self.idents = {}

    def ident(self, key):
        return self.idents.setdefault(key, len(self.idents))

    def __call__(self, *jobs):
        jobs = list(jobs)
        return pl.pallas_call(
            functools.partial(exchange_body, jobs),
            out_shape=tuple(job.out for job in jobs),
            in_specs=[job.in_spec for job in jobs],
            out_specs=tuple(job.out_spec for job in jobs),
            scratch_shapes=[one for job in jobs for one in job.scratch],
            compiler_params=pltpu.CompilerParams(
                collective_id=self.ident(tuple(job.key() for job in jobs)),
                has_side_effects=True,
                vmem_limit_bytes=32 * 2**20,
            ),
        )(*[job.x for job in jobs])


CHUNK = 256


def table_body(
    by_section, by_dp, jobs, g_ref, ids_ref, u_ref, gx_ref, *refs
):
    riders = len(jobs)
    xs, (out_ref, *outs), refs = refs[:riders], refs[riders : 2 * riders + 1], refs[2 * riders + 1 :]
    (g_buf, to_partner, from_partner, to_dp, from_dp, own, result,
    g_sem, ps_send, ps_recv, dp_send, dp_recv, ag_send, ag_recv, fw_send, fw_recv, own_sem,
    ) = refs[:17]
    s, j = by_section.me(), by_dp.me()
    partner = 1 - s
    peers = by_dp.peers() + [j]
    count = by_dp.count
    block = own.shape[0]
    subs = block // CHUNK
    tokens = u_ref.shape[0]
    greet([by_section, by_dp] + job_groups(jobs))
    parts = split_scratch(jobs, refs[17:])
    ends = [job.start(xs[n], outs[n], *parts[n]) for n, job in enumerate(jobs)]

    def chunk(half, place, sub):
        return (half * count + place) * subs + sub

    order = [(number, half) for number in range(count) for half in (0, 1)]

    def fetch(index, sub, slot):
        number, away = order[index]
        half = partner if away == 0 else s
        return pltpu.make_async_copy(
            g_ref.at[chunk(half, peers[number], sub)], g_buf.at[slot], g_sem.at[slot]
        )

    def remote(group, peer, number, sub, src, dst, send_sem, recv_sem):
        return pltpu.make_async_remote_copy(
            src_ref=src,
            dst_ref=dst,
            send_sem=send_sem.at[number, sub],
            recv_sem=recv_sem.at[number, sub],
            device_id=group.device(peer),
            device_id_type=MESH,
        )

    def rows(sub):
        return pl.ds(pl.multiple_of(sub * CHUNK, CHUNK), CHUNK)

    def partner_copy(number, sub):
        return remote(
            by_section, partner, number, sub,
            to_partner.at[number, rows(sub)], from_partner.at[number, rows(sub)],
            ps_send, ps_recv,
        )

    def chip_copy(number, sub):
        return remote(
            by_dp, peers[number], number, sub,
            to_dp.at[number, rows(sub)], from_dp.at[number, rows(sub)], dp_send, dp_recv,
        )

    def spread_copy(number, sub):
        return remote(
            by_dp, peers[number], number, sub,
            result.at[rows(sub)], out_ref.at[chunk(s, j, sub)], ag_send, ag_recv,
        )

    sources = [lax.rem(j + count - 1 - number, count) for number in range(count - 1)] + [j]

    def forward_copy(number, sub):
        target = out_ref.at[chunk(s, sources[number], sub)]
        origin = result.at[rows(sub)] if number == count - 1 else target
        return remote(by_section, partner, number, sub, origin, target, fw_send, fw_recv)

    def own_copy(sub):
        return pltpu.make_async_copy(
            result.at[rows(sub)], out_ref.at[chunk(s, j, sub)], own_sem.at[sub]
        )

    fetch(0, 0, 0).start()
    for index, (number, away) in enumerate(order):
        half = partner if away == 0 else s

        def one(sub, carry, index=index, number=number, away=away, half=half):
            slot = lax.rem(sub, 2)
            fetch(index, sub, slot).wait()

            @pl.when(sub + 1 < subs)
            def _():
                fetch(index, sub + 1, 1 - slot).start()

            if index + 1 < len(order):

                @pl.when(sub + 1 == subs)
                def _():
                    fetch(index + 1, 0, 1 - slot).start()

            base = chunk(half, peers[number], sub) * CHUNK
            place = base + lax.broadcasted_iota(jnp.int32, (CHUNK, tokens), 0)
            chosen = jnp.where(place == ids_ref[...], 1.0, 0.0).astype(BF16)
            term = outer_sum(g_buf[slot], u_ref[...]) + matmul(chosen, gx_ref[...])
            if away == 0:
                to_partner[number, rows(sub), :] = term.astype(BF16)
                partner_copy(number, sub).start()
            else:
                partner_copy(number, sub).wait_recv()
                term = term + from_partner[number, rows(sub), :].astype(F32)
                if number < count - 1:
                    to_dp[number, rows(sub), :] = term.astype(BF16)
                    chip_copy(number, sub).start()
                else:
                    own[rows(sub), :] = term
            return carry

        lax.fori_loop(0, subs, one, 0)

    def finish(sub, carry):
        term = own[rows(sub), :]
        for number in range(count - 1):
            chip_copy(number, sub).wait_recv()
            term = term + from_dp[number, rows(sub), :].astype(F32)
        result[rows(sub), :] = term.astype(BF16)
        for number in range(count - 1):
            spread_copy(number, sub).start()
        forward_copy(count - 1, sub).start()
        own_copy(sub).start()
        return carry

    lax.fori_loop(0, subs, finish, 0)

    def take(sub, carry):
        for number in range(count - 1):
            spread_copy(number, sub).wait_recv()
            forward_copy(number, sub).start()
        return carry

    lax.fori_loop(0, subs, take, 0)

    def drain(sub, carry):
        own_copy(sub).wait()
        for number in range(count):
            partner_copy(number, sub).wait_send()
            forward_copy(number, sub).wait()
        for number in range(count - 1):
            chip_copy(number, sub).wait_send()
            spread_copy(number, sub).wait_send()
        return carry

    lax.fori_loop(0, subs, drain, 0)
    for end in ends:
        end()


def across(me, step):
    bits = jnp.int32(step + 1)
    x, y = lax.rem(me, 2), lax.div(me, 2)
    return 2 * lax.rem(y + lax.div(bits, 2), 2) + lax.rem(x + lax.rem(bits, 2), 2)


SQUARE_HALF = (0, 1, 1, 0, 0, 1)
SQUARE_STEP = (0, 0, 1, 1, 1, 0)


def table_square_body(by_section, by_dp, jobs, g_ref, ids_ref, u_ref, gx_ref, *refs):
    riders = len(jobs)
    xs, (out_ref, *outs), refs = refs[:riders], refs[riders : 2 * riders + 1], refs[2 * riders + 1 :]
    (
        g_buf, to_partner, from_partner, to_dp, hop_land, from_dp, own, result,
        g_sem, ps_send, ps_recv, hop_send, hop_recv, dp_send, dp_recv, ag_send, ag_recv,
        fw_send, fw_recv, own_sem,
    ) = refs[:20]
    s, j = by_section.me(), by_dp.me()
    partner = 1 - s
    near_x, near_y, far = (across(j, step) for step in range(3))
    peers = [far, near_y, near_x, j]
    count = 4
    block = own.shape[0]
    subs = block // CHUNK
    half_rows = CHUNK // 2
    tokens = u_ref.shape[0]
    greet([by_section, by_dp] + job_groups(jobs))
    parts = split_scratch(jobs, refs[20:])
    ends = [job.start(xs[n], outs[n], *parts[n]) for n, job in enumerate(jobs)]

    def chunk(half, place, sub):
        return (half * count + place) * subs + sub

    order = [(number, away) for number in range(count) for away in (0, 1)]

    def fetch(index, sub, slot):
        number, away = order[index]
        half = partner if away == 0 else s
        return pltpu.make_async_copy(
            g_ref.at[chunk(half, peers[number], sub)], g_buf.at[slot], g_sem.at[slot]
        )

    def remote(group, peer, number, sub, src, dst, send_sem, recv_sem):
        return pltpu.make_async_remote_copy(
            src_ref=src,
            dst_ref=dst,
            send_sem=send_sem.at[number, sub],
            recv_sem=recv_sem.at[number, sub],
            device_id=group.device(peer),
            device_id_type=MESH,
        )

    def rows(sub):
        return pl.ds(pl.multiple_of(sub * CHUNK, CHUNK), CHUNK)

    def half_of(sub, which):
        return pl.ds(pl.multiple_of(sub * CHUNK + which * half_rows, half_rows), half_rows)

    def partner_copy(number, sub):
        return remote(
            by_section, partner, number, sub,
            to_partner.at[number, rows(sub)], from_partner.at[number, rows(sub)],
            ps_send, ps_recv,
        )

    def hop_copy(which, sub):
        return remote(
            by_dp, (near_x, near_y)[which], which, sub,
            to_dp.at[0, half_of(sub, which)], hop_land.at[half_of(sub, which)], hop_send, hop_recv,
        )

    def chip_copy(number, sub):
        return remote(
            by_dp, (near_y, near_x)[number], number, sub,
            to_dp.at[number + 1, rows(sub)], from_dp.at[number, rows(sub)], dp_send, dp_recv,
        )

    def spread_copy(number, sub):
        which = SQUARE_HALF[number]
        place = j if number < 4 else (near_x, near_y)[number - 4]
        dst = out_ref.at[chunk(s, place, sub), pl.ds(which * half_rows, half_rows)]
        src = result.at[half_of(sub, which)] if number < 4 else dst
        peer = (near_x, near_y)[SQUARE_STEP[number]]
        return remote(by_dp, peer, number, sub, src, dst, ag_send, ag_recv)

    sources = [near_x, near_y, far, j]

    def forward_copy(number, sub):
        target = out_ref.at[chunk(s, sources[number], sub)]
        origin = result.at[rows(sub)] if number == count - 1 else target
        return remote(by_section, partner, number, sub, origin, target, fw_send, fw_recv)

    def own_copy(sub):
        return pltpu.make_async_copy(
            result.at[rows(sub)], out_ref.at[chunk(s, j, sub)], own_sem.at[sub]
        )

    fetch(0, 0, 0).start()
    for index, (number, away) in enumerate(order):
        half = partner if away == 0 else s

        def one(sub, carry, index=index, number=number, away=away, half=half):
            slot = lax.rem(sub, 2)
            fetch(index, sub, slot).wait()

            @pl.when(sub + 1 < subs)
            def _():
                fetch(index, sub + 1, 1 - slot).start()

            if index + 1 < len(order):

                @pl.when(sub + 1 == subs)
                def _():
                    fetch(index + 1, 0, 1 - slot).start()

            base = chunk(half, peers[number], sub) * CHUNK
            place = base + lax.broadcasted_iota(jnp.int32, (CHUNK, tokens), 0)
            chosen = jnp.where(place == ids_ref[...], 1.0, 0.0).astype(BF16)
            term = outer_sum(g_buf[slot], u_ref[...]) + matmul(chosen, gx_ref[...])
            if away == 0:
                to_partner[number, rows(sub), :] = term.astype(BF16)
                partner_copy(number, sub).start()
                return carry
            partner_copy(number, sub).wait_recv()
            term = term + from_partner[number, rows(sub), :].astype(F32)
            if number == 0:
                to_dp[0, rows(sub), :] = term.astype(BF16)
                for which in range(2):
                    hop_copy(which, sub).start()
            elif number < 3:
                which = number - 1
                hop_copy(which, sub).wait_recv()
                mine = slice(which * half_rows, (which + 1) * half_rows)
                rest = slice((1 - which) * half_rows, (2 - which) * half_rows)
                to_dp[number, half_of(sub, which), :] = (
                    term[mine] + hop_land[half_of(sub, which), :].astype(F32)
                ).astype(BF16)
                to_dp[number, half_of(sub, 1 - which), :] = term[rest].astype(BF16)
                chip_copy(which, sub).start()
            else:
                own[rows(sub), :] = term
            return carry

        lax.fori_loop(0, subs, one, 0)

    def finish(sub, carry):
        term = own[rows(sub), :]
        for number in range(2):
            chip_copy(number, sub).wait_recv()
            term = term + from_dp[number, rows(sub), :].astype(F32)
        result[rows(sub), :] = term.astype(BF16)
        for number in (0, 2, 1, 3):
            spread_copy(number, sub).start()
        forward_copy(count - 1, sub).start()
        own_copy(sub).start()
        return carry

    lax.fori_loop(0, subs, finish, 0)

    def pass_on(sub, carry):
        for number in (0, 2):
            spread_copy(number, sub).wait_recv()
            spread_copy(4 + number // 2, sub).start()
        for number in (0, 1):
            spread_copy(2 * number + 1, sub).wait_recv()
            forward_copy(number, sub).start()
        return carry

    lax.fori_loop(0, subs, pass_on, 0)

    def last(sub, carry):
        for number in (4, 5):
            spread_copy(number, sub).wait_recv()
        forward_copy(2, sub).start()
        return carry

    lax.fori_loop(0, subs, last, 0)

    def drain(sub, carry):
        own_copy(sub).wait()
        for number in range(count):
            partner_copy(number, sub).wait_send()
            forward_copy(number, sub).wait()
        for number in range(2):
            hop_copy(number, sub).wait_send()
            chip_copy(number, sub).wait_send()
        for number in range(6):
            spread_copy(number, sub).wait_send()
        return carry

    lax.fori_loop(0, subs, drain, 0)
    for end in ends:
        end()


def table_sum(by_section, by_dp, jobs, grads, ids, final, grad_rows, ident):
    chunks, tokens, _ = grads.shape
    width = final.shape[1]
    count = by_dp.count
    subs = chunks // (2 * count)
    block = subs * CHUNK
    assert subs % 2 == 0
    dma = pltpu.SemaphoreType.DMA
    low = functools.partial(pltpu.VMEM, dtype=BF16)
    square = by_dp.square
    scratch = [
        low((2, tokens, CHUNK)),
        low((count, block, width)),
        low((count, block, width)),
        low((count - 1, block, width)),
    ]
    scratch += [low((block, width)), low((2, block, width))] if square else [
        low((count - 1, block, width))
    ]
    scratch += [pltpu.VMEM((block, width), F32), low((block, width)), dma((2,))]
    copies = (count, 2, 2, 6, count) if square else (count, count - 1, count - 1, count)
    scratch += [dma((copy, subs)) for copy in copies for _ in range(2)] + [dma((subs,))]
    vmem = pl.BlockSpec(memory_space=pltpu.VMEM)
    hbm = pl.BlockSpec(memory_space=pl.ANY)
    return pl.pallas_call(
        functools.partial(
            table_square_body if by_dp.square else table_body, by_section, by_dp, jobs
        ),
        out_shape=(jax.ShapeDtypeStruct((chunks, CHUNK, width), BF16),)
        + tuple(job.out for job in jobs),
        in_specs=[hbm, vmem, vmem, vmem] + [job.in_spec for job in jobs],
        out_specs=(hbm,) + tuple(job.out_spec for job in jobs),
        scratch_shapes=scratch + [one for job in jobs for one in job.scratch],
        compiler_params=pltpu.CompilerParams(
            collective_id=ident, has_side_effects=True, vmem_limit_bytes=56 * 2**20
        ),
    )(grads, ids, final, grad_rows, *[job.x for job in jobs])


LANES = 128


def head_logits_body(u_ref, e_ref, ids_ref, logits_ref, top_ref, total_ref, pick_ref):
    step = pl.program_id(0)
    tokens, tile = logits_ref.shape[1:]

    @pl.when(step == 0)
    def _():
        top_ref[...] = jnp.full_like(top_ref, NEG)
        total_ref[...] = jnp.zeros_like(total_ref)
        pick_ref[...] = jnp.zeros_like(pick_ref)

    logits = matmul_t(u_ref[...], e_ref[...])
    logits_ref[0] = logits
    place = step * tile + lax.broadcasted_iota(jnp.int32, (tokens, tile), 1)
    picked = jnp.where(place == ids_ref[...], logits, 0.0)
    pieces = [logits[:, at : at + LANES] for at in range(0, tile, LANES)]
    before = top_ref[...]
    top = functools.reduce(jnp.maximum, pieces, before)
    total = total_ref[...] * jnp.exp(before - top)
    pick = pick_ref[...]
    for number, piece in enumerate(pieces):
        total = total + jnp.exp(piece - top)
        pick = pick + picked[:, number * LANES : (number + 1) * LANES]
    top_ref[...] = top
    total_ref[...] = total
    pick_ref[...] = pick


def head_logits(final, embedding, ids):
    tokens, width = final.shape
    vocab = embedding.shape[0]
    fixed = pl.BlockSpec((tokens, LANES), lambda step: (0, 0))
    stat = jax.ShapeDtypeStruct((tokens, LANES), F32)
    return pl.pallas_call(
        head_logits_body,
        grid=(vocab // CHUNK,),
        out_shape=(
            jax.ShapeDtypeStruct((vocab // CHUNK, tokens, CHUNK), F32), stat, stat, stat
        ),
        in_specs=[
            pl.BlockSpec((tokens, width), lambda step: (0, 0)),
            pl.BlockSpec((CHUNK, width), lambda step: (step, 0)),
            pl.BlockSpec((tokens, 1), lambda step: (0, 0)),
        ],
        out_specs=(
            pl.BlockSpec((1, tokens, CHUNK), lambda step: (step, 0, 0)), fixed, fixed, fixed
        ),
        compiler_params=pltpu.CompilerParams(vmem_limit_bytes=40 * 2**20),
        cost_estimate=pl.CostEstimate(
            flops=2 * tokens * vocab * width,
            bytes_accessed=4 * tokens * vocab + 2 * vocab * width,
            transcendentals=tokens * vocab,
        ),
    )(final, embedding, ids)


def head_grads_body(logits_ref, e_ref, ids_ref, norm_ref, weight_ref, grads_ref, back_ref, acc):
    step = pl.program_id(0)
    tokens, tile = grads_ref.shape[1:]

    @pl.when(step == 0)
    def _():
        acc[...] = jnp.zeros_like(acc)

    place = step * tile + lax.broadcasted_iota(jnp.int32, (tokens, tile), 1)
    probs = jnp.exp(logits_ref[0] - norm_ref[...])
    grads = (jnp.where(place == ids_ref[...], probs - 1.0, probs) * weight_ref[...]).astype(BF16)
    grads_ref[0] = grads
    acc[...] += matmul(grads, e_ref[...])

    @pl.when(step == pl.num_programs(0) - 1)
    def _():
        back_ref[...] = acc[...].astype(BF16)


def head_grads(logits, embedding, ids, norm, weight):
    chunks, tokens, _ = logits.shape
    vocab, width = embedding.shape
    column = pl.BlockSpec((tokens, 1), lambda step: (0, 0))
    tile = pl.BlockSpec((1, tokens, CHUNK), lambda step: (step, 0, 0))
    return pl.pallas_call(
        head_grads_body,
        grid=(chunks,),
        out_shape=(
            jax.ShapeDtypeStruct(logits.shape, BF16),
            jax.ShapeDtypeStruct((tokens, width), BF16),
        ),
        in_specs=[
            tile, pl.BlockSpec((CHUNK, width), lambda step: (step, 0)), column, column, column
        ],
        out_specs=(tile, pl.BlockSpec((tokens, width), lambda step: (0, 0))),
        scratch_shapes=[pltpu.VMEM((tokens, width), F32)],
        compiler_params=pltpu.CompilerParams(vmem_limit_bytes=40 * 2**20),
        cost_estimate=pl.CostEstimate(
            flops=2 * tokens * vocab * width,
            bytes_accessed=6 * tokens * vocab + 2 * vocab * width,
            transcendentals=tokens * vocab,
        ),
    )(logits, embedding, ids, norm, weight)


BLOCK = 256


def masked_scores(queries, keys, slope, length, first):
    rows, cols = queries.shape[0], keys.shape[0]
    raw = matmul_t(queries, keys)
    i = first + lax.broadcasted_iota(jnp.int32, (rows, cols), 0)
    j = lax.broadcasted_iota(jnp.int32, (rows, cols), 1)
    scores = raw * HEAD_DIM ** (-0.5) - slope * (i - j).astype(F32)
    return jnp.where((j <= i) & (j < length), scores, NEG)


SMEM = pl.BlockSpec(memory_space=pltpu.SMEM)
VMEM = pl.BlockSpec(memory_space=pltpu.VMEM)


class TeamRows:
    def __init__(self, team, x_ref, full, stage, slots, own, ag_send, ag_recv, rs_send, rs_recv):
        self.team, self.count, self.me = team, team.count, team.me()
        self.x_ref, self.full, self.stage, self.slots, self.own = x_ref, full, stage, slots, own
        self.ag_sems, self.rs_sems = (ag_send, ag_recv), (rs_send, rs_recv)

    def shifted(self, step):
        return across(self.me, step)

    def peer(self, step):
        if self.team.square:
            return self.shifted(step)
        return lax.rem(self.me + 1 + step, self.count)

    def source(self, step):
        if self.team.square:
            return self.shifted(step)
        return lax.rem(self.me + self.count - 1 - step, self.count)

    def back_step(self, place):
        if self.team.square:
            flip_x = lax.rem(lax.rem(self.me, 2) + lax.rem(place, 2), 2)
            flip_y = lax.rem(lax.div(self.me, 2) + lax.div(place, 2), 2)
            return 2 * flip_y + flip_x - 1
        return lax.rem(place + self.count - 1 - self.me, self.count)

    def remote(self, number, peer, src, dst, sems):
        return pltpu.make_async_remote_copy(
            src_ref=src,
            dst_ref=dst,
            send_sem=sems[0].at[number],
            recv_sem=sems[1].at[number],
            device_id=self.team.device(peer),
            device_id_type=MESH,
        )

    def ag(self, number):
        if not self.team.square:
            return self.remote(
                number, self.peer(number), self.x_ref, self.full.at[self.me], self.ag_sems
            )
        half = self.x_ref.shape[0] // 2
        which = SQUARE_HALF[number]
        rows = pl.ds(which * half, half)
        peer = self.shifted(SQUARE_STEP[number])
        if number < 4:
            src, place = self.x_ref.at[rows], self.me
        else:
            place = self.shifted(number - 4)
            src = self.full.at[place, rows]
        return self.remote(number, peer, src, self.full.at[place, rows], self.ag_sems)

    def rs(self, step):
        return self.remote(
            step, self.peer(step), self.stage.at[self.peer(step)], self.slots.at[step], self.rs_sems
        )

    def send_rows(self):
        for number in (0, 2, 1, 3) if self.team.square else range(self.count - 1):
            self.ag(number).start()
        self.full[self.me] = self.x_ref[...]

    def pass_on(self):
        if self.team.square:
            for number in (0, 2):
                self.ag(number).wait_recv()
                self.ag(4 + number // 2).start()

    def wait_rows(self, step):
        if not self.team.square:
            self.ag(step).wait_recv()
            return
        for number, these in enumerate(((1,), (3,), (4, 5))):

            @pl.when(step == number)
            def _(these=these):
                for one in these:
                    self.ag(one).wait_recv()

    def each_arrival(self, work):
        work(self.me)
        self.pass_on()

        def one(step, carry):
            self.wait_rows(step)
            work(self.source(step))
            return carry

        lax.fori_loop(0, self.count - 1, one, 0)

    def each_arrival_and_back(self, term):
        self.own[...] = term(self.me)
        self.pass_on()

        def one(step, carry):
            self.wait_rows(step)
            place = self.source(step)
            self.stage[place] = term(place).astype(BF16)
            self.rs(self.back_step(place)).start()
            return carry

        lax.fori_loop(0, self.count - 1, one, 0)

    def finish(self, total_ref):
        for step in range(self.count - 1):
            self.rs(step).wait()
        total = self.own[...]
        for step in range(self.count - 1):
            total = total + self.slots[step].astype(F32)
        total_ref[...] = total
        for number in range(6 if self.team.square else self.count - 1):
            self.ag(number).wait_send()


def team_scratch(team, part, model):
    count = team.count
    dma = pltpu.SemaphoreType.DMA
    copies = 6 if team.square else count - 1
    return [
        pltpu.VMEM((count, part, model), BF16),
        pltpu.VMEM((count, part, model), BF16),
        pltpu.VMEM((count - 1, part, model), BF16),
        pltpu.VMEM((part, model), F32),
        dma((copies,)),
        dma((copies,)),
        dma((count - 1,)),
        dma((count - 1,)),
    ]


def team_call(body, team, ident, jobs, arrays, specs, outs, out_specs, scratch):
    part, model = arrays[0].shape
    count_in, count_out, riders = len(arrays), len(outs), len(jobs)
    own_scratch = team_scratch(team, part, model)

    def kernel(*refs):
        ins, refs = refs[:count_in], refs[count_in:]
        xs, refs = refs[:riders], refs[riders:]
        results, refs = refs[:count_out], refs[count_out:]
        landings, refs = refs[:riders], refs[riders:]
        rows = TeamRows(team, ins[0], *refs[: len(own_scratch)])
        refs = refs[len(own_scratch) :]
        mine, refs = refs[: len(scratch)], refs[len(scratch) :]
        greet([team] + job_groups(jobs))
        rows.send_rows()
        parts = split_scratch(jobs, refs)
        ends = [job.start(xs[n], landings[n], *parts[n]) for n, job in enumerate(jobs)]
        body(rows, ins, results, mine)
        for end in ends:
            end()

    out = pl.pallas_call(
        kernel,
        out_shape=tuple(outs) + tuple(job.out for job in jobs),
        in_specs=list(specs) + [job.in_spec for job in jobs],
        out_specs=tuple(out_specs) + tuple(job.out_spec for job in jobs),
        scratch_shapes=own_scratch + list(scratch) + [one for job in jobs for one in job.scratch],
        compiler_params=pltpu.CompilerParams(
            collective_id=ident, has_side_effects=True, vmem_limit_bytes=58 * 2**20
        ),
    )(*arrays, *[job.x for job in jobs])
    return out[:count_out], list(out[count_out:])


def part_rows(place, part):
    return pl.ds(pl.multiple_of(place * part, part), part)


def attend_body(rows, ins, outs, scratch):
    x_ref, length_ref, slope_ref, qk_ref, vo_ref, bias_ref = ins
    total_ref, full_out, q_ref, k_ref, v_ref, mixed_ref, lse_ref = outs
    (full_sem,) = scratch
    part = x_ref.shape[0]
    width = q_ref.shape[1]

    def project(place):
        at = part_rows(place, part)
        block = rows.full[place]
        q_ref[at, :] = (matmul_t(block, qk_ref[0]) + bias_ref[0:1, :]).astype(BF16)
        k_ref[at, :] = matmul_t(block, qk_ref[1]).astype(BF16)
        v_ref[at, :] = (matmul_t(block, vo_ref[0]) + bias_ref[1:2, :]).astype(BF16)

    rows.each_arrival(project)
    keep = pltpu.make_async_copy(rows.full, full_out, full_sem)
    keep.start()

    def one(turn, carry):
        step = lax.rem(2 * rows.count - 2 - turn, rows.count)
        place = rows.peer(step)
        for block in range(rows.count):

            @pl.when(place == block)
            def _(first=block * part, upto=(block + 1) * part):
                for head in range(width // HEAD_DIM):
                    lanes = slice(head * HEAD_DIM, (head + 1) * HEAD_DIM)
                    scores = masked_scores(
                        q_ref[first:upto, lanes], k_ref[:upto, lanes], slope_ref[head],
                        length_ref[0], first,
                    )
                    highest = jnp.max(scores, axis=-1, keepdims=True)
                    powers = jnp.exp(scores - highest)
                    total = jnp.sum(powers, axis=-1, keepdims=True)
                    probs = (powers * (1.0 / total)).astype(BF16)
                    mixed_ref[first:upto, lanes] = matmul(probs, v_ref[:upto, lanes]).astype(BF16)
                    lse_ref[head, first:upto, :] = highest + jnp.log(total)

        term = matmul(mixed_ref[part_rows(place, part), :], vo_ref[1])

        @pl.when(step < rows.count - 1)
        def _():
            rows.stage[place] = term.astype(BF16)
            rows.rs(step).start()

        @pl.when(step == rows.count - 1)
        def _():
            rows.own[...] = term

        return carry

    lax.fori_loop(0, rows.count, one, 0)
    rows.finish(total_ref)
    keep.wait()


HBM = pl.BlockSpec(memory_space=pl.ANY)


def attend(team, ident, jobs, x, length, slopes, qk, vo, bias):
    part, model = x.shape
    seq = part * team.count
    width = qk.shape[1]
    low = jax.ShapeDtypeStruct((seq, width), BF16)
    return team_call(
        attend_body, team, ident, jobs,
        [x, length, slopes, qk, vo, bias],
        [VMEM, SMEM, SMEM, VMEM, VMEM, VMEM],
        (
            jax.ShapeDtypeStruct((part, model), F32),
            jax.ShapeDtypeStruct((team.count, part, model), BF16),
            low, low, low, low,
            jax.ShapeDtypeStruct((width // HEAD_DIM, seq, 1), F32),
        ),
        (VMEM, HBM, VMEM, VMEM, VMEM, VMEM, VMEM),
        [pltpu.SemaphoreType.DMA],
    )


def attend_back_body(rows, ins, outs, scratch):
    gy_ref, length_ref, slope_ref, a_ref, qk_ref, vo_ref, q_ref, k_ref, v_ref, mixed_ref, lse_ref = ins
    total_ref, grads_ref, sums_ref = outs
    go, gq, gk, gv, gk_sum, gv_sum = scratch
    part = gy_ref.shape[0]
    seq, width = q_ref.shape
    heads = width // HEAD_DIM
    gk_sum[...] = jnp.zeros_like(gk_sum)
    gv_sum[...] = jnp.zeros_like(gv_sum)
    sums_ref[...] = jnp.zeros_like(sums_ref)

    def open_block(place):
        go[part_rows(place, part), :] = matmul_t(rows.full[place], vo_ref[1]).astype(BF16)

    rows.each_arrival(open_block)
    for block in reversed(range(rows.count)):
        first, upto = block * part, (block + 1) * part
        for head in range(heads):
            lanes = slice(head * HEAD_DIM, (head + 1) * HEAD_DIM)
            queries, grads = q_ref[first:upto, lanes], go[first:upto, lanes]
            keys, values = k_ref[:upto, lanes], v_ref[:upto, lanes]
            scores = masked_scores(queries, keys, slope_ref[head], length_ref[0], first)
            probs = jnp.exp(scores - lse_ref[head, first:upto, :])
            grad_probs = matmul_t(grads, values)
            inner = jnp.sum(probs * grad_probs, axis=-1, keepdims=True)
            grad_scores = (probs * (grad_probs - inner) * HEAD_DIM ** (-0.5)).astype(BF16)
            piece = matmul(grad_scores, keys)
            sums_ref[0:1, lanes] += jnp.sum(piece, axis=0, keepdims=True)
            gq[first:upto, lanes] = piece.astype(BF16)
            gk_sum[:upto, lanes] += outer_sum(grad_scores, queries)
            gv_sum[:upto, lanes] += outer_sum(probs.astype(BF16), grads)
        gk[first:upto, :] = gk_sum[first:upto, :].astype(BF16)
        gv[first:upto, :] = gv_sum[first:upto, :].astype(BF16)
        term = (
            matmul(gq[first:upto, :], qk_ref[0]) + matmul(gk[first:upto, :], qk_ref[1])
            + matmul(gv[first:upto, :], vo_ref[0])
        )

        @pl.when(rows.me != block)
        def _(block=block, term=term):
            rows.stage[block] = term.astype(BF16)
            rows.rs(rows.back_step(block)).start()

        @pl.when(rows.me == block)
        def _(term=term):
            rows.own[...] = term

    sums_ref[1:2, :] = jnp.sum(gv_sum[...], axis=0, keepdims=True)
    model = gy_ref.shape[1]
    grads_ref[3] = outer_sum(mixed_ref[...], rows.full[...].reshape(seq, model))
    grads_ref[0] = outer_sum(gq[...], a_ref[...])
    grads_ref[1] = outer_sum(gv[...], a_ref[...])
    grads_ref[2] = outer_sum(gk[...], a_ref[...])
    rows.finish(total_ref)


def attend_back(team, ident, jobs, gy, length, slopes, a, qk, vo, q, k, v, mixed, lse):
    part, model = gy.shape
    seq, width = q.shape
    return team_call(
        attend_back_body, team, ident, jobs,
        [gy, length, slopes, a, qk, vo, q, k, v, mixed, lse],
        [VMEM, SMEM, SMEM] + [VMEM] * 8,
        (
            jax.ShapeDtypeStruct((part, model), F32),
            jax.ShapeDtypeStruct((4, width, model), F32),
            jax.ShapeDtypeStruct((2, width), F32),
        ),
        (VMEM,) * 3,
        [pltpu.VMEM((seq, width), BF16)] * 4 + [pltpu.VMEM((seq, width), F32)] * 2,
    )


GELU_A = 0.7978845608028654
GELU_B = 0.044715


def feed_body(rows, ins, outs, scratch):
    x_ref, up_ref, down_ref, bias_ref = ins
    total_ref, full_out, before_ref = outs
    (full_sem,) = scratch
    part = x_ref.shape[0]
    units = up_ref.shape[0]
    tile = min(units, BLOCK)

    def term(place):
        at = part_rows(place, part)
        block = rows.full[place]
        total = None
        for first in range(0, units, tile):
            lanes = slice(first, first + tile)
            before = matmul_t(block, up_ref[lanes, :]) + bias_ref[:, lanes]
            before_ref[at, lanes] = before
            bend = jnp.tanh(GELU_A * (before + GELU_B * before * before * before))
            active = (0.5 * before * (1.0 + bend)).astype(BF16)
            piece = matmul(active, down_ref[lanes, :])
            total = piece if total is None else total + piece
        return total

    rows.each_arrival_and_back(term)
    keep = pltpu.make_async_copy(rows.full, full_out, full_sem)
    keep.start()
    rows.finish(total_ref)
    keep.wait()


def feed(team, ident, jobs, x, up, down, bias):
    part, model = x.shape
    units = up.shape[0]
    return team_call(
        feed_body, team, ident, jobs,
        [x, up, down, bias],
        [VMEM] * 4,
        (
            jax.ShapeDtypeStruct((part, model), F32),
            jax.ShapeDtypeStruct((team.count, part, model), BF16),
            jax.ShapeDtypeStruct((part * team.count, units), F32),
        ),
        (VMEM, HBM, VMEM),
        [pltpu.SemaphoreType.DMA],
    )


def feed_back_body(rows, ins, outs, scratch):
    gz_ref, c_ref, before_ref, up_ref, down_ref = ins
    total_ref, grads_ref, sums_ref = outs
    active, low = scratch
    part, model = gz_ref.shape
    seq = part * rows.count
    units = up_ref.shape[0]
    tile = min(units, BLOCK)
    sums_ref[...] = jnp.zeros_like(sums_ref)

    def term(place):
        at = part_rows(place, part)
        gz = rows.full[place]
        for first in range(0, units, tile):
            lanes = slice(first, first + tile)
            before = before_ref[at, lanes]
            square = before * before
            bend = jnp.tanh(GELU_A * before * (1.0 + GELU_B * square))
            half = 0.5 * (1.0 + bend)
            slope = half + 0.5 * before * (1.0 - bend * bend) * (
                GELU_A * (1.0 + 3.0 * GELU_B * square)
            )
            grad = matmul_t(gz, down_ref[lanes, :]) * slope
            sums_ref[:, lanes] += jnp.sum(grad, axis=0, keepdims=True)
            active[at, lanes] = (before * half).astype(BF16)
            low[at, lanes] = grad.astype(BF16)
        return matmul(low[at, :], up_ref[...])

    rows.each_arrival_and_back(term)
    for first in range(0, units, tile):
        lanes = slice(first, first + tile)
        grads_ref[0, lanes, :] = outer_sum(low[:, lanes], c_ref[...])
        grads_ref[1, lanes, :] = outer_sum(active[:, lanes], rows.full[...].reshape(seq, model))
    rows.finish(total_ref)


def feed_back(team, ident, jobs, gz, c, before, up, down):
    part, model = gz.shape
    seq = part * team.count
    units = up.shape[0]
    return team_call(
        feed_back_body, team, ident, jobs,
        [gz, c, before, up, down],
        [VMEM] * 5,
        (
            jax.ShapeDtypeStruct((part, model), F32),
            jax.ShapeDtypeStruct((2, units, model), F32),
            jax.ShapeDtypeStruct((1, units), F32),
        ),
        (VMEM,) * 3,
        [pltpu.VMEM((seq, units), BF16)] * 2,
    )


def per_device(
    mesh_shape,
    token_ids,
    target_ids,
    lengths,
    embedding,
    outer_gain,
    outer_bias,
    norm_gain,
    norm_bias,
    qkv_weight,
    qv_bias,
    out_weight,
    up_weight,
    up_bias,
    down_weight,
    row_bias,
):
    sections, groups, shards = (mesh_shape[name] for name in ("section", "dp", "tensor"))
    s, j, z = (lax.axis_index(name) for name in ("section", "dp", "tensor"))
    by_section = Group(("section",), (sections,))
    by_dp = Group(("dp",), (groups,))
    by_tensor = Group(("tensor",), (shards,))
    exchange = Exchanges()
    layers = sections
    vocab, width = embedding.shape
    seq = token_ids.shape[1]
    rows = token_ids.shape[0] * groups
    local_cols = qkv_weight.shape[-1]
    planes = rows == sections * shards and local_cols % (groups * HEAD_DIM) == 0
    by_dp.square = planes and groups == 4
    team = by_dp if planes else by_tensor
    cut = groups if planes else 1
    fan = shards if planes else 1
    halves = 2 if planes else 1
    part = seq // team.count
    cols = local_cols // cut
    hidden = up_weight.shape[-1] // cut
    strip = hidden // halves
    cut_index = j if planes else 0
    my_row = z * sections + s if planes else j * sections + s
    length = lax.dynamic_slice(lengths, (my_row,), (1,))
    token_count = jnp.sum(lengths).astype(F32)
    vocab_start = z * vocab

    def chosen_cols(array, size):
        return lax.dynamic_slice_in_dim(array, cut_index * size, size, array.ndim - 1).T

    def chosen_rows(array, size):
        return lax.dynamic_slice_in_dim(array, cut_index * size, size, 0)

    def pad_rows(array, count):
        return jnp.pad(array, ((0, count - array.shape[0]), (0, width - array.shape[1])))

    sides = jnp.stack(
        [
            jnp.concatenate(
                [
                    chosen_cols(qkv_weight[0, 0], cols),
                    chosen_cols(qkv_weight[0, 2], cols),
                    chosen_cols(up_weight[0], hidden),
                ]
            ),
            jnp.concatenate(
                [
                    chosen_cols(qkv_weight[0, 1], cols),
                    chosen_rows(out_weight[0], cols),
                    chosen_rows(down_weight[0], hidden),
                ]
            ),
        ]
    )
    qv_piece = lax.dynamic_slice_in_dim(qv_bias[0], cut_index * cols, cols, 1)
    up_piece = lax.dynamic_slice_in_dim(up_bias[0], cut_index * hidden, hidden, 0)
    small = jnp.concatenate(
        [
            outer_gain,
            outer_bias,
            norm_gain[0],
            norm_bias[0],
            row_bias[0],
            pad_rows(qv_piece, 2),
            pad_rows(up_piece[None], 6),
        ]
    )

    def gather(group, x):
        return Job("gather", [group], x)

    def deal(group, x, axis=0):
        return Job("deal", [group], x, axis)

    def own_and_dealt(x, dealt, place, axis=0):
        own = lax.dynamic_index_in_dim(x, place, axis, keepdims=False).astype(F32)
        return own + jnp.sum(dealt.astype(F32), axis=0)

    if planes:
        other, both, small_all = exchange(
            deal(by_section, sides),
            gather(by_dp, jnp.stack([token_ids, target_ids])),
            gather(Group(("section", "tensor"), (sections, shards)), small),
        )
        small_all = small_all.reshape((sections, shards) + small.shape)
        own_side = lax.dynamic_index_in_dim(sides, s, 0, keepdims=False)
        side = [jnp.where(s == l, own_side, other[0]) for l in range(layers)]
        both = jnp.swapaxes(both, 0, 1).reshape(2, shards, sections, groups, part)
        both = lax.dynamic_index_in_dim(
            lax.dynamic_index_in_dim(both, s, 2, keepdims=False), j, 2, keepdims=False
        )
        ids, targets = both[0].reshape(-1), both[1].reshape(-1)
        group_lengths = lax.dynamic_index_in_dim(
            lengths.reshape(shards, sections), s, 1, keepdims=False
        )
        places = jnp.broadcast_to(j * part + jnp.arange(part), (shards, part))
        valid = (places < group_lengths[:, None]).reshape(-1)
    else:
        sides_all, small_all = exchange(gather(by_section, sides), gather(by_section, small))
        small_all = small_all[:, None]
        ids, targets = token_ids[s], target_ids[s]
        valid = jnp.arange(seq) < lengths[my_row]

    outer_gains = [small_all[l, 0, 0] for l in range(layers)]
    outer_offsets = [small_all[l, 0, 1] for l in range(layers)]
    params = []
    for l in range(layers):
        biases = [small_all[l, :, 8 + n, :cols].reshape(-1) for n in range(2)]
        units = small_all[l, :, 10, :hidden].reshape(fan, halves, strip)
        params.append(
            dict(
                gains=small_all[l, 0, 2:4],
                offsets=small_all[l, 0, 4:6],
                row_bias=small_all[l, 0, 6:8],
                bias=jnp.stack(biases),
                up_bias=jnp.swapaxes(units, 0, 1).reshape(1, -1),
            )
        )
        if not planes:
            block = sides_all[l]
            params[l].update(
                qk=block[:, :cols],
                vo=block[:, cols : 2 * cols],
                up=block[0, 2 * cols :],
                down=block[1, 2 * cols :],
            )
    head_number = (
        (jnp.arange(fan)[:, None] if planes else z) * (local_cols // HEAD_DIM)
        + cut_index * (cols // HEAD_DIM)
        + jnp.arange(cols // HEAD_DIM)
    ).reshape(-1)
    slopes = jnp.exp2(-8.0 * (head_number + 1).astype(F32) / HEADS)

    def attn_jobs(l):
        if not planes or l >= layers:
            return []
        return [
            Job("spread", [by_tensor, by_section], side[l][first : first + cols])
            for first in (0, cols)
        ]

    def feed_jobs(l, n):
        if not planes or l >= layers:
            return []
        first = 2 * cols + n * strip
        return [Job("spread", [by_tensor, by_section], side[l][first : first + strip])]

    def take_attn(l, got):
        if got:
            params[l]["qk"], params[l]["vo"] = (
                one.reshape(2, fan * cols, width) for one in got
            )

    def take_feed(l, got):
        if got:
            strips = [one.reshape(2, fan * strip, width) for one in got]
            params[l]["up"], params[l]["down"] = (
                jnp.concatenate([one[n] for one in strips]) for n in range(2)
            )

    def ident(kind, jobs):
        return exchange.ident((kind,) + tuple(job.key() for job in jobs))

    local_ids = ids - vocab_start
    inside = (local_ids >= 0) & (local_ids < vocab)
    looked = jnp.where(
        inside[:, None], jnp.take(embedding, jnp.clip(local_ids, 0, vocab - 1), axis=0), 0
    )
    group_part = looked.shape[0] // shards
    x, *got = exchange(
        Job("reduce", [by_tensor], looked.reshape(shards, group_part, width)), *attn_jobs(0)
    )
    take_attn(0, got)
    h = layer_norm(x, outer_gains[0], outer_offsets[0])

    kept = []
    strips = []
    for l, p in enumerate(params):
        jobs = (feed_jobs(l, 0) if l == 0 else []) + feed_jobs(l, 1)
        normed = layer_norm(h, p["gains"][0], p["offsets"][0]).astype(BF16)
        (total, normed, q, k, v, mixed, lse), got = attend(
            team, ident("attend", jobs), jobs, normed, length, slopes, p["qk"], p["vo"], p["bias"]
        )
        take_feed(l, strips + got)
        middle = h + total + p["row_bias"][0]
        jobs = attn_jobs(l + 1) + feed_jobs(l + 1, 0)
        second = layer_norm(middle, p["gains"][1], p["offsets"][1]).astype(BF16)
        (total, second, before), got = feed(
            team, ident("feed", jobs), jobs, second, p["up"], p["down"], p["up_bias"]
        )
        take_attn(l + 1, got[:2])
        strips = got[2:]
        kept.append((h, normed.reshape(seq, width), q, k, v, mixed, lse, middle, second, before))
        h = middle + total + p["row_bias"][1]

    (final,) = exchange(
        gather(by_tensor, layer_norm(h, outer_gains[-1], outer_offsets[-1]).astype(BF16))
    )
    final = final.reshape(-1, width)
    tokens = final.shape[0]
    columns_of = (targets - vocab_start)[:, None]
    logits, tops, totals, picks = head_logits(final, embedding, columns_of)
    top = jnp.max(tops, axis=1)
    total = jnp.sum(totals * jnp.exp(tops - top[:, None]), axis=1)
    pick = jnp.sum(picks, axis=1)
    (stats,) = exchange(
        gather(by_tensor, jnp.pad(jnp.stack([top, total, pick]), ((0, 5), (0, 0))))
    )
    top_all = jnp.max(stats[:, 0], axis=0)
    log_norm = top_all + jnp.log(jnp.sum(stats[:, 1] * jnp.exp(stats[:, 0] - top_all), axis=0))
    terms = jnp.where(valid, log_norm - jnp.sum(stats[:, 2], axis=0), 0.0)
    loss_part = jnp.sum(
        lax.dynamic_index_in_dim(terms.reshape(shards, -1), z, 0, keepdims=False)
    )
    row_weight = jnp.where(valid, 1.0 / token_count, 0.0)
    grad_logits, back = head_grads(
        logits, embedding, columns_of, log_norm[:, None], row_weight[:, None]
    )
    (grad_final,) = exchange(
        Job("reduce", [by_tensor], back.reshape(shards, group_part, width))
    )
    _, final_back = jax.vjp(layer_norm, h, outer_gains[-1], outer_offsets[-1])
    grad, final_gain, final_offset = final_back(grad_final)

    def section_jobs(pair):
        return [deal(by_section, one) for one in pair] if planes else []

    def section_sums(pair, got):
        out = []
        for one, dealt in zip(pair, got):
            low = own_and_dealt(one, dealt, s).astype(BF16)
            if one.ndim == 4:
                out.append(low.reshape(low.shape[0], fan, cols, width))
            else:
                out.append(low.reshape(halves, fan, strip, width))
        return out

    def tensor_jobs(lows):
        return [deal(by_tensor, low, 1) for low in lows]

    def tensor_sums(lows, got):
        return [
            own_and_dealt(low, dealt, z, 1).astype(BF16) for low, dealt in zip(lows, got)
        ]

    def spread_jobs(pieces):
        return [Job("spread", [by_dp, by_section], piece) for piece in pieces]

    small_rows = [None] * layers
    pairs = [None] * layers
    done = [None] * layers
    feed_low = [None] * layers
    for l in reversed(range(layers)):
        p = params[l]
        section_in, normed, q, k, v, mixed, lse, middle, second, before = kept[l]
        late = planes and l + 1 < layers
        jobs = section_jobs([pairs[l + 1][0]]) + tensor_jobs(feed_low[l + 1]) if late else []
        (total, g_feed, up_sum), got = feed_back(
            team, ident("feed back", jobs), jobs, grad.astype(BF16), second.reshape(seq, width),
            before, p["up"], p["down"],
        )
        if late:
            attn_low = section_sums([pairs[l + 1][0]], got[:1])
            feed_done = tensor_sums(feed_low[l + 1], got[1:])
        _, norm_back = jax.vjp(layer_norm, middle, p["gains"][1], p["offsets"][1])
        grad_mid, gain_two, offset_two = norm_back(total)
        grad_mid = grad_mid + grad
        jobs = section_jobs([g_feed]) + (tensor_jobs(attn_low) if late else [])
        (total, g_attn, qv_sum), got = attend_back(
            team, ident("attend back", jobs), jobs, grad_mid.astype(BF16), length, slopes, normed,
            p["qk"], p["vo"], q, k, v, mixed, lse,
        )
        if planes:
            feed_low[l] = section_sums([g_feed], got[:1])
        if late:
            done[l + 1] = tensor_sums(attn_low, got[1:]) + feed_done
        _, norm_back = jax.vjp(layer_norm, section_in, p["gains"][0], p["offsets"][0])
        grad_in, gain_one, offset_one = norm_back(total)
        bias_two = jnp.sum(grad, axis=0)
        grad = grad_in + grad_mid
        pairs[l] = (g_attn.reshape((2, 2) + g_attn.shape[1:]), g_feed)

        def placed(values, size):
            out = jnp.zeros((fan if planes else shards, cut, size), F32)
            at = (0, j, 0) if planes else (z, 0, 0)
            return lax.dynamic_update_slice(out, values.reshape(fan, 1, size), at).reshape(
                -1, width
            )

        units = jnp.swapaxes(up_sum.reshape(halves, fan, strip), 0, 1)
        small_rows[l] = [
            gain_one[None],
            gain_two[None],
            offset_one[None],
            offset_two[None],
            jnp.sum(grad_mid, axis=0)[None],
            bias_two[None],
            placed(qv_sum[0], cols),
            placed(qv_sum[1], cols),
            placed(units, hidden),
        ]

    _, embed_back = jax.vjp(layer_norm, x, outer_gains[0], outer_offsets[0])
    grad_rows, embed_gain, embed_offset = embed_back(grad)
    packed = jnp.concatenate(
        [row for l in range(layers) for row in small_rows[l]]
        + [embed_gain[None], final_gain[None], embed_offset[None], final_offset[None]]
        + [jnp.broadcast_to(loss_part, (1, width))]
    )
    used = packed.shape[0]
    packed = jnp.pad(packed, ((0, -used % 8), (0, 0)))
    jobs = [gather(by_tensor, grad_rows.astype(BF16)), gather(by_dp, packed)]
    if planes:
        jobs += section_jobs(pairs[0][:1]) + spread_jobs(done[1])
    grad_rows, packed, *got = exchange(*jobs)
    grad_rows = grad_rows.reshape(tokens, width)
    packed = jnp.sum(packed, axis=0)
    jobs = [gather(Group(("section", "tensor"), (sections, shards)), packed)]
    if planes:
        lows = section_sums(pairs[0][:1], got[:1]) + feed_low[0]
        spread_one = got[1:]
        jobs += tensor_jobs(lows)
    embed_sum, packed, *got = table_sum(
        by_section, by_dp, jobs, grad_logits, ids[None, :] - vocab_start, final, grad_rows,
        exchange.ident("table"),
    )
    packed = jnp.sum(packed, axis=0)
    if planes:
        spread_zero = exchange(*spread_jobs(tensor_sums(lows, got)))
        attn_sum, feed_sum = (
            jnp.where(s == 0, zero, one) for zero, one in zip(spread_zero, spread_one)
        )
    else:
        chosen = [
            lax.dynamic_index_in_dim(
                lax.psum(jnp.stack([pair[n] for pair in pairs]), ("section", "dp")),
                s, 0, keepdims=False,
            )
            for n in range(2)
        ]
        attn_sum = chosen[0][:, None]
        feed_sum = chosen[1][:, None, None]
    embed_sum = embed_sum.reshape(vocab, width).astype(F32)
    per_layer = (used - 5) // layers
    mine = lax.dynamic_slice_in_dim(packed, s * per_layer, per_layer, 0)
    qv_rows = mine[6:8].reshape(2, -1)
    ff_row = mine[8:].reshape(-1)
    grad_qv = lax.dynamic_slice_in_dim(qv_rows, z * local_cols, local_cols, 1)
    grad_up_bias = lax.dynamic_slice_in_dim(ff_row, z * hidden * cut, hidden * cut, 0)
    base = per_layer * layers
    grad_outer_gain = lax.dynamic_slice_in_dim(packed, base + s, 1, 0)
    grad_outer_bias = lax.dynamic_slice_in_dim(packed, base + 2 + s, 1, 0)
    loss = packed[base + 4, 0] / token_count

    def columns(array):
        return array.astype(F32).reshape(-1, width).T

    grad_qkv = jnp.stack(
        [columns(attn_sum[0, :, 0]), columns(attn_sum[1, :, 0]), columns(attn_sum[0, :, 1])]
    )
    grad_out_mat = attn_sum[1, :, 1].astype(F32).reshape(-1, width)
    grad_up = columns(feed_sum[0])
    grad_down = feed_sum[1].astype(F32).reshape(-1, width)
    return (
        loss,
        embed_sum,
        grad_outer_gain,
        grad_outer_bias,
        mine[0:2][None],
        mine[2:4][None],
        grad_qkv[None],
        grad_qv[None],
        grad_out_mat[None],
        grad_up[None],
        grad_up_bias[None],
        grad_down[None],
        mine[4:6][None],
    )


def solution(mesh):
    return jax.shard_map(
        functools.partial(per_device, dict(mesh.shape)),
        mesh=mesh,
        in_specs=(
            P("dp", None),
            P("dp", None),
            P(),
            P("tensor", None),
            P("section", None),
            P("section", None),
            P("section", None, None),
            P("section", None, None),
            P("section", None, None, "tensor"),
            P("section", None, "tensor"),
            P("section", "tensor", None),
            P("section", None, "tensor"),
            P("section", "tensor"),
            P("section", "tensor", None),
            P("section", None, None),
        ),
        out_specs=(
            P(),
            P("tensor", None),
            P("section", None),
            P("section", None),
            P("section", None, None),
            P("section", None, None),
            P("section", None, None, "tensor"),
            P("section", None, "tensor"),
            P("section", "tensor", None),
            P("section", None, "tensor"),
            P("section", "tensor"),
            P("section", "tensor", None),
            P("section", None, None),
        ),
        check_vma=False,
    )
```

```python
import functools
import math

import jax
import jax.numpy as jnp
from jax import lax
from jax.experimental import pallas as pl
from jax.experimental.pallas import tpu as pltpu
from jax.sharding import PartitionSpec as P

HEADS = 16
HEAD_DIM = 64
EPS = 1e-05
NEG = -1e30
MESH = pl.DeviceIdType.MESH
F32 = jnp.float32
BF16 = jnp.bfloat16


def matmul(former, latter):
    return jnp.dot(former, latter, preferred_element_type=F32)


def matmul_t(former, latter):
    return lax.dot_general(
        former, latter, (((1,), (1,)), ((), ())), preferred_element_type=F32
    )


def outer_sum(former, latter):
    return lax.dot_general(
        former, latter, (((0,), (0,)), ((), ())), preferred_element_type=F32
    )


def layer_norm(inputs, weight, offset):
    centre = inputs - jnp.mean(inputs, axis=-1, keepdims=True)
    spread = jnp.mean(centre * centre, axis=-1, keepdims=True)
    return centre * lax.rsqrt(spread + EPS) * weight + offset


def gelu_tanh(inputs):
    return jax.nn.gelu(inputs, approximate=True)


class Group:
    def __init__(self, axes, sizes, square=False, line=False):
        self.square = square
        self.line = line
        self.axes = axes
        self.sizes = sizes
        self.count = math.prod(sizes)

    def me(self):
        place = 0
        for axis, size in zip(self.axes, self.sizes):
            place = place * size + lax.axis_index(axis)
        return place

    def device(self, place):
        spot = {}
        for axis, size in reversed(list(zip(self.axes, self.sizes))):
            spot[axis] = lax.rem(place, size)
            place = lax.div(place, size)
        return spot

    def peers(self):
        me = self.me()
        return [lax.rem(me + step, self.count) for step in range(1, self.count)]


def greet(groups):
    barrier = pltpu.get_barrier_semaphore()
    total = 0
    for group in groups:
        for peer in group.peers():
            pl.semaphore_signal(
                barrier, inc=1, device_id=group.device(peer), device_id_type=MESH
            )
            total += 1
    pl.semaphore_wait(barrier, total)


def send(group, peer, step, src, dst, send_sem, recv_sem):
    copy = pltpu.make_async_remote_copy(
        src_ref=src,
        dst_ref=dst,
        send_sem=send_sem.at[step],
        recv_sem=recv_sem.at[step],
        device_id=group.device(peer),
        device_id_type=MESH,
    )
    copy.start()
    return copy


def tie(*arrays):
    return lax.optimization_barrier(arrays)


class LineRows:
    def __init__(self, group, x, full, send_sem, recv_sem):
        self.group, self.count, self.me = group, group.count, group.me()
        self.x, self.full, self.sems = x, full, (send_sem, recv_sem)

    def copy(self, up, step):
        place = self.me - step if up else self.me + step
        place = jnp.clip(place, 0, self.count - 1)
        number = step if up else self.count - 1 + step
        src = self.x if step == 0 else self.full.at[place]
        return pltpu.make_async_remote_copy(
            src_ref=src,
            dst_ref=self.full.at[place],
            send_sem=self.sems[0].at[number],
            recv_sem=self.sems[1].at[number],
            device_id=self.group.device(
                jnp.clip(self.me + 1 if up else self.me - 1, 0, self.count - 1)
            ),
            device_id_type=MESH,
        )

    def leaves(self, up, step):
        if up:
            return (self.me - step >= 0) & (self.me < self.count - 1)
        return (self.me + step < self.count) & (self.me > 0)

    def arrives(self, up, step):
        return self.me - 1 - step >= 0 if up else self.me + 1 + step < self.count

    def start(self):
        for up in (True, False):

            @pl.when(self.leaves(up, 0))
            def _(up=up):
                self.copy(up, 0).start()

    def step(self, step):
        for up in (True, False):

            @pl.when(self.arrives(up, step - 1))
            def _(up=up):
                self.copy(up, step - 1).wait_recv()

            if step < self.count - 1:

                @pl.when(self.leaves(up, step))
                def _(up=up):
                    self.copy(up, step).start()

    def wait_sends(self):
        for step in range(self.count - 1):
            for up in (True, False):

                @pl.when(self.leaves(up, step))
                def _(up=up, step=step):
                    self.copy(up, step).wait_send()

    def finish(self):
        for step in range(1, self.count):
            self.step(step)
        self.wait_sends()


class LineSum:
    def __init__(self, group, x, stage, land, send_sem, recv_sem):
        self.group, self.count, self.me = group, group.count, group.me()
        self.x, self.stage, self.land, self.sems = x, stage, land, (send_sem, recv_sem)

    def copy(self, up, step):
        side = 0 if up else 1
        return pltpu.make_async_remote_copy(
            src_ref=self.stage.at[side, step],
            dst_ref=self.land.at[side, step],
            send_sem=self.sems[0].at[side, step],
            recv_sem=self.sems[1].at[side, step],
            device_id=self.group.device(
                jnp.clip(self.me + 1 if up else self.me - 1, 0, self.count - 1)
            ),
            device_id_type=MESH,
        )

    def leaves(self, up, step):
        return self.me < self.count - 1 - step if up else self.me > step

    def behind(self, up):
        return self.me > 0 if up else self.me < self.count - 1

    def step(self, step):
        for up in (True, False):
            place = self.count - 1 - step if up else step
            side = 0 if up else 1

            @pl.when(self.leaves(up, step) & self.behind(up))
            def _(up=up, place=place, side=side):
                self.copy(up, step).wait_recv()
                total = self.x[place].astype(F32) + self.land[side, step].astype(F32)
                self.stage[side, step] = total.astype(self.stage.dtype)
                self.copy(up, step).start()

            @pl.when(self.leaves(up, step) & jnp.logical_not(self.behind(up)))
            def _(up=up, place=place, side=side):
                self.stage[side, step] = self.x[place]
                self.copy(up, step).start()

    def finish(self, out):
        out[...] = self.x[self.me].astype(F32)
        for up in (True, False):
            side = 0 if up else 1
            for step in range(self.count - 1):

                @pl.when(self.behind(up) & (self.me == (self.count - 1 - step if up else step)))
                def _(up=up, step=step, side=side):
                    self.copy(up, step).wait_recv()
                    out[...] += self.land[side, step].astype(F32)

        for up in (True, False):
            for step in range(self.count - 1):

                @pl.when(self.leaves(up, step))
                def _(up=up, step=step):
                    self.copy(up, step).wait_send()


class Job:
    def __init__(self, kind, groups, x, axis=0, late=False):
        self.late = late
        self.kind, self.groups, self.x, self.axis = kind, groups, x, axis
        count = groups[0].count
        rest = x.shape[:axis] + x.shape[axis + 1 :]
        dma = pltpu.SemaphoreType.DMA
        self.in_spec = pl.BlockSpec(memory_space=pl.ANY)
        self.out_spec = pl.BlockSpec(memory_space=pl.ANY)
        self.scratch = [dma((count - 1,)), dma((count - 1,)), dma]
        if kind in ("gather", "spread"):
            self.in_spec = pl.BlockSpec(memory_space=pltpu.VMEM)
        if kind == "gather" and groups[0].line:
            self.scratch = [dma((2 * count - 2,)), dma((2 * count - 2,)), dma]
        if kind == "gather":
            self.out = jax.ShapeDtypeStruct((count,) + x.shape, x.dtype)
        elif kind == "spread":
            self.out = jax.ShapeDtypeStruct((groups[1].count, count) + x.shape, x.dtype)
            copies = 7 if groups[0].square else count
            if groups[0].square:
                self.scratch = [dma((6,)), dma((6,)), dma]
            self.scratch += [dma((copies,)), dma((copies,))]
        elif kind == "deal":
            self.out = jax.ShapeDtypeStruct((count - 1,) + rest, x.dtype)
        else:
            self.out = jax.ShapeDtypeStruct(rest, F32)
            self.out_spec = pl.BlockSpec(memory_space=pltpu.VMEM)
            if groups[0].line:
                self.in_spec = pl.BlockSpec(memory_space=pltpu.VMEM)
                self.scratch = [dma((2, count - 1)), dma((2, count - 1)), dma]
                self.scratch += [pltpu.VMEM((2, count - 1) + rest, x.dtype)] * 2
            else:
                self.scratch += [
                    pltpu.VMEM(rest, x.dtype), pltpu.VMEM((count - 1,) + rest, x.dtype)
                ]

    def key(self):
        return (self.kind, tuple(g.axes for g in self.groups), self.x.shape, str(self.x.dtype), self.axis)

    def start(self, x, out, send_sem, recv_sem, own_sem, *more):
        group = self.groups[0]
        me = group.me()
        peers = list(enumerate(group.peers()))

        def block(place):
            return x.at[(slice(None),) * self.axis + (place,)]

        if self.kind == "gather" and group.line:
            line = LineRows(group, x, out, send_sem, recv_sem)
            line.start()
            own = pltpu.make_async_copy(x, out.at[me], own_sem)
            own.start()

            def finish():
                line.finish()
                own.wait()

        elif self.kind == "reduce" and group.line:
            line = LineSum(group, x, *more, send_sem, recv_sem)
            line.step(0)

            def finish():
                for step in range(1, group.count - 1):
                    line.step(step)
                line.finish(out)

        elif self.kind == "gather":
            copies = [send(group, p, k, x, out.at[me], send_sem, recv_sem) for k, p in peers]
            own = pltpu.make_async_copy(x, out.at[me], own_sem)
            own.start()

            def finish():
                for copy in copies + [own]:
                    copy.wait()

        elif self.kind == "spread" and group.square:
            pair = self.groups[1]
            side = pair.me()
            fw_send, fw_recv = more
            size = self.x.shape[0] // 2
            near = [across(me, 0), across(me, 1)]

            def copy_of(number):
                at = pl.ds(SQUARE_HALF[number] * size, size)
                place = me if number < 4 else near[number - 4]
                dst = out.at[side, place, at]
                src = x.at[at] if number < 4 else dst
                copy = pltpu.make_async_remote_copy(
                    src_ref=src, dst_ref=dst, send_sem=send_sem.at[number],
                    recv_sem=recv_sem.at[number], device_id=group.device(near[SQUARE_STEP[number]]),
                    device_id_type=MESH,
                )
                origin = near[SQUARE_STEP[number]] if number < 4 else across(me, 2)
                return copy, out.at[side, origin, at]

            copies = [copy_of(number) for number in range(6)]
            for number in (0, 2, 1, 3):
                copies[number][0].start()
            passed = [send(pair, 1 - side, 6, x, out.at[side, me], fw_send, fw_recv)]
            own = pltpu.make_async_copy(x, out.at[side, me], own_sem)
            own.start()

            def arrived(number):
                copy, landed = copies[number]
                copy.wait_recv()
                passed.append(send(pair, 1 - side, number, landed, landed, fw_send, fw_recv))

            def finish():
                for number in (0, 2):
                    copies[number][0].wait_recv()
                    copies[4 + number // 2][0].start()
                    landed = copies[number][1]
                    passed.append(send(pair, 1 - side, number, landed, landed, fw_send, fw_recv))
                for number in (1, 3, 4, 5):
                    arrived(number)
                for copy in passed:
                    copy.wait()
                for copy, _ in copies:
                    copy.wait_send()
                own.wait()

        elif self.kind == "spread":
            pair = self.groups[1]
            side = pair.me()
            fw_send, fw_recv = more
            home = out.at[side, me]
            copies = [send(group, p, k, x, home, send_sem, recv_sem) for k, p in peers]
            last = group.count - 1
            passed = [send(pair, 1 - side, last, x, home, fw_send, fw_recv)]
            own = pltpu.make_async_copy(x, home, own_sem)
            own.start()

            def finish():
                for k, copy in enumerate(copies):
                    copy.wait_recv()
                    place = out.at[side, lax.rem(me + group.count - 1 - k, group.count)]
                    passed.append(send(pair, 1 - side, k, place, place, fw_send, fw_recv))
                for copy in passed:
                    copy.wait()
                for copy in copies:
                    copy.wait_send()
                own.wait()

        elif self.kind == "deal":
            copies = [send(group, p, k, block(p), out.at[k], send_sem, recv_sem) for k, p in peers]

            def finish():
                for copy in copies:
                    copy.wait()

        else:
            kept, slots = more
            copies = [send(group, p, k, block(p), slots.at[k], send_sem, recv_sem) for k, p in peers]
            own = pltpu.make_async_copy(block(me), kept, own_sem)
            own.start()

            def finish():
                own.wait()
                for copy in copies:
                    copy.wait()
                total = kept[...].astype(F32)
                for k in range(group.count - 1):
                    total = total + slots[k].astype(F32)
                out[...] = total

        return finish


def job_groups(jobs):
    return [group for job in jobs for group in job.groups]


def split_scratch(jobs, scratch):
    parts, at = [], 0
    for job in jobs:
        parts.append(scratch[at : at + len(job.scratch)])
        at += len(job.scratch)
    return parts


def exchange_body(jobs, *refs):
    count = len(jobs)
    greet(job_groups(jobs))
    parts = split_scratch(jobs, refs[2 * count :])
    ends = [
        job.start(refs[n], refs[count + n], *parts[n]) for n, job in enumerate(jobs)
    ]
    for end in ends:
        end()


class Exchanges:
    def __init__(self):
        self.idents = {}

    def ident(self, key):
        return self.idents.setdefault(key, len(self.idents))

    def __call__(self, *jobs):
        jobs = list(jobs)
        return pl.pallas_call(
            functools.partial(exchange_body, jobs),
            out_shape=tuple(job.out for job in jobs),
            in_specs=[job.in_spec for job in jobs],
            out_specs=tuple(job.out_spec for job in jobs),
            scratch_shapes=[one for job in jobs for one in job.scratch],
            compiler_params=pltpu.CompilerParams(
                collective_id=self.ident(tuple(job.key() for job in jobs)),
                has_side_effects=True,
                vmem_limit_bytes=32 * 2**20,
            ),
        )(*[job.x for job in jobs])


CHUNK = 512


def start_rows(group, x_ref, full, send_sem, recv_sem):
    me = group.me()
    full[me] = x_ref[...]
    return [
        send(group, peer, step, x_ref, full.at[me], send_sem, recv_sem)
        for step, peer in enumerate(group.peers())
    ]


def table_body(
    by_section, by_dp, by_tensor, jobs, g_ref, ids_ref, u_ref, gx_ref, *refs
):
    riders = len(jobs)
    xs, (out_ref, *outs), refs = refs[:riders], refs[riders : 2 * riders + 1], refs[2 * riders + 1 :]
    (g_buf, to_partner, from_partner, to_dp, from_dp, own, result,
    g_sem, ps_send, ps_recv, dp_send, dp_recv, ag_send, ag_recv, fw_send, fw_recv, own_sem,
    ) = refs[:17]
    gx_full, gx_send, gx_recv = refs[17:20]
    s, j = by_section.me(), by_dp.me()
    partner = 1 - s
    peers = by_dp.peers() + [j]
    count = by_dp.count
    block = own.shape[0]
    subs = block // CHUNK
    tokens = u_ref.shape[0]
    greet([by_section, by_dp, by_tensor] + job_groups(jobs))
    gx_copies = start_rows(by_tensor, gx_ref, gx_full, gx_send, gx_recv)
    parts = split_scratch(jobs, refs[20:])
    ends = [job.start(xs[n], outs[n], *parts[n]) for n, job in enumerate(jobs)]

    def chunk(half, place, sub):
        return (half * count + place) * subs + sub

    order = [(number, half) for number in range(count) for half in (0, 1)]

    def fetch(index, sub, slot):
        number, away = order[index]
        half = partner if away == 0 else s
        return pltpu.make_async_copy(
            g_ref.at[chunk(half, peers[number], sub)], g_buf.at[slot], g_sem.at[slot]
        )

    def remote(group, peer, number, sub, src, dst, send_sem, recv_sem):
        return pltpu.make_async_remote_copy(
            src_ref=src,
            dst_ref=dst,
            send_sem=send_sem.at[number, sub],
            recv_sem=recv_sem.at[number, sub],
            device_id=group.device(peer),
            device_id_type=MESH,
        )

    def rows(sub):
        return pl.ds(pl.multiple_of(sub * CHUNK, CHUNK), CHUNK)

    def partner_copy(number, sub):
        return remote(
            by_section, partner, number, sub,
            to_partner.at[number, rows(sub)], from_partner.at[number, rows(sub)],
            ps_send, ps_recv,
        )

    def chip_copy(number, sub):
        return remote(
            by_dp, peers[number], number, sub,
            to_dp.at[number, rows(sub)], from_dp.at[number, rows(sub)], dp_send, dp_recv,
        )

    def spread_copy(number, sub):
        return remote(
            by_dp, peers[number], number, sub,
            result.at[rows(sub)], out_ref.at[chunk(s, j, sub)], ag_send, ag_recv,
        )

    sources = [lax.rem(j + count - 1 - number, count) for number in range(count - 1)] + [j]

    def forward_copy(number, sub):
        target = out_ref.at[chunk(s, sources[number], sub)]
        origin = result.at[rows(sub)] if number == count - 1 else target
        return remote(by_section, partner, number, sub, origin, target, fw_send, fw_recv)

    def own_copy(sub):
        return pltpu.make_async_copy(
            result.at[rows(sub)], out_ref.at[chunk(s, j, sub)], own_sem.at[sub]
        )

    for copy in gx_copies:
        copy.wait()
    fetch(0, 0, 0).start()
    for index, (number, away) in enumerate(order):
        half = partner if away == 0 else s

        def one(sub, carry, index=index, number=number, away=away, half=half):
            slot = lax.rem(sub, 2)
            fetch(index, sub, slot).wait()

            @pl.when(sub + 1 < subs)
            def _():
                fetch(index, sub + 1, 1 - slot).start()

            if index + 1 < len(order):

                @pl.when(sub + 1 == subs)
                def _():
                    fetch(index + 1, 0, 1 - slot).start()

            base = chunk(half, peers[number], sub) * CHUNK
            place = base + lax.broadcasted_iota(jnp.int32, (CHUNK, tokens), 0)
            chosen = jnp.where(place == ids_ref[...], 1.0, 0.0).astype(BF16)
            term = outer_sum(g_buf[slot], u_ref[...]) + matmul(
                chosen, gx_full[...].reshape(tokens, gx_full.shape[2])
            )
            if away == 0:
                to_partner[number, rows(sub), :] = term.astype(BF16)
                partner_copy(number, sub).start()
            else:
                partner_copy(number, sub).wait_recv()
                term = term + from_partner[number, rows(sub), :].astype(F32)
                if number < count - 1:
                    to_dp[number, rows(sub), :] = term.astype(BF16)
                    chip_copy(number, sub).start()
                else:
                    own[rows(sub), :] = term
            return carry

        lax.fori_loop(0, subs, one, 0)

    def finish(sub, carry):
        term = own[rows(sub), :]
        for number in range(count - 1):
            chip_copy(number, sub).wait_recv()
            term = term + from_dp[number, rows(sub), :].astype(F32)
        result[rows(sub), :] = term.astype(BF16)
        for number in range(count - 1):
            spread_copy(number, sub).start()
        forward_copy(count - 1, sub).start()
        own_copy(sub).start()
        return carry

    lax.fori_loop(0, subs, finish, 0)

    def take(sub, carry):
        for number in range(count - 1):
            spread_copy(number, sub).wait_recv()
            forward_copy(number, sub).start()
        return carry

    lax.fori_loop(0, subs, take, 0)

    def drain(sub, carry):
        own_copy(sub).wait()
        for number in range(count):
            partner_copy(number, sub).wait_send()
            forward_copy(number, sub).wait()
        for number in range(count - 1):
            chip_copy(number, sub).wait_send()
            spread_copy(number, sub).wait_send()
        return carry

    lax.fori_loop(0, subs, drain, 0)
    for end in ends:
        end()


def across(me, step):
    bits = jnp.int32(step + 1)
    x, y = lax.rem(me, 2), lax.div(me, 2)
    return 2 * lax.rem(y + lax.div(bits, 2), 2) + lax.rem(x + lax.rem(bits, 2), 2)


SQUARE_HALF = (0, 1, 1, 0, 0, 1)
SQUARE_STEP = (0, 0, 1, 1, 1, 0)


def table_square_body(by_section, by_dp, by_tensor, jobs, g_ref, ids_ref, u_ref, gx_ref, *refs):
    riders = len(jobs)
    xs, (out_ref, *outs), refs = refs[:riders], refs[riders : 2 * riders + 1], refs[2 * riders + 1 :]
    (
        g_buf, to_partner, from_partner, to_dp, hop_land, from_dp, own, result,
        g_sem, ps_send, ps_recv, hop_send, hop_recv, dp_send, dp_recv, ag_send, ag_recv,
        fw_send, fw_recv, own_sem,
    ) = refs[:20]
    gx_full, gx_send, gx_recv = refs[20:23]
    s, j = by_section.me(), by_dp.me()
    partner = 1 - s
    near_x, near_y, far = (across(j, step) for step in range(3))
    peers = [far, near_y, near_x, j]
    count = 4
    block = own.shape[0]
    subs = block // CHUNK
    half_rows = CHUNK // 2
    tokens = u_ref.shape[0]
    greet([by_section, by_dp, by_tensor] + job_groups(jobs))
    line = LineRows(by_tensor, gx_ref, gx_full, gx_send, gx_recv)
    line.start()
    gx_full[line.me] = gx_ref[...]
    parts = split_scratch(jobs, refs[23:])
    ends = [
        job.start(xs[n], outs[n], *parts[n]) for n, job in enumerate(jobs) if not job.late
    ]

    def chunk(half, place, sub):
        return (half * count + place) * subs + sub

    order = [(number, away) for number in range(count) for away in (0, 1)]

    def fetch(index, sub, slot):
        number, away = order[index]
        half = partner if away == 0 else s
        return pltpu.make_async_copy(
            g_ref.at[chunk(half, peers[number], sub)], g_buf.at[slot], g_sem.at[slot]
        )

    def remote(group, peer, number, sub, src, dst, send_sem, recv_sem):
        return pltpu.make_async_remote_copy(
            src_ref=src,
            dst_ref=dst,
            send_sem=send_sem.at[number, sub],
            recv_sem=recv_sem.at[number, sub],
            device_id=group.device(peer),
            device_id_type=MESH,
        )

    def rows(sub):
        return pl.ds(pl.multiple_of(sub * CHUNK, CHUNK), CHUNK)

    def half_of(sub, which):
        return pl.ds(pl.multiple_of(sub * CHUNK + which * half_rows, half_rows), half_rows)

    def partner_copy(number, sub):
        return remote(
            by_section, partner, number, sub,
            to_partner.at[number, rows(sub)], from_partner.at[number, rows(sub)],
            ps_send, ps_recv,
        )

    def hop_copy(which, sub):
        return remote(
            by_dp, (near_x, near_y)[which], which, sub,
            to_dp.at[0, half_of(sub, which)], hop_land.at[half_of(sub, which)], hop_send, hop_recv,
        )

    def chip_copy(number, sub):
        return remote(
            by_dp, (near_y, near_x)[number], number, sub,
            to_dp.at[number + 1, rows(sub)], from_dp.at[number, rows(sub)], dp_send, dp_recv,
        )

    def spread_copy(number, sub):
        which = SQUARE_HALF[number]
        place = j if number < 4 else (near_x, near_y)[number - 4]
        dst = out_ref.at[chunk(s, place, sub), pl.ds(which * half_rows, half_rows)]
        src = result.at[half_of(sub, which)] if number < 4 else dst
        peer = (near_x, near_y)[SQUARE_STEP[number]]
        return remote(by_dp, peer, number, sub, src, dst, ag_send, ag_recv)

    sources = [near_x, near_y, far, j]

    def forward_copy(number, sub):
        target = out_ref.at[chunk(s, sources[number], sub)]
        origin = result.at[rows(sub)] if number == count - 1 else target
        return remote(by_section, partner, number, sub, origin, target, fw_send, fw_recv)

    def own_copy(sub):
        return pltpu.make_async_copy(
            result.at[rows(sub)], out_ref.at[chunk(s, j, sub)], own_sem.at[sub]
        )

    def slot_of(number, away):
        if away == 0:
            return to_partner.at[number]
        return to_dp.at[number] if number < 3 else own

    fetch(0, 0, 0).start()
    stops = {(step * len(order)) // line.count: step for step in range(1, line.count - 1)}
    for index, (number, away) in enumerate(order):
        if index in stops:
            line.step(stops[index])

        def share(sub, carry, index=index, number=number, away=away):
            slot = lax.rem(sub, 2)
            fetch(index, sub, slot).wait()

            @pl.when(sub + 1 < subs)
            def _():
                fetch(index, sub + 1, 1 - slot).start()

            if index + 1 < len(order):

                @pl.when(sub + 1 == subs)
                def _():
                    fetch(index + 1, 0, 1 - slot).start()

            held = slot_of(number, away)
            held[rows(sub), :] = outer_sum(g_buf[slot], u_ref[...]).astype(held.dtype)
            return carry

        lax.fori_loop(0, subs, share, 0)
    line.step(line.count - 1)
    line.wait_sends()
    ends += [job.start(xs[n], outs[n], *parts[n]) for n, job in enumerate(jobs) if job.late]

    for index, (number, away) in enumerate(order):
        half = partner if away == 0 else s

        def one(sub, carry, number=number, away=away, half=half):
            base = chunk(half, peers[number], sub) * CHUNK
            place = base + lax.broadcasted_iota(jnp.int32, (CHUNK, tokens), 0)
            chosen = jnp.where(place == ids_ref[...], 1.0, 0.0).astype(BF16)
            term = matmul(chosen, gx_full[...].reshape(tokens, gx_full.shape[2]))
            term = term + slot_of(number, away)[rows(sub), :].astype(F32)
            if away == 0:
                to_partner[number, rows(sub), :] = term.astype(BF16)
                partner_copy(number, sub).start()
                return carry
            partner_copy(number, sub).wait_recv()
            term = term + from_partner[number, rows(sub), :].astype(F32)
            if number == 0:
                to_dp[0, rows(sub), :] = term.astype(BF16)
                for which in range(2):
                    hop_copy(which, sub).start()
            elif number < 3:
                which = number - 1
                hop_copy(which, sub).wait_recv()
                mine = slice(which * half_rows, (which + 1) * half_rows)
                rest = slice((1 - which) * half_rows, (2 - which) * half_rows)
                to_dp[number, half_of(sub, which), :] = (
                    term[mine] + hop_land[half_of(sub, which), :].astype(F32)
                ).astype(BF16)
                to_dp[number, half_of(sub, 1 - which), :] = term[rest].astype(BF16)
                chip_copy(which, sub).start()
            else:
                own[rows(sub), :] = term
            return carry

        lax.fori_loop(0, subs, one, 0)

    def finish(sub, carry):
        term = own[rows(sub), :]
        for number in range(2):
            chip_copy(number, sub).wait_recv()
            term = term + from_dp[number, rows(sub), :].astype(F32)
        result[rows(sub), :] = term.astype(BF16)
        for number in (0, 2, 1, 3):
            spread_copy(number, sub).start()
        forward_copy(count - 1, sub).start()
        own_copy(sub).start()
        return carry

    lax.fori_loop(0, subs, finish, 0)

    def pass_on(sub, carry):
        for number in (0, 2):
            spread_copy(number, sub).wait_recv()
            spread_copy(4 + number // 2, sub).start()
        for number in (0, 1):
            spread_copy(2 * number + 1, sub).wait_recv()
            forward_copy(number, sub).start()
        return carry

    lax.fori_loop(0, subs, pass_on, 0)

    def last(sub, carry):
        for number in (4, 5):
            spread_copy(number, sub).wait_recv()
        forward_copy(2, sub).start()
        return carry

    lax.fori_loop(0, subs, last, 0)

    def drain(sub, carry):
        own_copy(sub).wait()
        for number in range(count):
            partner_copy(number, sub).wait_send()
            forward_copy(number, sub).wait()
        for number in range(2):
            hop_copy(number, sub).wait_send()
            chip_copy(number, sub).wait_send()
        for number in range(6):
            spread_copy(number, sub).wait_send()
        return carry

    lax.fori_loop(0, subs, drain, 0)
    for end in ends:
        end()


def table_sum(by_section, by_dp, by_tensor, jobs, grads, ids, final, grad_rows, ident):
    chunks, tokens, _ = grads.shape
    width = final.shape[1]
    count = by_dp.count
    subs = chunks // (2 * count)
    block = subs * CHUNK
    assert subs % 2 == 0
    dma = pltpu.SemaphoreType.DMA
    low = functools.partial(pltpu.VMEM, dtype=BF16)
    square = by_dp.square
    scratch = [
        low((2, tokens, CHUNK)),
        low((count, block, width)),
        low((count, block, width)),
        low((count - 1, block, width)),
    ]
    scratch += [low((block, width)), low((2, block, width))] if square else [
        low((count - 1, block, width))
    ]
    scratch += [pltpu.VMEM((block, width), F32), low((block, width)), dma((2,))]
    copies = (count, 2, 2, 6, count) if square else (count, count - 1, count - 1, count)
    scratch += [dma((copy, subs)) for copy in copies for _ in range(2)] + [dma((subs,))]
    scratch += [low((by_tensor.count,) + grad_rows.shape)]
    scratch += [dma(((by_tensor.count - 1) * (2 if square else 1),))] * 2
    vmem = pl.BlockSpec(memory_space=pltpu.VMEM)
    hbm = pl.BlockSpec(memory_space=pl.ANY)
    return pl.pallas_call(
        functools.partial(
            table_square_body if by_dp.square else table_body, by_section, by_dp, by_tensor, jobs
        ),
        out_shape=(jax.ShapeDtypeStruct((chunks, CHUNK, width), BF16),)
        + tuple(job.out for job in jobs),
        in_specs=[hbm, vmem, vmem, vmem] + [job.in_spec for job in jobs],
        out_specs=(hbm,) + tuple(job.out_spec for job in jobs),
        scratch_shapes=scratch + [one for job in jobs for one in job.scratch],
        compiler_params=pltpu.CompilerParams(
            collective_id=ident, has_side_effects=True, vmem_limit_bytes=56 * 2**20
        ),
    )(grads, ids, final, grad_rows, *[job.x for job in jobs])


LANES = 128


def head_logits_body(u_ref, e_ref, ids_ref, logits_ref, top_ref, total_ref, pick_ref):
    step = pl.program_id(0)
    tokens, tile = logits_ref.shape[1:]

    @pl.when(step == 0)
    def _():
        top_ref[...] = jnp.full_like(top_ref, NEG)
        total_ref[...] = jnp.zeros_like(total_ref)
        pick_ref[...] = jnp.zeros_like(pick_ref)

    logits = matmul_t(u_ref[...], e_ref[...])
    logits_ref[0] = logits
    place = step * tile + lax.broadcasted_iota(jnp.int32, (tokens, tile), 1)
    picked = jnp.where(place == ids_ref[...], logits, 0.0)
    pieces = [logits[:, at : at + LANES] for at in range(0, tile, LANES)]
    before = top_ref[...]
    top = functools.reduce(jnp.maximum, pieces, before)
    total = total_ref[...] * jnp.exp(before - top)
    pick = pick_ref[...]
    for number, piece in enumerate(pieces):
        total = total + jnp.exp(piece - top)
        pick = pick + picked[:, number * LANES : (number + 1) * LANES]
    top_ref[...] = top
    total_ref[...] = total
    pick_ref[...] = pick


def head_logits(final, embedding, ids):
    tokens, width = final.shape
    vocab = embedding.shape[0]
    fixed = pl.BlockSpec((tokens, LANES), lambda step: (0, 0))
    stat = jax.ShapeDtypeStruct((tokens, LANES), F32)
    return pl.pallas_call(
        head_logits_body,
        grid=(vocab // CHUNK,),
        out_shape=(
            jax.ShapeDtypeStruct((vocab // CHUNK, tokens, CHUNK), F32), stat, stat, stat
        ),
        in_specs=[
            pl.BlockSpec((tokens, width), lambda step: (0, 0)),
            pl.BlockSpec((CHUNK, width), lambda step: (step, 0)),
            pl.BlockSpec((tokens, 1), lambda step: (0, 0)),
        ],
        out_specs=(
            pl.BlockSpec((1, tokens, CHUNK), lambda step: (step, 0, 0)), fixed, fixed, fixed
        ),
        compiler_params=pltpu.CompilerParams(vmem_limit_bytes=40 * 2**20),
        cost_estimate=pl.CostEstimate(
            flops=2 * tokens * vocab * width,
            bytes_accessed=4 * tokens * vocab + 2 * vocab * width,
            transcendentals=tokens * vocab,
        ),
    )(final, embedding, ids)


def head_grads_body(logits_ref, e_ref, ids_ref, norm_ref, weight_ref, grads_ref, back_ref, acc):
    step = pl.program_id(0)
    tokens, tile = grads_ref.shape[1:]

    @pl.when(step == 0)
    def _():
        acc[...] = jnp.zeros_like(acc)

    place = step * tile + lax.broadcasted_iota(jnp.int32, (tokens, tile), 1)
    probs = jnp.exp(logits_ref[0] - norm_ref[...])
    grads = (jnp.where(place == ids_ref[...], probs - 1.0, probs) * weight_ref[...]).astype(BF16)
    grads_ref[0] = grads
    acc[...] += matmul(grads, e_ref[...])

    @pl.when(step == pl.num_programs(0) - 1)
    def _():
        back_ref[...] = acc[...].astype(BF16)


def head_grads(logits, embedding, ids, norm, weight):
    chunks, tokens, _ = logits.shape
    vocab, width = embedding.shape
    column = pl.BlockSpec((tokens, 1), lambda step: (0, 0))
    tile = pl.BlockSpec((1, tokens, CHUNK), lambda step: (step, 0, 0))
    return pl.pallas_call(
        head_grads_body,
        grid=(chunks,),
        out_shape=(
            jax.ShapeDtypeStruct(logits.shape, BF16),
            jax.ShapeDtypeStruct((tokens, width), BF16),
        ),
        in_specs=[
            tile, pl.BlockSpec((CHUNK, width), lambda step: (step, 0)), column, column, column
        ],
        out_specs=(tile, pl.BlockSpec((tokens, width), lambda step: (0, 0))),
        scratch_shapes=[pltpu.VMEM((tokens, width), F32)],
        compiler_params=pltpu.CompilerParams(vmem_limit_bytes=40 * 2**20),
        cost_estimate=pl.CostEstimate(
            flops=2 * tokens * vocab * width,
            bytes_accessed=6 * tokens * vocab + 2 * vocab * width,
            transcendentals=tokens * vocab,
        ),
    )(logits, embedding, ids, norm, weight)


BLOCK = 256


def masked_scores(queries, keys, slope, length, first):
    rows, cols = queries.shape[0], keys.shape[0]
    raw = matmul_t(queries, keys)
    i = first + lax.broadcasted_iota(jnp.int32, (rows, cols), 0)
    j = lax.broadcasted_iota(jnp.int32, (rows, cols), 1)
    scores = raw * HEAD_DIM ** (-0.5) - slope * (i - j).astype(F32)
    return jnp.where((j <= i) & (j < length), scores, NEG)


SMEM = pl.BlockSpec(memory_space=pltpu.SMEM)
VMEM = pl.BlockSpec(memory_space=pltpu.VMEM)


class TeamRows:
    def __init__(self, team, x_ref, full, stage, slots, own, ag_send, ag_recv, rs_send, rs_recv):
        self.team, self.count, self.me = team, team.count, team.me()
        self.x_ref, self.full, self.stage, self.slots, self.own = x_ref, full, stage, slots, own
        self.ag_sems, self.rs_sems = (ag_send, ag_recv), (rs_send, rs_recv)

    def shifted(self, step):
        return across(self.me, step)

    def peer(self, step):
        if self.team.square:
            return self.shifted(step)
        return lax.rem(self.me + 1 + step, self.count)

    def source(self, step):
        if self.team.square:
            return self.shifted(step)
        return lax.rem(self.me + self.count - 1 - step, self.count)

    def back_step(self, place):
        if self.team.square:
            flip_x = lax.rem(lax.rem(self.me, 2) + lax.rem(place, 2), 2)
            flip_y = lax.rem(lax.div(self.me, 2) + lax.div(place, 2), 2)
            return 2 * flip_y + flip_x - 1
        return lax.rem(place + self.count - 1 - self.me, self.count)

    def remote(self, number, peer, src, dst, sems):
        return pltpu.make_async_remote_copy(
            src_ref=src,
            dst_ref=dst,
            send_sem=sems[0].at[number],
            recv_sem=sems[1].at[number],
            device_id=self.team.device(peer),
            device_id_type=MESH,
        )

    def ag(self, number):
        if not self.team.square:
            return self.remote(
                number, self.peer(number), self.x_ref, self.full.at[self.me], self.ag_sems
            )
        half = self.x_ref.shape[0] // 2
        which = SQUARE_HALF[number]
        rows = pl.ds(which * half, half)
        peer = self.shifted(SQUARE_STEP[number])
        if number < 4:
            src, place = self.x_ref.at[rows], self.me
        else:
            place = self.shifted(number - 4)
            src = self.full.at[place, rows]
        return self.remote(number, peer, src, self.full.at[place, rows], self.ag_sems)

    def rs(self, step):
        return self.remote(
            step, self.peer(step), self.stage.at[self.peer(step)], self.slots.at[step], self.rs_sems
        )

    def send_rows(self):
        for number in (0, 2, 1, 3) if self.team.square else range(self.count - 1):
            self.ag(number).start()
        self.full[self.me] = self.x_ref[...]

    def pass_on(self):
        if self.team.square:
            for number in (0, 2):
                self.ag(number).wait_recv()
                self.ag(4 + number // 2).start()

    def wait_rows(self, step):
        if not self.team.square:
            self.ag(step).wait_recv()
            return
        for number, these in enumerate(((1,), (3,), (4, 5))):

            @pl.when(step == number)
            def _(these=these):
                for one in these:
                    self.ag(one).wait_recv()

    def each_arrival(self, work):
        work(self.me)
        self.pass_on()

        def one(step, carry):
            self.wait_rows(step)
            work(self.source(step))
            return carry

        lax.fori_loop(0, self.count - 1, one, 0)

    def each_arrival_and_back(self, term):
        self.own[...] = term(self.me)
        self.pass_on()

        def one(step, carry):
            self.wait_rows(step)
            place = self.source(step)
            self.stage[place] = term(place).astype(BF16)
            self.rs(self.back_step(place)).start()
            return carry

        lax.fori_loop(0, self.count - 1, one, 0)

    def finish(self, total_ref):
        for step in range(self.count - 1):
            self.rs(step).wait()
        total = self.own[...]
        for step in range(self.count - 1):
            total = total + self.slots[step].astype(F32)
        total_ref[...] = total
        for number in range(6 if self.team.square else self.count - 1):
            self.ag(number).wait_send()


def team_scratch(team, part, model):
    count = team.count
    dma = pltpu.SemaphoreType.DMA
    copies = 6 if team.square else count - 1
    return [
        pltpu.VMEM((count, part, model), BF16),
        pltpu.VMEM((count, part, model), BF16),
        pltpu.VMEM((count - 1, part, model), BF16),
        pltpu.VMEM((part, model), F32),
        dma((copies,)),
        dma((copies,)),
        dma((count - 1,)),
        dma((count - 1,)),
    ]


class LateDeal:
    def __init__(self, pair, landing, send_sem, recv_sem):
        self.pair, self.landing, self.sems = pair, landing, (send_sem, recv_sem)

    def other(self):
        return 1 - self.pair.me()

    def start(self, src):
        self.copy = send(self.pair, self.other(), 0, src, self.landing, *self.sems)

    def wait(self):
        self.copy.wait()


def team_call(body, team, ident, jobs, arrays, specs, outs, out_specs, scratch, pair=None, dealt=None):
    if pair is not None:
        outs, out_specs = tuple(outs) + (dealt,), tuple(out_specs) + (HBM,)
        scratch = list(scratch) + [pltpu.SemaphoreType.DMA((1,))] * 2
    part, model = arrays[0].shape
    count_in, count_out, riders = len(arrays), len(outs), len(jobs)
    own_scratch = team_scratch(team, part, model)

    def kernel(*refs):
        ins, refs = refs[:count_in], refs[count_in:]
        xs, refs = refs[:riders], refs[riders:]
        results, refs = refs[:count_out], refs[count_out:]
        landings, refs = refs[:riders], refs[riders:]
        rows = TeamRows(team, ins[0], *refs[: len(own_scratch)])
        refs = refs[len(own_scratch) :]
        mine, refs = refs[: len(scratch)], refs[len(scratch) :]
        greet([team] + job_groups(jobs) + ([] if pair is None else [pair]))
        rows.send_rows()
        parts = split_scratch(jobs, refs)
        ends = [job.start(xs[n], landings[n], *parts[n]) for n, job in enumerate(jobs)]
        if pair is None:
            body(rows, ins, results, mine)
        else:
            body(rows, ins, results[:-1], mine[:-2], LateDeal(pair, results[-1], *mine[-2:]))
        for end in ends:
            end()

    out = pl.pallas_call(
        kernel,
        out_shape=tuple(outs) + tuple(job.out for job in jobs),
        in_specs=list(specs) + [job.in_spec for job in jobs],
        out_specs=tuple(out_specs) + tuple(job.out_spec for job in jobs),
        scratch_shapes=own_scratch + list(scratch) + [one for job in jobs for one in job.scratch],
        compiler_params=pltpu.CompilerParams(
            collective_id=ident, has_side_effects=True, vmem_limit_bytes=58 * 2**20
        ),
    )(*arrays, *[job.x for job in jobs])
    return out[:count_out], list(out[count_out:])


def part_rows(place, part):
    return pl.ds(pl.multiple_of(place * part, part), part)


def attend_body(rows, ins, outs, scratch):
    x_ref, length_ref, slope_ref, qk_ref, vo_ref, bias_ref = ins
    total_ref, full_out, q_ref, k_ref, v_ref, mixed_ref, lse_ref = outs
    (full_sem,) = scratch
    part = x_ref.shape[0]
    width = q_ref.shape[1]

    def project(place):
        at = part_rows(place, part)
        block = rows.full[place]
        q_ref[at, :] = (matmul_t(block, qk_ref[0]) + bias_ref[0:1, :]).astype(BF16)
        k_ref[at, :] = matmul_t(block, qk_ref[1]).astype(BF16)
        v_ref[at, :] = (matmul_t(block, vo_ref[0]) + bias_ref[1:2, :]).astype(BF16)

    rows.each_arrival(project)
    keep = pltpu.make_async_copy(rows.full, full_out, full_sem)
    keep.start()

    def one(turn, carry):
        step = lax.rem(2 * rows.count - 2 - turn, rows.count)
        place = rows.peer(step)
        for block in range(rows.count):

            @pl.when(place == block)
            def _(first=block * part, upto=(block + 1) * part):
                for head in range(width // HEAD_DIM):
                    lanes = slice(head * HEAD_DIM, (head + 1) * HEAD_DIM)
                    scores = masked_scores(
                        q_ref[first:upto, lanes], k_ref[:upto, lanes], slope_ref[head],
                        length_ref[0], first,
                    )
                    highest = jnp.max(scores, axis=-1, keepdims=True)
                    powers = jnp.exp(scores - highest)
                    total = jnp.sum(powers, axis=-1, keepdims=True)
                    probs = (powers * (1.0 / total)).astype(BF16)
                    mixed_ref[first:upto, lanes] = matmul(probs, v_ref[:upto, lanes]).astype(BF16)
                    lse_ref[head, first:upto, :] = highest + jnp.log(total)

        term = matmul(mixed_ref[part_rows(place, part), :], vo_ref[1])

        @pl.when(step < rows.count - 1)
        def _():
            rows.stage[place] = term.astype(BF16)
            rows.rs(step).start()

        @pl.when(step == rows.count - 1)
        def _():
            rows.own[...] = term

        return carry

    lax.fori_loop(0, rows.count, one, 0)
    rows.finish(total_ref)
    keep.wait()


HBM = pl.BlockSpec(memory_space=pl.ANY)


def attend(team, ident, jobs, x, length, slopes, qk, vo, bias):
    part, model = x.shape
    seq = part * team.count
    width = qk.shape[1]
    low = jax.ShapeDtypeStruct((seq, width), BF16)
    return team_call(
        attend_body, team, ident, jobs,
        [x, length, slopes, qk, vo, bias],
        [VMEM, SMEM, SMEM, VMEM, VMEM, VMEM],
        (
            jax.ShapeDtypeStruct((part, model), F32),
            jax.ShapeDtypeStruct((team.count, part, model), BF16),
            low, low, low, low,
            jax.ShapeDtypeStruct((width // HEAD_DIM, seq, 1), F32),
        ),
        (VMEM, HBM, VMEM, VMEM, VMEM, VMEM, VMEM),
        [pltpu.SemaphoreType.DMA],
    )


def attend_back_body(rows, ins, outs, scratch, late=None):
    gy_ref, length_ref, slope_ref, a_ref, qk_ref, vo_ref, q_ref, k_ref, v_ref, mixed_ref, lse_ref = ins
    total_ref, grads_ref, sums_ref = outs
    go, gq, gk, gv, gk_sum, gv_sum = scratch
    part = gy_ref.shape[0]
    seq, width = q_ref.shape
    heads = width // HEAD_DIM
    gk_sum[...] = jnp.zeros_like(gk_sum)
    gv_sum[...] = jnp.zeros_like(gv_sum)
    sums_ref[...] = jnp.zeros_like(sums_ref)

    def open_block(place):
        go[part_rows(place, part), :] = matmul_t(rows.full[place], vo_ref[1]).astype(BF16)

    rows.each_arrival(open_block)
    for block in reversed(range(rows.count)):
        first, upto = block * part, (block + 1) * part
        for head in range(heads):
            lanes = slice(head * HEAD_DIM, (head + 1) * HEAD_DIM)
            queries, grads = q_ref[first:upto, lanes], go[first:upto, lanes]
            keys, values = k_ref[:upto, lanes], v_ref[:upto, lanes]
            scores = masked_scores(queries, keys, slope_ref[head], length_ref[0], first)
            probs = jnp.exp(scores - lse_ref[head, first:upto, :])
            grad_probs = matmul_t(grads, values)
            inner = jnp.sum(probs * grad_probs, axis=-1, keepdims=True)
            grad_scores = (probs * (grad_probs - inner) * HEAD_DIM ** (-0.5)).astype(BF16)
            piece = matmul(grad_scores, keys)
            sums_ref[0:1, lanes] += jnp.sum(piece, axis=0, keepdims=True)
            gq[first:upto, lanes] = piece.astype(BF16)
            gk_sum[:upto, lanes] += outer_sum(grad_scores, queries)
            gv_sum[:upto, lanes] += outer_sum(probs.astype(BF16), grads)
        gk[first:upto, :] = gk_sum[first:upto, :].astype(BF16)
        gv[first:upto, :] = gv_sum[first:upto, :].astype(BF16)
        term = (
            matmul(gq[first:upto, :], qk_ref[0]) + matmul(gk[first:upto, :], qk_ref[1])
            + matmul(gv[first:upto, :], vo_ref[0])
        )

        @pl.when(rows.me != block)
        def _(block=block, term=term):
            rows.stage[block] = term.astype(BF16)
            rows.rs(rows.back_step(block)).start()

        @pl.when(rows.me == block)
        def _(term=term):
            rows.own[...] = term

    sums_ref[1:2, :] = jnp.sum(gv_sum[...], axis=0, keepdims=True)
    model = gy_ref.shape[1]
    grads_ref[3] = outer_sum(mixed_ref[...], rows.full[...].reshape(seq, model))
    grads_ref[0] = outer_sum(gq[...], a_ref[...])
    grads_ref[1] = outer_sum(gv[...], a_ref[...])
    grads_ref[2] = outer_sum(gk[...], a_ref[...])
    if late is not None:
        late.start(grads_ref.at[pl.ds(2 * late.other(), 2)])
    rows.finish(total_ref)
    if late is not None:
        late.wait()


def attend_back(team, ident, jobs, pair, gy, length, slopes, a, qk, vo, q, k, v, mixed, lse):
    part, model = gy.shape
    seq, width = q.shape
    return team_call(
        attend_back_body, team, ident, jobs,
        [gy, length, slopes, a, qk, vo, q, k, v, mixed, lse],
        [VMEM, SMEM, SMEM] + [VMEM] * 8,
        (
            jax.ShapeDtypeStruct((part, model), F32),
            jax.ShapeDtypeStruct((4, width, model), F32),
            jax.ShapeDtypeStruct((2, width), F32),
        ),
        (VMEM,) * 3,
        [pltpu.VMEM((seq, width), BF16)] * 4 + [pltpu.VMEM((seq, width), F32)] * 2,
        pair,
        jax.ShapeDtypeStruct((2, width, model), F32),
    )


GELU_A = 0.7978845608028654
GELU_B = 0.044715


def feed_body(rows, ins, outs, scratch):
    x_ref, up_ref, down_ref, bias_ref = ins
    total_ref, full_out, before_ref = outs
    (full_sem,) = scratch
    part = x_ref.shape[0]
    units = up_ref.shape[0]
    tile = min(units, BLOCK)

    def term(place):
        at = part_rows(place, part)
        block = rows.full[place]
        total = None
        for first in range(0, units, tile):
            lanes = slice(first, first + tile)
            before = matmul_t(block, up_ref[lanes, :]) + bias_ref[:, lanes]
            before_ref[at, lanes] = before
            bend = jnp.tanh(GELU_A * (before + GELU_B * before * before * before))
            active = (0.5 * before * (1.0 + bend)).astype(BF16)
            piece = matmul(active, down_ref[lanes, :])
            total = piece if total is None else total + piece
        return total

    rows.each_arrival_and_back(term)
    keep = pltpu.make_async_copy(rows.full, full_out, full_sem)
    keep.start()
    rows.finish(total_ref)
    keep.wait()


def feed(team, ident, jobs, x, up, down, bias):
    part, model = x.shape
    units = up.shape[0]
    return team_call(
        feed_body, team, ident, jobs,
        [x, up, down, bias],
        [VMEM] * 4,
        (
            jax.ShapeDtypeStruct((part, model), F32),
            jax.ShapeDtypeStruct((team.count, part, model), BF16),
            jax.ShapeDtypeStruct((part * team.count, units), F32),
        ),
        (VMEM, HBM, VMEM),
        [pltpu.SemaphoreType.DMA],
    )


def feed_back_body(rows, ins, outs, scratch, late=None):
    gz_ref, c_ref, before_ref, up_ref, down_ref = ins
    total_ref, grads_ref, sums_ref = outs
    active, low = scratch
    part, model = gz_ref.shape
    seq = part * rows.count
    units = up_ref.shape[0]
    tile = min(units, BLOCK)
    sums_ref[...] = jnp.zeros_like(sums_ref)

    def term(place):
        at = part_rows(place, part)
        gz = rows.full[place]
        for first in range(0, units, tile):
            lanes = slice(first, first + tile)
            before = before_ref[at, lanes]
            square = before * before
            bend = jnp.tanh(GELU_A * before * (1.0 + GELU_B * square))
            half = 0.5 * (1.0 + bend)
            slope = half + 0.5 * before * (1.0 - bend * bend) * (
                GELU_A * (1.0 + 3.0 * GELU_B * square)
            )
            grad = matmul_t(gz, down_ref[lanes, :]) * slope
            sums_ref[:, lanes] += jnp.sum(grad, axis=0, keepdims=True)
            active[at, lanes] = (before * half).astype(BF16)
            low[at, lanes] = grad.astype(BF16)
        return matmul(low[at, :], up_ref[...])

    rows.each_arrival_and_back(term)
    for first in range(0, units, tile):
        lanes = slice(first, first + tile)
        grads_ref[0, lanes, :] = outer_sum(low[:, lanes], c_ref[...])
        grads_ref[1, lanes, :] = outer_sum(active[:, lanes], rows.full[...].reshape(seq, model))
    if late is not None:
        late.start(grads_ref.at[late.other()])
    rows.finish(total_ref)
    if late is not None:
        late.wait()


def feed_back(team, ident, jobs, pair, gz, c, before, up, down):
    part, model = gz.shape
    seq = part * team.count
    units = up.shape[0]
    return team_call(
        feed_back_body, team, ident, jobs,
        [gz, c, before, up, down],
        [VMEM] * 5,
        (
            jax.ShapeDtypeStruct((part, model), F32),
            jax.ShapeDtypeStruct((2, units, model), F32),
            jax.ShapeDtypeStruct((1, units), F32),
        ),
        (VMEM,) * 3,
        [pltpu.VMEM((seq, units), BF16)] * 2,
        pair,
        jax.ShapeDtypeStruct((units, model), F32),
    )


def per_device(
    mesh_shape,
    token_ids,
    target_ids,
    lengths,
    embedding,
    outer_gain,
    outer_bias,
    norm_gain,
    norm_bias,
    qkv_weight,
    qv_bias,
    out_weight,
    up_weight,
    up_bias,
    down_weight,
    row_bias,
):
    sections, groups, shards = (mesh_shape[name] for name in ("section", "dp", "tensor"))
    s, j, z = (lax.axis_index(name) for name in ("section", "dp", "tensor"))
    by_section = Group(("section",), (sections,))
    by_dp = Group(("dp",), (groups,))
    by_tensor = Group(("tensor",), (shards,))
    exchange = Exchanges()
    layers = sections
    vocab, width = embedding.shape
    seq = token_ids.shape[1]
    rows = token_ids.shape[0] * groups
    local_cols = qkv_weight.shape[-1]
    planes = rows == sections * shards and local_cols % (groups * HEAD_DIM) == 0
    by_dp.square = planes and groups == 4
    by_tensor.line = planes
    team = by_dp if planes else by_tensor
    cut = groups if planes else 1
    fan = shards if planes else 1
    halves = 2 if planes else 1
    part = seq // team.count
    cols = local_cols // cut
    hidden = up_weight.shape[-1] // cut
    strip = hidden // halves
    cut_index = j if planes else 0
    my_row = z * sections + s if planes else j * sections + s
    length = lax.dynamic_slice(lengths, (my_row,), (1,))
    token_count = jnp.sum(lengths).astype(F32)
    vocab_start = z * vocab

    def chosen_cols(array, size):
        return lax.dynamic_slice_in_dim(array, cut_index * size, size, array.ndim - 1).T

    def chosen_rows(array, size):
        return lax.dynamic_slice_in_dim(array, cut_index * size, size, 0)

    def pad_rows(array, count):
        return jnp.pad(array, ((0, count - array.shape[0]), (0, width - array.shape[1])))

    sides = jnp.stack(
        [
            jnp.concatenate(
                [
                    chosen_cols(qkv_weight[0, 0], cols),
                    chosen_cols(qkv_weight[0, 2], cols),
                    chosen_cols(up_weight[0], hidden),
                ]
            ),
            jnp.concatenate(
                [
                    chosen_cols(qkv_weight[0, 1], cols),
                    chosen_rows(out_weight[0], cols),
                    chosen_rows(down_weight[0], hidden),
                ]
            ),
        ]
    )
    qv_piece = lax.dynamic_slice_in_dim(qv_bias[0], cut_index * cols, cols, 1)
    up_piece = lax.dynamic_slice_in_dim(up_bias[0], cut_index * hidden, hidden, 0)
    small = jnp.concatenate(
        [
            outer_gain,
            outer_bias,
            norm_gain[0],
            norm_bias[0],
            row_bias[0],
            pad_rows(qv_piece, 2),
            pad_rows(up_piece[None], 6),
        ]
    )

    def gather(group, x):
        return Job("gather", [group], x)

    def deal(group, x, axis=0):
        return Job("deal", [group], x, axis)

    def own_and_dealt(x, dealt, place, axis=0):
        own = lax.dynamic_index_in_dim(x, place, axis, keepdims=False).astype(F32)
        return own + jnp.sum(dealt.astype(F32), axis=0)

    if planes:
        other, both, small_all = exchange(
            deal(by_section, sides),
            gather(by_dp, jnp.stack([token_ids, target_ids])),
            gather(Group(("section", "tensor"), (sections, shards)), small),
        )
        small_all = small_all.reshape((sections, shards) + small.shape)
        own_side = lax.dynamic_index_in_dim(sides, s, 0, keepdims=False)
        side = [jnp.where(s == l, own_side, other[0]) for l in range(layers)]
        both = jnp.swapaxes(both, 0, 1).reshape(2, shards, sections, groups, part)
        both = lax.dynamic_index_in_dim(
            lax.dynamic_index_in_dim(both, s, 2, keepdims=False), j, 2, keepdims=False
        )
        ids, targets = both[0].reshape(-1), both[1].reshape(-1)
        group_lengths = lax.dynamic_index_in_dim(
            lengths.reshape(shards, sections), s, 1, keepdims=False
        )
        places = jnp.broadcast_to(j * part + jnp.arange(part), (shards, part))
        valid = (places < group_lengths[:, None]).reshape(-1)
    else:
        sides_all, small_all = exchange(gather(by_section, sides), gather(by_section, small))
        small_all = small_all[:, None]
        ids, targets = token_ids[s], target_ids[s]
        valid = jnp.arange(seq) < lengths[my_row]

    outer_gains = [small_all[l, 0, 0] for l in range(layers)]
    outer_offsets = [small_all[l, 0, 1] for l in range(layers)]
    params = []
    for l in range(layers):
        biases = [small_all[l, :, 8 + n, :cols].reshape(-1) for n in range(2)]
        units = small_all[l, :, 10, :hidden].reshape(fan, halves, strip)
        params.append(
            dict(
                gains=small_all[l, 0, 2:4],
                offsets=small_all[l, 0, 4:6],
                row_bias=small_all[l, 0, 6:8],
                bias=jnp.stack(biases),
                up_bias=jnp.swapaxes(units, 0, 1).reshape(1, -1),
            )
        )
        if not planes:
            block = sides_all[l]
            params[l].update(
                qk=block[:, :cols],
                vo=block[:, cols : 2 * cols],
                up=block[0, 2 * cols :],
                down=block[1, 2 * cols :],
            )
    head_number = (
        (jnp.arange(fan)[:, None] if planes else z) * (local_cols // HEAD_DIM)
        + cut_index * (cols // HEAD_DIM)
        + jnp.arange(cols // HEAD_DIM)
    ).reshape(-1)
    slopes = jnp.exp2(-8.0 * (head_number + 1).astype(F32) / HEADS)

    def attn_jobs(l):
        if not planes or l >= layers:
            return []
        return [
            Job("spread", [by_tensor, by_section], side[l][first : first + cols])
            for first in (0, cols)
        ]

    def feed_jobs(l, n):
        if not planes or l >= layers:
            return []
        first = 2 * cols + n * strip
        return [Job("spread", [by_tensor, by_section], side[l][first : first + strip])]

    def take_attn(l, got):
        if got:
            params[l]["qk"], params[l]["vo"] = (
                one.reshape(2, fan * cols, width) for one in got
            )

    def take_feed(l, got):
        if got:
            strips = [one.reshape(2, fan * strip, width) for one in got]
            params[l]["up"], params[l]["down"] = (
                jnp.concatenate([one[n] for one in strips]) for n in range(2)
            )

    def ident(kind, jobs):
        return exchange.ident((kind,) + tuple(job.key() for job in jobs))

    local_ids = ids - vocab_start
    inside = (local_ids >= 0) & (local_ids < vocab)
    looked = jnp.where(
        inside[:, None], jnp.take(embedding, jnp.clip(local_ids, 0, vocab - 1), axis=0), 0
    )
    group_part = looked.shape[0] // shards
    x, *got = exchange(
        Job("reduce", [by_tensor], looked.reshape(shards, group_part, width)), *attn_jobs(0)
    )
    take_attn(0, got)
    h = layer_norm(x, outer_gains[0], outer_offsets[0])

    kept = []
    strips = []
    for l, p in enumerate(params):
        jobs = (feed_jobs(l, 0) if l == 0 else []) + feed_jobs(l, 1)
        normed = layer_norm(h, p["gains"][0], p["offsets"][0]).astype(BF16)
        (total, normed, q, k, v, mixed, lse), got = attend(
            team, ident("attend", jobs), jobs, normed, length, slopes, p["qk"], p["vo"], p["bias"]
        )
        take_feed(l, strips + got)
        middle = h + total + p["row_bias"][0]
        jobs = attn_jobs(l + 1) + feed_jobs(l + 1, 0)
        second = layer_norm(middle, p["gains"][1], p["offsets"][1]).astype(BF16)
        (total, second, before), got = feed(
            team, ident("feed", jobs), jobs, second, p["up"], p["down"], p["up_bias"]
        )
        take_attn(l + 1, got[:2])
        strips = got[2:]
        kept.append((h, normed.reshape(seq, width), q, k, v, mixed, lse, middle, second, before))
        h = middle + total + p["row_bias"][1]

    (final,) = exchange(
        gather(by_tensor, layer_norm(h, outer_gains[-1], outer_offsets[-1]).astype(BF16))
    )
    final = final.reshape(-1, width)
    tokens = final.shape[0]
    columns_of = (targets - vocab_start)[:, None]
    logits, tops, totals, picks = head_logits(final, embedding, columns_of)
    top = jnp.max(tops, axis=1)
    total = jnp.sum(totals * jnp.exp(tops - top[:, None]), axis=1)
    pick = jnp.sum(picks, axis=1)
    (stats,) = exchange(
        gather(by_tensor, jnp.pad(jnp.stack([top, total, pick]), ((0, 5), (0, 0))))
    )
    top_all = jnp.max(stats[:, 0], axis=0)
    log_norm = top_all + jnp.log(jnp.sum(stats[:, 1] * jnp.exp(stats[:, 0] - top_all), axis=0))
    terms = jnp.where(valid, log_norm - jnp.sum(stats[:, 2], axis=0), 0.0)
    loss_part = jnp.sum(
        lax.dynamic_index_in_dim(terms.reshape(shards, -1), z, 0, keepdims=False)
    )
    row_weight = jnp.where(valid, 1.0 / token_count, 0.0)
    grad_logits, back = head_grads(
        logits, embedding, columns_of, log_norm[:, None], row_weight[:, None]
    )
    (grad_final,) = exchange(
        Job("reduce", [by_tensor], back.reshape(shards, group_part, width))
    )
    _, final_back = jax.vjp(layer_norm, h, outer_gains[-1], outer_offsets[-1])
    grad, final_gain, final_offset = final_back(grad_final)

    def section_sums(pair, got):
        out = []
        for one, dealt in zip(pair, got):
            low = own_and_dealt(one, dealt, s).astype(BF16)
            if one.ndim == 4:
                out.append(low.reshape(low.shape[0], fan, cols, width))
            else:
                out.append(low.reshape(halves, fan, strip, width))
        return out

    def tensor_jobs(lows):
        return [deal(by_tensor, low, 1) for low in lows]

    def tensor_sums(lows, got):
        return [
            own_and_dealt(low, dealt, z, 1).astype(BF16) for low, dealt in zip(lows, got)
        ]

    def spread_jobs(pieces):
        return [Job("spread", [by_dp, by_section], piece) for piece in pieces]

    small_rows = [None] * layers
    pairs = [None] * layers
    attn_low, attn_done, feed_done = ([None] * layers for _ in range(3))
    for l in reversed(range(layers)):
        p = params[l]
        section_in, normed, q, k, v, mixed, lse, middle, second, before = kept[l]
        pair = by_section if planes else None
        late = planes and l + 1 < layers
        jobs = tensor_jobs(attn_low[l + 1]) if late else []
        (total, g_feed, up_sum, *dealt), got = feed_back(
            team, ident("feed back", jobs), jobs, pair, grad.astype(BF16),
            second.reshape(seq, width), before, p["up"], p["down"],
        )
        if late:
            attn_done[l + 1] = tensor_sums(attn_low[l + 1], got)
        if planes:
            feed_low = section_sums([g_feed], [one[None] for one in dealt])
        _, norm_back = jax.vjp(layer_norm, middle, p["gains"][1], p["offsets"][1])
        grad_mid, gain_two, offset_two = norm_back(total)
        grad_mid = grad_mid + grad
        jobs = tensor_jobs(feed_low) if planes else []
        (total, g_attn, qv_sum, *dealt), got = attend_back(
            team, ident("attend back", jobs), jobs, pair, grad_mid.astype(BF16), length, slopes,
            normed, p["qk"], p["vo"], q, k, v, mixed, lse,
        )
        g_attn = g_attn.reshape((2, 2) + g_attn.shape[1:])
        if planes:
            feed_done[l] = tensor_sums(feed_low, got)
            attn_low[l] = section_sums([g_attn], [one[None] for one in dealt])
        _, norm_back = jax.vjp(layer_norm, section_in, p["gains"][0], p["offsets"][0])
        grad_in, gain_one, offset_one = norm_back(total)
        bias_two = jnp.sum(grad, axis=0)
        grad = grad_in + grad_mid
        pairs[l] = (g_attn, g_feed)

        def placed(values, size):
            out = jnp.zeros((fan if planes else shards, cut, size), F32)
            at = (0, j, 0) if planes else (z, 0, 0)
            return lax.dynamic_update_slice(out, values.reshape(fan, 1, size), at).reshape(
                -1, width
            )

        units = jnp.swapaxes(up_sum.reshape(halves, fan, strip), 0, 1)
        small_rows[l] = [
            gain_one[None],
            gain_two[None],
            offset_one[None],
            offset_two[None],
            jnp.sum(grad_mid, axis=0)[None],
            bias_two[None],
            placed(qv_sum[0], cols),
            placed(qv_sum[1], cols),
            placed(units, hidden),
        ]

    _, embed_back = jax.vjp(layer_norm, x, outer_gains[0], outer_offsets[0])
    grad_rows, embed_gain, embed_offset = embed_back(grad)
    packed = jnp.concatenate(
        [row for l in range(layers) for row in small_rows[l]]
        + [embed_gain[None], final_gain[None], embed_offset[None], final_offset[None]]
        + [jnp.broadcast_to(loss_part, (1, width))]
    )
    used = packed.shape[0]
    packed = jnp.pad(packed, ((0, -used % 8), (0, 0)))
    jobs = [Job("gather", [Group(("section", "tensor"), (sections, shards))], packed, late=True)]
    if planes:
        jobs += spread_jobs(attn_done[1] + feed_done[1])
        jobs += [Job("deal", [by_tensor], low, 1, late=True) for low in attn_low[0]]
    embed_sum, packed, *got = table_sum(
        by_section, by_dp, by_tensor, jobs, grad_logits, ids[None, :] - vocab_start, final,
        grad_rows.astype(BF16), exchange.ident("table"),
    )
    packed = jnp.sum(packed, axis=0)
    jobs = [gather(by_dp, packed)]
    if planes:
        spread_one = got[:2]
        jobs += spread_jobs(tensor_sums(attn_low[0], got[2:]) + feed_done[0])
    packed, *spread_zero = exchange(*jobs)
    packed = jnp.sum(packed, axis=0)
    if planes:
        attn_sum, feed_sum = (
            jnp.where(s == 0, zero, one) for zero, one in zip(spread_zero, spread_one)
        )
    else:
        chosen = [
            lax.dynamic_index_in_dim(
                lax.psum(jnp.stack([pair[n] for pair in pairs]), ("section", "dp")),
                s, 0, keepdims=False,
            )
            for n in range(2)
        ]
        attn_sum = chosen[0][:, None]
        feed_sum = chosen[1][:, None, None]
    embed_sum = embed_sum.reshape(vocab, width).astype(F32)
    per_layer = (used - 5) // layers
    mine = lax.dynamic_slice_in_dim(packed, s * per_layer, per_layer, 0)
    qv_rows = mine[6:8].reshape(2, -1)
    ff_row = mine[8:].reshape(-1)
    grad_qv = lax.dynamic_slice_in_dim(qv_rows, z * local_cols, local_cols, 1)
    grad_up_bias = lax.dynamic_slice_in_dim(ff_row, z * hidden * cut, hidden * cut, 0)
    base = per_layer * layers
    grad_outer_gain = lax.dynamic_slice_in_dim(packed, base + s, 1, 0)
    grad_outer_bias = lax.dynamic_slice_in_dim(packed, base + 2 + s, 1, 0)
    loss = packed[base + 4, 0] / token_count

    def columns(array):
        return array.astype(F32).reshape(-1, width).T

    grad_qkv = jnp.stack(
        [columns(attn_sum[0, :, 0]), columns(attn_sum[1, :, 0]), columns(attn_sum[0, :, 1])]
    )
    grad_out_mat = attn_sum[1, :, 1].astype(F32).reshape(-1, width)
    grad_up = columns(feed_sum[0])
    grad_down = feed_sum[1].astype(F32).reshape(-1, width)
    return (
        loss,
        embed_sum,
        grad_outer_gain,
        grad_outer_bias,
        mine[0:2][None],
        mine[2:4][None],
        grad_qkv[None],
        grad_qv[None],
        grad_out_mat[None],
        grad_up[None],
        grad_up_bias[None],
        grad_down[None],
        mine[4:6][None],
    )


def solution(mesh):
    return jax.shard_map(
        functools.partial(per_device, dict(mesh.shape)),
        mesh=mesh,
        in_specs=(
            P("dp", None),
            P("dp", None),
            P(),
            P("tensor", None),
            P("section", None),
            P("section", None),
            P("section", None, None),
            P("section", None, None),
            P("section", None, None, "tensor"),
            P("section", None, "tensor"),
            P("section", "tensor", None),
            P("section", None, "tensor"),
            P("section", "tensor"),
            P("section", "tensor", None),
            P("section", None, None),
        ),
        out_specs=(
            P(),
            P("tensor", None),
            P("section", None),
            P("section", None),
            P("section", None, None),
            P("section", None, None),
            P("section", None, None, "tensor"),
            P("section", None, "tensor"),
            P("section", "tensor", None),
            P("section", None, "tensor"),
            P("section", "tensor"),
            P("section", "tensor", None),
            P("section", None, None),
        ),
        check_vma=False,
    )
```

```python
import functools
import math

import jax
import jax.numpy as jnp
from jax import lax
from jax.experimental import pallas as pl
from jax.experimental.pallas import tpu as pltpu
from jax.sharding import PartitionSpec as P

HEADS = 16
HEAD_DIM = 64
EPS = 1e-05
NEG = -1e30
MESH = pl.DeviceIdType.MESH
F32 = jnp.float32
BF16 = jnp.bfloat16


def matmul(former, latter):
    return jnp.dot(former, latter, preferred_element_type=F32)


def matmul_t(former, latter):
    return lax.dot_general(
        former, latter, (((1,), (1,)), ((), ())), preferred_element_type=F32
    )


def outer_sum(former, latter):
    return lax.dot_general(
        former, latter, (((0,), (0,)), ((), ())), preferred_element_type=F32
    )


def layer_norm(inputs, weight, offset):
    centre = inputs - jnp.mean(inputs, axis=-1, keepdims=True)
    spread = jnp.mean(centre * centre, axis=-1, keepdims=True)
    return centre * lax.rsqrt(spread + EPS) * weight + offset


def gelu_tanh(inputs):
    return jax.nn.gelu(inputs, approximate=True)


class Group:
    def __init__(self, axes, sizes, square=False, line=False):
        self.square = square
        self.line = line
        self.axes = axes
        self.sizes = sizes
        self.count = math.prod(sizes)

    def me(self):
        place = 0
        for axis, size in zip(self.axes, self.sizes):
            place = place * size + lax.axis_index(axis)
        return place

    def device(self, place):
        spot = {}
        for axis, size in reversed(list(zip(self.axes, self.sizes))):
            spot[axis] = lax.rem(place, size)
            place = lax.div(place, size)
        return spot

    def peers(self):
        me = self.me()
        return [lax.rem(me + step, self.count) for step in range(1, self.count)]


def greet(groups):
    barrier = pltpu.get_barrier_semaphore()
    total = 0
    for group in groups:
        for peer in group.peers():
            pl.semaphore_signal(
                barrier, inc=1, device_id=group.device(peer), device_id_type=MESH
            )
            total += 1
    pl.semaphore_wait(barrier, total)


def send(group, peer, step, src, dst, send_sem, recv_sem):
    copy = pltpu.make_async_remote_copy(
        src_ref=src,
        dst_ref=dst,
        send_sem=send_sem.at[step],
        recv_sem=recv_sem.at[step],
        device_id=group.device(peer),
        device_id_type=MESH,
    )
    copy.start()
    return copy


def tie(*arrays):
    return lax.optimization_barrier(arrays)


class LineRows:
    def __init__(self, group, x, full, send_sem, recv_sem):
        self.group, self.count, self.me = group, group.count, group.me()
        self.x, self.full, self.sems = x, full, (send_sem, recv_sem)

    def copy(self, up, step):
        place = self.me - step if up else self.me + step
        place = jnp.clip(place, 0, self.count - 1)
        number = step if up else self.count - 1 + step
        src = self.x if step == 0 else self.full.at[place]
        return pltpu.make_async_remote_copy(
            src_ref=src,
            dst_ref=self.full.at[place],
            send_sem=self.sems[0].at[number],
            recv_sem=self.sems[1].at[number],
            device_id=self.group.device(
                jnp.clip(self.me + 1 if up else self.me - 1, 0, self.count - 1)
            ),
            device_id_type=MESH,
        )

    def leaves(self, up, step):
        if up:
            return (self.me - step >= 0) & (self.me < self.count - 1)
        return (self.me + step < self.count) & (self.me > 0)

    def arrives(self, up, step):
        return self.me - 1 - step >= 0 if up else self.me + 1 + step < self.count

    def start(self):
        for up in (True, False):

            @pl.when(self.leaves(up, 0))
            def _(up=up):
                self.copy(up, 0).start()

    def step(self, step):
        for up in (True, False):

            @pl.when(self.arrives(up, step - 1))
            def _(up=up):
                self.copy(up, step - 1).wait_recv()

            if step < self.count - 1:

                @pl.when(self.leaves(up, step))
                def _(up=up):
                    self.copy(up, step).start()

    def wait_sends(self):
        for step in range(self.count - 1):
            for up in (True, False):

                @pl.when(self.leaves(up, step))
                def _(up=up, step=step):
                    self.copy(up, step).wait_send()

    def finish(self):
        for step in range(1, self.count):
            self.step(step)
        self.wait_sends()


class LineSum:
    def __init__(self, group, x, stage, land, send_sem, recv_sem):
        self.group, self.count, self.me = group, group.count, group.me()
        self.x, self.stage, self.land, self.sems = x, stage, land, (send_sem, recv_sem)

    def copy(self, up, step):
        side = 0 if up else 1
        return pltpu.make_async_remote_copy(
            src_ref=self.stage.at[side, step],
            dst_ref=self.land.at[side, step],
            send_sem=self.sems[0].at[side, step],
            recv_sem=self.sems[1].at[side, step],
            device_id=self.group.device(
                jnp.clip(self.me + 1 if up else self.me - 1, 0, self.count - 1)
            ),
            device_id_type=MESH,
        )

    def leaves(self, up, step):
        return self.me < self.count - 1 - step if up else self.me > step

    def behind(self, up):
        return self.me > 0 if up else self.me < self.count - 1

    def first(self, step):
        for up in (True, False):
            place = self.count - 1 - step if up else step
            side = 0 if up else 1

            @pl.when(self.leaves(up, step) & jnp.logical_not(self.behind(up)))
            def _(up=up, place=place, side=side):
                self.stage[side, step] = self.x[place]
                self.copy(up, step).start()

    def rest(self, step, near=None):
        for up in (True, False):
            place = self.count - 1 - step if up else step
            side = 0 if up else 1
            here = self.leaves(up, step) & self.behind(up)
            if near is not None:
                by_end = self.me == (1 if up else self.count - 2)
                here = here & (by_end if near else jnp.logical_not(by_end))

            @pl.when(here)
            def _(up=up, place=place, side=side):
                self.copy(up, step).wait_recv()
                total = self.x[place].astype(F32) + self.land[side, step].astype(F32)
                self.stage[side, step] = total.astype(self.stage.dtype)
                self.copy(up, step).start()

    def finish(self, out):
        out[...] = self.x[self.me].astype(F32)
        for up in (True, False):
            side = 0 if up else 1
            for step in range(self.count - 1):

                @pl.when(self.behind(up) & (self.me == (self.count - 1 - step if up else step)))
                def _(up=up, step=step, side=side):
                    self.copy(up, step).wait_recv()
                    out[...] += self.land[side, step].astype(F32)

        for up in (True, False):
            for step in range(self.count - 1):

                @pl.when(self.leaves(up, step))
                def _(up=up, step=step):
                    self.copy(up, step).wait_send()


class Job:
    def __init__(self, kind, groups, x, axis=0, late=False):
        self.late = late
        self.kind, self.groups, self.x, self.axis = kind, groups, x, axis
        count = groups[0].count
        rest = x.shape[:axis] + x.shape[axis + 1 :]
        dma = pltpu.SemaphoreType.DMA
        self.in_spec = pl.BlockSpec(memory_space=pl.ANY)
        self.out_spec = pl.BlockSpec(memory_space=pl.ANY)
        self.scratch = [dma((count - 1,)), dma((count - 1,)), dma]
        if kind in ("gather", "spread"):
            self.in_spec = pl.BlockSpec(memory_space=pltpu.VMEM)
        if kind == "gather" and groups[0].line:
            self.scratch = [dma((2 * count - 2,)), dma((2 * count - 2,)), dma]
        if kind == "gather":
            self.out = jax.ShapeDtypeStruct((count,) + x.shape, x.dtype)
        elif kind == "spread":
            self.out = jax.ShapeDtypeStruct((groups[1].count, count) + x.shape, x.dtype)
            copies = 7 if groups[0].square else count
            if groups[0].square:
                self.scratch = [dma((6,)), dma((6,)), dma]
            self.scratch += [dma((copies,)), dma((copies,))]
        elif kind == "deal":
            self.out = jax.ShapeDtypeStruct((count - 1,) + rest, x.dtype)
        else:
            self.out = jax.ShapeDtypeStruct(rest, F32)
            self.out_spec = pl.BlockSpec(memory_space=pltpu.VMEM)
            if groups[0].line:
                self.in_spec = pl.BlockSpec(memory_space=pltpu.VMEM)
                self.scratch = [dma((2, count - 1)), dma((2, count - 1)), dma]
                self.scratch += [pltpu.VMEM((2, count - 1) + rest, x.dtype)] * 2
            else:
                self.scratch += [
                    pltpu.VMEM(rest, x.dtype), pltpu.VMEM((count - 1,) + rest, x.dtype)
                ]

    def key(self):
        return (self.kind, tuple(g.axes for g in self.groups), self.x.shape, str(self.x.dtype), self.axis)

    def start(self, x, out, send_sem, recv_sem, own_sem, *more):
        group = self.groups[0]
        me = group.me()
        peers = list(enumerate(group.peers()))

        def block(place):
            return x.at[(slice(None),) * self.axis + (place,)]

        if self.kind == "gather" and group.line:
            line = LineRows(group, x, out, send_sem, recv_sem)
            line.start()
            own = pltpu.make_async_copy(x, out.at[me], own_sem)
            own.start()

            def finish():
                line.finish()
                own.wait()

        elif self.kind == "reduce" and group.line:
            line = LineSum(group, x, *more, send_sem, recv_sem)
            for step in range(group.count - 1):
                line.first(step)

            def finish():
                for step in range(group.count - 1):
                    line.rest(step)
                line.finish(out)

        elif self.kind == "gather":
            copies = [send(group, p, k, x, out.at[me], send_sem, recv_sem) for k, p in peers]
            own = pltpu.make_async_copy(x, out.at[me], own_sem)
            own.start()

            def finish():
                for copy in copies + [own]:
                    copy.wait()

        elif self.kind == "spread" and group.square:
            pair = self.groups[1]
            side = pair.me()
            fw_send, fw_recv = more
            size = self.x.shape[0] // 2
            near = [across(me, 0), across(me, 1)]

            def copy_of(number):
                at = pl.ds(SQUARE_HALF[number] * size, size)
                place = me if number < 4 else near[number - 4]
                dst = out.at[side, place, at]
                src = x.at[at] if number < 4 else dst
                copy = pltpu.make_async_remote_copy(
                    src_ref=src, dst_ref=dst, send_sem=send_sem.at[number],
                    recv_sem=recv_sem.at[number], device_id=group.device(near[SQUARE_STEP[number]]),
                    device_id_type=MESH,
                )
                origin = near[SQUARE_STEP[number]] if number < 4 else across(me, 2)
                return copy, out.at[side, origin, at]

            copies = [copy_of(number) for number in range(6)]
            for number in (0, 2, 1, 3):
                copies[number][0].start()
            passed = [send(pair, 1 - side, 6, x, out.at[side, me], fw_send, fw_recv)]
            own = pltpu.make_async_copy(x, out.at[side, me], own_sem)
            own.start()

            def arrived(number):
                copy, landed = copies[number]
                copy.wait_recv()
                passed.append(send(pair, 1 - side, number, landed, landed, fw_send, fw_recv))

            def finish():
                for number in (0, 2):
                    copies[number][0].wait_recv()
                    copies[4 + number // 2][0].start()
                    landed = copies[number][1]
                    passed.append(send(pair, 1 - side, number, landed, landed, fw_send, fw_recv))
                for number in (1, 3, 4, 5):
                    arrived(number)
                for copy in passed:
                    copy.wait()
                for copy, _ in copies:
                    copy.wait_send()
                own.wait()

        elif self.kind == "spread":
            pair = self.groups[1]
            side = pair.me()
            fw_send, fw_recv = more
            home = out.at[side, me]
            copies = [send(group, p, k, x, home, send_sem, recv_sem) for k, p in peers]
            last = group.count - 1
            passed = [send(pair, 1 - side, last, x, home, fw_send, fw_recv)]
            own = pltpu.make_async_copy(x, home, own_sem)
            own.start()

            def finish():
                for k, copy in enumerate(copies):
                    copy.wait_recv()
                    place = out.at[side, lax.rem(me + group.count - 1 - k, group.count)]
                    passed.append(send(pair, 1 - side, k, place, place, fw_send, fw_recv))
                for copy in passed:
                    copy.wait()
                for copy in copies:
                    copy.wait_send()
                own.wait()

        elif self.kind == "deal":
            copies = [send(group, p, k, block(p), out.at[k], send_sem, recv_sem) for k, p in peers]

            def finish():
                for copy in copies:
                    copy.wait()

        else:
            kept, slots = more
            copies = [send(group, p, k, block(p), slots.at[k], send_sem, recv_sem) for k, p in peers]
            own = pltpu.make_async_copy(block(me), kept, own_sem)
            own.start()

            def finish():
                own.wait()
                for copy in copies:
                    copy.wait()
                total = kept[...].astype(F32)
                for k in range(group.count - 1):
                    total = total + slots[k].astype(F32)
                out[...] = total

        return finish


def job_groups(jobs):
    return [group for job in jobs for group in job.groups]


def split_scratch(jobs, scratch):
    parts, at = [], 0
    for job in jobs:
        parts.append(scratch[at : at + len(job.scratch)])
        at += len(job.scratch)
    return parts


def exchange_body(jobs, *refs):
    count = len(jobs)
    greet(job_groups(jobs))
    parts = split_scratch(jobs, refs[2 * count :])
    ends = [
        job.start(refs[n], refs[count + n], *parts[n]) for n, job in enumerate(jobs)
    ]
    for end in ends:
        end()


class Exchanges:
    def __init__(self):
        self.idents = {}

    def ident(self, key):
        return self.idents.setdefault(key, len(self.idents))

    def __call__(self, *jobs):
        jobs = list(jobs)
        return pl.pallas_call(
            functools.partial(exchange_body, jobs),
            out_shape=tuple(job.out for job in jobs),
            in_specs=[job.in_spec for job in jobs],
            out_specs=tuple(job.out_spec for job in jobs),
            scratch_shapes=[one for job in jobs for one in job.scratch],
            compiler_params=pltpu.CompilerParams(
                collective_id=self.ident(tuple(job.key() for job in jobs)),
                has_side_effects=True,
                vmem_limit_bytes=32 * 2**20,
            ),
        )(*[job.x for job in jobs])


CHUNK = 512


def start_rows(group, x_ref, full, send_sem, recv_sem):
    me = group.me()
    full[me] = x_ref[...]
    return [
        send(group, peer, step, x_ref, full.at[me], send_sem, recv_sem)
        for step, peer in enumerate(group.peers())
    ]


def table_body(
    by_section, by_dp, by_tensor, jobs, g_ref, ids_ref, u_ref, gx_ref, *refs
):
    riders = len(jobs)
    xs, (out_ref, *outs), refs = refs[:riders], refs[riders : 2 * riders + 1], refs[2 * riders + 1 :]
    (g_buf, to_partner, from_partner, to_dp, from_dp, own, result,
    g_sem, ps_send, ps_recv, dp_send, dp_recv, ag_send, ag_recv, fw_send, fw_recv, own_sem,
    ) = refs[:17]
    gx_full, gx_send, gx_recv = refs[17:20]
    s, j = by_section.me(), by_dp.me()
    partner = 1 - s
    peers = by_dp.peers() + [j]
    count = by_dp.count
    block = own.shape[0]
    subs = block // CHUNK
    tokens = u_ref.shape[0]
    greet([by_section, by_dp, by_tensor] + job_groups(jobs))
    gx_copies = start_rows(by_tensor, gx_ref, gx_full, gx_send, gx_recv)
    parts = split_scratch(jobs, refs[20:])
    ends = [job.start(xs[n], outs[n], *parts[n]) for n, job in enumerate(jobs)]

    def chunk(half, place, sub):
        return (half * count + place) * subs + sub

    order = [(number, half) for number in range(count) for half in (0, 1)]

    def fetch(index, sub, slot):
        number, away = order[index]
        half = partner if away == 0 else s
        return pltpu.make_async_copy(
            g_ref.at[chunk(half, peers[number], sub)], g_buf.at[slot], g_sem.at[slot]
        )

    def remote(group, peer, number, sub, src, dst, send_sem, recv_sem):
        return pltpu.make_async_remote_copy(
            src_ref=src,
            dst_ref=dst,
            send_sem=send_sem.at[number, sub],
            recv_sem=recv_sem.at[number, sub],
            device_id=group.device(peer),
            device_id_type=MESH,
        )

    def rows(sub):
        return pl.ds(pl.multiple_of(sub * CHUNK, CHUNK), CHUNK)

    def partner_copy(number, sub):
        return remote(
            by_section, partner, number, sub,
            to_partner.at[number, rows(sub)], from_partner.at[number, rows(sub)],
            ps_send, ps_recv,
        )

    def chip_copy(number, sub):
        return remote(
            by_dp, peers[number], number, sub,
            to_dp.at[number, rows(sub)], from_dp.at[number, rows(sub)], dp_send, dp_recv,
        )

    def spread_copy(number, sub):
        return remote(
            by_dp, peers[number], number, sub,
            result.at[rows(sub)], out_ref.at[chunk(s, j, sub)], ag_send, ag_recv,
        )

    sources = [lax.rem(j + count - 1 - number, count) for number in range(count - 1)] + [j]

    def forward_copy(number, sub):
        target = out_ref.at[chunk(s, sources[number], sub)]
        origin = result.at[rows(sub)] if number == count - 1 else target
        return remote(by_section, partner, number, sub, origin, target, fw_send, fw_recv)

    def own_copy(sub):
        return pltpu.make_async_copy(
            result.at[rows(sub)], out_ref.at[chunk(s, j, sub)], own_sem.at[sub]
        )

    for copy in gx_copies:
        copy.wait()
    fetch(0, 0, 0).start()
    for index, (number, away) in enumerate(order):
        half = partner if away == 0 else s

        def one(sub, carry, index=index, number=number, away=away, half=half):
            slot = lax.rem(sub, 2)
            fetch(index, sub, slot).wait()

            @pl.when(sub + 1 < subs)
            def _():
                fetch(index, sub + 1, 1 - slot).start()

            if index + 1 < len(order):

                @pl.when(sub + 1 == subs)
                def _():
                    fetch(index + 1, 0, 1 - slot).start()

            base = chunk(half, peers[number], sub) * CHUNK
            place = base + lax.broadcasted_iota(jnp.int32, (CHUNK, tokens), 0)
            chosen = jnp.where(place == ids_ref[...], 1.0, 0.0).astype(BF16)
            term = outer_sum(g_buf[slot], u_ref[...]) + matmul(
                chosen, gx_full[...].reshape(tokens, gx_full.shape[2])
            )
            if away == 0:
                to_partner[number, rows(sub), :] = term.astype(BF16)
                partner_copy(number, sub).start()
            else:
                partner_copy(number, sub).wait_recv()
                term = term + from_partner[number, rows(sub), :].astype(F32)
                if number < count - 1:
                    to_dp[number, rows(sub), :] = term.astype(BF16)
                    chip_copy(number, sub).start()
                else:
                    own[rows(sub), :] = term
            return carry

        lax.fori_loop(0, subs, one, 0)

    def finish(sub, carry):
        term = own[rows(sub), :]
        for number in range(count - 1):
            chip_copy(number, sub).wait_recv()
            term = term + from_dp[number, rows(sub), :].astype(F32)
        result[rows(sub), :] = term.astype(BF16)
        for number in range(count - 1):
            spread_copy(number, sub).start()
        forward_copy(count - 1, sub).start()
        own_copy(sub).start()
        return carry

    lax.fori_loop(0, subs, finish, 0)

    def take(sub, carry):
        for number in range(count - 1):
            spread_copy(number, sub).wait_recv()
            forward_copy(number, sub).start()
        return carry

    lax.fori_loop(0, subs, take, 0)

    def drain(sub, carry):
        own_copy(sub).wait()
        for number in range(count):
            partner_copy(number, sub).wait_send()
            forward_copy(number, sub).wait()
        for number in range(count - 1):
            chip_copy(number, sub).wait_send()
            spread_copy(number, sub).wait_send()
        return carry

    lax.fori_loop(0, subs, drain, 0)
    for end in ends:
        end()


def across(me, step):
    bits = jnp.int32(step + 1)
    x, y = lax.rem(me, 2), lax.div(me, 2)
    return 2 * lax.rem(y + lax.div(bits, 2), 2) + lax.rem(x + lax.rem(bits, 2), 2)


SQUARE_HALF = (0, 1, 1, 0, 0, 1)
SQUARE_STEP = (0, 0, 1, 1, 1, 0)


def table_square_body(by_section, by_dp, by_tensor, jobs, g_ref, ids_ref, u_ref, gx_ref, *refs):
    riders = len(jobs)
    xs, (out_ref, *outs), refs = refs[:riders], refs[riders : 2 * riders + 1], refs[2 * riders + 1 :]
    (
        g_buf, to_partner, from_partner, to_dp, hop_land, from_dp, own, result,
        g_sem, ps_send, ps_recv, hop_send, hop_recv, dp_send, dp_recv, ag_send, ag_recv,
        fw_send, fw_recv, own_sem,
    ) = refs[:20]
    gx_full, gx_send, gx_recv = refs[20:23]
    s, j = by_section.me(), by_dp.me()
    partner = 1 - s
    near_x, near_y, far = (across(j, step) for step in range(3))
    peers = [far, near_y, near_x, j]
    count = 4
    block = own.shape[0]
    subs = block // CHUNK
    half_rows = CHUNK // 2
    tokens = u_ref.shape[0]
    greet([by_section, by_dp, by_tensor] + job_groups(jobs))
    line = LineRows(by_tensor, gx_ref, gx_full, gx_send, gx_recv)
    line.start()
    gx_full[line.me] = gx_ref[...]
    parts = split_scratch(jobs, refs[23:])
    ends = [
        job.start(xs[n], outs[n], *parts[n]) for n, job in enumerate(jobs) if not job.late
    ]

    def chunk(half, place, sub):
        return (half * count + place) * subs + sub

    order = [(number, away) for number in range(count) for away in (0, 1)]

    def fetch(index, sub, slot):
        number, away = order[index]
        half = partner if away == 0 else s
        return pltpu.make_async_copy(
            g_ref.at[chunk(half, peers[number], sub)], g_buf.at[slot], g_sem.at[slot]
        )

    def remote(group, peer, number, sub, src, dst, send_sem, recv_sem):
        return pltpu.make_async_remote_copy(
            src_ref=src,
            dst_ref=dst,
            send_sem=send_sem.at[number, sub],
            recv_sem=recv_sem.at[number, sub],
            device_id=group.device(peer),
            device_id_type=MESH,
        )

    def rows(sub):
        return pl.ds(pl.multiple_of(sub * CHUNK, CHUNK), CHUNK)

    def half_of(sub, which):
        return pl.ds(pl.multiple_of(sub * CHUNK + which * half_rows, half_rows), half_rows)

    def partner_copy(number, sub):
        return remote(
            by_section, partner, number, sub,
            to_partner.at[number, rows(sub)], from_partner.at[number, rows(sub)],
            ps_send, ps_recv,
        )

    def hop_copy(which, sub):
        return remote(
            by_dp, (near_x, near_y)[which], which, sub,
            to_dp.at[0, half_of(sub, which)], hop_land.at[half_of(sub, which)], hop_send, hop_recv,
        )

    def chip_copy(number, sub):
        return remote(
            by_dp, (near_y, near_x)[number], number, sub,
            to_dp.at[number + 1, rows(sub)], from_dp.at[number, rows(sub)], dp_send, dp_recv,
        )

    def spread_copy(number, sub):
        which = SQUARE_HALF[number]
        place = j if number < 4 else (near_x, near_y)[number - 4]
        dst = out_ref.at[chunk(s, place, sub), pl.ds(which * half_rows, half_rows)]
        src = result.at[half_of(sub, which)] if number < 4 else dst
        peer = (near_x, near_y)[SQUARE_STEP[number]]
        return remote(by_dp, peer, number, sub, src, dst, ag_send, ag_recv)

    sources = [near_x, near_y, far, j]

    def forward_copy(number, sub):
        target = out_ref.at[chunk(s, sources[number], sub)]
        origin = result.at[rows(sub)] if number == count - 1 else target
        return remote(by_section, partner, number, sub, origin, target, fw_send, fw_recv)

    def own_copy(sub):
        return pltpu.make_async_copy(
            result.at[rows(sub)], out_ref.at[chunk(s, j, sub)], own_sem.at[sub]
        )

    def slot_of(number, away):
        if away == 0:
            return to_partner.at[number]
        return to_dp.at[number] if number < 3 else own

    fetch(0, 0, 0).start()
    stops = {(step * len(order)) // line.count: step for step in range(1, line.count - 1)}
    for index, (number, away) in enumerate(order):
        if index in stops:
            line.step(stops[index])

        def share(sub, carry, index=index, number=number, away=away):
            slot = lax.rem(sub, 2)
            fetch(index, sub, slot).wait()

            @pl.when(sub + 1 < subs)
            def _():
                fetch(index, sub + 1, 1 - slot).start()

            if index + 1 < len(order):

                @pl.when(sub + 1 == subs)
                def _():
                    fetch(index + 1, 0, 1 - slot).start()

            held = slot_of(number, away)
            held[rows(sub), :] = outer_sum(g_buf[slot], u_ref[...]).astype(held.dtype)
            return carry

        lax.fori_loop(0, subs, share, 0)
    line.step(line.count - 1)
    line.wait_sends()
    ends += [job.start(xs[n], outs[n], *parts[n]) for n, job in enumerate(jobs) if job.late]

    for index, (number, away) in enumerate(order):
        half = partner if away == 0 else s

        def one(sub, carry, number=number, away=away, half=half):
            base = chunk(half, peers[number], sub) * CHUNK
            place = base + lax.broadcasted_iota(jnp.int32, (CHUNK, tokens), 0)
            chosen = jnp.where(place == ids_ref[...], 1.0, 0.0).astype(BF16)
            term = matmul(chosen, gx_full[...].reshape(tokens, gx_full.shape[2]))
            term = term + slot_of(number, away)[rows(sub), :].astype(F32)
            if away == 0:
                to_partner[number, rows(sub), :] = term.astype(BF16)
                partner_copy(number, sub).start()
                return carry
            partner_copy(number, sub).wait_recv()
            term = term + from_partner[number, rows(sub), :].astype(F32)
            if number == 0:
                to_dp[0, rows(sub), :] = term.astype(BF16)
                for which in range(2):
                    hop_copy(which, sub).start()
            elif number < 3:
                which = number - 1
                hop_copy(which, sub).wait_recv()
                mine = slice(which * half_rows, (which + 1) * half_rows)
                rest = slice((1 - which) * half_rows, (2 - which) * half_rows)
                to_dp[number, half_of(sub, which), :] = (
                    term[mine] + hop_land[half_of(sub, which), :].astype(F32)
                ).astype(BF16)
                to_dp[number, half_of(sub, 1 - which), :] = term[rest].astype(BF16)
                chip_copy(which, sub).start()
            else:
                own[rows(sub), :] = term
            return carry

        lax.fori_loop(0, subs, one, 0)

    def finish(sub, carry):
        term = own[rows(sub), :]
        for number in range(2):
            chip_copy(number, sub).wait_recv()
            term = term + from_dp[number, rows(sub), :].astype(F32)
        result[rows(sub), :] = term.astype(BF16)
        for number in (0, 2, 1, 3):
            spread_copy(number, sub).start()
        forward_copy(count - 1, sub).start()
        own_copy(sub).start()
        return carry

    lax.fori_loop(0, subs, finish, 0)

    def pass_on(sub, carry):
        for number in (0, 2):
            spread_copy(number, sub).wait_recv()
            spread_copy(4 + number // 2, sub).start()
        for number in (0, 1):
            spread_copy(2 * number + 1, sub).wait_recv()
            forward_copy(number, sub).start()
        return carry

    lax.fori_loop(0, subs, pass_on, 0)

    def last(sub, carry):
        for number in (4, 5):
            spread_copy(number, sub).wait_recv()
        forward_copy(2, sub).start()
        return carry

    lax.fori_loop(0, subs, last, 0)

    def drain(sub, carry):
        own_copy(sub).wait()
        for number in range(count):
            partner_copy(number, sub).wait_send()
            forward_copy(number, sub).wait()
        for number in range(2):
            hop_copy(number, sub).wait_send()
            chip_copy(number, sub).wait_send()
        for number in range(6):
            spread_copy(number, sub).wait_send()
        return carry

    lax.fori_loop(0, subs, drain, 0)
    for end in ends:
        end()


def table_sum(by_section, by_dp, by_tensor, jobs, grads, ids, final, grad_rows, ident):
    chunks, tokens, _ = grads.shape
    width = final.shape[1]
    count = by_dp.count
    subs = chunks // (2 * count)
    block = subs * CHUNK
    assert subs % 2 == 0
    dma = pltpu.SemaphoreType.DMA
    low = functools.partial(pltpu.VMEM, dtype=BF16)
    square = by_dp.square
    scratch = [
        low((2, tokens, CHUNK)),
        low((count, block, width)),
        low((count, block, width)),
        low((count - 1, block, width)),
    ]
    scratch += [low((block, width)), low((2, block, width))] if square else [
        low((count - 1, block, width))
    ]
    scratch += [pltpu.VMEM((block, width), F32), low((block, width)), dma((2,))]
    copies = (count, 2, 2, 6, count) if square else (count, count - 1, count - 1, count)
    scratch += [dma((copy, subs)) for copy in copies for _ in range(2)] + [dma((subs,))]
    scratch += [low((by_tensor.count,) + grad_rows.shape)]
    scratch += [dma(((by_tensor.count - 1) * (2 if square else 1),))] * 2
    vmem = pl.BlockSpec(memory_space=pltpu.VMEM)
    hbm = pl.BlockSpec(memory_space=pl.ANY)
    return pl.pallas_call(
        functools.partial(
            table_square_body if by_dp.square else table_body, by_section, by_dp, by_tensor, jobs
        ),
        out_shape=(jax.ShapeDtypeStruct((chunks, CHUNK, width), BF16),)
        + tuple(job.out for job in jobs),
        in_specs=[hbm, vmem, vmem, vmem] + [job.in_spec for job in jobs],
        out_specs=(hbm,) + tuple(job.out_spec for job in jobs),
        scratch_shapes=scratch + [one for job in jobs for one in job.scratch],
        compiler_params=pltpu.CompilerParams(
            collective_id=ident, has_side_effects=True, vmem_limit_bytes=56 * 2**20
        ),
    )(grads, ids, final, grad_rows, *[job.x for job in jobs])


LANES = 128


def head_logits_body(u_ref, e_ref, ids_ref, logits_ref, top_ref, total_ref, pick_ref):
    step = pl.program_id(0)
    tokens, tile = logits_ref.shape[1:]

    @pl.when(step == 0)
    def _():
        top_ref[...] = jnp.full_like(top_ref, NEG)
        total_ref[...] = jnp.zeros_like(total_ref)
        pick_ref[...] = jnp.zeros_like(pick_ref)

    logits = matmul_t(u_ref[...], e_ref[...])
    logits_ref[0] = logits
    place = step * tile + lax.broadcasted_iota(jnp.int32, (tokens, tile), 1)
    picked = jnp.where(place == ids_ref[...], logits, 0.0)
    pieces = [logits[:, at : at + LANES] for at in range(0, tile, LANES)]
    before = top_ref[...]
    top = functools.reduce(jnp.maximum, pieces, before)
    total = total_ref[...] * jnp.exp(before - top)
    pick = pick_ref[...]
    for number, piece in enumerate(pieces):
        total = total + jnp.exp(piece - top)
        pick = pick + picked[:, number * LANES : (number + 1) * LANES]
    top_ref[...] = top
    total_ref[...] = total
    pick_ref[...] = pick


def head_logits(final, embedding, ids):
    tokens, width = final.shape
    vocab = embedding.shape[0]
    fixed = pl.BlockSpec((tokens, LANES), lambda step: (0, 0))
    stat = jax.ShapeDtypeStruct((tokens, LANES), F32)
    return pl.pallas_call(
        head_logits_body,
        grid=(vocab // CHUNK,),
        out_shape=(
            jax.ShapeDtypeStruct((vocab // CHUNK, tokens, CHUNK), F32), stat, stat, stat
        ),
        in_specs=[
            pl.BlockSpec((tokens, width), lambda step: (0, 0)),
            pl.BlockSpec((CHUNK, width), lambda step: (step, 0)),
            pl.BlockSpec((tokens, 1), lambda step: (0, 0)),
        ],
        out_specs=(
            pl.BlockSpec((1, tokens, CHUNK), lambda step: (step, 0, 0)), fixed, fixed, fixed
        ),
        compiler_params=pltpu.CompilerParams(vmem_limit_bytes=40 * 2**20),
        cost_estimate=pl.CostEstimate(
            flops=2 * tokens * vocab * width,
            bytes_accessed=4 * tokens * vocab + 2 * vocab * width,
            transcendentals=tokens * vocab,
        ),
    )(final, embedding, ids)


def head_grads_body(logits_ref, e_ref, ids_ref, norm_ref, weight_ref, grads_ref, back_ref, acc):
    step = pl.program_id(0)
    tokens, tile = grads_ref.shape[1:]

    @pl.when(step == 0)
    def _():
        acc[...] = jnp.zeros_like(acc)

    place = step * tile + lax.broadcasted_iota(jnp.int32, (tokens, tile), 1)
    probs = jnp.exp(logits_ref[0] - norm_ref[...])
    grads = (jnp.where(place == ids_ref[...], probs - 1.0, probs) * weight_ref[...]).astype(BF16)
    grads_ref[0] = grads
    acc[...] += matmul(grads, e_ref[...])

    @pl.when(step == pl.num_programs(0) - 1)
    def _():
        back_ref[...] = acc[...].astype(BF16)


def head_grads(logits, embedding, ids, norm, weight):
    chunks, tokens, _ = logits.shape
    vocab, width = embedding.shape
    column = pl.BlockSpec((tokens, 1), lambda step: (0, 0))
    tile = pl.BlockSpec((1, tokens, CHUNK), lambda step: (step, 0, 0))
    return pl.pallas_call(
        head_grads_body,
        grid=(chunks,),
        out_shape=(
            jax.ShapeDtypeStruct(logits.shape, BF16),
            jax.ShapeDtypeStruct((tokens, width), BF16),
        ),
        in_specs=[
            tile, pl.BlockSpec((CHUNK, width), lambda step: (step, 0)), column, column, column
        ],
        out_specs=(tile, pl.BlockSpec((tokens, width), lambda step: (0, 0))),
        scratch_shapes=[pltpu.VMEM((tokens, width), F32)],
        compiler_params=pltpu.CompilerParams(vmem_limit_bytes=40 * 2**20),
        cost_estimate=pl.CostEstimate(
            flops=2 * tokens * vocab * width,
            bytes_accessed=6 * tokens * vocab + 2 * vocab * width,
            transcendentals=tokens * vocab,
        ),
    )(logits, embedding, ids, norm, weight)


BLOCK = 256


def masked_scores(queries, keys, slope, length, first):
    rows, cols = queries.shape[0], keys.shape[0]
    raw = matmul_t(queries, keys)
    i = first + lax.broadcasted_iota(jnp.int32, (rows, cols), 0)
    j = lax.broadcasted_iota(jnp.int32, (rows, cols), 1)
    scores = raw * HEAD_DIM ** (-0.5) - slope * (i - j).astype(F32)
    return jnp.where((j <= i) & (j < length), scores, NEG)


SMEM = pl.BlockSpec(memory_space=pltpu.SMEM)
VMEM = pl.BlockSpec(memory_space=pltpu.VMEM)


class TeamRows:
    def __init__(self, team, x_ref, full, stage, slots, own, ag_send, ag_recv, rs_send, rs_recv):
        self.team, self.count, self.me = team, team.count, team.me()
        self.x_ref, self.full, self.stage, self.slots, self.own = x_ref, full, stage, slots, own
        self.ag_sems, self.rs_sems = (ag_send, ag_recv), (rs_send, rs_recv)

    def shifted(self, step):
        return across(self.me, step)

    def peer(self, step):
        if self.team.square:
            return self.shifted(step)
        return lax.rem(self.me + 1 + step, self.count)

    def source(self, step):
        if self.team.square:
            return self.shifted(step)
        return lax.rem(self.me + self.count - 1 - step, self.count)

    def back_step(self, place):
        if self.team.square:
            flip_x = lax.rem(lax.rem(self.me, 2) + lax.rem(place, 2), 2)
            flip_y = lax.rem(lax.div(self.me, 2) + lax.div(place, 2), 2)
            return 2 * flip_y + flip_x - 1
        return lax.rem(place + self.count - 1 - self.me, self.count)

    def remote(self, number, peer, src, dst, sems):
        return pltpu.make_async_remote_copy(
            src_ref=src,
            dst_ref=dst,
            send_sem=sems[0].at[number],
            recv_sem=sems[1].at[number],
            device_id=self.team.device(peer),
            device_id_type=MESH,
        )

    def ag(self, number):
        if not self.team.square:
            return self.remote(
                number, self.peer(number), self.x_ref, self.full.at[self.me], self.ag_sems
            )
        half = self.x_ref.shape[0] // 2
        which = SQUARE_HALF[number]
        rows = pl.ds(which * half, half)
        peer = self.shifted(SQUARE_STEP[number])
        if number < 4:
            src, place = self.x_ref.at[rows], self.me
        else:
            place = self.shifted(number - 4)
            src = self.full.at[place, rows]
        return self.remote(number, peer, src, self.full.at[place, rows], self.ag_sems)

    def rs(self, step):
        return self.remote(
            step, self.peer(step), self.stage.at[self.peer(step)], self.slots.at[step], self.rs_sems
        )

    def send_rows(self):
        for number in (0, 2, 1, 3) if self.team.square else range(self.count - 1):
            self.ag(number).start()
        self.full[self.me] = self.x_ref[...]

    def pass_on(self):
        if self.team.square:
            for number in (0, 2):
                self.ag(number).wait_recv()
                self.ag(4 + number // 2).start()

    def wait_rows(self, step):
        if not self.team.square:
            self.ag(step).wait_recv()
            return
        for number, these in enumerate(((1,), (3,), (4, 5))):

            @pl.when(step == number)
            def _(these=these):
                for one in these:
                    self.ag(one).wait_recv()

    def each_arrival(self, work):
        work(self.me)
        self.pass_on()

        def one(step, carry):
            self.wait_rows(step)
            work(self.source(step))
            return carry

        lax.fori_loop(0, self.count - 1, one, 0)

    def each_arrival_and_back(self, term):
        self.own[...] = term(self.me)
        self.pass_on()

        def one(step, carry):
            self.wait_rows(step)
            place = self.source(step)
            self.stage[place] = term(place).astype(BF16)
            self.rs(self.back_step(place)).start()
            return carry

        lax.fori_loop(0, self.count - 1, one, 0)

    def finish(self, total_ref):
        for step in range(self.count - 1):
            self.rs(step).wait()
        total = self.own[...]
        for step in range(self.count - 1):
            total = total + self.slots[step].astype(F32)
        total_ref[...] = total
        for number in range(6 if self.team.square else self.count - 1):
            self.ag(number).wait_send()


def team_scratch(team, part, model):
    count = team.count
    dma = pltpu.SemaphoreType.DMA
    copies = 6 if team.square else count - 1
    return [
        pltpu.VMEM((count, part, model), BF16),
        pltpu.VMEM((count, part, model), BF16),
        pltpu.VMEM((count - 1, part, model), BF16),
        pltpu.VMEM((part, model), F32),
        dma((copies,)),
        dma((copies,)),
        dma((count - 1,)),
        dma((count - 1,)),
    ]


class LateDeal:
    def __init__(self, pair, landing, send_sem, recv_sem):
        self.pair, self.landing, self.sems = pair, landing, (send_sem, recv_sem)

    def other(self):
        return 1 - self.pair.me()

    def start(self, src):
        self.copy = send(self.pair, self.other(), 0, src, self.landing, *self.sems)

    def wait(self):
        self.copy.wait()


def team_call(body, team, ident, jobs, arrays, specs, outs, out_specs, scratch, pair=None, dealt=None):
    if pair is not None:
        outs, out_specs = tuple(outs) + (dealt,), tuple(out_specs) + (HBM,)
        scratch = list(scratch) + [pltpu.SemaphoreType.DMA((1,))] * 2
    part, model = arrays[0].shape
    count_in, count_out, riders = len(arrays), len(outs), len(jobs)
    own_scratch = team_scratch(team, part, model)

    def kernel(*refs):
        ins, refs = refs[:count_in], refs[count_in:]
        xs, refs = refs[:riders], refs[riders:]
        results, refs = refs[:count_out], refs[count_out:]
        landings, refs = refs[:riders], refs[riders:]
        rows = TeamRows(team, ins[0], *refs[: len(own_scratch)])
        refs = refs[len(own_scratch) :]
        mine, refs = refs[: len(scratch)], refs[len(scratch) :]
        greet([team] + job_groups(jobs) + ([] if pair is None else [pair]))
        rows.send_rows()
        parts = split_scratch(jobs, refs)
        ends = [job.start(xs[n], landings[n], *parts[n]) for n, job in enumerate(jobs)]
        if pair is None:
            body(rows, ins, results, mine)
        else:
            body(rows, ins, results[:-1], mine[:-2], LateDeal(pair, results[-1], *mine[-2:]))
        for end in ends:
            end()

    out = pl.pallas_call(
        kernel,
        out_shape=tuple(outs) + tuple(job.out for job in jobs),
        in_specs=list(specs) + [job.in_spec for job in jobs],
        out_specs=tuple(out_specs) + tuple(job.out_spec for job in jobs),
        scratch_shapes=own_scratch + list(scratch) + [one for job in jobs for one in job.scratch],
        compiler_params=pltpu.CompilerParams(
            collective_id=ident, has_side_effects=True, vmem_limit_bytes=58 * 2**20
        ),
    )(*arrays, *[job.x for job in jobs])
    return out[:count_out], list(out[count_out:])


def part_rows(place, part):
    return pl.ds(pl.multiple_of(place * part, part), part)


def attend_body(rows, ins, outs, scratch):
    x_ref, length_ref, slope_ref, qk_ref, vo_ref, bias_ref = ins
    total_ref, full_out, q_ref, k_ref, v_ref, mixed_ref, lse_ref = outs
    (full_sem,) = scratch
    part = x_ref.shape[0]
    width = q_ref.shape[1]

    def project(place):
        at = part_rows(place, part)
        block = rows.full[place]
        q_ref[at, :] = (matmul_t(block, qk_ref[0]) + bias_ref[0:1, :]).astype(BF16)
        k_ref[at, :] = matmul_t(block, qk_ref[1]).astype(BF16)
        v_ref[at, :] = (matmul_t(block, vo_ref[0]) + bias_ref[1:2, :]).astype(BF16)

    rows.each_arrival(project)
    keep = pltpu.make_async_copy(rows.full, full_out, full_sem)
    keep.start()

    def one(turn, carry):
        step = lax.rem(2 * rows.count - 2 - turn, rows.count)
        place = rows.peer(step)
        for block in range(rows.count):

            @pl.when(place == block)
            def _(first=block * part, upto=(block + 1) * part):
                for head in range(width // HEAD_DIM):
                    lanes = slice(head * HEAD_DIM, (head + 1) * HEAD_DIM)
                    scores = masked_scores(
                        q_ref[first:upto, lanes], k_ref[:upto, lanes], slope_ref[head],
                        length_ref[0], first,
                    )
                    highest = jnp.max(scores, axis=-1, keepdims=True)
                    powers = jnp.exp(scores - highest)
                    total = jnp.sum(powers, axis=-1, keepdims=True)
                    probs = (powers * (1.0 / total)).astype(BF16)
                    mixed_ref[first:upto, lanes] = matmul(probs, v_ref[:upto, lanes]).astype(BF16)
                    lse_ref[head, first:upto, :] = highest + jnp.log(total)

        term = matmul(mixed_ref[part_rows(place, part), :], vo_ref[1])

        @pl.when(step < rows.count - 1)
        def _():
            rows.stage[place] = term.astype(BF16)
            rows.rs(step).start()

        @pl.when(step == rows.count - 1)
        def _():
            rows.own[...] = term

        return carry

    lax.fori_loop(0, rows.count, one, 0)
    rows.finish(total_ref)
    keep.wait()


HBM = pl.BlockSpec(memory_space=pl.ANY)


def attend(team, ident, jobs, x, length, slopes, qk, vo, bias):
    part, model = x.shape
    seq = part * team.count
    width = qk.shape[1]
    low = jax.ShapeDtypeStruct((seq, width), BF16)
    return team_call(
        attend_body, team, ident, jobs,
        [x, length, slopes, qk, vo, bias],
        [VMEM, SMEM, SMEM, VMEM, VMEM, VMEM],
        (
            jax.ShapeDtypeStruct((part, model), F32),
            jax.ShapeDtypeStruct((team.count, part, model), BF16),
            low, low, low, low,
            jax.ShapeDtypeStruct((width // HEAD_DIM, seq, 1), F32),
        ),
        (VMEM, HBM, VMEM, VMEM, VMEM, VMEM, VMEM),
        [pltpu.SemaphoreType.DMA],
    )


def attend_back_body(rows, ins, outs, scratch, late=None):
    gy_ref, length_ref, slope_ref, a_ref, qk_ref, vo_ref, q_ref, k_ref, v_ref, mixed_ref, lse_ref = ins
    total_ref, grads_ref, sums_ref = outs
    go, gq, gk, gv, gk_sum, gv_sum = scratch
    part = gy_ref.shape[0]
    seq, width = q_ref.shape
    heads = width // HEAD_DIM
    gk_sum[...] = jnp.zeros_like(gk_sum)
    gv_sum[...] = jnp.zeros_like(gv_sum)
    sums_ref[...] = jnp.zeros_like(sums_ref)

    def open_block(place):
        go[part_rows(place, part), :] = matmul_t(rows.full[place], vo_ref[1]).astype(BF16)

    rows.each_arrival(open_block)
    for block in reversed(range(rows.count)):
        first, upto = block * part, (block + 1) * part
        for head in range(heads):
            lanes = slice(head * HEAD_DIM, (head + 1) * HEAD_DIM)
            queries, grads = q_ref[first:upto, lanes], go[first:upto, lanes]
            keys, values = k_ref[:upto, lanes], v_ref[:upto, lanes]
            scores = masked_scores(queries, keys, slope_ref[head], length_ref[0], first)
            probs = jnp.exp(scores - lse_ref[head, first:upto, :])
            grad_probs = matmul_t(grads, values)
            inner = jnp.sum(probs * grad_probs, axis=-1, keepdims=True)
            grad_scores = (probs * (grad_probs - inner) * HEAD_DIM ** (-0.5)).astype(BF16)
            piece = matmul(grad_scores, keys)
            sums_ref[0:1, lanes] += jnp.sum(piece, axis=0, keepdims=True)
            gq[first:upto, lanes] = piece.astype(BF16)
            gk_sum[:upto, lanes] += outer_sum(grad_scores, queries)
            gv_sum[:upto, lanes] += outer_sum(probs.astype(BF16), grads)
        gk[first:upto, :] = gk_sum[first:upto, :].astype(BF16)
        gv[first:upto, :] = gv_sum[first:upto, :].astype(BF16)
        term = (
            matmul(gq[first:upto, :], qk_ref[0]) + matmul(gk[first:upto, :], qk_ref[1])
            + matmul(gv[first:upto, :], vo_ref[0])
        )

        @pl.when(rows.me != block)
        def _(block=block, term=term):
            rows.stage[block] = term.astype(BF16)
            rows.rs(rows.back_step(block)).start()

        @pl.when(rows.me == block)
        def _(term=term):
            rows.own[...] = term

    sums_ref[1:2, :] = jnp.sum(gv_sum[...], axis=0, keepdims=True)
    model = gy_ref.shape[1]
    grads_ref[3] = outer_sum(mixed_ref[...], rows.full[...].reshape(seq, model))
    grads_ref[0] = outer_sum(gq[...], a_ref[...])
    grads_ref[1] = outer_sum(gv[...], a_ref[...])
    grads_ref[2] = outer_sum(gk[...], a_ref[...])
    if late is not None:
        late.start(grads_ref.at[pl.ds(2 * late.other(), 2)])
    rows.finish(total_ref)
    if late is not None:
        late.wait()


def attend_back(team, ident, jobs, pair, gy, length, slopes, a, qk, vo, q, k, v, mixed, lse):
    part, model = gy.shape
    seq, width = q.shape
    return team_call(
        attend_back_body, team, ident, jobs,
        [gy, length, slopes, a, qk, vo, q, k, v, mixed, lse],
        [VMEM, SMEM, SMEM] + [VMEM] * 8,
        (
            jax.ShapeDtypeStruct((part, model), F32),
            jax.ShapeDtypeStruct((4, width, model), F32),
            jax.ShapeDtypeStruct((2, width), F32),
        ),
        (VMEM,) * 3,
        [pltpu.VMEM((seq, width), BF16)] * 4 + [pltpu.VMEM((seq, width), F32)] * 2,
        pair,
        jax.ShapeDtypeStruct((2, width, model), F32),
    )


GELU_A = 0.7978845608028654
GELU_B = 0.044715


def strip_rows(strips, which, first, size):
    length = strips[0].shape[1]
    return strips[first // length][which, first % length : first % length + size, :]


def feed_body(rows, ins, outs, scratch):
    x_ref, bias_ref, *strips = ins
    total_ref, full_out, before_ref = outs
    (full_sem,) = scratch
    part = x_ref.shape[0]
    units = bias_ref.shape[1]
    tile = min(units, BLOCK)

    def term(place):
        at = part_rows(place, part)
        block = rows.full[place]
        total = None
        for first in range(0, units, tile):
            lanes = slice(first, first + tile)
            before = matmul_t(block, strip_rows(strips, 0, first, tile)) + bias_ref[:, lanes]
            before_ref[at, lanes] = before
            bend = jnp.tanh(GELU_A * (before + GELU_B * before * before * before))
            active = (0.5 * before * (1.0 + bend)).astype(BF16)
            piece = matmul(active, strip_rows(strips, 1, first, tile))
            total = piece if total is None else total + piece
        return total

    rows.each_arrival_and_back(term)
    keep = pltpu.make_async_copy(rows.full, full_out, full_sem)
    keep.start()
    rows.finish(total_ref)
    keep.wait()


def feed(team, ident, jobs, x, strips, bias):
    part, model = x.shape
    units = bias.shape[1]
    return team_call(
        feed_body, team, ident, jobs,
        [x, bias] + strips,
        [VMEM] * (2 + len(strips)),
        (
            jax.ShapeDtypeStruct((part, model), F32),
            jax.ShapeDtypeStruct((team.count, part, model), BF16),
            jax.ShapeDtypeStruct((part * team.count, units), F32),
        ),
        (VMEM, HBM, VMEM),
        [pltpu.SemaphoreType.DMA],
    )


def feed_back_body(rows, ins, outs, scratch, late=None):
    gz_ref, c_ref, before_ref, *strips = ins
    total_ref, grads_ref, sums_ref = outs
    active, low = scratch
    part, model = gz_ref.shape
    seq = part * rows.count
    units = before_ref.shape[1]
    tile = min(units, BLOCK)
    sums_ref[...] = jnp.zeros_like(sums_ref)

    def term(place):
        at = part_rows(place, part)
        gz = rows.full[place]
        for first in range(0, units, tile):
            lanes = slice(first, first + tile)
            before = before_ref[at, lanes]
            square = before * before
            bend = jnp.tanh(GELU_A * before * (1.0 + GELU_B * square))
            half = 0.5 * (1.0 + bend)
            slope = half + 0.5 * before * (1.0 - bend * bend) * (
                GELU_A * (1.0 + 3.0 * GELU_B * square)
            )
            grad = matmul_t(gz, strip_rows(strips, 1, first, tile)) * slope
            sums_ref[:, lanes] += jnp.sum(grad, axis=0, keepdims=True)
            active[at, lanes] = (before * half).astype(BF16)
            low[at, lanes] = grad.astype(BF16)
        length = strips[0].shape[1]
        return sum(
            matmul(low[at, n * length : (n + 1) * length], strip[0])
            for n, strip in enumerate(strips)
        )

    rows.each_arrival_and_back(term)
    for first in range(0, units, tile):
        lanes = slice(first, first + tile)
        grads_ref[0, lanes, :] = outer_sum(low[:, lanes], c_ref[...])
        grads_ref[1, lanes, :] = outer_sum(active[:, lanes], rows.full[...].reshape(seq, model))
    if late is not None:
        late.start(grads_ref.at[late.other()])
    rows.finish(total_ref)
    if late is not None:
        late.wait()


def feed_back(team, ident, jobs, pair, gz, c, before, strips):
    part, model = gz.shape
    seq = part * team.count
    units = before.shape[1]
    return team_call(
        feed_back_body, team, ident, jobs,
        [gz, c, before] + strips,
        [VMEM] * (3 + len(strips)),
        (
            jax.ShapeDtypeStruct((part, model), F32),
            jax.ShapeDtypeStruct((2, units, model), F32),
            jax.ShapeDtypeStruct((1, units), F32),
        ),
        (VMEM,) * 3,
        [pltpu.VMEM((seq, units), BF16)] * 2,
        pair,
        jax.ShapeDtypeStruct((units, model), F32),
    )


def line_head_logits_body(
    group, x_ref, e_ref, ids_ref, logits_ref, full_out, stats_out,
    full, table, staged, top, total, pick, stats,
    ag_send, ag_recv, e_sem, out_sem, full_sem, st_send, st_recv,
):
    count, me = group.count, group.me()
    part = x_ref.shape[0]
    tiles = e_ref.shape[0] // CHUNK
    line = LineRows(group, x_ref, full, ag_send, ag_recv)
    greet([group])
    line.start()
    full[me] = x_ref[...]
    top[...] = jnp.full_like(top, NEG)
    total[...] = jnp.zeros_like(total)
    pick[...] = jnp.zeros_like(pick)

    def rows_of(tile):
        return pl.ds(pl.multiple_of(tile * CHUNK, CHUNK), CHUNK)

    def load(tile):
        return pltpu.make_async_copy(
            e_ref.at[rows_of(tile)], table.at[rows_of(tile)], e_sem.at[tile]
        )

    def leave(tile, place, slot):
        return pltpu.make_async_copy(
            staged.at[slot], logits_ref.at[tile, part_rows(place, part)], out_sem.at[slot]
        )

    for tile in range(tiles):
        load(tile).start()

    def work(place, first):
        at = part_rows(place, part)
        ids = ids_ref[at, :]

        def one(pair, carry):
            for slot in range(2):
                tile = 2 * pair + slot
                if first:
                    load(tile).wait()

                    @pl.when(pair > 0)
                    def _(slot=slot, tile=tile):
                        leave(tile, place, slot).wait()

                else:
                    leave(tile, place, slot).wait()
                logits = matmul_t(full[place], table[rows_of(tile), :])
                staged[slot] = logits
                leave(tile, place, slot).start()
                column = tile * CHUNK + lax.broadcasted_iota(jnp.int32, (part, CHUNK), 1)
                picked = jnp.where(column == ids, logits, 0.0)
                pieces = [logits[:, at : at + LANES] for at in range(0, CHUNK, LANES)]
                before = top[at, :]
                high = functools.reduce(jnp.maximum, pieces, before)
                sums = total[at, :] * jnp.exp(before - high)
                found = pick[at, :]
                for number, piece in enumerate(pieces):
                    sums = sums + jnp.exp(piece - high)
                    found = found + picked[:, number * LANES : (number + 1) * LANES]
                top[at, :] = high
                total[at, :] = sums
                pick[at, :] = found
            return carry

        lax.fori_loop(0, tiles // 2, one, 0)

    work(me, True)
    for step in range(1, count):
        line.step(step)

        @pl.when(me >= step)
        def _(step=step):
            work(me - step, False)

        @pl.when(me + step < count)
        def _(step=step):
            work(me + step, False)

    keep = pltpu.make_async_copy(full, full_out, full_sem)
    keep.start()
    tall = top[...].T
    high = jnp.max(tall, axis=0, keepdims=True)
    stats[me] = jnp.zeros(stats.shape[1:], F32)
    stats[me, 0:1, :] = high
    stats[me, 1:2, :] = jnp.sum(total[...].T * jnp.exp(tall - high), axis=0, keepdims=True)
    stats[me, 2:3, :] = jnp.sum(pick[...].T, axis=0, keepdims=True)
    copies = [
        send(group, peer, step, stats.at[me], stats.at[me], st_send, st_recv)
        for step, peer in enumerate(group.peers())
    ]
    for slot in range(2):
        leave(0, me, slot).wait()
    line.wait_sends()
    for copy in copies:
        copy.wait()
    stats_out[...] = stats[...]
    keep.wait()


def line_head_logits(group, ident, x, embedding, ids):
    part, width = x.shape
    vocab = embedding.shape[0]
    count = group.count
    tokens = part * count
    tiles = vocab // CHUNK
    assert tiles % 2 == 0
    dma = pltpu.SemaphoreType.DMA
    return pl.pallas_call(
        functools.partial(line_head_logits_body, group),
        out_shape=(
            jax.ShapeDtypeStruct((tiles, tokens, CHUNK), F32),
            jax.ShapeDtypeStruct((count, part, width), BF16),
            jax.ShapeDtypeStruct((count, 8, tokens), F32),
        ),
        in_specs=[VMEM, HBM, VMEM],
        out_specs=(HBM, HBM, VMEM),
        scratch_shapes=[
            pltpu.VMEM((count, part, width), BF16),
            pltpu.VMEM((vocab, width), BF16),
            pltpu.VMEM((2, part, CHUNK), F32),
            pltpu.VMEM((tokens, LANES), F32),
            pltpu.VMEM((tokens, LANES), F32),
            pltpu.VMEM((tokens, LANES), F32),
            pltpu.VMEM((count, 8, tokens), F32),
            dma((2 * count - 2,)),
            dma((2 * count - 2,)),
            dma((tiles,)),
            dma((2,)),
            dma,
            dma((count - 1,)),
            dma((count - 1,)),
        ],
        compiler_params=pltpu.CompilerParams(
            collective_id=ident, has_side_effects=True, vmem_limit_bytes=56 * 2**20
        ),
    )(x, embedding, ids)


def line_head_grads_body(
    group, logits_ref, e_ref, ids_ref, norm_ref, weight_ref, grads_ref, total_ref,
    terms, stage, land, table, staged, low, acc,
    rs_send, rs_recv, e_sem, in_sem, out_sem,
):
    count, me = group.count, group.me()
    part = terms.shape[1]
    tiles = e_ref.shape[0] // CHUNK
    line = LineSum(group, terms, stage, land, rs_send, rs_recv)
    greet([group])

    def rows_of(tile):
        return pl.ds(pl.multiple_of(tile * CHUNK, CHUNK), CHUNK)

    def load(tile):
        return pltpu.make_async_copy(
            e_ref.at[rows_of(tile)], table.at[rows_of(tile)], e_sem.at[tile]
        )

    def enter(tile, place, slot):
        return pltpu.make_async_copy(
            logits_ref.at[tile, part_rows(place, part)], staged.at[slot], in_sem.at[slot]
        )

    def leave(tile, place, slot):
        return pltpu.make_async_copy(
            low.at[:, pl.ds(slot * CHUNK, CHUNK)],
            grads_ref.at[tile, part_rows(place, part)],
            out_sem.at[slot],
        )

    for tile in range(tiles):
        load(tile).start()
    for tile in range(tiles):
        load(tile).wait()

    def work(place):
        at = part_rows(place, part)
        ids, norm, weight = ids_ref[at, :], norm_ref[at, :], weight_ref[at, :]
        for slot in range(2):
            enter(slot, place, slot).start()
        acc[...] = jnp.zeros_like(acc)

        def one(pair, carry):
            for slot in range(2):
                tile = 2 * pair + slot
                enter(tile, place, slot).wait()
                column = tile * CHUNK + lax.broadcasted_iota(jnp.int32, (part, CHUNK), 1)
                probs = jnp.exp(staged[slot] - norm)
                grads = (jnp.where(column == ids, probs - 1.0, probs) * weight).astype(BF16)

                @pl.when(pair > 0)
                def _(slot=slot, tile=tile):
                    leave(tile, place, slot).wait()

                low[:, slot * CHUNK : (slot + 1) * CHUNK] = grads
                leave(tile, place, slot).start()

                @pl.when(pair + 1 < tiles // 2)
                def _(slot=slot, tile=tile):
                    enter(tile + 2, place, slot).start()

            rows = pl.ds(pl.multiple_of(pair * 2 * CHUNK, 2 * CHUNK), 2 * CHUNK)
            acc[...] += matmul(low[...], table[rows, :])
            return carry

        lax.fori_loop(0, tiles // 2, one, 0)
        for slot in range(2):
            leave(0, place, slot).wait()
        terms[place] = acc[...].astype(BF16)

    for step in range(count - 1):

        @pl.when(me < count - 1 - step)
        def _(step=step):
            work(count - 1 - step)

        @pl.when(me > step)
        def _(step=step):
            work(step)

        line.first(step)
        if step == 1:
            line.rest(0, near=True)
    work(me)
    line.rest(0, near=False)
    for step in range(1, count - 1):
        line.rest(step)
    line.finish(total_ref)


def line_head_grads(group, ident, logits, embedding, ids, norm, weight):
    tiles, tokens, _ = logits.shape
    vocab, width = embedding.shape
    count = group.count
    part = tokens // count
    dma = pltpu.SemaphoreType.DMA
    return pl.pallas_call(
        functools.partial(line_head_grads_body, group),
        out_shape=(
            jax.ShapeDtypeStruct(logits.shape, BF16),
            jax.ShapeDtypeStruct((part, width), F32),
        ),
        in_specs=[HBM, HBM, VMEM, VMEM, VMEM],
        out_specs=(HBM, VMEM),
        scratch_shapes=[
            pltpu.VMEM((count, part, width), BF16),
            pltpu.VMEM((2, count - 1, part, width), BF16),
            pltpu.VMEM((2, count - 1, part, width), BF16),
            pltpu.VMEM((vocab, width), BF16),
            pltpu.VMEM((2, part, CHUNK), F32),
            pltpu.VMEM((part, 2 * CHUNK), BF16),
            pltpu.VMEM((part, width), F32),
            dma((2, count - 1)),
            dma((2, count - 1)),
            dma((tiles,)),
            dma((2,)),
            dma((2,)),
        ],
        compiler_params=pltpu.CompilerParams(
            collective_id=ident, has_side_effects=True, vmem_limit_bytes=56 * 2**20
        ),
    )(logits, embedding, ids, norm, weight)


def per_device(
    mesh_shape,
    token_ids,
    target_ids,
    lengths,
    embedding,
    outer_gain,
    outer_bias,
    norm_gain,
    norm_bias,
    qkv_weight,
    qv_bias,
    out_weight,
    up_weight,
    up_bias,
    down_weight,
    row_bias,
):
    sections, groups, shards = (mesh_shape[name] for name in ("section", "dp", "tensor"))
    s, j, z = (lax.axis_index(name) for name in ("section", "dp", "tensor"))
    by_section = Group(("section",), (sections,))
    by_dp = Group(("dp",), (groups,))
    by_tensor = Group(("tensor",), (shards,))
    exchange = Exchanges()
    layers = sections
    vocab, width = embedding.shape
    seq = token_ids.shape[1]
    rows = token_ids.shape[0] * groups
    local_cols = qkv_weight.shape[-1]
    planes = rows == sections * shards and local_cols % (groups * HEAD_DIM) == 0
    by_dp.square = planes and groups == 4
    by_tensor.line = planes
    team = by_dp if planes else by_tensor
    cut = groups if planes else 1
    fan = shards if planes else 1
    halves = 2 if planes else 1
    part = seq // team.count
    cols = local_cols // cut
    hidden = up_weight.shape[-1] // cut
    strip = hidden // halves
    cut_index = j if planes else 0
    my_row = z * sections + s if planes else j * sections + s
    length = lax.dynamic_slice(lengths, (my_row,), (1,))
    token_count = jnp.sum(lengths).astype(F32)
    vocab_start = z * vocab

    def chosen_cols(array, size):
        return lax.dynamic_slice_in_dim(array, cut_index * size, size, array.ndim - 1).T

    def chosen_rows(array, size):
        return lax.dynamic_slice_in_dim(array, cut_index * size, size, 0)

    def pad_rows(array, count):
        return jnp.pad(array, ((0, count - array.shape[0]), (0, width - array.shape[1])))

    sides = jnp.stack(
        [
            jnp.concatenate(
                [
                    chosen_cols(qkv_weight[0, 0], cols),
                    chosen_cols(qkv_weight[0, 2], cols),
                    chosen_cols(up_weight[0], hidden),
                ]
            ),
            jnp.concatenate(
                [
                    chosen_cols(qkv_weight[0, 1], cols),
                    chosen_rows(out_weight[0], cols),
                    chosen_rows(down_weight[0], hidden),
                ]
            ),
        ]
    )
    qv_piece = lax.dynamic_slice_in_dim(qv_bias[0], cut_index * cols, cols, 1)
    up_piece = lax.dynamic_slice_in_dim(up_bias[0], cut_index * hidden, hidden, 0)
    small = jnp.concatenate(
        [
            outer_gain,
            outer_bias,
            norm_gain[0],
            norm_bias[0],
            row_bias[0],
            pad_rows(qv_piece, 2),
            pad_rows(up_piece[None], 6),
        ]
    )

    def gather(group, x):
        return Job("gather", [group], x)

    def deal(group, x, axis=0):
        return Job("deal", [group], x, axis)

    def own_and_dealt(x, dealt, place, axis=0):
        own = lax.dynamic_index_in_dim(x, place, axis, keepdims=False).astype(F32)
        return own + jnp.sum(dealt.astype(F32), axis=0)

    if planes:
        other, both, small_all = exchange(
            deal(by_section, sides),
            gather(by_dp, jnp.stack([token_ids, target_ids])),
            gather(Group(("section", "tensor"), (sections, shards)), small),
        )
        small_all = small_all.reshape((sections, shards) + small.shape)
        own_side = lax.dynamic_index_in_dim(sides, s, 0, keepdims=False)
        side = [jnp.where(s == l, own_side, other[0]) for l in range(layers)]
        both = jnp.swapaxes(both, 0, 1).reshape(2, shards, sections, groups, part)
        both = lax.dynamic_index_in_dim(
            lax.dynamic_index_in_dim(both, s, 2, keepdims=False), j, 2, keepdims=False
        )
        ids, targets = both[0].reshape(-1), both[1].reshape(-1)
        group_lengths = lax.dynamic_index_in_dim(
            lengths.reshape(shards, sections), s, 1, keepdims=False
        )
        places = jnp.broadcast_to(j * part + jnp.arange(part), (shards, part))
        valid = (places < group_lengths[:, None]).reshape(-1)
    else:
        sides_all, small_all = exchange(gather(by_section, sides), gather(by_section, small))
        small_all = small_all[:, None]
        ids, targets = token_ids[s], target_ids[s]
        valid = jnp.arange(seq) < lengths[my_row]

    outer_gains = [small_all[l, 0, 0] for l in range(layers)]
    outer_offsets = [small_all[l, 0, 1] for l in range(layers)]
    params = []
    for l in range(layers):
        biases = [small_all[l, :, 8 + n, :cols].reshape(-1) for n in range(2)]
        units = small_all[l, :, 10, :hidden].reshape(fan, halves, strip)
        params.append(
            dict(
                gains=small_all[l, 0, 2:4],
                offsets=small_all[l, 0, 4:6],
                row_bias=small_all[l, 0, 6:8],
                bias=jnp.stack(biases),
                up_bias=jnp.swapaxes(units, 0, 1).reshape(1, -1),
            )
        )
        if not planes:
            block = sides_all[l]
            params[l].update(
                qk=block[:, :cols],
                vo=block[:, cols : 2 * cols],
                strips=[block[:, 2 * cols :]],
            )
    head_number = (
        (jnp.arange(fan)[:, None] if planes else z) * (local_cols // HEAD_DIM)
        + cut_index * (cols // HEAD_DIM)
        + jnp.arange(cols // HEAD_DIM)
    ).reshape(-1)
    slopes = jnp.exp2(-8.0 * (head_number + 1).astype(F32) / HEADS)

    def attn_jobs(l):
        if not planes or l >= layers:
            return []
        return [
            Job("spread", [by_tensor, by_section], side[l][first : first + cols])
            for first in (0, cols)
        ]

    def feed_jobs(l, n):
        if not planes or l >= layers:
            return []
        first = 2 * cols + n * strip
        return [Job("spread", [by_tensor, by_section], side[l][first : first + strip])]

    def take_attn(l, got):
        if got:
            params[l]["qk"], params[l]["vo"] = (
                one.reshape(2, fan * cols, width) for one in got
            )

    def take_feed(l, got):
        if got:
            params[l]["strips"] = [one.reshape(2, fan * strip, width) for one in got]

    def ident(kind, jobs):
        return exchange.ident((kind,) + tuple(job.key() for job in jobs))

    local_ids = ids - vocab_start
    inside = (local_ids >= 0) & (local_ids < vocab)
    looked = jnp.where(
        inside[:, None], jnp.take(embedding, jnp.clip(local_ids, 0, vocab - 1), axis=0), 0
    )
    group_part = looked.shape[0] // shards
    x, *got = exchange(
        Job("reduce", [by_tensor], looked.reshape(shards, group_part, width)), *attn_jobs(0)
    )
    take_attn(0, got)
    h = layer_norm(x, outer_gains[0], outer_offsets[0])

    kept = []
    strips = []
    for l, p in enumerate(params):
        jobs = (feed_jobs(l, 0) if l == 0 else []) + feed_jobs(l, 1)
        normed = layer_norm(h, p["gains"][0], p["offsets"][0]).astype(BF16)
        (total, normed, q, k, v, mixed, lse), got = attend(
            team, ident("attend", jobs), jobs, normed, length, slopes, p["qk"], p["vo"], p["bias"]
        )
        take_feed(l, strips + got)
        middle = h + total + p["row_bias"][0]
        jobs = attn_jobs(l + 1) + feed_jobs(l + 1, 0)
        second = layer_norm(middle, p["gains"][1], p["offsets"][1]).astype(BF16)
        (total, second, before), got = feed(
            team, ident("feed", jobs), jobs, second, p["strips"], p["up_bias"]
        )
        take_attn(l + 1, got[:2])
        strips = got[2:]
        kept.append((h, normed.reshape(seq, width), q, k, v, mixed, lse, middle, second, before))
        h = middle + total + p["row_bias"][1]

    final = layer_norm(h, outer_gains[-1], outer_offsets[-1]).astype(BF16)
    columns_of = (targets - vocab_start)[:, None]
    if planes:
        logits, final, stats = line_head_logits(
            by_tensor, exchange.ident("head logits"), final, embedding, columns_of
        )
        final = final.reshape(-1, width)
    else:
        (final,) = exchange(gather(by_tensor, final))
        final = final.reshape(-1, width)
        logits, tops, totals, picks = head_logits(final, embedding, columns_of)
        top = jnp.max(tops, axis=1)
        total = jnp.sum(totals * jnp.exp(tops - top[:, None]), axis=1)
        pick = jnp.sum(picks, axis=1)
        (stats,) = exchange(
            gather(by_tensor, jnp.pad(jnp.stack([top, total, pick]), ((0, 5), (0, 0))))
        )
    tokens = final.shape[0]
    top_all = jnp.max(stats[:, 0], axis=0)
    log_norm = top_all + jnp.log(jnp.sum(stats[:, 1] * jnp.exp(stats[:, 0] - top_all), axis=0))
    terms = jnp.where(valid, log_norm - jnp.sum(stats[:, 2], axis=0), 0.0)
    loss_part = jnp.sum(
        lax.dynamic_index_in_dim(terms.reshape(shards, -1), z, 0, keepdims=False)
    )
    row_weight = jnp.where(valid, 1.0 / token_count, 0.0)
    if planes:
        grad_logits, grad_final = line_head_grads(
            by_tensor, exchange.ident("head grads"), logits, embedding, columns_of,
            log_norm[:, None], row_weight[:, None],
        )
    else:
        grad_logits, back = head_grads(
            logits, embedding, columns_of, log_norm[:, None], row_weight[:, None]
        )
        (grad_final,) = exchange(
            Job("reduce", [by_tensor], back.reshape(shards, group_part, width))
        )
    _, final_back = jax.vjp(layer_norm, h, outer_gains[-1], outer_offsets[-1])
    grad, final_gain, final_offset = final_back(grad_final)

    def section_sums(pair, got):
        out = []
        for one, dealt in zip(pair, got):
            low = own_and_dealt(one, dealt, s).astype(BF16)
            if one.ndim == 4:
                out.append(low.reshape(low.shape[0], fan, cols, width))
            else:
                out.append(low.reshape(halves, fan, strip, width))
        return out

    def tensor_jobs(lows):
        return [deal(by_tensor, low, 1) for low in lows]

    def tensor_sums(lows, got):
        return [
            own_and_dealt(low, dealt, z, 1).astype(BF16) for low, dealt in zip(lows, got)
        ]

    def spread_jobs(pieces):
        return [Job("spread", [by_dp, by_section], piece) for piece in pieces]

    small_rows = [None] * layers
    pairs = [None] * layers
    attn_low, attn_done, feed_done = ([None] * layers for _ in range(3))
    for l in reversed(range(layers)):
        p = params[l]
        section_in, normed, q, k, v, mixed, lse, middle, second, before = kept[l]
        pair = by_section if planes else None
        late = planes and l + 1 < layers
        jobs = tensor_jobs(attn_low[l + 1]) if late else []
        (total, g_feed, up_sum, *dealt), got = feed_back(
            team, ident("feed back", jobs), jobs, pair, grad.astype(BF16),
            second.reshape(seq, width), before, p["strips"],
        )
        if late:
            attn_done[l + 1] = tensor_sums(attn_low[l + 1], got)
        if planes:
            feed_low = section_sums([g_feed], [one[None] for one in dealt])
        _, norm_back = jax.vjp(layer_norm, middle, p["gains"][1], p["offsets"][1])
        grad_mid, gain_two, offset_two = norm_back(total)
        grad_mid = grad_mid + grad
        jobs = tensor_jobs(feed_low) if planes else []
        (total, g_attn, qv_sum, *dealt), got = attend_back(
            team, ident("attend back", jobs), jobs, pair, grad_mid.astype(BF16), length, slopes,
            normed, p["qk"], p["vo"], q, k, v, mixed, lse,
        )
        g_attn = g_attn.reshape((2, 2) + g_attn.shape[1:])
        if planes:
            feed_done[l] = tensor_sums(feed_low, got)
            attn_low[l] = section_sums([g_attn], [one[None] for one in dealt])
        _, norm_back = jax.vjp(layer_norm, section_in, p["gains"][0], p["offsets"][0])
        grad_in, gain_one, offset_one = norm_back(total)
        bias_two = jnp.sum(grad, axis=0)
        grad = grad_in + grad_mid
        pairs[l] = (g_attn, g_feed)

        def placed(values, size):
            out = jnp.zeros((fan if planes else shards, cut, size), F32)
            at = (0, j, 0) if planes else (z, 0, 0)
            return lax.dynamic_update_slice(out, values.reshape(fan, 1, size), at).reshape(
                -1, width
            )

        units = jnp.swapaxes(up_sum.reshape(halves, fan, strip), 0, 1)
        small_rows[l] = [
            gain_one[None],
            gain_two[None],
            offset_one[None],
            offset_two[None],
            jnp.sum(grad_mid, axis=0)[None],
            bias_two[None],
            placed(qv_sum[0], cols),
            placed(qv_sum[1], cols),
            placed(units, hidden),
        ]

    _, embed_back = jax.vjp(layer_norm, x, outer_gains[0], outer_offsets[0])
    grad_rows, embed_gain, embed_offset = embed_back(grad)
    packed = jnp.concatenate(
        [row for l in range(layers) for row in small_rows[l]]
        + [embed_gain[None], final_gain[None], embed_offset[None], final_offset[None]]
        + [jnp.broadcast_to(loss_part, (1, width))]
    )
    used = packed.shape[0]
    packed = jnp.pad(packed, ((0, -used % 8), (0, 0)))
    jobs = [Job("gather", [Group(("section", "tensor"), (sections, shards))], packed, late=True)]
    if planes:
        jobs += spread_jobs(attn_done[1] + feed_done[1] + feed_done[0])
        jobs += [Job("deal", [by_tensor], low, 1, late=True) for low in attn_low[0]]
    embed_sum, packed, *got = table_sum(
        by_section, by_dp, by_tensor, jobs, grad_logits, ids[None, :] - vocab_start, final,
        grad_rows.astype(BF16), exchange.ident("table"),
    )
    packed = jnp.sum(packed, axis=0)
    jobs = [gather(by_dp, packed)]
    if planes:
        spread_one = got[:2]
        jobs += spread_jobs(tensor_sums(attn_low[0], got[3:]))
    packed, *spread_zero = exchange(*jobs)
    packed = jnp.sum(packed, axis=0)
    if planes:
        spread_zero.append(got[2])
        attn_sum, feed_sum = (
            jnp.where(s == 0, zero, one) for zero, one in zip(spread_zero, spread_one)
        )
    else:
        chosen = [
            lax.dynamic_index_in_dim(
                lax.psum(jnp.stack([pair[n] for pair in pairs]), ("section", "dp")),
                s, 0, keepdims=False,
            )
            for n in range(2)
        ]
        attn_sum = chosen[0][:, None]
        feed_sum = chosen[1][:, None, None]
    embed_sum = embed_sum.reshape(vocab, width).astype(F32)
    per_layer = (used - 5) // layers
    mine = lax.dynamic_slice_in_dim(packed, s * per_layer, per_layer, 0)
    qv_rows = mine[6:8].reshape(2, -1)
    ff_row = mine[8:].reshape(-1)
    grad_qv = lax.dynamic_slice_in_dim(qv_rows, z * local_cols, local_cols, 1)
    grad_up_bias = lax.dynamic_slice_in_dim(ff_row, z * hidden * cut, hidden * cut, 0)
    base = per_layer * layers
    grad_outer_gain = lax.dynamic_slice_in_dim(packed, base + s, 1, 0)
    grad_outer_bias = lax.dynamic_slice_in_dim(packed, base + 2 + s, 1, 0)
    loss = packed[base + 4, 0] / token_count

    def columns(array):
        return array.astype(F32).reshape(-1, width).T

    grad_qkv = jnp.stack(
        [columns(attn_sum[0, :, 0]), columns(attn_sum[1, :, 0]), columns(attn_sum[0, :, 1])]
    )
    grad_out_mat = attn_sum[1, :, 1].astype(F32).reshape(-1, width)
    grad_up = columns(feed_sum[0])
    grad_down = feed_sum[1].astype(F32).reshape(-1, width)
    return (
        loss,
        embed_sum,
        grad_outer_gain,
        grad_outer_bias,
        mine[0:2][None],
        mine[2:4][None],
        grad_qkv[None],
        grad_qv[None],
        grad_out_mat[None],
        grad_up[None],
        grad_up_bias[None],
        grad_down[None],
        mine[4:6][None],
    )


def solution(mesh):
    return jax.shard_map(
        functools.partial(per_device, dict(mesh.shape)),
        mesh=mesh,
        in_specs=(
            P("dp", None),
            P("dp", None),
            P(),
            P("tensor", None),
            P("section", None),
            P("section", None),
            P("section", None, None),
            P("section", None, None),
            P("section", None, None, "tensor"),
            P("section", None, "tensor"),
            P("section", "tensor", None),
            P("section", None, "tensor"),
            P("section", "tensor"),
            P("section", "tensor", None),
            P("section", None, None),
        ),
        out_specs=(
            P(),
            P("tensor", None),
            P("section", None),
            P("section", None),
            P("section", None, None),
            P("section", None, None),
            P("section", None, None, "tensor"),
            P("section", None, "tensor"),
            P("section", "tensor", None),
            P("section", None, "tensor"),
            P("section", "tensor"),
            P("section", "tensor", None),
            P("section", None, None),
        ),
        check_vma=False,
    )
```

```python
import functools
import math

import jax
import jax.numpy as jnp
from jax import lax
from jax.experimental import pallas as pl
from jax.experimental.pallas import tpu as pltpu
from jax.sharding import PartitionSpec as P

HEADS = 16
HEAD_DIM = 64
EPS = 1e-05
NEG = -1e30
MESH = pl.DeviceIdType.MESH
F32 = jnp.float32
BF16 = jnp.bfloat16


def matmul(former, latter):
    return jnp.dot(former, latter, preferred_element_type=F32)


def matmul_t(former, latter):
    return lax.dot_general(
        former, latter, (((1,), (1,)), ((), ())), preferred_element_type=F32
    )


def outer_sum(former, latter):
    return lax.dot_general(
        former, latter, (((0,), (0,)), ((), ())), preferred_element_type=F32
    )


def layer_norm(inputs, weight, offset):
    centre = inputs - jnp.mean(inputs, axis=-1, keepdims=True)
    spread = jnp.mean(centre * centre, axis=-1, keepdims=True)
    return centre * lax.rsqrt(spread + EPS) * weight + offset


def gelu_tanh(inputs):
    return jax.nn.gelu(inputs, approximate=True)


class Group:
    def __init__(self, axes, sizes, square=False, line=False):
        self.square = square
        self.line = line
        self.axes = axes
        self.sizes = sizes
        self.count = math.prod(sizes)

    def me(self):
        place = 0
        for axis, size in zip(self.axes, self.sizes):
            place = place * size + lax.axis_index(axis)
        return place

    def device(self, place):
        spot = {}
        for axis, size in reversed(list(zip(self.axes, self.sizes))):
            spot[axis] = lax.rem(place, size)
            place = lax.div(place, size)
        return spot

    def peers(self):
        me = self.me()
        return [lax.rem(me + step, self.count) for step in range(1, self.count)]


def greet(groups):
    barrier = pltpu.get_barrier_semaphore()
    total = 0
    for group in groups:
        for peer in group.peers():
            pl.semaphore_signal(
                barrier, inc=1, device_id=group.device(peer), device_id_type=MESH
            )
            total += 1
    pl.semaphore_wait(barrier, total)


def send(group, peer, step, src, dst, send_sem, recv_sem):
    copy = pltpu.make_async_remote_copy(
        src_ref=src,
        dst_ref=dst,
        send_sem=send_sem.at[step],
        recv_sem=recv_sem.at[step],
        device_id=group.device(peer),
        device_id_type=MESH,
    )
    copy.start()
    return copy


def tie(*arrays):
    return lax.optimization_barrier(arrays)


class LineRows:
    def __init__(self, group, x, full, send_sem, recv_sem):
        self.group, self.count, self.me = group, group.count, group.me()
        self.x, self.full, self.sems = x, full, (send_sem, recv_sem)

    def copy(self, up, step):
        place = self.me - step if up else self.me + step
        place = jnp.clip(place, 0, self.count - 1)
        number = step if up else self.count - 1 + step
        src = self.x if step == 0 else self.full.at[place]
        return pltpu.make_async_remote_copy(
            src_ref=src,
            dst_ref=self.full.at[place],
            send_sem=self.sems[0].at[number],
            recv_sem=self.sems[1].at[number],
            device_id=self.group.device(
                jnp.clip(self.me + 1 if up else self.me - 1, 0, self.count - 1)
            ),
            device_id_type=MESH,
        )

    def leaves(self, up, step):
        if up:
            return (self.me - step >= 0) & (self.me < self.count - 1)
        return (self.me + step < self.count) & (self.me > 0)

    def arrives(self, up, step):
        return self.me - 1 - step >= 0 if up else self.me + 1 + step < self.count

    def start(self):
        for up in (True, False):

            @pl.when(self.leaves(up, 0))
            def _(up=up):
                self.copy(up, 0).start()

    def step(self, step):
        for up in (True, False):

            @pl.when(self.arrives(up, step - 1))
            def _(up=up):
                self.copy(up, step - 1).wait_recv()

            if step < self.count - 1:

                @pl.when(self.leaves(up, step))
                def _(up=up):
                    self.copy(up, step).start()

    def wait_sends(self):
        for step in range(self.count - 1):
            for up in (True, False):

                @pl.when(self.leaves(up, step))
                def _(up=up, step=step):
                    self.copy(up, step).wait_send()

    def finish(self):
        for step in range(1, self.count):
            self.step(step)
        self.wait_sends()


class LineSum:
    def __init__(self, group, x, stage, land, send_sem, recv_sem):
        self.group, self.count, self.me = group, group.count, group.me()
        self.x, self.stage, self.land, self.sems = x, stage, land, (send_sem, recv_sem)

    def copy(self, up, step):
        side = 0 if up else 1
        return pltpu.make_async_remote_copy(
            src_ref=self.stage.at[side, step],
            dst_ref=self.land.at[side, step],
            send_sem=self.sems[0].at[side, step],
            recv_sem=self.sems[1].at[side, step],
            device_id=self.group.device(
                jnp.clip(self.me + 1 if up else self.me - 1, 0, self.count - 1)
            ),
            device_id_type=MESH,
        )

    def leaves(self, up, step):
        return self.me < self.count - 1 - step if up else self.me > step

    def behind(self, up):
        return self.me > 0 if up else self.me < self.count - 1

    def first(self, step):
        for up in (True, False):
            place = self.count - 1 - step if up else step
            side = 0 if up else 1

            @pl.when(self.leaves(up, step) & jnp.logical_not(self.behind(up)))
            def _(up=up, place=place, side=side):
                self.stage[side, step] = self.x[place]
                self.copy(up, step).start()

    def rest(self, step, near=None):
        for up in (True, False):
            place = self.count - 1 - step if up else step
            side = 0 if up else 1
            here = self.leaves(up, step) & self.behind(up)
            if near is not None:
                by_end = self.me == (1 if up else self.count - 2)
                here = here & (by_end if near else jnp.logical_not(by_end))

            @pl.when(here)
            def _(up=up, place=place, side=side):
                self.copy(up, step).wait_recv()
                total = self.x[place].astype(F32) + self.land[side, step].astype(F32)
                self.stage[side, step] = total.astype(self.stage.dtype)
                self.copy(up, step).start()

    def finish(self, out):
        out[...] = self.x[self.me].astype(F32)
        for up in (True, False):
            side = 0 if up else 1
            for step in range(self.count - 1):

                @pl.when(self.behind(up) & (self.me == (self.count - 1 - step if up else step)))
                def _(up=up, step=step, side=side):
                    self.copy(up, step).wait_recv()
                    out[...] += self.land[side, step].astype(F32)

        for up in (True, False):
            for step in range(self.count - 1):

                @pl.when(self.leaves(up, step))
                def _(up=up, step=step):
                    self.copy(up, step).wait_send()


class Job:
    def __init__(self, kind, groups, x, axis=0, late=False):
        self.late = late
        self.kind, self.groups, self.x, self.axis = kind, groups, x, axis
        count = groups[0].count
        rest = x.shape[:axis] + x.shape[axis + 1 :]
        dma = pltpu.SemaphoreType.DMA
        self.in_spec = pl.BlockSpec(memory_space=pl.ANY)
        self.out_spec = pl.BlockSpec(memory_space=pl.ANY)
        self.scratch = [dma((count - 1,)), dma((count - 1,)), dma]
        if kind in ("gather", "spread"):
            self.in_spec = pl.BlockSpec(memory_space=pltpu.VMEM)
        if kind == "gather" and groups[0].line:
            self.scratch = [dma((2 * count - 2,)), dma((2 * count - 2,)), dma]
        if kind == "gather":
            self.out = jax.ShapeDtypeStruct((count,) + x.shape, x.dtype)
        elif kind == "spread":
            self.out = jax.ShapeDtypeStruct((groups[1].count, count) + x.shape, x.dtype)
            copies = 7 if groups[0].square else count
            if groups[0].square:
                self.scratch = [dma((6,)), dma((6,)), dma]
            self.scratch += [dma((copies,)), dma((copies,))]
        elif kind == "deal":
            self.out = jax.ShapeDtypeStruct((count - 1,) + rest, x.dtype)
        else:
            self.out = jax.ShapeDtypeStruct(rest, F32)
            self.out_spec = pl.BlockSpec(memory_space=pltpu.VMEM)
            if groups[0].line:
                self.in_spec = pl.BlockSpec(memory_space=pltpu.VMEM)
                self.scratch = [dma((2, count - 1)), dma((2, count - 1)), dma]
                self.scratch += [pltpu.VMEM((2, count - 1) + rest, x.dtype)] * 2
            else:
                self.scratch += [
                    pltpu.VMEM(rest, x.dtype), pltpu.VMEM((count - 1,) + rest, x.dtype)
                ]

    def key(self):
        return (self.kind, tuple(g.axes for g in self.groups), self.x.shape, str(self.x.dtype), self.axis)

    def start(self, x, out, send_sem, recv_sem, own_sem, *more):
        group = self.groups[0]
        me = group.me()
        peers = list(enumerate(group.peers()))

        def block(place):
            return x.at[(slice(None),) * self.axis + (place,)]

        if self.kind == "gather" and group.line:
            line = LineRows(group, x, out, send_sem, recv_sem)
            line.start()
            own = pltpu.make_async_copy(x, out.at[me], own_sem)
            own.start()

            def finish():
                line.finish()
                own.wait()

        elif self.kind == "reduce" and group.line:
            line = LineSum(group, x, *more, send_sem, recv_sem)
            for step in range(group.count - 1):
                line.first(step)

            def finish():
                for step in range(group.count - 1):
                    line.rest(step)
                line.finish(out)

        elif self.kind == "gather":
            copies = [send(group, p, k, x, out.at[me], send_sem, recv_sem) for k, p in peers]
            own = pltpu.make_async_copy(x, out.at[me], own_sem)
            own.start()

            def finish():
                for copy in copies + [own]:
                    copy.wait()

        elif self.kind == "spread" and group.square:
            pair = self.groups[1]
            side = pair.me()
            fw_send, fw_recv = more
            size = self.x.shape[0] // 2
            near = [across(me, 0), across(me, 1)]

            def copy_of(number):
                at = pl.ds(SQUARE_HALF[number] * size, size)
                place = me if number < 4 else near[number - 4]
                dst = out.at[side, place, at]
                src = x.at[at] if number < 4 else dst
                copy = pltpu.make_async_remote_copy(
                    src_ref=src, dst_ref=dst, send_sem=send_sem.at[number],
                    recv_sem=recv_sem.at[number], device_id=group.device(near[SQUARE_STEP[number]]),
                    device_id_type=MESH,
                )
                origin = near[SQUARE_STEP[number]] if number < 4 else across(me, 2)
                return copy, out.at[side, origin, at]

            copies = [copy_of(number) for number in range(6)]
            for number in (0, 2, 1, 3):
                copies[number][0].start()
            passed = [send(pair, 1 - side, 6, x, out.at[side, me], fw_send, fw_recv)]
            own = pltpu.make_async_copy(x, out.at[side, me], own_sem)
            own.start()

            def arrived(number):
                copy, landed = copies[number]
                copy.wait_recv()
                passed.append(send(pair, 1 - side, number, landed, landed, fw_send, fw_recv))

            def finish():
                for number in (0, 2):
                    copies[number][0].wait_recv()
                    copies[4 + number // 2][0].start()
                    landed = copies[number][1]
                    passed.append(send(pair, 1 - side, number, landed, landed, fw_send, fw_recv))
                for number in (1, 3, 4, 5):
                    arrived(number)
                for copy in passed:
                    copy.wait()
                for copy, _ in copies:
                    copy.wait_send()
                own.wait()

        elif self.kind == "spread":
            pair = self.groups[1]
            side = pair.me()
            fw_send, fw_recv = more
            home = out.at[side, me]
            copies = [send(group, p, k, x, home, send_sem, recv_sem) for k, p in peers]
            last = group.count - 1
            passed = [send(pair, 1 - side, last, x, home, fw_send, fw_recv)]
            own = pltpu.make_async_copy(x, home, own_sem)
            own.start()

            def finish():
                for k, copy in enumerate(copies):
                    copy.wait_recv()
                    place = out.at[side, lax.rem(me + group.count - 1 - k, group.count)]
                    passed.append(send(pair, 1 - side, k, place, place, fw_send, fw_recv))
                for copy in passed:
                    copy.wait()
                for copy in copies:
                    copy.wait_send()
                own.wait()

        elif self.kind == "deal":
            copies = [send(group, p, k, block(p), out.at[k], send_sem, recv_sem) for k, p in peers]

            def finish():
                for copy in copies:
                    copy.wait()

        else:
            kept, slots = more
            copies = [send(group, p, k, block(p), slots.at[k], send_sem, recv_sem) for k, p in peers]
            own = pltpu.make_async_copy(block(me), kept, own_sem)
            own.start()

            def finish():
                own.wait()
                for copy in copies:
                    copy.wait()
                total = kept[...].astype(F32)
                for k in range(group.count - 1):
                    total = total + slots[k].astype(F32)
                out[...] = total

        return finish


def job_groups(jobs):
    return [group for job in jobs for group in job.groups]


def split_scratch(jobs, scratch):
    parts, at = [], 0
    for job in jobs:
        parts.append(scratch[at : at + len(job.scratch)])
        at += len(job.scratch)
    return parts


def exchange_body(jobs, *refs):
    count = len(jobs)
    greet(job_groups(jobs))
    parts = split_scratch(jobs, refs[2 * count :])
    ends = [
        job.start(refs[n], refs[count + n], *parts[n]) for n, job in enumerate(jobs)
    ]
    for end in ends:
        end()


class Exchanges:
    def __init__(self):
        self.idents = {}

    def ident(self, key):
        return self.idents.setdefault(key, len(self.idents))

    def __call__(self, *jobs):
        jobs = list(jobs)
        return pl.pallas_call(
            functools.partial(exchange_body, jobs),
            out_shape=tuple(job.out for job in jobs),
            in_specs=[job.in_spec for job in jobs],
            out_specs=tuple(job.out_spec for job in jobs),
            scratch_shapes=[one for job in jobs for one in job.scratch],
            compiler_params=pltpu.CompilerParams(
                collective_id=self.ident(tuple(job.key() for job in jobs)),
                has_side_effects=True,
                vmem_limit_bytes=32 * 2**20,
            ),
        )(*[job.x for job in jobs])


CHUNK = 512


def start_rows(group, x_ref, full, send_sem, recv_sem):
    me = group.me()
    full[me] = x_ref[...]
    return [
        send(group, peer, step, x_ref, full.at[me], send_sem, recv_sem)
        for step, peer in enumerate(group.peers())
    ]


def table_body(
    by_section, by_dp, by_tensor, jobs, g_ref, ids_ref, u_ref, gx_ref, *refs
):
    riders = len(jobs)
    xs, (out_ref, *outs), refs = refs[:riders], refs[riders : 2 * riders + 1], refs[2 * riders + 1 :]
    (g_buf, to_partner, from_partner, to_dp, from_dp, own, result,
    g_sem, ps_send, ps_recv, dp_send, dp_recv, ag_send, ag_recv, fw_send, fw_recv, own_sem,
    ) = refs[:17]
    gx_full, gx_send, gx_recv = refs[17:20]
    s, j = by_section.me(), by_dp.me()
    partner = 1 - s
    peers = by_dp.peers() + [j]
    count = by_dp.count
    block = own.shape[0]
    subs = block // CHUNK
    tokens = u_ref.shape[0]
    greet([by_section, by_dp, by_tensor] + job_groups(jobs))
    gx_copies = start_rows(by_tensor, gx_ref, gx_full, gx_send, gx_recv)
    parts = split_scratch(jobs, refs[20:])
    ends = [job.start(xs[n], outs[n], *parts[n]) for n, job in enumerate(jobs)]

    def chunk(half, place, sub):
        return (half * count + place) * subs + sub

    order = [(number, half) for number in range(count) for half in (0, 1)]

    def fetch(index, sub, slot):
        number, away = order[index]
        half = partner if away == 0 else s
        return pltpu.make_async_copy(
            g_ref.at[chunk(half, peers[number], sub)], g_buf.at[slot], g_sem.at[slot]
        )

    def remote(group, peer, number, sub, src, dst, send_sem, recv_sem):
        return pltpu.make_async_remote_copy(
            src_ref=src,
            dst_ref=dst,
            send_sem=send_sem.at[number, sub],
            recv_sem=recv_sem.at[number, sub],
            device_id=group.device(peer),
            device_id_type=MESH,
        )

    def rows(sub):
        return pl.ds(pl.multiple_of(sub * CHUNK, CHUNK), CHUNK)

    def partner_copy(number, sub):
        return remote(
            by_section, partner, number, sub,
            to_partner.at[number, rows(sub)], from_partner.at[number, rows(sub)],
            ps_send, ps_recv,
        )

    def chip_copy(number, sub):
        return remote(
            by_dp, peers[number], number, sub,
            to_dp.at[number, rows(sub)], from_dp.at[number, rows(sub)], dp_send, dp_recv,
        )

    def spread_copy(number, sub):
        return remote(
            by_dp, peers[number], number, sub,
            result.at[rows(sub)], out_ref.at[chunk(s, j, sub)], ag_send, ag_recv,
        )

    sources = [lax.rem(j + count - 1 - number, count) for number in range(count - 1)] + [j]

    def forward_copy(number, sub):
        target = out_ref.at[chunk(s, sources[number], sub)]
        origin = result.at[rows(sub)] if number == count - 1 else target
        return remote(by_section, partner, number, sub, origin, target, fw_send, fw_recv)

    def own_copy(sub):
        return pltpu.make_async_copy(
            result.at[rows(sub)], out_ref.at[chunk(s, j, sub)], own_sem.at[sub]
        )

    for copy in gx_copies:
        copy.wait()
    fetch(0, 0, 0).start()
    for index, (number, away) in enumerate(order):
        half = partner if away == 0 else s

        def one(sub, carry, index=index, number=number, away=away, half=half):
            slot = lax.rem(sub, 2)
            fetch(index, sub, slot).wait()

            @pl.when(sub + 1 < subs)
            def _():
                fetch(index, sub + 1, 1 - slot).start()

            if index + 1 < len(order):

                @pl.when(sub + 1 == subs)
                def _():
                    fetch(index + 1, 0, 1 - slot).start()

            base = chunk(half, peers[number], sub) * CHUNK
            place = base + lax.broadcasted_iota(jnp.int32, (CHUNK, tokens), 0)
            chosen = jnp.where(place == ids_ref[...], 1.0, 0.0).astype(BF16)
            term = outer_sum(g_buf[slot], u_ref[...]) + matmul(
                chosen, gx_full[...].reshape(tokens, gx_full.shape[2])
            )
            if away == 0:
                to_partner[number, rows(sub), :] = term.astype(BF16)
                partner_copy(number, sub).start()
            else:
                partner_copy(number, sub).wait_recv()
                term = term + from_partner[number, rows(sub), :].astype(F32)
                if number < count - 1:
                    to_dp[number, rows(sub), :] = term.astype(BF16)
                    chip_copy(number, sub).start()
                else:
                    own[rows(sub), :] = term
            return carry

        lax.fori_loop(0, subs, one, 0)

    def finish(sub, carry):
        term = own[rows(sub), :]
        for number in range(count - 1):
            chip_copy(number, sub).wait_recv()
            term = term + from_dp[number, rows(sub), :].astype(F32)
        result[rows(sub), :] = term.astype(BF16)
        for number in range(count - 1):
            spread_copy(number, sub).start()
        forward_copy(count - 1, sub).start()
        own_copy(sub).start()
        return carry

    lax.fori_loop(0, subs, finish, 0)

    def take(sub, carry):
        for number in range(count - 1):
            spread_copy(number, sub).wait_recv()
            forward_copy(number, sub).start()
        return carry

    lax.fori_loop(0, subs, take, 0)

    def drain(sub, carry):
        own_copy(sub).wait()
        for number in range(count):
            partner_copy(number, sub).wait_send()
            forward_copy(number, sub).wait()
        for number in range(count - 1):
            chip_copy(number, sub).wait_send()
            spread_copy(number, sub).wait_send()
        return carry

    lax.fori_loop(0, subs, drain, 0)
    for end in ends:
        end()


def across(me, step):
    bits = jnp.int32(step + 1)
    x, y = lax.rem(me, 2), lax.div(me, 2)
    return 2 * lax.rem(y + lax.div(bits, 2), 2) + lax.rem(x + lax.rem(bits, 2), 2)


SQUARE_HALF = (0, 1, 1, 0, 0, 1)
SQUARE_STEP = (0, 0, 1, 1, 1, 0)


def table_square_body(by_section, by_dp, by_tensor, jobs, g_ref, ids_ref, u_ref, gx_ref, *refs):
    riders = len(jobs)
    xs, (out_ref, *outs), refs = refs[:riders], refs[riders : 2 * riders + 1], refs[2 * riders + 1 :]
    (
        g_buf, to_partner, from_partner, to_dp, hop_land, from_dp, own, result,
        g_sem, ps_send, ps_recv, hop_send, hop_recv, dp_send, dp_recv, ag_send, ag_recv,
        fw_send, fw_recv, own_sem,
    ) = refs[:20]
    gx_full, gx_send, gx_recv = refs[20:23]
    s, j = by_section.me(), by_dp.me()
    partner = 1 - s
    near_x, near_y, far = (across(j, step) for step in range(3))
    peers = [far, near_y, near_x, j]
    count = 4
    block = own.shape[0]
    subs = block // CHUNK
    half_rows = CHUNK // 2
    tokens = u_ref.shape[0]
    greet([by_section, by_dp, by_tensor] + job_groups(jobs))
    line = LineRows(by_tensor, gx_ref, gx_full, gx_send, gx_recv)
    line.start()
    gx_full[line.me] = gx_ref[...]
    parts = split_scratch(jobs, refs[23:])
    ends = [
        job.start(xs[n], outs[n], *parts[n]) for n, job in enumerate(jobs) if not job.late
    ]

    def chunk(half, place, sub):
        return (half * count + place) * subs + sub

    order = [(number, away) for number in range(count) for away in (0, 1)]

    def fetch(index, sub, slot):
        number, away = order[index]
        half = partner if away == 0 else s
        return pltpu.make_async_copy(
            g_ref.at[chunk(half, peers[number], sub)], g_buf.at[slot], g_sem.at[slot]
        )

    def remote(group, peer, number, sub, src, dst, send_sem, recv_sem):
        return pltpu.make_async_remote_copy(
            src_ref=src,
            dst_ref=dst,
            send_sem=send_sem.at[number, sub],
            recv_sem=recv_sem.at[number, sub],
            device_id=group.device(peer),
            device_id_type=MESH,
        )

    def rows(sub):
        return pl.ds(pl.multiple_of(sub * CHUNK, CHUNK), CHUNK)

    def half_of(sub, which):
        return pl.ds(pl.multiple_of(sub * CHUNK + which * half_rows, half_rows), half_rows)

    def partner_copy(number, sub):
        return remote(
            by_section, partner, number, sub,
            to_partner.at[number, rows(sub)], from_partner.at[number, rows(sub)],
            ps_send, ps_recv,
        )

    def hop_copy(which, sub):
        return remote(
            by_dp, (near_x, near_y)[which], which, sub,
            to_dp.at[0, half_of(sub, which)], hop_land.at[half_of(sub, which)], hop_send, hop_recv,
        )

    def chip_copy(number, sub):
        return remote(
            by_dp, (near_y, near_x)[number], number, sub,
            to_dp.at[number + 1, rows(sub)], from_dp.at[number, rows(sub)], dp_send, dp_recv,
        )

    def spread_copy(number, sub):
        which = SQUARE_HALF[number]
        place = j if number < 4 else (near_x, near_y)[number - 4]
        dst = out_ref.at[chunk(s, place, sub), pl.ds(which * half_rows, half_rows)]
        src = result.at[half_of(sub, which)] if number < 4 else dst
        peer = (near_x, near_y)[SQUARE_STEP[number]]
        return remote(by_dp, peer, number, sub, src, dst, ag_send, ag_recv)

    sources = [near_x, near_y, far, j]

    def forward_copy(number, sub):
        target = out_ref.at[chunk(s, sources[number], sub)]
        origin = result.at[rows(sub)] if number == count - 1 else target
        return remote(by_section, partner, number, sub, origin, target, fw_send, fw_recv)

    def own_copy(sub):
        return pltpu.make_async_copy(
            result.at[rows(sub)], out_ref.at[chunk(s, j, sub)], own_sem.at[sub]
        )

    def slot_of(number, away):
        if away == 0:
            return to_partner.at[number]
        return to_dp.at[number] if number < 3 else own

    fetch(0, 0, 0).start()
    stops = {(step * len(order)) // line.count: step for step in range(1, line.count - 1)}
    for index, (number, away) in enumerate(order):
        if index in stops:
            line.step(stops[index])

        def share(sub, carry, index=index, number=number, away=away):
            slot = lax.rem(sub, 2)
            fetch(index, sub, slot).wait()

            @pl.when(sub + 1 < subs)
            def _():
                fetch(index, sub + 1, 1 - slot).start()

            if index + 1 < len(order):

                @pl.when(sub + 1 == subs)
                def _():
                    fetch(index + 1, 0, 1 - slot).start()

            held = slot_of(number, away)
            held[rows(sub), :] = outer_sum(g_buf[slot], u_ref[...]).astype(held.dtype)
            return carry

        lax.fori_loop(0, subs, share, 0)
    for end in ends:
        end()
    line.step(line.count - 1)
    line.wait_sends()
    ends = [job.start(xs[n], outs[n], *parts[n]) for n, job in enumerate(jobs) if job.late]

    for index, (number, away) in enumerate(order):
        half = partner if away == 0 else s

        def one(sub, carry, number=number, away=away, half=half):
            base = chunk(half, peers[number], sub) * CHUNK
            place = base + lax.broadcasted_iota(jnp.int32, (CHUNK, tokens), 0)
            chosen = jnp.where(place == ids_ref[...], 1.0, 0.0).astype(BF16)
            term = matmul(chosen, gx_full[...].reshape(tokens, gx_full.shape[2]))
            term = term + slot_of(number, away)[rows(sub), :].astype(F32)
            if away == 0:
                to_partner[number, rows(sub), :] = term.astype(BF16)
                partner_copy(number, sub).start()
                return carry
            partner_copy(number, sub).wait_recv()
            term = term + from_partner[number, rows(sub), :].astype(F32)
            if number == 0:
                to_dp[0, rows(sub), :] = term.astype(BF16)
                for which in range(2):
                    hop_copy(which, sub).start()
            elif number < 3:
                which = number - 1
                hop_copy(which, sub).wait_recv()
                mine = slice(which * half_rows, (which + 1) * half_rows)
                rest = slice((1 - which) * half_rows, (2 - which) * half_rows)
                to_dp[number, half_of(sub, which), :] = (
                    term[mine] + hop_land[half_of(sub, which), :].astype(F32)
                ).astype(BF16)
                to_dp[number, half_of(sub, 1 - which), :] = term[rest].astype(BF16)
                chip_copy(which, sub).start()
            else:
                own[rows(sub), :] = term
            return carry

        lax.fori_loop(0, subs, one, 0)

    def finish(sub, carry):
        term = own[rows(sub), :]
        for number in range(2):
            chip_copy(number, sub).wait_recv()
            term = term + from_dp[number, rows(sub), :].astype(F32)
        result[rows(sub), :] = term.astype(BF16)
        for number in (0, 2, 1, 3):
            spread_copy(number, sub).start()
        forward_copy(count - 1, sub).start()
        own_copy(sub).start()
        return carry

    lax.fori_loop(0, subs, finish, 0)

    def pass_on(sub, carry):
        for number in (0, 2):
            spread_copy(number, sub).wait_recv()
            spread_copy(4 + number // 2, sub).start()
        for number in (0, 1):
            spread_copy(2 * number + 1, sub).wait_recv()
            forward_copy(number, sub).start()
        return carry

    lax.fori_loop(0, subs, pass_on, 0)

    def last(sub, carry):
        for number in (4, 5):
            spread_copy(number, sub).wait_recv()
        forward_copy(2, sub).start()
        return carry

    lax.fori_loop(0, subs, last, 0)

    def drain(sub, carry):
        own_copy(sub).wait()
        for number in range(count):
            partner_copy(number, sub).wait_send()
            forward_copy(number, sub).wait()
        for number in range(2):
            hop_copy(number, sub).wait_send()
            chip_copy(number, sub).wait_send()
        for number in range(6):
            spread_copy(number, sub).wait_send()
        return carry

    lax.fori_loop(0, subs, drain, 0)
    for end in ends:
        end()


def table_sum(by_section, by_dp, by_tensor, jobs, grads, ids, final, grad_rows, ident):
    chunks, tokens, _ = grads.shape
    width = final.shape[1]
    count = by_dp.count
    subs = chunks // (2 * count)
    block = subs * CHUNK
    assert subs % 2 == 0
    dma = pltpu.SemaphoreType.DMA
    low = functools.partial(pltpu.VMEM, dtype=BF16)
    square = by_dp.square
    scratch = [
        low((2, tokens, CHUNK)),
        low((count, block, width)),
        low((count, block, width)),
        low((count - 1, block, width)),
    ]
    scratch += [low((block, width)), low((2, block, width))] if square else [
        low((count - 1, block, width))
    ]
    scratch += [pltpu.VMEM((block, width), F32), low((block, width)), dma((2,))]
    copies = (count, 2, 2, 6, count) if square else (count, count - 1, count - 1, count)
    scratch += [dma((copy, subs)) for copy in copies for _ in range(2)] + [dma((subs,))]
    scratch += [low((by_tensor.count,) + grad_rows.shape)]
    scratch += [dma(((by_tensor.count - 1) * (2 if square else 1),))] * 2
    vmem = pl.BlockSpec(memory_space=pltpu.VMEM)
    hbm = pl.BlockSpec(memory_space=pl.ANY)
    return pl.pallas_call(
        functools.partial(
            table_square_body if by_dp.square else table_body, by_section, by_dp, by_tensor, jobs
        ),
        out_shape=(jax.ShapeDtypeStruct((chunks, CHUNK, width), BF16),)
        + tuple(job.out for job in jobs),
        in_specs=[hbm, vmem, vmem, vmem] + [job.in_spec for job in jobs],
        out_specs=(hbm,) + tuple(job.out_spec for job in jobs),
        scratch_shapes=scratch + [one for job in jobs for one in job.scratch],
        compiler_params=pltpu.CompilerParams(
            collective_id=ident, has_side_effects=True, vmem_limit_bytes=56 * 2**20
        ),
    )(grads, ids, final, grad_rows, *[job.x for job in jobs])


LANES = 128


def head_logits_body(u_ref, e_ref, ids_ref, logits_ref, top_ref, total_ref, pick_ref):
    step = pl.program_id(0)
    tokens, tile = logits_ref.shape[1:]

    @pl.when(step == 0)
    def _():
        top_ref[...] = jnp.full_like(top_ref, NEG)
        total_ref[...] = jnp.zeros_like(total_ref)
        pick_ref[...] = jnp.zeros_like(pick_ref)

    logits = matmul_t(u_ref[...], e_ref[...])
    logits_ref[0] = logits
    place = step * tile + lax.broadcasted_iota(jnp.int32, (tokens, tile), 1)
    picked = jnp.where(place == ids_ref[...], logits, 0.0)
    pieces = [logits[:, at : at + LANES] for at in range(0, tile, LANES)]
    before = top_ref[...]
    top = functools.reduce(jnp.maximum, pieces, before)
    total = total_ref[...] * jnp.exp(before - top)
    pick = pick_ref[...]
    for number, piece in enumerate(pieces):
        total = total + jnp.exp(piece - top)
        pick = pick + picked[:, number * LANES : (number + 1) * LANES]
    top_ref[...] = top
    total_ref[...] = total
    pick_ref[...] = pick


def head_logits(final, embedding, ids):
    tokens, width = final.shape
    vocab = embedding.shape[0]
    fixed = pl.BlockSpec((tokens, LANES), lambda step: (0, 0))
    stat = jax.ShapeDtypeStruct((tokens, LANES), F32)
    return pl.pallas_call(
        head_logits_body,
        grid=(vocab // CHUNK,),
        out_shape=(
            jax.ShapeDtypeStruct((vocab // CHUNK, tokens, CHUNK), F32), stat, stat, stat
        ),
        in_specs=[
            pl.BlockSpec((tokens, width), lambda step: (0, 0)),
            pl.BlockSpec((CHUNK, width), lambda step: (step, 0)),
            pl.BlockSpec((tokens, 1), lambda step: (0, 0)),
        ],
        out_specs=(
            pl.BlockSpec((1, tokens, CHUNK), lambda step: (step, 0, 0)), fixed, fixed, fixed
        ),
        compiler_params=pltpu.CompilerParams(vmem_limit_bytes=40 * 2**20),
        cost_estimate=pl.CostEstimate(
            flops=2 * tokens * vocab * width,
            bytes_accessed=4 * tokens * vocab + 2 * vocab * width,
            transcendentals=tokens * vocab,
        ),
    )(final, embedding, ids)


def head_grads_body(logits_ref, e_ref, ids_ref, norm_ref, weight_ref, grads_ref, back_ref, acc):
    step = pl.program_id(0)
    tokens, tile = grads_ref.shape[1:]

    @pl.when(step == 0)
    def _():
        acc[...] = jnp.zeros_like(acc)

    place = step * tile + lax.broadcasted_iota(jnp.int32, (tokens, tile), 1)
    probs = jnp.exp(logits_ref[0] - norm_ref[...])
    grads = (jnp.where(place == ids_ref[...], probs - 1.0, probs) * weight_ref[...]).astype(BF16)
    grads_ref[0] = grads
    acc[...] += matmul(grads, e_ref[...])

    @pl.when(step == pl.num_programs(0) - 1)
    def _():
        back_ref[...] = acc[...].astype(BF16)


def head_grads(logits, embedding, ids, norm, weight):
    chunks, tokens, _ = logits.shape
    vocab, width = embedding.shape
    column = pl.BlockSpec((tokens, 1), lambda step: (0, 0))
    tile = pl.BlockSpec((1, tokens, CHUNK), lambda step: (step, 0, 0))
    return pl.pallas_call(
        head_grads_body,
        grid=(chunks,),
        out_shape=(
            jax.ShapeDtypeStruct(logits.shape, BF16),
            jax.ShapeDtypeStruct((tokens, width), BF16),
        ),
        in_specs=[
            tile, pl.BlockSpec((CHUNK, width), lambda step: (step, 0)), column, column, column
        ],
        out_specs=(tile, pl.BlockSpec((tokens, width), lambda step: (0, 0))),
        scratch_shapes=[pltpu.VMEM((tokens, width), F32)],
        compiler_params=pltpu.CompilerParams(vmem_limit_bytes=40 * 2**20),
        cost_estimate=pl.CostEstimate(
            flops=2 * tokens * vocab * width,
            bytes_accessed=6 * tokens * vocab + 2 * vocab * width,
            transcendentals=tokens * vocab,
        ),
    )(logits, embedding, ids, norm, weight)


BLOCK = 256


def masked_scores(queries, keys, slope, length, first):
    rows, cols = queries.shape[0], keys.shape[0]
    raw = matmul_t(queries, keys)
    i = first + lax.broadcasted_iota(jnp.int32, (rows, cols), 0)
    j = lax.broadcasted_iota(jnp.int32, (rows, cols), 1)
    scores = raw * HEAD_DIM ** (-0.5) - slope * (i - j).astype(F32)
    return jnp.where((j <= i) & (j < length), scores, NEG)


SMEM = pl.BlockSpec(memory_space=pltpu.SMEM)
VMEM = pl.BlockSpec(memory_space=pltpu.VMEM)


class TeamRows:
    def __init__(self, team, x_ref, full, stage, slots, own, ag_send, ag_recv, rs_send, rs_recv):
        self.team, self.count, self.me = team, team.count, team.me()
        self.x_ref, self.full, self.stage, self.slots, self.own = x_ref, full, stage, slots, own
        self.ag_sems, self.rs_sems = (ag_send, ag_recv), (rs_send, rs_recv)

    def shifted(self, step):
        return across(self.me, step)

    def peer(self, step):
        if self.team.square:
            return self.shifted(step)
        return lax.rem(self.me + 1 + step, self.count)

    def source(self, step):
        if self.team.square:
            return self.shifted(step)
        return lax.rem(self.me + self.count - 1 - step, self.count)

    def back_step(self, place):
        if self.team.square:
            flip_x = lax.rem(lax.rem(self.me, 2) + lax.rem(place, 2), 2)
            flip_y = lax.rem(lax.div(self.me, 2) + lax.div(place, 2), 2)
            return 2 * flip_y + flip_x - 1
        return lax.rem(place + self.count - 1 - self.me, self.count)

    def remote(self, number, peer, src, dst, sems):
        return pltpu.make_async_remote_copy(
            src_ref=src,
            dst_ref=dst,
            send_sem=sems[0].at[number],
            recv_sem=sems[1].at[number],
            device_id=self.team.device(peer),
            device_id_type=MESH,
        )

    def ag(self, number):
        if not self.team.square:
            return self.remote(
                number, self.peer(number), self.x_ref, self.full.at[self.me], self.ag_sems
            )
        half = self.x_ref.shape[0] // 2
        which = SQUARE_HALF[number]
        rows = pl.ds(which * half, half)
        peer = self.shifted(SQUARE_STEP[number])
        if number < 4:
            src, place = self.x_ref.at[rows], self.me
        else:
            place = self.shifted(number - 4)
            src = self.full.at[place, rows]
        return self.remote(number, peer, src, self.full.at[place, rows], self.ag_sems)

    def rs(self, step):
        return self.remote(
            step, self.peer(step), self.stage.at[self.peer(step)], self.slots.at[step], self.rs_sems
        )

    def send_rows(self):
        for number in (0, 2, 1, 3) if self.team.square else range(self.count - 1):
            self.ag(number).start()
        self.full[self.me] = self.x_ref[...]

    def pass_on(self):
        if self.team.square:
            for number in (0, 2):
                self.ag(number).wait_recv()
                self.ag(4 + number // 2).start()

    def wait_rows(self, step):
        if not self.team.square:
            self.ag(step).wait_recv()
            return
        for number, these in enumerate(((1,), (3,), (4, 5))):

            @pl.when(step == number)
            def _(these=these):
                for one in these:
                    self.ag(one).wait_recv()

    def each_arrival(self, work):
        work(self.me)
        self.pass_on()

        def one(step, carry):
            self.wait_rows(step)
            work(self.source(step))
            return carry

        lax.fori_loop(0, self.count - 1, one, 0)

    def each_arrival_and_back(self, term):
        self.own[...] = term(self.me)
        self.pass_on()

        def one(step, carry):
            self.wait_rows(step)
            place = self.source(step)
            self.stage[place] = term(place).astype(BF16)
            self.rs(self.back_step(place)).start()
            return carry

        lax.fori_loop(0, self.count - 1, one, 0)

    def finish(self, total_ref):
        for end in self.ends:
            end()
        for step in range(self.count - 1):
            self.rs(step).wait()
        total = self.own[...]
        for step in range(self.count - 1):
            total = total + self.slots[step].astype(F32)
        total_ref[...] = total
        for number in range(6 if self.team.square else self.count - 1):
            self.ag(number).wait_send()


def team_scratch(team, part, model):
    count = team.count
    dma = pltpu.SemaphoreType.DMA
    copies = 6 if team.square else count - 1
    return [
        pltpu.VMEM((count, part, model), BF16),
        pltpu.VMEM((count, part, model), BF16),
        pltpu.VMEM((count - 1, part, model), BF16),
        pltpu.VMEM((part, model), F32),
        dma((copies,)),
        dma((copies,)),
        dma((count - 1,)),
        dma((count - 1,)),
    ]


class LateDeal:
    def __init__(self, pair, landing, send_sem, recv_sem):
        self.pair, self.landing, self.sems = pair, landing, (send_sem, recv_sem)

    def other(self):
        return 1 - self.pair.me()

    def start(self, src):
        self.copy = send(self.pair, self.other(), 0, src, self.landing, *self.sems)

    def wait(self):
        self.copy.wait()


def team_call(body, team, ident, jobs, arrays, specs, outs, out_specs, scratch, pair=None, dealt=None, ahead=0):
    if pair is not None:
        outs, out_specs = tuple(outs) + (dealt,), tuple(out_specs) + (HBM,)
        scratch = list(scratch) + [pltpu.SemaphoreType.DMA((1,))] * 2
    part, model = arrays[0].shape
    count_in, count_out, riders = len(arrays), len(outs), len(jobs)
    own_scratch = team_scratch(team, part, model)

    def kernel(*refs):
        ins, refs = refs[:count_in], refs[count_in:]
        xs, refs = refs[:riders], refs[riders:]
        results, refs = refs[:count_out], refs[count_out:]
        landings, refs = refs[:riders], refs[riders:]
        rows = TeamRows(team, ins[0], *refs[: len(own_scratch)])
        refs = refs[len(own_scratch) :]
        mine, refs = refs[: len(scratch)], refs[len(scratch) :]
        greet([team] + job_groups(jobs) + ([] if pair is None else [pair]))
        rows.send_rows()
        parts = split_scratch(jobs, refs)

        def start(numbers):
            return [jobs[n].start(xs[n], landings[n], *parts[n]) for n in numbers]

        rows.landings = landings
        first = start(range(ahead if ahead else riders))
        if ahead:

            def ready():
                for end in first:
                    end()
                rows.ends = start(range(ahead, riders))

            rows.ready = ready
        else:
            rows.ends = first
        if pair is None:
            body(rows, ins, results, mine)
        else:
            body(rows, ins, results[:-1], mine[:-2], LateDeal(pair, results[-1], *mine[-2:]))

    out = pl.pallas_call(
        kernel,
        out_shape=tuple(outs) + tuple(job.out for job in jobs),
        in_specs=list(specs) + [job.in_spec for job in jobs],
        out_specs=tuple(out_specs) + tuple(job.out_spec for job in jobs),
        scratch_shapes=own_scratch + list(scratch) + [one for job in jobs for one in job.scratch],
        compiler_params=pltpu.CompilerParams(
            collective_id=ident, has_side_effects=True, vmem_limit_bytes=58 * 2**20
        ),
    )(*arrays, *[job.x for job in jobs])
    return out[:count_out], list(out[count_out:])


def part_rows(place, part):
    return pl.ds(pl.multiple_of(place * part, part), part)


def attend_body(rows, ins, outs, scratch):
    x_ref, length_ref, slope_ref, bias_ref, *weights = ins
    total_ref, full_out, q_ref, k_ref, v_ref, mixed_ref, lse_ref = outs
    full_sem, *buffers = scratch
    if not weights:
        *weights, sems = buffers
        rows.ready()
        copies = [
            pltpu.make_async_copy(rows.landings[n], weights[n], sems.at[n]) for n in range(2)
        ]
        for copy in copies:
            copy.start()
        for copy in copies:
            copy.wait()
    qk_ref, vo_ref = weights

    def weight(ref, n):
        block = ref[n]
        return block.reshape(-1, block.shape[-1])

    part = x_ref.shape[0]
    width = q_ref.shape[1]

    def project(place):
        at = part_rows(place, part)
        block = rows.full[place]
        q_ref[at, :] = (matmul_t(block, weight(qk_ref, 0)) + bias_ref[0:1, :]).astype(BF16)
        k_ref[at, :] = matmul_t(block, weight(qk_ref, 1)).astype(BF16)
        v_ref[at, :] = (matmul_t(block, weight(vo_ref, 0)) + bias_ref[1:2, :]).astype(BF16)

    rows.each_arrival(project)
    keep = pltpu.make_async_copy(rows.full, full_out, full_sem)
    keep.start()

    def one(turn, carry):
        step = lax.rem(2 * rows.count - 2 - turn, rows.count)
        place = rows.peer(step)
        for block in range(rows.count):

            @pl.when(place == block)
            def _(first=block * part, upto=(block + 1) * part):
                for head in range(width // HEAD_DIM):
                    lanes = slice(head * HEAD_DIM, (head + 1) * HEAD_DIM)
                    scores = masked_scores(
                        q_ref[first:upto, lanes], k_ref[:upto, lanes], slope_ref[head],
                        length_ref[0], first,
                    )
                    highest = jnp.max(scores, axis=-1, keepdims=True)
                    powers = jnp.exp(scores - highest)
                    total = jnp.sum(powers, axis=-1, keepdims=True)
                    probs = (powers * (1.0 / total)).astype(BF16)
                    mixed_ref[first:upto, lanes] = matmul(probs, v_ref[:upto, lanes]).astype(BF16)
                    lse_ref[head, first:upto, :] = highest + jnp.log(total)

        term = matmul(mixed_ref[part_rows(place, part), :], weight(vo_ref, 1))

        @pl.when(step < rows.count - 1)
        def _():
            rows.stage[place] = term.astype(BF16)
            rows.rs(step).start()

        @pl.when(step == rows.count - 1)
        def _():
            rows.own[...] = term

        return carry

    lax.fori_loop(0, rows.count, one, 0)
    rows.finish(total_ref)
    keep.wait()


HBM = pl.BlockSpec(memory_space=pl.ANY)


def attend(team, ident, jobs, x, length, slopes, bias, weights):
    part, model = x.shape
    seq = part * team.count
    width = bias.shape[1]
    scratch = [pltpu.SemaphoreType.DMA]
    if not weights:
        scratch += [pltpu.VMEM(job.out.shape, BF16) for job in jobs[:2]]
        scratch.append(pltpu.SemaphoreType.DMA((2,)))
    low = jax.ShapeDtypeStruct((seq, width), BF16)
    return team_call(
        attend_body, team, ident, jobs,
        [x, length, slopes, bias] + weights,
        [VMEM, SMEM, SMEM, VMEM] + [VMEM] * len(weights),
        (
            jax.ShapeDtypeStruct((part, model), F32),
            jax.ShapeDtypeStruct((team.count, part, model), BF16),
            low, low, low, low,
            jax.ShapeDtypeStruct((width // HEAD_DIM, seq, 1), F32),
        ),
        (VMEM, HBM, VMEM, VMEM, VMEM, VMEM, VMEM),
        scratch,
        ahead=0 if weights else 2,
    )


def attend_back_body(rows, ins, outs, scratch, late=None):
    gy_ref, length_ref, slope_ref, a_ref, qk_ref, vo_ref, q_ref, k_ref, v_ref, mixed_ref, lse_ref = ins
    total_ref, grads_ref, sums_ref = outs
    go, gq, gk, gv, gk_sum, gv_sum = scratch
    part = gy_ref.shape[0]
    seq, width = q_ref.shape
    heads = width // HEAD_DIM
    gk_sum[...] = jnp.zeros_like(gk_sum)
    gv_sum[...] = jnp.zeros_like(gv_sum)
    sums_ref[...] = jnp.zeros_like(sums_ref)

    def open_block(place):
        go[part_rows(place, part), :] = matmul_t(rows.full[place], vo_ref[1]).astype(BF16)

    rows.each_arrival(open_block)
    for block in reversed(range(rows.count)):
        first, upto = block * part, (block + 1) * part
        for head in range(heads):
            lanes = slice(head * HEAD_DIM, (head + 1) * HEAD_DIM)
            queries, grads = q_ref[first:upto, lanes], go[first:upto, lanes]
            keys, values = k_ref[:upto, lanes], v_ref[:upto, lanes]
            scores = masked_scores(queries, keys, slope_ref[head], length_ref[0], first)
            probs = jnp.exp(scores - lse_ref[head, first:upto, :])
            grad_probs = matmul_t(grads, values)
            inner = jnp.sum(probs * grad_probs, axis=-1, keepdims=True)
            grad_scores = (probs * (grad_probs - inner) * HEAD_DIM ** (-0.5)).astype(BF16)
            piece = matmul(grad_scores, keys)
            sums_ref[0:1, lanes] += jnp.sum(piece, axis=0, keepdims=True)
            gq[first:upto, lanes] = piece.astype(BF16)
            gk_sum[:upto, lanes] += outer_sum(grad_scores, queries)
            gv_sum[:upto, lanes] += outer_sum(probs.astype(BF16), grads)
        gk[first:upto, :] = gk_sum[first:upto, :].astype(BF16)
        gv[first:upto, :] = gv_sum[first:upto, :].astype(BF16)
        term = (
            matmul(gq[first:upto, :], qk_ref[0]) + matmul(gk[first:upto, :], qk_ref[1])
            + matmul(gv[first:upto, :], vo_ref[0])
        )

        @pl.when(rows.me != block)
        def _(block=block, term=term):
            rows.stage[block] = term.astype(BF16)
            rows.rs(rows.back_step(block)).start()

        @pl.when(rows.me == block)
        def _(term=term):
            rows.own[...] = term

    sums_ref[1:2, :] = jnp.sum(gv_sum[...], axis=0, keepdims=True)
    model = gy_ref.shape[1]
    grads_ref[3] = outer_sum(mixed_ref[...], rows.full[...].reshape(seq, model))
    grads_ref[0] = outer_sum(gq[...], a_ref[...])
    grads_ref[1] = outer_sum(gv[...], a_ref[...])
    grads_ref[2] = outer_sum(gk[...], a_ref[...])
    if late is not None:
        late.start(grads_ref.at[pl.ds(2 * late.other(), 2)])
    rows.finish(total_ref)
    if late is not None:
        late.wait()


def attend_back(team, ident, jobs, pair, gy, length, slopes, a, qk, vo, q, k, v, mixed, lse):
    part, model = gy.shape
    seq, width = q.shape
    return team_call(
        attend_back_body, team, ident, jobs,
        [gy, length, slopes, a, qk, vo, q, k, v, mixed, lse],
        [VMEM, SMEM, SMEM] + [VMEM] * 8,
        (
            jax.ShapeDtypeStruct((part, model), F32),
            jax.ShapeDtypeStruct((4, width, model), F32),
            jax.ShapeDtypeStruct((2, width), F32),
        ),
        (VMEM,) * 3,
        [pltpu.VMEM((seq, width), BF16)] * 4 + [pltpu.VMEM((seq, width), F32)] * 2,
        pair,
        jax.ShapeDtypeStruct((2, width, model), F32),
    )


GELU_A = 0.7978845608028654
GELU_B = 0.044715


def strip_rows(strips, which, first, size):
    length = strips[0].shape[1]
    return strips[first // length][which, first % length : first % length + size, :]


def feed_body(rows, ins, outs, scratch):
    x_ref, bias_ref, *strips = ins
    total_ref, full_out, before_ref = outs
    (full_sem,) = scratch
    part = x_ref.shape[0]
    units = bias_ref.shape[1]
    tile = min(units, BLOCK)

    def term(place):
        at = part_rows(place, part)
        block = rows.full[place]
        total = None
        for first in range(0, units, tile):
            lanes = slice(first, first + tile)
            before = matmul_t(block, strip_rows(strips, 0, first, tile)) + bias_ref[:, lanes]
            before_ref[at, lanes] = before
            bend = jnp.tanh(GELU_A * (before + GELU_B * before * before * before))
            active = (0.5 * before * (1.0 + bend)).astype(BF16)
            piece = matmul(active, strip_rows(strips, 1, first, tile))
            total = piece if total is None else total + piece
        return total

    rows.each_arrival_and_back(term)
    keep = pltpu.make_async_copy(rows.full, full_out, full_sem)
    keep.start()
    rows.finish(total_ref)
    keep.wait()


def feed(team, ident, jobs, x, strips, bias):
    part, model = x.shape
    units = bias.shape[1]
    return team_call(
        feed_body, team, ident, jobs,
        [x, bias] + strips,
        [VMEM] * (2 + len(strips)),
        (
            jax.ShapeDtypeStruct((part, model), F32),
            jax.ShapeDtypeStruct((team.count, part, model), BF16),
            jax.ShapeDtypeStruct((part * team.count, units), F32),
        ),
        (VMEM, HBM, VMEM),
        [pltpu.SemaphoreType.DMA],
    )


def feed_back_body(rows, ins, outs, scratch, late=None):
    gz_ref, c_ref, before_ref, *strips = ins
    total_ref, grads_ref, sums_ref = outs
    active, low = scratch
    part, model = gz_ref.shape
    seq = part * rows.count
    units = before_ref.shape[1]
    tile = min(units, BLOCK)
    sums_ref[...] = jnp.zeros_like(sums_ref)

    def term(place):
        at = part_rows(place, part)
        gz = rows.full[place]
        for first in range(0, units, tile):
            lanes = slice(first, first + tile)
            before = before_ref[at, lanes]
            square = before * before
            bend = jnp.tanh(GELU_A * before * (1.0 + GELU_B * square))
            half = 0.5 * (1.0 + bend)
            slope = half + 0.5 * before * (1.0 - bend * bend) * (
                GELU_A * (1.0 + 3.0 * GELU_B * square)
            )
            grad = matmul_t(gz, strip_rows(strips, 1, first, tile)) * slope
            sums_ref[:, lanes] += jnp.sum(grad, axis=0, keepdims=True)
            active[at, lanes] = (before * half).astype(BF16)
            low[at, lanes] = grad.astype(BF16)
        length = strips[0].shape[1]
        return sum(
            matmul(low[at, n * length : (n + 1) * length], strip[0])
            for n, strip in enumerate(strips)
        )

    rows.each_arrival_and_back(term)
    for first in range(0, units, tile):
        lanes = slice(first, first + tile)
        grads_ref[0, lanes, :] = outer_sum(low[:, lanes], c_ref[...])
        grads_ref[1, lanes, :] = outer_sum(active[:, lanes], rows.full[...].reshape(seq, model))
    if late is not None:
        late.start(grads_ref.at[late.other()])
    rows.finish(total_ref)
    if late is not None:
        late.wait()


def feed_back(team, ident, jobs, pair, gz, c, before, strips):
    part, model = gz.shape
    seq = part * team.count
    units = before.shape[1]
    return team_call(
        feed_back_body, team, ident, jobs,
        [gz, c, before] + strips,
        [VMEM] * (3 + len(strips)),
        (
            jax.ShapeDtypeStruct((part, model), F32),
            jax.ShapeDtypeStruct((2, units, model), F32),
            jax.ShapeDtypeStruct((1, units), F32),
        ),
        (VMEM,) * 3,
        [pltpu.VMEM((seq, units), BF16)] * 2,
        pair,
        jax.ShapeDtypeStruct((units, model), F32),
    )


def line_head_logits_body(
    group, x_ref, e_ref, ids_ref, logits_ref, full_out, stats_out,
    full, table, staged, top, total, pick, stats,
    ag_send, ag_recv, e_sem, out_sem, full_sem, st_send, st_recv,
):
    count, me = group.count, group.me()
    part = x_ref.shape[0]
    tiles = e_ref.shape[0] // CHUNK
    line = LineRows(group, x_ref, full, ag_send, ag_recv)
    greet([group])
    line.start()
    full[me] = x_ref[...]
    top[...] = jnp.full_like(top, NEG)
    total[...] = jnp.zeros_like(total)
    pick[...] = jnp.zeros_like(pick)

    def rows_of(tile):
        return pl.ds(pl.multiple_of(tile * CHUNK, CHUNK), CHUNK)

    def load(tile):
        return pltpu.make_async_copy(
            e_ref.at[rows_of(tile)], table.at[rows_of(tile)], e_sem.at[tile]
        )

    def leave(tile, place, slot):
        return pltpu.make_async_copy(
            staged.at[slot], logits_ref.at[tile, part_rows(place, part)], out_sem.at[slot]
        )

    for tile in range(tiles):
        load(tile).start()

    def work(place, first):
        at = part_rows(place, part)
        ids = ids_ref[at, :]

        def one(pair, carry):
            for slot in range(2):
                tile = 2 * pair + slot
                if first:
                    load(tile).wait()

                    @pl.when(pair > 0)
                    def _(slot=slot, tile=tile):
                        leave(tile, place, slot).wait()

                else:
                    leave(tile, place, slot).wait()
                logits = matmul_t(full[place], table[rows_of(tile), :])
                staged[slot] = logits
                leave(tile, place, slot).start()
                column = tile * CHUNK + lax.broadcasted_iota(jnp.int32, (part, CHUNK), 1)
                picked = jnp.where(column == ids, logits, 0.0)
                pieces = [logits[:, at : at + LANES] for at in range(0, CHUNK, LANES)]
                before = top[at, :]
                high = functools.reduce(jnp.maximum, pieces, before)
                sums = total[at, :] * jnp.exp(before - high)
                found = pick[at, :]
                for number, piece in enumerate(pieces):
                    sums = sums + jnp.exp(piece - high)
                    found = found + picked[:, number * LANES : (number + 1) * LANES]
                top[at, :] = high
                total[at, :] = sums
                pick[at, :] = found
            return carry

        lax.fori_loop(0, tiles // 2, one, 0)

    work(me, True)
    for step in range(1, count):
        line.step(step)

        @pl.when(me >= step)
        def _(step=step):
            work(me - step, False)

        @pl.when(me + step < count)
        def _(step=step):
            work(me + step, False)

    keep = pltpu.make_async_copy(full, full_out, full_sem)
    keep.start()
    tall = top[...].T
    high = jnp.max(tall, axis=0, keepdims=True)
    stats[me] = jnp.zeros(stats.shape[1:], F32)
    stats[me, 0:1, :] = high
    stats[me, 1:2, :] = jnp.sum(total[...].T * jnp.exp(tall - high), axis=0, keepdims=True)
    stats[me, 2:3, :] = jnp.sum(pick[...].T, axis=0, keepdims=True)
    copies = [
        send(group, peer, step, stats.at[me], stats.at[me], st_send, st_recv)
        for step, peer in enumerate(group.peers())
    ]
    for slot in range(2):
        leave(0, me, slot).wait()
    line.wait_sends()
    for copy in copies:
        copy.wait()
    stats_out[...] = stats[...]
    keep.wait()


def line_head_logits(group, ident, x, embedding, ids):
    part, width = x.shape
    vocab = embedding.shape[0]
    count = group.count
    tokens = part * count
    tiles = vocab // CHUNK
    assert tiles % 2 == 0
    dma = pltpu.SemaphoreType.DMA
    return pl.pallas_call(
        functools.partial(line_head_logits_body, group),
        out_shape=(
            jax.ShapeDtypeStruct((tiles, tokens, CHUNK), F32),
            jax.ShapeDtypeStruct((count, part, width), BF16),
            jax.ShapeDtypeStruct((count, 8, tokens), F32),
        ),
        in_specs=[VMEM, HBM, VMEM],
        out_specs=(HBM, HBM, VMEM),
        scratch_shapes=[
            pltpu.VMEM((count, part, width), BF16),
            pltpu.VMEM((vocab, width), BF16),
            pltpu.VMEM((2, part, CHUNK), F32),
            pltpu.VMEM((tokens, LANES), F32),
            pltpu.VMEM((tokens, LANES), F32),
            pltpu.VMEM((tokens, LANES), F32),
            pltpu.VMEM((count, 8, tokens), F32),
            dma((2 * count - 2,)),
            dma((2 * count - 2,)),
            dma((tiles,)),
            dma((2,)),
            dma,
            dma((count - 1,)),
            dma((count - 1,)),
        ],
        compiler_params=pltpu.CompilerParams(
            collective_id=ident, has_side_effects=True, vmem_limit_bytes=56 * 2**20
        ),
    )(x, embedding, ids)


def line_head_grads_body(
    group, logits_ref, e_ref, ids_ref, norm_ref, weight_ref, grads_ref, total_ref,
    terms, stage, land, table, staged, low, acc,
    rs_send, rs_recv, e_sem, in_sem, out_sem,
):
    count, me = group.count, group.me()
    part = terms.shape[1]
    tiles = e_ref.shape[0] // CHUNK
    line = LineSum(group, terms, stage, land, rs_send, rs_recv)
    greet([group])

    def rows_of(tile):
        return pl.ds(pl.multiple_of(tile * CHUNK, CHUNK), CHUNK)

    def load(tile):
        return pltpu.make_async_copy(
            e_ref.at[rows_of(tile)], table.at[rows_of(tile)], e_sem.at[tile]
        )

    def enter(tile, place, slot):
        return pltpu.make_async_copy(
            logits_ref.at[tile, part_rows(place, part)], staged.at[slot], in_sem.at[slot]
        )

    def leave(tile, place, slot):
        return pltpu.make_async_copy(
            low.at[:, pl.ds(slot * CHUNK, CHUNK)],
            grads_ref.at[tile, part_rows(place, part)],
            out_sem.at[slot],
        )

    for tile in range(tiles):
        load(tile).start()

    def work(place, fresh=False):
        at = part_rows(place, part)
        ids, norm, weight = ids_ref[at, :], norm_ref[at, :], weight_ref[at, :]
        for slot in range(2):
            enter(slot, place, slot).start()
        acc[...] = jnp.zeros_like(acc)

        def one(pair, carry):
            for slot in range(2):
                tile = 2 * pair + slot
                enter(tile, place, slot).wait()
                if fresh:
                    load(tile).wait()
                column = tile * CHUNK + lax.broadcasted_iota(jnp.int32, (part, CHUNK), 1)
                probs = jnp.exp(staged[slot] - norm)
                grads = (jnp.where(column == ids, probs - 1.0, probs) * weight).astype(BF16)

                @pl.when(pair > 0)
                def _(slot=slot, tile=tile):
                    leave(tile, place, slot).wait()

                low[:, slot * CHUNK : (slot + 1) * CHUNK] = grads
                leave(tile, place, slot).start()

                @pl.when(pair + 1 < tiles // 2)
                def _(slot=slot, tile=tile):
                    enter(tile + 2, place, slot).start()

            rows = pl.ds(pl.multiple_of(pair * 2 * CHUNK, 2 * CHUNK), 2 * CHUNK)
            acc[...] += matmul(low[...], table[rows, :])
            return carry

        lax.fori_loop(0, tiles // 2, one, 0)
        for slot in range(2):
            leave(0, place, slot).wait()
        terms[place] = acc[...].astype(BF16)

    for step in range(count - 1):

        @pl.when(me < count - 1 - step)
        def _(step=step):
            work(count - 1 - step, fresh=step == 0)

        if step == 0:

            @pl.when(me == count - 1)
            def _():
                work(0, fresh=True)

        @pl.when((me > step) & ((me < count - 1) | (step > 0)))
        def _(step=step):
            work(step)

        line.first(step)
        if step == 1:
            line.rest(0, near=True)
    work(me)
    line.rest(0, near=False)
    for step in range(1, count - 1):
        line.rest(step)
    line.finish(total_ref)


def line_head_grads(group, ident, logits, embedding, ids, norm, weight):
    tiles, tokens, _ = logits.shape
    vocab, width = embedding.shape
    count = group.count
    part = tokens // count
    dma = pltpu.SemaphoreType.DMA
    return pl.pallas_call(
        functools.partial(line_head_grads_body, group),
        out_shape=(
            jax.ShapeDtypeStruct(logits.shape, BF16),
            jax.ShapeDtypeStruct((part, width), F32),
        ),
        in_specs=[HBM, HBM, VMEM, VMEM, VMEM],
        out_specs=(HBM, VMEM),
        scratch_shapes=[
            pltpu.VMEM((count, part, width), BF16),
            pltpu.VMEM((2, count - 1, part, width), BF16),
            pltpu.VMEM((2, count - 1, part, width), BF16),
            pltpu.VMEM((vocab, width), BF16),
            pltpu.VMEM((2, part, CHUNK), F32),
            pltpu.VMEM((part, 2 * CHUNK), BF16),
            pltpu.VMEM((part, width), F32),
            dma((2, count - 1)),
            dma((2, count - 1)),
            dma((tiles,)),
            dma((2,)),
            dma((2,)),
        ],
        compiler_params=pltpu.CompilerParams(
            collective_id=ident, has_side_effects=True, vmem_limit_bytes=56 * 2**20
        ),
    )(logits, embedding, ids, norm, weight)


def per_device(
    mesh_shape,
    token_ids,
    target_ids,
    lengths,
    embedding,
    outer_gain,
    outer_bias,
    norm_gain,
    norm_bias,
    qkv_weight,
    qv_bias,
    out_weight,
    up_weight,
    up_bias,
    down_weight,
    row_bias,
):
    sections, groups, shards = (mesh_shape[name] for name in ("section", "dp", "tensor"))
    s, j, z = (lax.axis_index(name) for name in ("section", "dp", "tensor"))
    by_section = Group(("section",), (sections,))
    by_dp = Group(("dp",), (groups,))
    by_tensor = Group(("tensor",), (shards,))
    exchange = Exchanges()
    layers = sections
    vocab, width = embedding.shape
    seq = token_ids.shape[1]
    rows = token_ids.shape[0] * groups
    local_cols = qkv_weight.shape[-1]
    planes = rows == sections * shards and local_cols % (groups * HEAD_DIM) == 0
    by_dp.square = planes and groups == 4
    by_tensor.line = planes
    team = by_dp if planes else by_tensor
    cut = groups if planes else 1
    fan = shards if planes else 1
    halves = 2 if planes else 1
    part = seq // team.count
    cols = local_cols // cut
    hidden = up_weight.shape[-1] // cut
    strip = hidden // halves
    cut_index = j if planes else 0
    my_row = z * sections + s if planes else j * sections + s
    length = lax.dynamic_slice(lengths, (my_row,), (1,))
    token_count = jnp.sum(lengths).astype(F32)
    vocab_start = z * vocab

    def chosen_cols(array, size):
        return lax.dynamic_slice_in_dim(array, cut_index * size, size, array.ndim - 1).T

    def chosen_rows(array, size):
        return lax.dynamic_slice_in_dim(array, cut_index * size, size, 0)

    def pad_rows(array, count):
        return jnp.pad(array, ((0, count - array.shape[0]), (0, width - array.shape[1])))

    sides = jnp.stack(
        [
            jnp.concatenate(
                [
                    chosen_cols(qkv_weight[0, 0], cols),
                    chosen_cols(qkv_weight[0, 2], cols),
                    chosen_cols(up_weight[0], hidden),
                ]
            ),
            jnp.concatenate(
                [
                    chosen_cols(qkv_weight[0, 1], cols),
                    chosen_rows(out_weight[0], cols),
                    chosen_rows(down_weight[0], hidden),
                ]
            ),
        ]
    )
    qv_piece = lax.dynamic_slice_in_dim(qv_bias[0], cut_index * cols, cols, 1)
    up_piece = lax.dynamic_slice_in_dim(up_bias[0], cut_index * hidden, hidden, 0)
    small = jnp.concatenate(
        [
            outer_gain,
            outer_bias,
            norm_gain[0],
            norm_bias[0],
            row_bias[0],
            pad_rows(qv_piece, 2),
            pad_rows(up_piece[None], 6),
        ]
    )

    def gather(group, x):
        return Job("gather", [group], x)

    def deal(group, x, axis=0):
        return Job("deal", [group], x, axis)

    def own_and_dealt(x, dealt, place, axis=0):
        own = lax.dynamic_index_in_dim(x, place, axis, keepdims=False).astype(F32)
        return own + jnp.sum(dealt.astype(F32), axis=0)

    if planes:
        other, both, small_all = exchange(
            deal(by_section, sides),
            gather(by_dp, jnp.stack([token_ids, target_ids])),
            gather(Group(("section", "tensor"), (sections, shards)), small),
        )
        small_all = small_all.reshape((sections, shards) + small.shape)
        own_side = lax.dynamic_index_in_dim(sides, s, 0, keepdims=False)
        side = [jnp.where(s == l, own_side, other[0]) for l in range(layers)]
        both = jnp.swapaxes(both, 0, 1).reshape(2, shards, sections, groups, part)
        both = lax.dynamic_index_in_dim(
            lax.dynamic_index_in_dim(both, s, 2, keepdims=False), j, 2, keepdims=False
        )
        ids, targets = both[0].reshape(-1), both[1].reshape(-1)
        group_lengths = lax.dynamic_index_in_dim(
            lengths.reshape(shards, sections), s, 1, keepdims=False
        )
        places = jnp.broadcast_to(j * part + jnp.arange(part), (shards, part))
        valid = (places < group_lengths[:, None]).reshape(-1)
    else:
        sides_all, small_all = exchange(gather(by_section, sides), gather(by_section, small))
        small_all = small_all[:, None]
        ids, targets = token_ids[s], target_ids[s]
        valid = jnp.arange(seq) < lengths[my_row]

    outer_gains = [small_all[l, 0, 0] for l in range(layers)]
    outer_offsets = [small_all[l, 0, 1] for l in range(layers)]
    params = []
    for l in range(layers):
        biases = [small_all[l, :, 8 + n, :cols].reshape(-1) for n in range(2)]
        units = small_all[l, :, 10, :hidden].reshape(fan, halves, strip)
        params.append(
            dict(
                gains=small_all[l, 0, 2:4],
                offsets=small_all[l, 0, 4:6],
                row_bias=small_all[l, 0, 6:8],
                bias=jnp.stack(biases),
                up_bias=jnp.swapaxes(units, 0, 1).reshape(1, -1),
            )
        )
        if not planes:
            block = sides_all[l]
            params[l].update(
                qk=block[:, :cols],
                vo=block[:, cols : 2 * cols],
                strips=[block[:, 2 * cols :]],
            )
    head_number = (
        (jnp.arange(fan)[:, None] if planes else z) * (local_cols // HEAD_DIM)
        + cut_index * (cols // HEAD_DIM)
        + jnp.arange(cols // HEAD_DIM)
    ).reshape(-1)
    slopes = jnp.exp2(-8.0 * (head_number + 1).astype(F32) / HEADS)

    def attn_jobs(l):
        if not planes or l >= layers:
            return []
        return [
            Job("spread", [by_tensor, by_section], side[l][first : first + cols])
            for first in (0, cols)
        ]

    def feed_jobs(l, n):
        if not planes or l >= layers:
            return []
        first = 2 * cols + n * strip
        return [Job("spread", [by_tensor, by_section], side[l][first : first + strip])]

    def take_attn(l, got):
        if got:
            params[l]["qk"], params[l]["vo"] = (
                one.reshape(2, fan * cols, width) for one in got
            )

    def take_feed(l, got):
        if got:
            params[l]["strips"] = [one.reshape(2, fan * strip, width) for one in got]

    def ident(kind, jobs):
        return exchange.ident((kind,) + tuple(job.key() for job in jobs))

    local_ids = ids - vocab_start
    inside = (local_ids >= 0) & (local_ids < vocab)
    looked = jnp.where(
        inside[:, None], jnp.take(embedding, jnp.clip(local_ids, 0, vocab - 1), axis=0), 0
    )
    group_part = looked.shape[0] // shards
    (x,) = exchange(Job("reduce", [by_tensor], looked.reshape(shards, group_part, width)))
    h = layer_norm(x, outer_gains[0], outer_offsets[0])

    kept = []
    strips = []
    for l, p in enumerate(params):
        jobs = (attn_jobs(l) + feed_jobs(l, 0) if l == 0 else []) + feed_jobs(l, 1)
        normed = layer_norm(h, p["gains"][0], p["offsets"][0]).astype(BF16)
        (total, normed, q, k, v, mixed, lse), got = attend(
            team, ident("attend", jobs), jobs, normed, length, slopes, p["bias"],
            [p["qk"], p["vo"]] if "qk" in p else [],
        )
        if "qk" not in p:
            take_attn(l, got[:2])
            got = got[2:]
        take_feed(l, strips + got)
        middle = h + total + p["row_bias"][0]
        jobs = attn_jobs(l + 1) + feed_jobs(l + 1, 0)
        second = layer_norm(middle, p["gains"][1], p["offsets"][1]).astype(BF16)
        (total, second, before), got = feed(
            team, ident("feed", jobs), jobs, second, p["strips"], p["up_bias"]
        )
        take_attn(l + 1, got[:2])
        strips = got[2:]
        kept.append((h, normed.reshape(seq, width), q, k, v, mixed, lse, middle, second, before))
        h = middle + total + p["row_bias"][1]

    final = layer_norm(h, outer_gains[-1], outer_offsets[-1]).astype(BF16)
    columns_of = (targets - vocab_start)[:, None]
    if planes:
        logits, final, stats = line_head_logits(
            by_tensor, exchange.ident("head logits"), final, embedding, columns_of
        )
        final = final.reshape(-1, width)
    else:
        (final,) = exchange(gather(by_tensor, final))
        final = final.reshape(-1, width)
        logits, tops, totals, picks = head_logits(final, embedding, columns_of)
        top = jnp.max(tops, axis=1)
        total = jnp.sum(totals * jnp.exp(tops - top[:, None]), axis=1)
        pick = jnp.sum(picks, axis=1)
        (stats,) = exchange(
            gather(by_tensor, jnp.pad(jnp.stack([top, total, pick]), ((0, 5), (0, 0))))
        )
    tokens = final.shape[0]
    top_all = jnp.max(stats[:, 0], axis=0)
    log_norm = top_all + jnp.log(jnp.sum(stats[:, 1] * jnp.exp(stats[:, 0] - top_all), axis=0))
    terms = jnp.where(valid, log_norm - jnp.sum(stats[:, 2], axis=0), 0.0)
    loss_part = jnp.sum(
        lax.dynamic_index_in_dim(terms.reshape(shards, -1), z, 0, keepdims=False)
    )
    row_weight = jnp.where(valid, 1.0 / token_count, 0.0)
    if planes:
        grad_logits, grad_final = line_head_grads(
            by_tensor, exchange.ident("head grads"), logits, embedding, columns_of,
            log_norm[:, None], row_weight[:, None],
        )
    else:
        grad_logits, back = head_grads(
            logits, embedding, columns_of, log_norm[:, None], row_weight[:, None]
        )
        (grad_final,) = exchange(
            Job("reduce", [by_tensor], back.reshape(shards, group_part, width))
        )
    _, final_back = jax.vjp(layer_norm, h, outer_gains[-1], outer_offsets[-1])
    grad, final_gain, final_offset = final_back(grad_final)

    def section_sums(pair, got):
        out = []
        for one, dealt in zip(pair, got):
            low = own_and_dealt(one, dealt, s).astype(BF16)
            if one.ndim == 4:
                out.append(low.reshape(low.shape[0], fan, cols, width))
            else:
                out.append(low.reshape(halves, fan, strip, width))
        return out

    def tensor_jobs(lows):
        return [deal(by_tensor, low, 1) for low in lows]

    def tensor_sums(lows, got):
        return [
            own_and_dealt(low, dealt, z, 1).astype(BF16) for low, dealt in zip(lows, got)
        ]

    def spread_jobs(pieces):
        return [Job("spread", [by_dp, by_section], piece) for piece in pieces]

    small_rows = [None] * layers
    pairs = [None] * layers
    attn_low, attn_done, feed_done = ([None] * layers for _ in range(3))
    for l in reversed(range(layers)):
        p = params[l]
        section_in, normed, q, k, v, mixed, lse, middle, second, before = kept[l]
        pair = by_section if planes else None
        late = planes and l + 1 < layers
        jobs = tensor_jobs(attn_low[l + 1]) if late else []
        (total, g_feed, up_sum, *dealt), got = feed_back(
            team, ident("feed back", jobs), jobs, pair, grad.astype(BF16),
            second.reshape(seq, width), before, p["strips"],
        )
        if late:
            attn_done[l + 1] = tensor_sums(attn_low[l + 1], got)
        if planes:
            feed_low = section_sums([g_feed], [one[None] for one in dealt])
        _, norm_back = jax.vjp(layer_norm, middle, p["gains"][1], p["offsets"][1])
        grad_mid, gain_two, offset_two = norm_back(total)
        grad_mid = grad_mid + grad
        jobs = tensor_jobs(feed_low) if planes else []
        (total, g_attn, qv_sum, *dealt), got = attend_back(
            team, ident("attend back", jobs), jobs, pair, grad_mid.astype(BF16), length, slopes,
            normed, p["qk"], p["vo"], q, k, v, mixed, lse,
        )
        g_attn = g_attn.reshape((2, 2) + g_attn.shape[1:])
        if planes:
            feed_done[l] = tensor_sums(feed_low, got)
            attn_low[l] = section_sums([g_attn], [one[None] for one in dealt])
        _, norm_back = jax.vjp(layer_norm, section_in, p["gains"][0], p["offsets"][0])
        grad_in, gain_one, offset_one = norm_back(total)
        bias_two = jnp.sum(grad, axis=0)
        grad = grad_in + grad_mid
        pairs[l] = (g_attn, g_feed)

        def placed(values, size):
            out = jnp.zeros((fan if planes else shards, cut, size), F32)
            at = (0, j, 0) if planes else (z, 0, 0)
            return lax.dynamic_update_slice(out, values.reshape(fan, 1, size), at).reshape(
                -1, width
            )

        units = jnp.swapaxes(up_sum.reshape(halves, fan, strip), 0, 1)
        small_rows[l] = [
            gain_one[None],
            gain_two[None],
            offset_one[None],
            offset_two[None],
            jnp.sum(grad_mid, axis=0)[None],
            bias_two[None],
            placed(qv_sum[0], cols),
            placed(qv_sum[1], cols),
            placed(units, hidden),
        ]

    _, embed_back = jax.vjp(layer_norm, x, outer_gains[0], outer_offsets[0])
    grad_rows, embed_gain, embed_offset = embed_back(grad)
    packed = jnp.concatenate(
        [row for l in range(layers) for row in small_rows[l]]
        + [embed_gain[None], final_gain[None], embed_offset[None], final_offset[None]]
        + [jnp.broadcast_to(loss_part, (1, width))]
    )
    used = packed.shape[0]
    packed = jnp.pad(packed, ((0, -used % 8), (0, 0)))
    jobs = [Job("gather", [Group(("section", "tensor"), (sections, shards))], packed, late=True)]
    if planes:
        jobs += spread_jobs(attn_done[1] + feed_done[1] + feed_done[0])
        jobs += [Job("deal", [by_tensor], low, 1, late=True) for low in attn_low[0]]
    embed_sum, packed, *got = table_sum(
        by_section, by_dp, by_tensor, jobs, grad_logits, ids[None, :] - vocab_start, final,
        grad_rows.astype(BF16), exchange.ident("table"),
    )
    packed = jnp.sum(packed, axis=0)
    jobs = [gather(by_dp, packed)]
    if planes:
        spread_one = got[:2]
        jobs += spread_jobs(tensor_sums(attn_low[0], got[3:]))
    packed, *spread_zero = exchange(*jobs)
    packed = jnp.sum(packed, axis=0)
    if planes:
        spread_zero.append(got[2])
        attn_sum, feed_sum = (
            jnp.where(s == 0, zero, one) for zero, one in zip(spread_zero, spread_one)
        )
    else:
        chosen = [
            lax.dynamic_index_in_dim(
                lax.psum(jnp.stack([pair[n] for pair in pairs]), ("section", "dp")),
                s, 0, keepdims=False,
            )
            for n in range(2)
        ]
        attn_sum = chosen[0][:, None]
        feed_sum = chosen[1][:, None, None]
    embed_sum = embed_sum.reshape(vocab, width).astype(F32)
    per_layer = (used - 5) // layers
    mine = lax.dynamic_slice_in_dim(packed, s * per_layer, per_layer, 0)
    qv_rows = mine[6:8].reshape(2, -1)
    ff_row = mine[8:].reshape(-1)
    grad_qv = lax.dynamic_slice_in_dim(qv_rows, z * local_cols, local_cols, 1)
    grad_up_bias = lax.dynamic_slice_in_dim(ff_row, z * hidden * cut, hidden * cut, 0)
    base = per_layer * layers
    grad_outer_gain = lax.dynamic_slice_in_dim(packed, base + s, 1, 0)
    grad_outer_bias = lax.dynamic_slice_in_dim(packed, base + 2 + s, 1, 0)
    loss = packed[base + 4, 0] / token_count

    def columns(array):
        return array.astype(F32).reshape(-1, width).T

    grad_qkv = jnp.stack(
        [columns(attn_sum[0, :, 0]), columns(attn_sum[1, :, 0]), columns(attn_sum[0, :, 1])]
    )
    grad_out_mat = attn_sum[1, :, 1].astype(F32).reshape(-1, width)
    grad_up = columns(feed_sum[0])
    grad_down = feed_sum[1].astype(F32).reshape(-1, width)
    return (
        loss,
        embed_sum,
        grad_outer_gain,
        grad_outer_bias,
        mine[0:2][None],
        mine[2:4][None],
        grad_qkv[None],
        grad_qv[None],
        grad_out_mat[None],
        grad_up[None],
        grad_up_bias[None],
        grad_down[None],
        mine[4:6][None],
    )


def solution(mesh):
    return jax.shard_map(
        functools.partial(per_device, dict(mesh.shape)),
        mesh=mesh,
        in_specs=(
            P("dp", None),
            P("dp", None),
            P(),
            P("tensor", None),
            P("section", None),
            P("section", None),
            P("section", None, None),
            P("section", None, None),
            P("section", None, None, "tensor"),
            P("section", None, "tensor"),
            P("section", "tensor", None),
            P("section", None, "tensor"),
            P("section", "tensor"),
            P("section", "tensor", None),
            P("section", None, None),
        ),
        out_specs=(
            P(),
            P("tensor", None),
            P("section", None),
            P("section", None),
            P("section", None, None),
            P("section", None, None),
            P("section", None, None, "tensor"),
            P("section", None, "tensor"),
            P("section", "tensor", None),
            P("section", None, "tensor"),
            P("section", "tensor"),
            P("section", "tensor", None),
            P("section", None, None),
        ),
        check_vma=False,
    )
```

```python
import functools
import math

import jax
import jax.numpy as jnp
from jax import lax
from jax.experimental import pallas as pl
from jax.experimental.pallas import tpu as pltpu
from jax.sharding import PartitionSpec as P

HEADS = 16
HEAD_DIM = 64
EPS = 1e-05
NEG = -1e30
MESH = pl.DeviceIdType.MESH
F32 = jnp.float32
BF16 = jnp.bfloat16


def matmul(former, latter):
    return jnp.dot(former, latter, preferred_element_type=F32)


def matmul_t(former, latter):
    return lax.dot_general(
        former, latter, (((1,), (1,)), ((), ())), preferred_element_type=F32
    )


def outer_sum(former, latter):
    return lax.dot_general(
        former, latter, (((0,), (0,)), ((), ())), preferred_element_type=F32
    )


def layer_norm(inputs, weight, offset):
    centre = inputs - jnp.mean(inputs, axis=-1, keepdims=True)
    spread = jnp.mean(centre * centre, axis=-1, keepdims=True)
    return centre * lax.rsqrt(spread + EPS) * weight + offset


def gelu_tanh(inputs):
    return jax.nn.gelu(inputs, approximate=True)


class Group:
    def __init__(self, axes, sizes, square=False, line=False):
        self.square = square
        self.line = line
        self.axes = axes
        self.sizes = sizes
        self.count = math.prod(sizes)

    def me(self):
        place = 0
        for axis, size in zip(self.axes, self.sizes):
            place = place * size + lax.axis_index(axis)
        return place

    def device(self, place):
        spot = {}
        for axis, size in reversed(list(zip(self.axes, self.sizes))):
            spot[axis] = lax.rem(place, size)
            place = lax.div(place, size)
        return spot

    def peers(self):
        me = self.me()
        return [lax.rem(me + step, self.count) for step in range(1, self.count)]


def greet(groups):
    barrier = pltpu.get_barrier_semaphore()
    total = 0
    for group in groups:
        for peer in group.peers():
            pl.semaphore_signal(
                barrier, inc=1, device_id=group.device(peer), device_id_type=MESH
            )
            total += 1
    pl.semaphore_wait(barrier, total)


def send(group, peer, step, src, dst, send_sem, recv_sem):
    copy = pltpu.make_async_remote_copy(
        src_ref=src,
        dst_ref=dst,
        send_sem=send_sem.at[step],
        recv_sem=recv_sem.at[step],
        device_id=group.device(peer),
        device_id_type=MESH,
    )
    copy.start()
    return copy


def tie(*arrays):
    return lax.optimization_barrier(arrays)


class LineRows:
    def __init__(self, group, x, full, send_sem, recv_sem):
        self.group, self.count, self.me = group, group.count, group.me()
        self.x, self.full, self.sems = x, full, (send_sem, recv_sem)

    def copy(self, up, step):
        place = self.me - step if up else self.me + step
        place = jnp.clip(place, 0, self.count - 1)
        number = step if up else self.count - 1 + step
        src = self.x if step == 0 else self.full.at[place]
        return pltpu.make_async_remote_copy(
            src_ref=src,
            dst_ref=self.full.at[place],
            send_sem=self.sems[0].at[number],
            recv_sem=self.sems[1].at[number],
            device_id=self.group.device(
                jnp.clip(self.me + 1 if up else self.me - 1, 0, self.count - 1)
            ),
            device_id_type=MESH,
        )

    def leaves(self, up, step):
        if up:
            return (self.me - step >= 0) & (self.me < self.count - 1)
        return (self.me + step < self.count) & (self.me > 0)

    def arrives(self, up, step):
        return self.me - 1 - step >= 0 if up else self.me + 1 + step < self.count

    def start(self):
        for up in (True, False):

            @pl.when(self.leaves(up, 0))
            def _(up=up):
                self.copy(up, 0).start()

    def step(self, step):
        for up in (True, False):

            @pl.when(self.arrives(up, step - 1))
            def _(up=up):
                self.copy(up, step - 1).wait_recv()

            if step < self.count - 1:

                @pl.when(self.leaves(up, step))
                def _(up=up):
                    self.copy(up, step).start()

    def wait_sends(self):
        for step in range(self.count - 1):
            for up in (True, False):

                @pl.when(self.leaves(up, step))
                def _(up=up, step=step):
                    self.copy(up, step).wait_send()

    def finish(self):
        for step in range(1, self.count):
            self.step(step)
        self.wait_sends()


class LineSum:
    def __init__(self, group, x, stage, land, send_sem, recv_sem):
        self.group, self.count, self.me = group, group.count, group.me()
        self.x, self.stage, self.land, self.sems = x, stage, land, (send_sem, recv_sem)

    def copy(self, up, step):
        side = 0 if up else 1
        return pltpu.make_async_remote_copy(
            src_ref=self.stage.at[side, step],
            dst_ref=self.land.at[side, step],
            send_sem=self.sems[0].at[side, step],
            recv_sem=self.sems[1].at[side, step],
            device_id=self.group.device(
                jnp.clip(self.me + 1 if up else self.me - 1, 0, self.count - 1)
            ),
            device_id_type=MESH,
        )

    def leaves(self, up, step):
        return self.me < self.count - 1 - step if up else self.me > step

    def behind(self, up):
        return self.me > 0 if up else self.me < self.count - 1

    def first(self, step):
        for up in (True, False):
            place = self.count - 1 - step if up else step
            side = 0 if up else 1

            @pl.when(self.leaves(up, step) & jnp.logical_not(self.behind(up)))
            def _(up=up, place=place, side=side):
                self.stage[side, step] = self.x[place]
                self.copy(up, step).start()

    def rest(self, step, near=None):
        for up in (True, False):
            place = self.count - 1 - step if up else step
            side = 0 if up else 1
            here = self.leaves(up, step) & self.behind(up)
            if near is not None:
                by_end = self.me == (1 if up else self.count - 2)
                here = here & (by_end if near else jnp.logical_not(by_end))

            @pl.when(here)
            def _(up=up, place=place, side=side):
                self.copy(up, step).wait_recv()
                total = self.x[place].astype(F32) + self.land[side, step].astype(F32)
                self.stage[side, step] = total.astype(self.stage.dtype)
                self.copy(up, step).start()

    def finish(self, out):
        out[...] = self.x[self.me].astype(F32)
        for up in (True, False):
            side = 0 if up else 1
            for step in range(self.count - 1):

                @pl.when(self.behind(up) & (self.me == (self.count - 1 - step if up else step)))
                def _(up=up, step=step, side=side):
                    self.copy(up, step).wait_recv()
                    out[...] += self.land[side, step].astype(F32)

        for up in (True, False):
            for step in range(self.count - 1):

                @pl.when(self.leaves(up, step))
                def _(up=up, step=step):
                    self.copy(up, step).wait_send()


class Job:
    def __init__(self, kind, groups, x, axis=0, late=False):
        self.late = late
        self.kind, self.groups, self.x, self.axis = kind, groups, x, axis
        count = groups[0].count
        rest = x.shape[:axis] + x.shape[axis + 1 :]
        dma = pltpu.SemaphoreType.DMA
        self.in_spec = pl.BlockSpec(memory_space=pl.ANY)
        self.out_spec = pl.BlockSpec(memory_space=pl.ANY)
        self.scratch = [dma((count - 1,)), dma((count - 1,)), dma]
        if kind in ("gather", "spread"):
            self.in_spec = pl.BlockSpec(memory_space=pltpu.VMEM)
        if kind == "gather" and groups[0].line:
            self.scratch = [dma((2 * count - 2,)), dma((2 * count - 2,)), dma]
        if kind == "gather":
            self.out = jax.ShapeDtypeStruct((count,) + x.shape, x.dtype)
        elif kind == "spread":
            self.out = jax.ShapeDtypeStruct((groups[1].count, count) + x.shape, x.dtype)
            copies = 7 if groups[0].square else count
            if groups[0].square:
                self.scratch = [dma((6,)), dma((6,)), dma]
            self.scratch += [dma((copies,)), dma((copies,))]
        elif kind == "deal":
            self.out = jax.ShapeDtypeStruct((count - 1,) + rest, x.dtype)
        else:
            self.out = jax.ShapeDtypeStruct(rest, F32)
            self.out_spec = pl.BlockSpec(memory_space=pltpu.VMEM)
            if groups[0].line:
                self.in_spec = pl.BlockSpec(memory_space=pltpu.VMEM)
                self.scratch = [dma((2, count - 1)), dma((2, count - 1)), dma]
                self.scratch += [pltpu.VMEM((2, count - 1) + rest, x.dtype)] * 2
            else:
                self.scratch += [
                    pltpu.VMEM(rest, x.dtype), pltpu.VMEM((count - 1,) + rest, x.dtype)
                ]

    def key(self):
        return (self.kind, tuple(g.axes for g in self.groups), self.x.shape, str(self.x.dtype), self.axis)

    def start(self, x, out, send_sem, recv_sem, own_sem, *more):
        group = self.groups[0]
        me = group.me()
        peers = list(enumerate(group.peers()))

        def block(place):
            return x.at[(slice(None),) * self.axis + (place,)]

        if self.kind == "gather" and group.line:
            line = LineRows(group, x, out, send_sem, recv_sem)
            line.start()
            own = pltpu.make_async_copy(x, out.at[me], own_sem)
            own.start()

            def finish():
                line.finish()
                own.wait()

        elif self.kind == "reduce" and group.line:
            line = LineSum(group, x, *more, send_sem, recv_sem)
            for step in range(group.count - 1):
                line.first(step)

            def finish():
                for step in range(group.count - 1):
                    line.rest(step)
                line.finish(out)

        elif self.kind == "gather":
            copies = [send(group, p, k, x, out.at[me], send_sem, recv_sem) for k, p in peers]
            own = pltpu.make_async_copy(x, out.at[me], own_sem)
            own.start()

            def finish():
                for copy in copies + [own]:
                    copy.wait()

        elif self.kind == "spread" and group.square:
            pair = self.groups[1]
            side = pair.me()
            fw_send, fw_recv = more
            size = self.x.shape[0] // 2
            near = [across(me, 0), across(me, 1)]

            def copy_of(number):
                at = pl.ds(SQUARE_HALF[number] * size, size)
                place = me if number < 4 else near[number - 4]
                dst = out.at[side, place, at]
                src = x.at[at] if number < 4 else dst
                copy = pltpu.make_async_remote_copy(
                    src_ref=src, dst_ref=dst, send_sem=send_sem.at[number],
                    recv_sem=recv_sem.at[number], device_id=group.device(near[SQUARE_STEP[number]]),
                    device_id_type=MESH,
                )
                origin = near[SQUARE_STEP[number]] if number < 4 else across(me, 2)
                return copy, out.at[side, origin, at]

            copies = [copy_of(number) for number in range(6)]
            for number in (0, 2, 1, 3):
                copies[number][0].start()
            passed = [send(pair, 1 - side, 6, x, out.at[side, me], fw_send, fw_recv)]
            own = pltpu.make_async_copy(x, out.at[side, me], own_sem)
            own.start()

            def arrived(number):
                copy, landed = copies[number]
                copy.wait_recv()
                passed.append(send(pair, 1 - side, number, landed, landed, fw_send, fw_recv))

            def middle():
                for number in (0, 2):
                    copies[number][0].wait_recv()
                    copies[4 + number // 2][0].start()
                    landed = copies[number][1]
                    passed.append(send(pair, 1 - side, number, landed, landed, fw_send, fw_recv))

            def finish():
                for number in (1, 3, 4, 5):
                    arrived(number)
                for copy in passed:
                    copy.wait()
                for copy, _ in copies:
                    copy.wait_send()
                own.wait()

            return middle, finish

        elif self.kind == "spread":
            pair = self.groups[1]
            side = pair.me()
            fw_send, fw_recv = more
            home = out.at[side, me]
            copies = [send(group, p, k, x, home, send_sem, recv_sem) for k, p in peers]
            last = group.count - 1
            passed = [send(pair, 1 - side, last, x, home, fw_send, fw_recv)]
            own = pltpu.make_async_copy(x, home, own_sem)
            own.start()

            def finish():
                for k, copy in enumerate(copies):
                    copy.wait_recv()
                    place = out.at[side, lax.rem(me + group.count - 1 - k, group.count)]
                    passed.append(send(pair, 1 - side, k, place, place, fw_send, fw_recv))
                for copy in passed:
                    copy.wait()
                for copy in copies:
                    copy.wait_send()
                own.wait()

        elif self.kind == "deal":
            copies = [send(group, p, k, block(p), out.at[k], send_sem, recv_sem) for k, p in peers]

            def finish():
                for copy in copies:
                    copy.wait()

        else:
            kept, slots = more
            copies = [send(group, p, k, block(p), slots.at[k], send_sem, recv_sem) for k, p in peers]
            own = pltpu.make_async_copy(block(me), kept, own_sem)
            own.start()

            def finish():
                own.wait()
                for copy in copies:
                    copy.wait()
                total = kept[...].astype(F32)
                for k in range(group.count - 1):
                    total = total + slots[k].astype(F32)
                out[...] = total

        return None, finish


def pass_on(ends):
    for middle, _ in ends:
        if middle is not None:
            middle()


def finish_jobs(ends):
    for _, finish in ends:
        finish()


def job_groups(jobs):
    return [group for job in jobs for group in job.groups]


def split_scratch(jobs, scratch):
    parts, at = [], 0
    for job in jobs:
        parts.append(scratch[at : at + len(job.scratch)])
        at += len(job.scratch)
    return parts


def exchange_body(jobs, *refs):
    count = len(jobs)
    greet(job_groups(jobs))
    parts = split_scratch(jobs, refs[2 * count :])
    ends = [
        job.start(refs[n], refs[count + n], *parts[n]) for n, job in enumerate(jobs)
    ]
    pass_on(ends)
    finish_jobs(ends)


class Exchanges:
    def __init__(self):
        self.idents = {}

    def ident(self, key):
        return self.idents.setdefault(key, len(self.idents))

    def __call__(self, *jobs):
        jobs = list(jobs)
        return pl.pallas_call(
            functools.partial(exchange_body, jobs),
            out_shape=tuple(job.out for job in jobs),
            in_specs=[job.in_spec for job in jobs],
            out_specs=tuple(job.out_spec for job in jobs),
            scratch_shapes=[one for job in jobs for one in job.scratch],
            compiler_params=pltpu.CompilerParams(
                collective_id=self.ident(tuple(job.key() for job in jobs)),
                has_side_effects=True,
                vmem_limit_bytes=32 * 2**20,
            ),
        )(*[job.x for job in jobs])


CHUNK = 512


def start_rows(group, x_ref, full, send_sem, recv_sem):
    me = group.me()
    full[me] = x_ref[...]
    return [
        send(group, peer, step, x_ref, full.at[me], send_sem, recv_sem)
        for step, peer in enumerate(group.peers())
    ]


def table_body(
    by_section, by_dp, by_tensor, jobs, g_ref, ids_ref, u_ref, gx_ref, *refs
):
    riders = len(jobs)
    xs, (out_ref, *outs), refs = refs[:riders], refs[riders : 2 * riders + 1], refs[2 * riders + 1 :]
    (g_buf, to_partner, from_partner, to_dp, from_dp, own, result,
    g_sem, ps_send, ps_recv, dp_send, dp_recv, ag_send, ag_recv, fw_send, fw_recv, own_sem,
    ) = refs[:17]
    gx_full, gx_send, gx_recv = refs[17:20]
    s, j = by_section.me(), by_dp.me()
    partner = 1 - s
    peers = by_dp.peers() + [j]
    count = by_dp.count
    block = own.shape[0]
    subs = block // CHUNK
    tokens = u_ref.shape[0]
    greet([by_section, by_dp, by_tensor] + job_groups(jobs))
    gx_copies = start_rows(by_tensor, gx_ref, gx_full, gx_send, gx_recv)
    parts = split_scratch(jobs, refs[20:])
    ends = [job.start(xs[n], outs[n], *parts[n]) for n, job in enumerate(jobs)]

    def chunk(half, place, sub):
        return (half * count + place) * subs + sub

    order = [(number, half) for number in range(count) for half in (0, 1)]

    def fetch(index, sub, slot):
        number, away = order[index]
        half = partner if away == 0 else s
        return pltpu.make_async_copy(
            g_ref.at[chunk(half, peers[number], sub)], g_buf.at[slot], g_sem.at[slot]
        )

    def remote(group, peer, number, sub, src, dst, send_sem, recv_sem):
        return pltpu.make_async_remote_copy(
            src_ref=src,
            dst_ref=dst,
            send_sem=send_sem.at[number, sub],
            recv_sem=recv_sem.at[number, sub],
            device_id=group.device(peer),
            device_id_type=MESH,
        )

    def rows(sub):
        return pl.ds(pl.multiple_of(sub * CHUNK, CHUNK), CHUNK)

    def partner_copy(number, sub):
        return remote(
            by_section, partner, number, sub,
            to_partner.at[number, rows(sub)], from_partner.at[number, rows(sub)],
            ps_send, ps_recv,
        )

    def chip_copy(number, sub):
        return remote(
            by_dp, peers[number], number, sub,
            to_dp.at[number, rows(sub)], from_dp.at[number, rows(sub)], dp_send, dp_recv,
        )

    def spread_copy(number, sub):
        return remote(
            by_dp, peers[number], number, sub,
            result.at[rows(sub)], out_ref.at[chunk(s, j, sub)], ag_send, ag_recv,
        )

    sources = [lax.rem(j + count - 1 - number, count) for number in range(count - 1)] + [j]

    def forward_copy(number, sub):
        target = out_ref.at[chunk(s, sources[number], sub)]
        origin = result.at[rows(sub)] if number == count - 1 else target
        return remote(by_section, partner, number, sub, origin, target, fw_send, fw_recv)

    def own_copy(sub):
        return pltpu.make_async_copy(
            result.at[rows(sub)], out_ref.at[chunk(s, j, sub)], own_sem.at[sub]
        )

    for copy in gx_copies:
        copy.wait()
    fetch(0, 0, 0).start()
    for index, (number, away) in enumerate(order):
        half = partner if away == 0 else s

        def one(sub, carry, index=index, number=number, away=away, half=half):
            slot = lax.rem(sub, 2)
            fetch(index, sub, slot).wait()

            @pl.when(sub + 1 < subs)
            def _():
                fetch(index, sub + 1, 1 - slot).start()

            if index + 1 < len(order):

                @pl.when(sub + 1 == subs)
                def _():
                    fetch(index + 1, 0, 1 - slot).start()

            base = chunk(half, peers[number], sub) * CHUNK
            place = base + lax.broadcasted_iota(jnp.int32, (CHUNK, tokens), 0)
            chosen = jnp.where(place == ids_ref[...], 1.0, 0.0).astype(BF16)
            term = outer_sum(g_buf[slot], u_ref[...]) + matmul(
                chosen, gx_full[...].reshape(tokens, gx_full.shape[2])
            )
            if away == 0:
                to_partner[number, rows(sub), :] = term.astype(BF16)
                partner_copy(number, sub).start()
            else:
                partner_copy(number, sub).wait_recv()
                term = term + from_partner[number, rows(sub), :].astype(F32)
                if number < count - 1:
                    to_dp[number, rows(sub), :] = term.astype(BF16)
                    chip_copy(number, sub).start()
                else:
                    own[rows(sub), :] = term
            return carry

        lax.fori_loop(0, subs, one, 0)

    def finish(sub, carry):
        term = own[rows(sub), :]
        for number in range(count - 1):
            chip_copy(number, sub).wait_recv()
            term = term + from_dp[number, rows(sub), :].astype(F32)
        result[rows(sub), :] = term.astype(BF16)
        for number in range(count - 1):
            spread_copy(number, sub).start()
        forward_copy(count - 1, sub).start()
        own_copy(sub).start()
        return carry

    lax.fori_loop(0, subs, finish, 0)

    def take(sub, carry):
        for number in range(count - 1):
            spread_copy(number, sub).wait_recv()
            forward_copy(number, sub).start()
        return carry

    lax.fori_loop(0, subs, take, 0)

    def drain(sub, carry):
        own_copy(sub).wait()
        for number in range(count):
            partner_copy(number, sub).wait_send()
            forward_copy(number, sub).wait()
        for number in range(count - 1):
            chip_copy(number, sub).wait_send()
            spread_copy(number, sub).wait_send()
        return carry

    lax.fori_loop(0, subs, drain, 0)
    pass_on(ends)
    finish_jobs(ends)


def across(me, step):
    bits = jnp.int32(step + 1)
    x, y = lax.rem(me, 2), lax.div(me, 2)
    return 2 * lax.rem(y + lax.div(bits, 2), 2) + lax.rem(x + lax.rem(bits, 2), 2)


SQUARE_HALF = (0, 1, 1, 0, 0, 1)
SQUARE_STEP = (0, 0, 1, 1, 1, 0)


def table_square_body(by_section, by_dp, by_tensor, jobs, g_ref, ids_ref, u_ref, gx_ref, *refs):
    riders = len(jobs)
    xs, (out_ref, *outs), refs = refs[:riders], refs[riders : 2 * riders + 1], refs[2 * riders + 1 :]
    (
        g_buf, to_partner, from_partner, to_dp, hop_land, from_dp, own, result,
        g_sem, ps_send, ps_recv, hop_send, hop_recv, dp_send, dp_recv, ag_send, ag_recv,
        fw_send, fw_recv, own_sem,
    ) = refs[:20]
    gx_full, gx_send, gx_recv = refs[20:23]
    s, j = by_section.me(), by_dp.me()
    partner = 1 - s
    near_x, near_y, far = (across(j, step) for step in range(3))
    peers = [far, near_y, near_x, j]
    count = 4
    block = own.shape[0]
    subs = block // CHUNK
    half_rows = CHUNK // 2
    tokens = u_ref.shape[0]
    greet([by_section, by_dp, by_tensor] + job_groups(jobs))
    line = LineRows(by_tensor, gx_ref, gx_full, gx_send, gx_recv)
    line.start()
    gx_full[line.me] = gx_ref[...]
    parts = split_scratch(jobs, refs[23:])
    ends = [
        job.start(xs[n], outs[n], *parts[n]) for n, job in enumerate(jobs) if not job.late
    ]

    def chunk(half, place, sub):
        return (half * count + place) * subs + sub

    order = [(number, away) for number in range(count) for away in (0, 1)]

    def fetch(index, sub, slot):
        number, away = order[index]
        half = partner if away == 0 else s
        return pltpu.make_async_copy(
            g_ref.at[chunk(half, peers[number], sub)], g_buf.at[slot], g_sem.at[slot]
        )

    def remote(group, peer, number, sub, src, dst, send_sem, recv_sem):
        return pltpu.make_async_remote_copy(
            src_ref=src,
            dst_ref=dst,
            send_sem=send_sem.at[number, sub],
            recv_sem=recv_sem.at[number, sub],
            device_id=group.device(peer),
            device_id_type=MESH,
        )

    def rows(sub):
        return pl.ds(pl.multiple_of(sub * CHUNK, CHUNK), CHUNK)

    def half_of(sub, which):
        return pl.ds(pl.multiple_of(sub * CHUNK + which * half_rows, half_rows), half_rows)

    def partner_copy(number, sub):
        return remote(
            by_section, partner, number, sub,
            to_partner.at[number, rows(sub)], from_partner.at[number, rows(sub)],
            ps_send, ps_recv,
        )

    def hop_copy(which, sub):
        return remote(
            by_dp, (near_x, near_y)[which], which, sub,
            to_dp.at[0, half_of(sub, which)], hop_land.at[half_of(sub, which)], hop_send, hop_recv,
        )

    def chip_copy(number, sub):
        return remote(
            by_dp, (near_y, near_x)[number], number, sub,
            to_dp.at[number + 1, rows(sub)], from_dp.at[number, rows(sub)], dp_send, dp_recv,
        )

    def spread_copy(number, sub):
        which = SQUARE_HALF[number]
        place = j if number < 4 else (near_x, near_y)[number - 4]
        dst = out_ref.at[chunk(s, place, sub), pl.ds(which * half_rows, half_rows)]
        src = result.at[half_of(sub, which)] if number < 4 else dst
        peer = (near_x, near_y)[SQUARE_STEP[number]]
        return remote(by_dp, peer, number, sub, src, dst, ag_send, ag_recv)

    sources = [near_x, near_y, far, j]

    def forward_copy(number, sub):
        target = out_ref.at[chunk(s, sources[number], sub)]
        origin = result.at[rows(sub)] if number == count - 1 else target
        return remote(by_section, partner, number, sub, origin, target, fw_send, fw_recv)

    def own_copy(sub):
        return pltpu.make_async_copy(
            result.at[rows(sub)], out_ref.at[chunk(s, j, sub)], own_sem.at[sub]
        )

    def slot_of(number, away):
        if away == 0:
            return to_partner.at[number]
        return to_dp.at[number] if number < 3 else own

    fetch(0, 0, 0).start()
    stops = {(step * len(order)) // line.count: step for step in range(1, line.count - 1)}
    for index, (number, away) in enumerate(order):
        if index in stops:
            line.step(stops[index])

        def share(sub, carry, index=index, number=number, away=away):
            slot = lax.rem(sub, 2)
            fetch(index, sub, slot).wait()

            @pl.when(sub + 1 < subs)
            def _():
                fetch(index, sub + 1, 1 - slot).start()

            if index + 1 < len(order):

                @pl.when(sub + 1 == subs)
                def _():
                    fetch(index + 1, 0, 1 - slot).start()

            held = slot_of(number, away)
            held[rows(sub), :] = outer_sum(g_buf[slot], u_ref[...]).astype(held.dtype)
            return carry

        lax.fori_loop(0, subs, share, 0)
    pass_on(ends)
    line.step(line.count - 1)
    line.wait_sends()
    late = [job.start(xs[n], outs[n], *parts[n]) for n, job in enumerate(jobs) if job.late]

    for index, (number, away) in enumerate(order):
        half = partner if away == 0 else s

        def one(sub, carry, number=number, away=away, half=half):
            base = chunk(half, peers[number], sub) * CHUNK
            place = base + lax.broadcasted_iota(jnp.int32, (CHUNK, tokens), 0)
            chosen = jnp.where(place == ids_ref[...], 1.0, 0.0).astype(BF16)
            term = matmul(chosen, gx_full[...].reshape(tokens, gx_full.shape[2]))
            term = term + slot_of(number, away)[rows(sub), :].astype(F32)
            if away == 0:
                to_partner[number, rows(sub), :] = term.astype(BF16)
                partner_copy(number, sub).start()
                return carry
            partner_copy(number, sub).wait_recv()
            term = term + from_partner[number, rows(sub), :].astype(F32)
            if number == 0:
                to_dp[0, rows(sub), :] = term.astype(BF16)
                for which in range(2):
                    hop_copy(which, sub).start()
            elif number < 3:
                which = number - 1
                hop_copy(which, sub).wait_recv()
                mine = slice(which * half_rows, (which + 1) * half_rows)
                rest = slice((1 - which) * half_rows, (2 - which) * half_rows)
                to_dp[number, half_of(sub, which), :] = (
                    term[mine] + hop_land[half_of(sub, which), :].astype(F32)
                ).astype(BF16)
                to_dp[number, half_of(sub, 1 - which), :] = term[rest].astype(BF16)
                chip_copy(which, sub).start()
            else:
                own[rows(sub), :] = term
            return carry

        lax.fori_loop(0, subs, one, 0)

    def finish(sub, carry):
        term = own[rows(sub), :]
        for number in range(2):
            chip_copy(number, sub).wait_recv()
            term = term + from_dp[number, rows(sub), :].astype(F32)
        result[rows(sub), :] = term.astype(BF16)
        for number in (0, 2, 1, 3):
            spread_copy(number, sub).start()
        forward_copy(count - 1, sub).start()
        own_copy(sub).start()
        return carry

    lax.fori_loop(0, subs, finish, 0)

    def pass_chunk(sub, carry):
        for number in (0, 2):
            spread_copy(number, sub).wait_recv()
            spread_copy(4 + number // 2, sub).start()
        for number in (0, 1):
            spread_copy(2 * number + 1, sub).wait_recv()
            forward_copy(number, sub).start()
        return carry

    lax.fori_loop(0, subs, pass_chunk, 0)

    def last(sub, carry):
        for number in (4, 5):
            spread_copy(number, sub).wait_recv()
        forward_copy(2, sub).start()
        return carry

    lax.fori_loop(0, subs, last, 0)

    def drain(sub, carry):
        own_copy(sub).wait()
        for number in range(count):
            partner_copy(number, sub).wait_send()
            forward_copy(number, sub).wait()
        for number in range(2):
            hop_copy(number, sub).wait_send()
            chip_copy(number, sub).wait_send()
        for number in range(6):
            spread_copy(number, sub).wait_send()
        return carry

    lax.fori_loop(0, subs, drain, 0)
    finish_jobs(ends)
    pass_on(late)
    finish_jobs(late)


def table_sum(by_section, by_dp, by_tensor, jobs, grads, ids, final, grad_rows, ident):
    chunks, tokens, _ = grads.shape
    width = final.shape[1]
    count = by_dp.count
    subs = chunks // (2 * count)
    block = subs * CHUNK
    assert subs % 2 == 0
    dma = pltpu.SemaphoreType.DMA
    low = functools.partial(pltpu.VMEM, dtype=BF16)
    square = by_dp.square
    scratch = [
        low((2, tokens, CHUNK)),
        low((count, block, width)),
        low((count, block, width)),
        low((count - 1, block, width)),
    ]
    scratch += [low((block, width)), low((2, block, width))] if square else [
        low((count - 1, block, width))
    ]
    scratch += [pltpu.VMEM((block, width), F32), low((block, width)), dma((2,))]
    copies = (count, 2, 2, 6, count) if square else (count, count - 1, count - 1, count)
    scratch += [dma((copy, subs)) for copy in copies for _ in range(2)] + [dma((subs,))]
    scratch += [low((by_tensor.count,) + grad_rows.shape)]
    scratch += [dma(((by_tensor.count - 1) * (2 if square else 1),))] * 2
    vmem = pl.BlockSpec(memory_space=pltpu.VMEM)
    hbm = pl.BlockSpec(memory_space=pl.ANY)
    return pl.pallas_call(
        functools.partial(
            table_square_body if by_dp.square else table_body, by_section, by_dp, by_tensor, jobs
        ),
        out_shape=(jax.ShapeDtypeStruct((chunks, CHUNK, width), BF16),)
        + tuple(job.out for job in jobs),
        in_specs=[hbm, vmem, vmem, vmem] + [job.in_spec for job in jobs],
        out_specs=(hbm,) + tuple(job.out_spec for job in jobs),
        scratch_shapes=scratch + [one for job in jobs for one in job.scratch],
        compiler_params=pltpu.CompilerParams(
            collective_id=ident, has_side_effects=True, vmem_limit_bytes=56 * 2**20
        ),
    )(grads, ids, final, grad_rows, *[job.x for job in jobs])


LANES = 128


def head_logits_body(u_ref, e_ref, ids_ref, logits_ref, top_ref, total_ref, pick_ref):
    step = pl.program_id(0)
    tokens, tile = logits_ref.shape[1:]

    @pl.when(step == 0)
    def _():
        top_ref[...] = jnp.full_like(top_ref, NEG)
        total_ref[...] = jnp.zeros_like(total_ref)
        pick_ref[...] = jnp.zeros_like(pick_ref)

    logits = matmul_t(u_ref[...], e_ref[...])
    logits_ref[0] = logits
    place = step * tile + lax.broadcasted_iota(jnp.int32, (tokens, tile), 1)
    picked = jnp.where(place == ids_ref[...], logits, 0.0)
    pieces = [logits[:, at : at + LANES] for at in range(0, tile, LANES)]
    before = top_ref[...]
    top = functools.reduce(jnp.maximum, pieces, before)
    total = total_ref[...] * jnp.exp(before - top)
    pick = pick_ref[...]
    for number, piece in enumerate(pieces):
        total = total + jnp.exp(piece - top)
        pick = pick + picked[:, number * LANES : (number + 1) * LANES]
    top_ref[...] = top
    total_ref[...] = total
    pick_ref[...] = pick


def head_logits(final, embedding, ids):
    tokens, width = final.shape
    vocab = embedding.shape[0]
    fixed = pl.BlockSpec((tokens, LANES), lambda step: (0, 0))
    stat = jax.ShapeDtypeStruct((tokens, LANES), F32)
    return pl.pallas_call(
        head_logits_body,
        grid=(vocab // CHUNK,),
        out_shape=(
            jax.ShapeDtypeStruct((vocab // CHUNK, tokens, CHUNK), F32), stat, stat, stat
        ),
        in_specs=[
            pl.BlockSpec((tokens, width), lambda step: (0, 0)),
            pl.BlockSpec((CHUNK, width), lambda step: (step, 0)),
            pl.BlockSpec((tokens, 1), lambda step: (0, 0)),
        ],
        out_specs=(
            pl.BlockSpec((1, tokens, CHUNK), lambda step: (step, 0, 0)), fixed, fixed, fixed
        ),
        compiler_params=pltpu.CompilerParams(vmem_limit_bytes=40 * 2**20),
        cost_estimate=pl.CostEstimate(
            flops=2 * tokens * vocab * width,
            bytes_accessed=4 * tokens * vocab + 2 * vocab * width,
            transcendentals=tokens * vocab,
        ),
    )(final, embedding, ids)


def head_grads_body(logits_ref, e_ref, ids_ref, norm_ref, weight_ref, grads_ref, back_ref, acc):
    step = pl.program_id(0)
    tokens, tile = grads_ref.shape[1:]

    @pl.when(step == 0)
    def _():
        acc[...] = jnp.zeros_like(acc)

    place = step * tile + lax.broadcasted_iota(jnp.int32, (tokens, tile), 1)
    probs = jnp.exp(logits_ref[0] - norm_ref[...])
    grads = (jnp.where(place == ids_ref[...], probs - 1.0, probs) * weight_ref[...]).astype(BF16)
    grads_ref[0] = grads
    acc[...] += matmul(grads, e_ref[...])

    @pl.when(step == pl.num_programs(0) - 1)
    def _():
        back_ref[...] = acc[...].astype(BF16)


def head_grads(logits, embedding, ids, norm, weight):
    chunks, tokens, _ = logits.shape
    vocab, width = embedding.shape
    column = pl.BlockSpec((tokens, 1), lambda step: (0, 0))
    tile = pl.BlockSpec((1, tokens, CHUNK), lambda step: (step, 0, 0))
    return pl.pallas_call(
        head_grads_body,
        grid=(chunks,),
        out_shape=(
            jax.ShapeDtypeStruct(logits.shape, BF16),
            jax.ShapeDtypeStruct((tokens, width), BF16),
        ),
        in_specs=[
            tile, pl.BlockSpec((CHUNK, width), lambda step: (step, 0)), column, column, column
        ],
        out_specs=(tile, pl.BlockSpec((tokens, width), lambda step: (0, 0))),
        scratch_shapes=[pltpu.VMEM((tokens, width), F32)],
        compiler_params=pltpu.CompilerParams(vmem_limit_bytes=40 * 2**20),
        cost_estimate=pl.CostEstimate(
            flops=2 * tokens * vocab * width,
            bytes_accessed=6 * tokens * vocab + 2 * vocab * width,
            transcendentals=tokens * vocab,
        ),
    )(logits, embedding, ids, norm, weight)


BLOCK = 256


def masked_scores(queries, keys, slope, length, first):
    rows, cols = queries.shape[0], keys.shape[0]
    raw = matmul_t(queries, keys)
    i = first + lax.broadcasted_iota(jnp.int32, (rows, cols), 0)
    j = lax.broadcasted_iota(jnp.int32, (rows, cols), 1)
    scores = raw * HEAD_DIM ** (-0.5) - slope * (i - j).astype(F32)
    return jnp.where((j <= i) & (j < length), scores, NEG)


SMEM = pl.BlockSpec(memory_space=pltpu.SMEM)
VMEM = pl.BlockSpec(memory_space=pltpu.VMEM)


class TeamRows:
    def __init__(self, team, x_ref, full, stage, slots, own, ag_send, ag_recv, rs_send, rs_recv):
        self.team, self.count, self.me = team, team.count, team.me()
        self.x_ref, self.full, self.stage, self.slots, self.own = x_ref, full, stage, slots, own
        self.ag_sems, self.rs_sems = (ag_send, ag_recv), (rs_send, rs_recv)

    def shifted(self, step):
        return across(self.me, step)

    def peer(self, step):
        if self.team.square:
            return self.shifted(step)
        return lax.rem(self.me + 1 + step, self.count)

    def source(self, step):
        if self.team.square:
            return self.shifted(step)
        return lax.rem(self.me + self.count - 1 - step, self.count)

    def back_step(self, place):
        if self.team.square:
            flip_x = lax.rem(lax.rem(self.me, 2) + lax.rem(place, 2), 2)
            flip_y = lax.rem(lax.div(self.me, 2) + lax.div(place, 2), 2)
            return 2 * flip_y + flip_x - 1
        return lax.rem(place + self.count - 1 - self.me, self.count)

    def remote(self, number, peer, src, dst, sems):
        return pltpu.make_async_remote_copy(
            src_ref=src,
            dst_ref=dst,
            send_sem=sems[0].at[number],
            recv_sem=sems[1].at[number],
            device_id=self.team.device(peer),
            device_id_type=MESH,
        )

    def ag(self, number):
        if not self.team.square:
            return self.remote(
                number, self.peer(number), self.x_ref, self.full.at[self.me], self.ag_sems
            )
        half = self.x_ref.shape[0] // 2
        which = SQUARE_HALF[number]
        rows = pl.ds(which * half, half)
        peer = self.shifted(SQUARE_STEP[number])
        if number < 4:
            src, place = self.x_ref.at[rows], self.me
        else:
            place = self.shifted(number - 4)
            src = self.full.at[place, rows]
        return self.remote(number, peer, src, self.full.at[place, rows], self.ag_sems)

    def rs(self, step):
        return self.remote(
            step, self.peer(step), self.stage.at[self.peer(step)], self.slots.at[step], self.rs_sems
        )

    def send_rows(self):
        for number in (0, 2, 1, 3) if self.team.square else range(self.count - 1):
            self.ag(number).start()
        self.full[self.me] = self.x_ref[...]

    def pass_on(self):
        if self.team.square:
            for number in (0, 2):
                self.ag(number).wait_recv()
                self.ag(4 + number // 2).start()

    def wait_rows(self, step):
        if not self.team.square:
            self.ag(step).wait_recv()
            return
        for number, these in enumerate(((1,), (3,), (4, 5))):

            @pl.when(step == number)
            def _(these=these):
                for one in these:
                    self.ag(one).wait_recv()

    def each_arrival(self, work):
        work(self.me)
        self.pass_on()

        def one(step, carry):
            self.wait_rows(step)
            work(self.source(step))
            return carry

        lax.fori_loop(0, self.count - 1, one, 0)

    def each_arrival_and_back(self, term):
        self.own[...] = term(self.me)
        self.pass_on()

        def one(step, carry):
            self.wait_rows(step)
            place = self.source(step)
            self.stage[place] = term(place).astype(BF16)
            self.rs(self.back_step(place)).start()
            return carry

        lax.fori_loop(0, self.count - 1, one, 0)

    def finish(self, total_ref):
        pass_on(self.ends)
        finish_jobs(self.ends)
        for step in range(self.count - 1):
            self.rs(step).wait()
        total = self.own[...]
        for step in range(self.count - 1):
            total = total + self.slots[step].astype(F32)
        total_ref[...] = total
        for number in range(6 if self.team.square else self.count - 1):
            self.ag(number).wait_send()


def team_scratch(team, part, model):
    count = team.count
    dma = pltpu.SemaphoreType.DMA
    copies = 6 if team.square else count - 1
    return [
        pltpu.VMEM((count, part, model), BF16),
        pltpu.VMEM((count, part, model), BF16),
        pltpu.VMEM((count - 1, part, model), BF16),
        pltpu.VMEM((part, model), F32),
        dma((copies,)),
        dma((copies,)),
        dma((count - 1,)),
        dma((count - 1,)),
    ]


class LateDeal:
    def __init__(self, pair, landing, send_sem, recv_sem):
        self.pair, self.landing, self.sems = pair, landing, (send_sem, recv_sem)

    def other(self):
        return 1 - self.pair.me()

    def start(self, src):
        self.copy = send(self.pair, self.other(), 0, src, self.landing, *self.sems)

    def wait(self):
        self.copy.wait()


def team_call(body, team, ident, jobs, arrays, specs, outs, out_specs, scratch, pair=None, dealt=None, ahead=0):
    if pair is not None:
        outs, out_specs = tuple(outs) + (dealt,), tuple(out_specs) + (HBM,)
        scratch = list(scratch) + [pltpu.SemaphoreType.DMA((1,))] * 2
    part, model = arrays[0].shape
    count_in, count_out, riders = len(arrays), len(outs), len(jobs)
    own_scratch = team_scratch(team, part, model)

    def kernel(*refs):
        ins, refs = refs[:count_in], refs[count_in:]
        xs, refs = refs[:riders], refs[riders:]
        results, refs = refs[:count_out], refs[count_out:]
        landings, refs = refs[:riders], refs[riders:]
        rows = TeamRows(team, ins[0], *refs[: len(own_scratch)])
        refs = refs[len(own_scratch) :]
        mine, refs = refs[: len(scratch)], refs[len(scratch) :]
        greet([team] + job_groups(jobs) + ([] if pair is None else [pair]))
        rows.send_rows()
        parts = split_scratch(jobs, refs)

        def start(numbers):
            return [jobs[n].start(xs[n], landings[n], *parts[n]) for n in numbers]

        rows.landings = landings
        first = start(range(ahead if ahead else riders))
        if ahead:

            def ready():
                pass_on(first)
                finish_jobs(first)
                rows.ends = start(range(ahead, riders))

            rows.ready = ready
        else:
            rows.ends = first
        if pair is None:
            body(rows, ins, results, mine)
        else:
            body(rows, ins, results[:-1], mine[:-2], LateDeal(pair, results[-1], *mine[-2:]))

    out = pl.pallas_call(
        kernel,
        out_shape=tuple(outs) + tuple(job.out for job in jobs),
        in_specs=list(specs) + [job.in_spec for job in jobs],
        out_specs=tuple(out_specs) + tuple(job.out_spec for job in jobs),
        scratch_shapes=own_scratch + list(scratch) + [one for job in jobs for one in job.scratch],
        compiler_params=pltpu.CompilerParams(
            collective_id=ident, has_side_effects=True, vmem_limit_bytes=58 * 2**20
        ),
    )(*arrays, *[job.x for job in jobs])
    return out[:count_out], list(out[count_out:])


def part_rows(place, part):
    return pl.ds(pl.multiple_of(place * part, part), part)


def attend_body(rows, ins, outs, scratch):
    x_ref, length_ref, slope_ref, bias_ref, *weights = ins
    total_ref, full_out, q_ref, k_ref, v_ref, mixed_ref, lse_ref = outs
    full_sem, *buffers = scratch
    if not weights:
        *weights, sems = buffers
        rows.ready()
        copies = [
            pltpu.make_async_copy(rows.landings[n], weights[n], sems.at[n]) for n in range(2)
        ]
        for copy in copies:
            copy.start()
        for copy in copies:
            copy.wait()
    qk_ref, vo_ref = weights

    def weight(ref, n):
        block = ref[n]
        return block.reshape(-1, block.shape[-1])

    part = x_ref.shape[0]
    width = q_ref.shape[1]

    def project(place):
        at = part_rows(place, part)
        block = rows.full[place]
        q_ref[at, :] = (matmul_t(block, weight(qk_ref, 0)) + bias_ref[0:1, :]).astype(BF16)
        k_ref[at, :] = matmul_t(block, weight(qk_ref, 1)).astype(BF16)
        v_ref[at, :] = (matmul_t(block, weight(vo_ref, 0)) + bias_ref[1:2, :]).astype(BF16)

    rows.each_arrival(project)
    keep = pltpu.make_async_copy(rows.full, full_out, full_sem)
    keep.start()

    def one(turn, carry):
        step = lax.rem(2 * rows.count - 2 - turn, rows.count)
        place = rows.peer(step)
        for block in range(rows.count):

            @pl.when(place == block)
            def _(first=block * part, upto=(block + 1) * part):
                for head in range(width // HEAD_DIM):
                    lanes = slice(head * HEAD_DIM, (head + 1) * HEAD_DIM)
                    scores = masked_scores(
                        q_ref[first:upto, lanes], k_ref[:upto, lanes], slope_ref[head],
                        length_ref[0], first,
                    )
                    highest = jnp.max(scores, axis=-1, keepdims=True)
                    powers = jnp.exp(scores - highest)
                    total = jnp.sum(powers, axis=-1, keepdims=True)
                    probs = (powers * (1.0 / total)).astype(BF16)
                    mixed_ref[first:upto, lanes] = matmul(probs, v_ref[:upto, lanes]).astype(BF16)
                    lse_ref[head, first:upto, :] = highest + jnp.log(total)

        term = matmul(mixed_ref[part_rows(place, part), :], weight(vo_ref, 1))

        @pl.when(step < rows.count - 1)
        def _():
            rows.stage[place] = term.astype(BF16)
            rows.rs(step).start()

        @pl.when(step == rows.count - 1)
        def _():
            rows.own[...] = term

        return carry

    lax.fori_loop(0, rows.count, one, 0)
    rows.finish(total_ref)
    keep.wait()


HBM = pl.BlockSpec(memory_space=pl.ANY)


def attend(team, ident, jobs, x, length, slopes, bias, weights):
    part, model = x.shape
    seq = part * team.count
    width = bias.shape[1]
    scratch = [pltpu.SemaphoreType.DMA]
    if not weights:
        scratch += [pltpu.VMEM(job.out.shape, BF16) for job in jobs[:2]]
        scratch.append(pltpu.SemaphoreType.DMA((2,)))
    low = jax.ShapeDtypeStruct((seq, width), BF16)
    return team_call(
        attend_body, team, ident, jobs,
        [x, length, slopes, bias] + weights,
        [VMEM, SMEM, SMEM, VMEM] + [VMEM] * len(weights),
        (
            jax.ShapeDtypeStruct((part, model), F32),
            jax.ShapeDtypeStruct((team.count, part, model), BF16),
            low, low, low, low,
            jax.ShapeDtypeStruct((width // HEAD_DIM, seq, 1), F32),
        ),
        (VMEM, HBM, VMEM, VMEM, VMEM, VMEM, VMEM),
        scratch,
        ahead=0 if weights else 2,
    )


def attend_back_body(rows, ins, outs, scratch, late=None):
    gy_ref, length_ref, slope_ref, a_ref, qk_ref, vo_ref, q_ref, k_ref, v_ref, mixed_ref, lse_ref = ins
    total_ref, grads_ref, sums_ref = outs
    go, gq, gk, gv, gk_sum, gv_sum = scratch
    part = gy_ref.shape[0]
    seq, width = q_ref.shape
    heads = width // HEAD_DIM
    gk_sum[...] = jnp.zeros_like(gk_sum)
    gv_sum[...] = jnp.zeros_like(gv_sum)
    sums_ref[...] = jnp.zeros_like(sums_ref)

    def open_block(place):
        go[part_rows(place, part), :] = matmul_t(rows.full[place], vo_ref[1]).astype(BF16)

    rows.each_arrival(open_block)
    for block in reversed(range(rows.count)):
        first, upto = block * part, (block + 1) * part
        for head in range(heads):
            lanes = slice(head * HEAD_DIM, (head + 1) * HEAD_DIM)
            queries, grads = q_ref[first:upto, lanes], go[first:upto, lanes]
            keys, values = k_ref[:upto, lanes], v_ref[:upto, lanes]
            scores = masked_scores(queries, keys, slope_ref[head], length_ref[0], first)
            probs = jnp.exp(scores - lse_ref[head, first:upto, :])
            grad_probs = matmul_t(grads, values)
            inner = jnp.sum(probs * grad_probs, axis=-1, keepdims=True)
            grad_scores = (probs * (grad_probs - inner) * HEAD_DIM ** (-0.5)).astype(BF16)
            piece = matmul(grad_scores, keys)
            sums_ref[0:1, lanes] += jnp.sum(piece, axis=0, keepdims=True)
            gq[first:upto, lanes] = piece.astype(BF16)
            gk_sum[:upto, lanes] += outer_sum(grad_scores, queries)
            gv_sum[:upto, lanes] += outer_sum(probs.astype(BF16), grads)
        gk[first:upto, :] = gk_sum[first:upto, :].astype(BF16)
        gv[first:upto, :] = gv_sum[first:upto, :].astype(BF16)
        term = (
            matmul(gq[first:upto, :], qk_ref[0]) + matmul(gk[first:upto, :], qk_ref[1])
            + matmul(gv[first:upto, :], vo_ref[0])
        )

        @pl.when(rows.me != block)
        def _(block=block, term=term):
            rows.stage[block] = term.astype(BF16)
            rows.rs(rows.back_step(block)).start()

        @pl.when(rows.me == block)
        def _(term=term):
            rows.own[...] = term

    sums_ref[1:2, :] = jnp.sum(gv_sum[...], axis=0, keepdims=True)
    model = gy_ref.shape[1]
    grads_ref[3] = outer_sum(mixed_ref[...], rows.full[...].reshape(seq, model))
    grads_ref[0] = outer_sum(gq[...], a_ref[...])
    grads_ref[1] = outer_sum(gv[...], a_ref[...])
    grads_ref[2] = outer_sum(gk[...], a_ref[...])
    if late is not None:
        late.start(grads_ref.at[pl.ds(2 * late.other(), 2)])
    rows.finish(total_ref)
    if late is not None:
        late.wait()


def attend_back(team, ident, jobs, pair, gy, length, slopes, a, qk, vo, q, k, v, mixed, lse):
    part, model = gy.shape
    seq, width = q.shape
    return team_call(
        attend_back_body, team, ident, jobs,
        [gy, length, slopes, a, qk, vo, q, k, v, mixed, lse],
        [VMEM, SMEM, SMEM] + [VMEM] * 8,
        (
            jax.ShapeDtypeStruct((part, model), F32),
            jax.ShapeDtypeStruct((4, width, model), F32),
            jax.ShapeDtypeStruct((2, width), F32),
        ),
        (VMEM,) * 3,
        [pltpu.VMEM((seq, width), BF16)] * 4 + [pltpu.VMEM((seq, width), F32)] * 2,
        pair,
        jax.ShapeDtypeStruct((2, width, model), F32),
    )


GELU_A = 0.7978845608028654
GELU_B = 0.044715


def strip_rows(strips, which, first, size):
    length = strips[0].shape[1]
    return strips[first // length][which, first % length : first % length + size, :]


def feed_body(rows, ins, outs, scratch):
    x_ref, bias_ref, *strips = ins
    total_ref, full_out, before_ref = outs
    (full_sem,) = scratch
    part = x_ref.shape[0]
    units = bias_ref.shape[1]
    tile = min(units, BLOCK)

    def term(place):
        at = part_rows(place, part)
        block = rows.full[place]
        total = None
        for first in range(0, units, tile):
            lanes = slice(first, first + tile)
            before = matmul_t(block, strip_rows(strips, 0, first, tile)) + bias_ref[:, lanes]
            before_ref[at, lanes] = before
            bend = jnp.tanh(GELU_A * (before + GELU_B * before * before * before))
            active = (0.5 * before * (1.0 + bend)).astype(BF16)
            piece = matmul(active, strip_rows(strips, 1, first, tile))
            total = piece if total is None else total + piece
        return total

    rows.each_arrival_and_back(term)
    keep = pltpu.make_async_copy(rows.full, full_out, full_sem)
    keep.start()
    rows.finish(total_ref)
    keep.wait()


def feed(team, ident, jobs, x, strips, bias):
    part, model = x.shape
    units = bias.shape[1]
    return team_call(
        feed_body, team, ident, jobs,
        [x, bias] + strips,
        [VMEM] * (2 + len(strips)),
        (
            jax.ShapeDtypeStruct((part, model), F32),
            jax.ShapeDtypeStruct((team.count, part, model), BF16),
            jax.ShapeDtypeStruct((part * team.count, units), F32),
        ),
        (VMEM, HBM, VMEM),
        [pltpu.SemaphoreType.DMA],
    )


def feed_back_body(rows, ins, outs, scratch, late=None):
    gz_ref, c_ref, before_ref, *strips = ins
    total_ref, grads_ref, sums_ref = outs
    active, low = scratch
    part, model = gz_ref.shape
    seq = part * rows.count
    units = before_ref.shape[1]
    tile = min(units, BLOCK)
    sums_ref[...] = jnp.zeros_like(sums_ref)

    def term(place):
        at = part_rows(place, part)
        gz = rows.full[place]
        for first in range(0, units, tile):
            lanes = slice(first, first + tile)
            before = before_ref[at, lanes]
            square = before * before
            bend = jnp.tanh(GELU_A * before * (1.0 + GELU_B * square))
            half = 0.5 * (1.0 + bend)
            slope = half + 0.5 * before * (1.0 - bend * bend) * (
                GELU_A * (1.0 + 3.0 * GELU_B * square)
            )
            grad = matmul_t(gz, strip_rows(strips, 1, first, tile)) * slope
            sums_ref[:, lanes] += jnp.sum(grad, axis=0, keepdims=True)
            active[at, lanes] = (before * half).astype(BF16)
            low[at, lanes] = grad.astype(BF16)
        length = strips[0].shape[1]
        return sum(
            matmul(low[at, n * length : (n + 1) * length], strip[0])
            for n, strip in enumerate(strips)
        )

    rows.each_arrival_and_back(term)
    for first in range(0, units, tile):
        lanes = slice(first, first + tile)
        grads_ref[0, lanes, :] = outer_sum(low[:, lanes], c_ref[...])
        grads_ref[1, lanes, :] = outer_sum(active[:, lanes], rows.full[...].reshape(seq, model))
    if late is not None:
        late.start(grads_ref.at[late.other()])
    rows.finish(total_ref)
    if late is not None:
        late.wait()


def feed_back(team, ident, jobs, pair, gz, c, before, strips):
    part, model = gz.shape
    seq = part * team.count
    units = before.shape[1]
    return team_call(
        feed_back_body, team, ident, jobs,
        [gz, c, before] + strips,
        [VMEM] * (3 + len(strips)),
        (
            jax.ShapeDtypeStruct((part, model), F32),
            jax.ShapeDtypeStruct((2, units, model), F32),
            jax.ShapeDtypeStruct((1, units), F32),
        ),
        (VMEM,) * 3,
        [pltpu.VMEM((seq, units), BF16)] * 2,
        pair,
        jax.ShapeDtypeStruct((units, model), F32),
    )


def line_head_logits_body(
    group, x_ref, e_ref, ids_ref, logits_ref, full_out, stats_out,
    full, table, staged, top, total, pick, stats,
    ag_send, ag_recv, e_sem, out_sem, full_sem, st_send, st_recv,
):
    count, me = group.count, group.me()
    part = x_ref.shape[0]
    tiles = e_ref.shape[0] // CHUNK
    line = LineRows(group, x_ref, full, ag_send, ag_recv)
    greet([group])
    line.start()
    full[me] = x_ref[...]
    top[...] = jnp.full_like(top, NEG)
    total[...] = jnp.zeros_like(total)
    pick[...] = jnp.zeros_like(pick)

    def rows_of(tile):
        return pl.ds(pl.multiple_of(tile * CHUNK, CHUNK), CHUNK)

    def load(tile):
        return pltpu.make_async_copy(
            e_ref.at[rows_of(tile)], table.at[rows_of(tile)], e_sem.at[tile]
        )

    def leave(tile, place, slot):
        return pltpu.make_async_copy(
            staged.at[slot], logits_ref.at[tile, part_rows(place, part)], out_sem.at[slot]
        )

    for tile in range(tiles):
        load(tile).start()

    def work(place, first):
        at = part_rows(place, part)
        ids = ids_ref[at, :]

        def one(pair, carry):
            for slot in range(2):
                tile = 2 * pair + slot
                if first:
                    load(tile).wait()

                    @pl.when(pair > 0)
                    def _(slot=slot, tile=tile):
                        leave(tile, place, slot).wait()

                else:
                    leave(tile, place, slot).wait()
                logits = matmul_t(full[place], table[rows_of(tile), :])
                staged[slot] = logits
                leave(tile, place, slot).start()
                column = tile * CHUNK + lax.broadcasted_iota(jnp.int32, (part, CHUNK), 1)
                picked = jnp.where(column == ids, logits, 0.0)
                pieces = [logits[:, at : at + LANES] for at in range(0, CHUNK, LANES)]
                before = top[at, :]
                high = functools.reduce(jnp.maximum, pieces, before)
                sums = total[at, :] * jnp.exp(before - high)
                found = pick[at, :]
                for number, piece in enumerate(pieces):
                    sums = sums + jnp.exp(piece - high)
                    found = found + picked[:, number * LANES : (number + 1) * LANES]
                top[at, :] = high
                total[at, :] = sums
                pick[at, :] = found
            return carry

        lax.fori_loop(0, tiles // 2, one, 0)

    work(me, True)
    for step in range(1, count):
        line.step(step)

        @pl.when(me >= step)
        def _(step=step):
            work(me - step, False)

        @pl.when(me + step < count)
        def _(step=step):
            work(me + step, False)

    keep = pltpu.make_async_copy(full, full_out, full_sem)
    keep.start()
    tall = top[...].T
    high = jnp.max(tall, axis=0, keepdims=True)
    stats[me] = jnp.zeros(stats.shape[1:], F32)
    stats[me, 0:1, :] = high
    stats[me, 1:2, :] = jnp.sum(total[...].T * jnp.exp(tall - high), axis=0, keepdims=True)
    stats[me, 2:3, :] = jnp.sum(pick[...].T, axis=0, keepdims=True)
    copies = [
        send(group, peer, step, stats.at[me], stats.at[me], st_send, st_recv)
        for step, peer in enumerate(group.peers())
    ]
    for slot in range(2):
        leave(0, me, slot).wait()
    line.wait_sends()
    for copy in copies:
        copy.wait()
    stats_out[...] = stats[...]
    keep.wait()


def line_head_logits(group, ident, x, embedding, ids):
    part, width = x.shape
    vocab = embedding.shape[0]
    count = group.count
    tokens = part * count
    tiles = vocab // CHUNK
    assert tiles % 2 == 0
    dma = pltpu.SemaphoreType.DMA
    return pl.pallas_call(
        functools.partial(line_head_logits_body, group),
        out_shape=(
            jax.ShapeDtypeStruct((tiles, tokens, CHUNK), F32),
            jax.ShapeDtypeStruct((count, part, width), BF16),
            jax.ShapeDtypeStruct((count, 8, tokens), F32),
        ),
        in_specs=[VMEM, HBM, VMEM],
        out_specs=(HBM, HBM, VMEM),
        scratch_shapes=[
            pltpu.VMEM((count, part, width), BF16),
            pltpu.VMEM((vocab, width), BF16),
            pltpu.VMEM((2, part, CHUNK), F32),
            pltpu.VMEM((tokens, LANES), F32),
            pltpu.VMEM((tokens, LANES), F32),
            pltpu.VMEM((tokens, LANES), F32),
            pltpu.VMEM((count, 8, tokens), F32),
            dma((2 * count - 2,)),
            dma((2 * count - 2,)),
            dma((tiles,)),
            dma((2,)),
            dma,
            dma((count - 1,)),
            dma((count - 1,)),
        ],
        compiler_params=pltpu.CompilerParams(
            collective_id=ident, has_side_effects=True, vmem_limit_bytes=56 * 2**20
        ),
    )(x, embedding, ids)


def line_head_grads_body(
    group, logits_ref, e_ref, ids_ref, norm_ref, weight_ref, grads_ref, total_ref,
    terms, stage, land, table, staged, low, acc,
    rs_send, rs_recv, e_sem, in_sem, out_sem,
):
    count, me = group.count, group.me()
    part = terms.shape[1]
    tiles = e_ref.shape[0] // CHUNK
    line = LineSum(group, terms, stage, land, rs_send, rs_recv)
    greet([group])

    def rows_of(tile):
        return pl.ds(pl.multiple_of(tile * CHUNK, CHUNK), CHUNK)

    def load(tile):
        return pltpu.make_async_copy(
            e_ref.at[rows_of(tile)], table.at[rows_of(tile)], e_sem.at[tile]
        )

    def enter(tile, place, slot):
        return pltpu.make_async_copy(
            logits_ref.at[tile, part_rows(place, part)], staged.at[slot], in_sem.at[slot]
        )

    def leave(tile, place, slot):
        return pltpu.make_async_copy(
            low.at[:, pl.ds(slot * CHUNK, CHUNK)],
            grads_ref.at[tile, part_rows(place, part)],
            out_sem.at[slot],
        )

    for tile in range(tiles):
        load(tile).start()

    def work(place, fresh=False):
        at = part_rows(place, part)
        ids, norm, weight = ids_ref[at, :], norm_ref[at, :], weight_ref[at, :]
        for slot in range(2):
            enter(slot, place, slot).start()
        acc[...] = jnp.zeros_like(acc)

        def one(pair, carry):
            for slot in range(2):
                tile = 2 * pair + slot
                enter(tile, place, slot).wait()
                if fresh:
                    load(tile).wait()
                column = tile * CHUNK + lax.broadcasted_iota(jnp.int32, (part, CHUNK), 1)
                probs = jnp.exp(staged[slot] - norm)
                grads = (jnp.where(column == ids, probs - 1.0, probs) * weight).astype(BF16)

                @pl.when(pair > 0)
                def _(slot=slot, tile=tile):
                    leave(tile, place, slot).wait()

                low[:, slot * CHUNK : (slot + 1) * CHUNK] = grads
                leave(tile, place, slot).start()

                @pl.when(pair + 1 < tiles // 2)
                def _(slot=slot, tile=tile):
                    enter(tile + 2, place, slot).start()

            rows = pl.ds(pl.multiple_of(pair * 2 * CHUNK, 2 * CHUNK), 2 * CHUNK)
            acc[...] += matmul(low[...], table[rows, :])
            return carry

        lax.fori_loop(0, tiles // 2, one, 0)
        for slot in range(2):
            leave(0, place, slot).wait()
        terms[place] = acc[...].astype(BF16)

    for step in range(count - 1):

        @pl.when(me < count - 1 - step)
        def _(step=step):
            work(count - 1 - step, fresh=step == 0)

        if step == 0:

            @pl.when(me == count - 1)
            def _():
                work(0, fresh=True)

        @pl.when((me > step) & ((me < count - 1) | (step > 0)))
        def _(step=step):
            work(step)

        line.first(step)
        if step == 1:
            line.rest(0, near=True)
    work(me)
    line.rest(0, near=False)
    for step in range(1, count - 1):
        line.rest(step)
    line.finish(total_ref)


def line_head_grads(group, ident, logits, embedding, ids, norm, weight):
    tiles, tokens, _ = logits.shape
    vocab, width = embedding.shape
    count = group.count
    part = tokens // count
    dma = pltpu.SemaphoreType.DMA
    return pl.pallas_call(
        functools.partial(line_head_grads_body, group),
        out_shape=(
            jax.ShapeDtypeStruct(logits.shape, BF16),
            jax.ShapeDtypeStruct((part, width), F32),
        ),
        in_specs=[HBM, HBM, VMEM, VMEM, VMEM],
        out_specs=(HBM, VMEM),
        scratch_shapes=[
            pltpu.VMEM((count, part, width), BF16),
            pltpu.VMEM((2, count - 1, part, width), BF16),
            pltpu.VMEM((2, count - 1, part, width), BF16),
            pltpu.VMEM((vocab, width), BF16),
            pltpu.VMEM((2, part, CHUNK), F32),
            pltpu.VMEM((part, 2 * CHUNK), BF16),
            pltpu.VMEM((part, width), F32),
            dma((2, count - 1)),
            dma((2, count - 1)),
            dma((tiles,)),
            dma((2,)),
            dma((2,)),
        ],
        compiler_params=pltpu.CompilerParams(
            collective_id=ident, has_side_effects=True, vmem_limit_bytes=56 * 2**20
        ),
    )(logits, embedding, ids, norm, weight)


def per_device(
    mesh_shape,
    token_ids,
    target_ids,
    lengths,
    embedding,
    outer_gain,
    outer_bias,
    norm_gain,
    norm_bias,
    qkv_weight,
    qv_bias,
    out_weight,
    up_weight,
    up_bias,
    down_weight,
    row_bias,
):
    sections, groups, shards = (mesh_shape[name] for name in ("section", "dp", "tensor"))
    s, j, z = (lax.axis_index(name) for name in ("section", "dp", "tensor"))
    by_section = Group(("section",), (sections,))
    by_dp = Group(("dp",), (groups,))
    by_tensor = Group(("tensor",), (shards,))
    exchange = Exchanges()
    layers = sections
    vocab, width = embedding.shape
    seq = token_ids.shape[1]
    rows = token_ids.shape[0] * groups
    local_cols = qkv_weight.shape[-1]
    planes = rows == sections * shards and local_cols % (groups * HEAD_DIM) == 0
    by_dp.square = planes and groups == 4
    by_tensor.line = planes
    team = by_dp if planes else by_tensor
    cut = groups if planes else 1
    fan = shards if planes else 1
    halves = 2 if planes else 1
    part = seq // team.count
    cols = local_cols // cut
    hidden = up_weight.shape[-1] // cut
    strip = hidden // halves
    cut_index = j if planes else 0
    my_row = z * sections + s if planes else j * sections + s
    length = lax.dynamic_slice(lengths, (my_row,), (1,))
    token_count = jnp.sum(lengths).astype(F32)
    vocab_start = z * vocab

    def chosen_cols(array, size):
        return lax.dynamic_slice_in_dim(array, cut_index * size, size, array.ndim - 1).T

    def chosen_rows(array, size):
        return lax.dynamic_slice_in_dim(array, cut_index * size, size, 0)

    def pad_rows(array, count):
        return jnp.pad(array, ((0, count - array.shape[0]), (0, width - array.shape[1])))

    sides = jnp.stack(
        [
            jnp.concatenate(
                [
                    chosen_cols(qkv_weight[0, 0], cols),
                    chosen_cols(qkv_weight[0, 2], cols),
                    chosen_cols(up_weight[0], hidden),
                ]
            ),
            jnp.concatenate(
                [
                    chosen_cols(qkv_weight[0, 1], cols),
                    chosen_rows(out_weight[0], cols),
                    chosen_rows(down_weight[0], hidden),
                ]
            ),
        ]
    )
    qv_piece = lax.dynamic_slice_in_dim(qv_bias[0], cut_index * cols, cols, 1)
    up_piece = lax.dynamic_slice_in_dim(up_bias[0], cut_index * hidden, hidden, 0)
    small = jnp.concatenate(
        [outer_gain, outer_bias, norm_gain[0], norm_bias[0], row_bias[0]]
    )
    bias_piece = jnp.concatenate([qv_piece[0], qv_piece[1], up_piece])
    bias_piece = jnp.pad(bias_piece, (0, -bias_piece.shape[0] % 1024)).reshape(-1, 128)

    def gather(group, x):
        return Job("gather", [group], x)

    def deal(group, x, axis=0):
        return Job("deal", [group], x, axis)

    def own_and_dealt(x, dealt, place, axis=0):
        own = lax.dynamic_index_in_dim(x, place, axis, keepdims=False).astype(F32)
        return own + jnp.sum(dealt.astype(F32), axis=0)

    if planes:
        other, both, small_all, bias_all = exchange(
            deal(by_section, sides),
            gather(by_dp, jnp.stack([token_ids, target_ids])),
            gather(by_section, small),
            gather(Group(("section", "tensor"), (sections, shards)), bias_piece),
        )
        bias_all = bias_all.reshape(sections, shards, -1)
        own_side = lax.dynamic_index_in_dim(sides, s, 0, keepdims=False)
        side = [jnp.where(s == l, own_side, other[0]) for l in range(layers)]
        both = jnp.swapaxes(both, 0, 1).reshape(2, shards, sections, groups, part)
        both = lax.dynamic_index_in_dim(
            lax.dynamic_index_in_dim(both, s, 2, keepdims=False), j, 2, keepdims=False
        )
        ids, targets = both[0].reshape(-1), both[1].reshape(-1)
        group_lengths = lax.dynamic_index_in_dim(
            lengths.reshape(shards, sections), s, 1, keepdims=False
        )
        places = jnp.broadcast_to(j * part + jnp.arange(part), (shards, part))
        valid = (places < group_lengths[:, None]).reshape(-1)
    else:
        sides_all, small_all, bias_all = exchange(
            gather(by_section, sides), gather(by_section, small), gather(by_section, bias_piece)
        )
        bias_all = bias_all.reshape(sections, 1, -1)
        ids, targets = token_ids[s], target_ids[s]
        valid = jnp.arange(seq) < lengths[my_row]

    outer_gains = [small_all[l, 0] for l in range(layers)]
    outer_offsets = [small_all[l, 1] for l in range(layers)]
    params = []
    for l in range(layers):
        biases = [bias_all[l, :, n * cols : (n + 1) * cols].reshape(-1) for n in range(2)]
        units = bias_all[l, :, 2 * cols : 2 * cols + hidden].reshape(fan, halves, strip)
        params.append(
            dict(
                gains=small_all[l, 2:4],
                offsets=small_all[l, 4:6],
                row_bias=small_all[l, 6:8],
                bias=jnp.stack(biases),
                up_bias=jnp.swapaxes(units, 0, 1).reshape(1, -1),
            )
        )
        if not planes:
            block = sides_all[l]
            params[l].update(
                qk=block[:, :cols],
                vo=block[:, cols : 2 * cols],
                strips=[block[:, 2 * cols :]],
            )
    head_number = (
        (jnp.arange(fan)[:, None] if planes else z) * (local_cols // HEAD_DIM)
        + cut_index * (cols // HEAD_DIM)
        + jnp.arange(cols // HEAD_DIM)
    ).reshape(-1)
    slopes = jnp.exp2(-8.0 * (head_number + 1).astype(F32) / HEADS)

    def attn_jobs(l):
        if not planes or l >= layers:
            return []
        return [
            Job("spread", [by_tensor, by_section], side[l][first : first + cols])
            for first in (0, cols)
        ]

    def feed_jobs(l, n):
        if not planes or l >= layers:
            return []
        first = 2 * cols + n * strip
        return [Job("spread", [by_tensor, by_section], side[l][first : first + strip])]

    def take_attn(l, got):
        if got:
            params[l]["qk"], params[l]["vo"] = (
                one.reshape(2, fan * cols, width) for one in got
            )

    def take_feed(l, got):
        if got:
            params[l]["strips"] = [one.reshape(2, fan * strip, width) for one in got]

    def ident(kind, jobs):
        return exchange.ident((kind,) + tuple(job.key() for job in jobs))

    local_ids = ids - vocab_start
    inside = (local_ids >= 0) & (local_ids < vocab)
    looked = jnp.where(
        inside[:, None], jnp.take(embedding, jnp.clip(local_ids, 0, vocab - 1), axis=0), 0
    )
    group_part = looked.shape[0] // shards
    (x,) = exchange(Job("reduce", [by_tensor], looked.reshape(shards, group_part, width)))
    h = layer_norm(x, outer_gains[0], outer_offsets[0])

    kept = []
    strips = []
    for l, p in enumerate(params):
        jobs = (attn_jobs(l) + feed_jobs(l, 0) if l == 0 else []) + feed_jobs(l, 1)
        normed = layer_norm(h, p["gains"][0], p["offsets"][0]).astype(BF16)
        (total, normed, q, k, v, mixed, lse), got = attend(
            team, ident("attend", jobs), jobs, normed, length, slopes, p["bias"],
            [p["qk"], p["vo"]] if "qk" in p else [],
        )
        if "qk" not in p:
            take_attn(l, got[:2])
            got = got[2:]
        take_feed(l, strips + got)
        middle = h + total + p["row_bias"][0]
        jobs = attn_jobs(l + 1) + feed_jobs(l + 1, 0)
        second = layer_norm(middle, p["gains"][1], p["offsets"][1]).astype(BF16)
        (total, second, before), got = feed(
            team, ident("feed", jobs), jobs, second, p["strips"], p["up_bias"]
        )
        take_attn(l + 1, got[:2])
        strips = got[2:]
        kept.append((h, normed.reshape(seq, width), q, k, v, mixed, lse, middle, second, before))
        h = middle + total + p["row_bias"][1]

    final = layer_norm(h, outer_gains[-1], outer_offsets[-1]).astype(BF16)
    columns_of = (targets - vocab_start)[:, None]
    if planes:
        logits, final, stats = line_head_logits(
            by_tensor, exchange.ident("head logits"), final, embedding, columns_of
        )
        final = final.reshape(-1, width)
    else:
        (final,) = exchange(gather(by_tensor, final))
        final = final.reshape(-1, width)
        logits, tops, totals, picks = head_logits(final, embedding, columns_of)
        top = jnp.max(tops, axis=1)
        total = jnp.sum(totals * jnp.exp(tops - top[:, None]), axis=1)
        pick = jnp.sum(picks, axis=1)
        (stats,) = exchange(
            gather(by_tensor, jnp.pad(jnp.stack([top, total, pick]), ((0, 5), (0, 0))))
        )
    tokens = final.shape[0]
    top_all = jnp.max(stats[:, 0], axis=0)
    log_norm = top_all + jnp.log(jnp.sum(stats[:, 1] * jnp.exp(stats[:, 0] - top_all), axis=0))
    terms = jnp.where(valid, log_norm - jnp.sum(stats[:, 2], axis=0), 0.0)
    loss_part = jnp.sum(
        lax.dynamic_index_in_dim(terms.reshape(shards, -1), z, 0, keepdims=False)
    )
    row_weight = jnp.where(valid, 1.0 / token_count, 0.0)
    if planes:
        grad_logits, grad_final = line_head_grads(
            by_tensor, exchange.ident("head grads"), logits, embedding, columns_of,
            log_norm[:, None], row_weight[:, None],
        )
    else:
        grad_logits, back = head_grads(
            logits, embedding, columns_of, log_norm[:, None], row_weight[:, None]
        )
        (grad_final,) = exchange(
            Job("reduce", [by_tensor], back.reshape(shards, group_part, width))
        )
    _, final_back = jax.vjp(layer_norm, h, outer_gains[-1], outer_offsets[-1])
    grad, final_gain, final_offset = final_back(grad_final)

    def section_sums(pair, got):
        out = []
        for one, dealt in zip(pair, got):
            low = own_and_dealt(one, dealt, s).astype(BF16)
            if one.ndim == 4:
                out.append(low.reshape(low.shape[0], fan, cols, width))
            else:
                out.append(low.reshape(halves, fan, strip, width))
        return out

    def tensor_jobs(lows):
        return [deal(by_tensor, low, 1) for low in lows]

    def tensor_sums(lows, got):
        return [
            own_and_dealt(low, dealt, z, 1).astype(BF16) for low, dealt in zip(lows, got)
        ]

    def spread_jobs(pieces):
        return [Job("spread", [by_dp, by_section], piece) for piece in pieces]

    small_rows = [None] * layers
    pairs = [None] * layers
    attn_low, attn_done, feed_done = ([None] * layers for _ in range(3))
    for l in reversed(range(layers)):
        p = params[l]
        section_in, normed, q, k, v, mixed, lse, middle, second, before = kept[l]
        pair = by_section if planes else None
        late = planes and l + 1 < layers
        jobs = tensor_jobs(attn_low[l + 1]) if late else []
        (total, g_feed, up_sum, *dealt), got = feed_back(
            team, ident("feed back", jobs), jobs, pair, grad.astype(BF16),
            second.reshape(seq, width), before, p["strips"],
        )
        if late:
            attn_done[l + 1] = tensor_sums(attn_low[l + 1], got)
        if planes:
            feed_low = section_sums([g_feed], [one[None] for one in dealt])
        _, norm_back = jax.vjp(layer_norm, middle, p["gains"][1], p["offsets"][1])
        grad_mid, gain_two, offset_two = norm_back(total)
        grad_mid = grad_mid + grad
        jobs = tensor_jobs(feed_low) if planes else []
        (total, g_attn, qv_sum, *dealt), got = attend_back(
            team, ident("attend back", jobs), jobs, pair, grad_mid.astype(BF16), length, slopes,
            normed, p["qk"], p["vo"], q, k, v, mixed, lse,
        )
        g_attn = g_attn.reshape((2, 2) + g_attn.shape[1:])
        if planes:
            feed_done[l] = tensor_sums(feed_low, got)
            attn_low[l] = section_sums([g_attn], [one[None] for one in dealt])
        _, norm_back = jax.vjp(layer_norm, section_in, p["gains"][0], p["offsets"][0])
        grad_in, gain_one, offset_one = norm_back(total)
        bias_two = jnp.sum(grad, axis=0)
        grad = grad_in + grad_mid
        pairs[l] = (g_attn, g_feed)

        def placed(values, size):
            out = jnp.zeros((fan if planes else shards, cut, size), F32)
            at = (0, j, 0) if planes else (z, 0, 0)
            return lax.dynamic_update_slice(out, values.reshape(fan, 1, size), at).reshape(
                -1, width
            )

        units = jnp.swapaxes(up_sum.reshape(halves, fan, strip), 0, 1)
        small_rows[l] = [
            gain_one[None],
            gain_two[None],
            offset_one[None],
            offset_two[None],
            jnp.sum(grad_mid, axis=0)[None],
            bias_two[None],
            placed(qv_sum[0], cols),
            placed(qv_sum[1], cols),
            placed(units, hidden),
        ]

    _, embed_back = jax.vjp(layer_norm, x, outer_gains[0], outer_offsets[0])
    grad_rows, embed_gain, embed_offset = embed_back(grad)
    packed = jnp.concatenate(
        [row for l in range(layers) for row in small_rows[l]]
        + [embed_gain[None], final_gain[None], embed_offset[None], final_offset[None]]
        + [jnp.broadcast_to(loss_part, (1, width))]
    )
    used = packed.shape[0]
    packed = jnp.pad(packed, ((0, -used % 8), (0, 0)))
    jobs = [Job("gather", [Group(("section", "tensor"), (sections, shards))], packed, late=True)]
    if planes:
        jobs += spread_jobs(attn_done[1] + feed_done[1] + feed_done[0])
        jobs += [Job("deal", [by_tensor], low, 1, late=True) for low in attn_low[0]]
    embed_sum, packed, *got = table_sum(
        by_section, by_dp, by_tensor, jobs, grad_logits, ids[None, :] - vocab_start, final,
        grad_rows.astype(BF16), exchange.ident("table"),
    )
    packed = jnp.sum(packed, axis=0)
    jobs = [gather(by_dp, packed)]
    if planes:
        spread_one = got[:2]
        jobs += spread_jobs(tensor_sums(attn_low[0], got[3:]))
    packed, *spread_zero = exchange(*jobs)
    packed = jnp.sum(packed, axis=0)
    if planes:
        spread_zero.append(got[2])
        attn_sum, feed_sum = (
            jnp.where(s == 0, zero, one) for zero, one in zip(spread_zero, spread_one)
        )
    else:
        chosen = [
            lax.dynamic_index_in_dim(
                lax.psum(jnp.stack([pair[n] for pair in pairs]), ("section", "dp")),
                s, 0, keepdims=False,
            )
            for n in range(2)
        ]
        attn_sum = chosen[0][:, None]
        feed_sum = chosen[1][:, None, None]
    embed_sum = embed_sum.reshape(vocab, width).astype(F32)
    per_layer = (used - 5) // layers
    mine = lax.dynamic_slice_in_dim(packed, s * per_layer, per_layer, 0)
    qv_rows = mine[6:8].reshape(2, -1)
    ff_row = mine[8:].reshape(-1)
    grad_qv = lax.dynamic_slice_in_dim(qv_rows, z * local_cols, local_cols, 1)
    grad_up_bias = lax.dynamic_slice_in_dim(ff_row, z * hidden * cut, hidden * cut, 0)
    base = per_layer * layers
    grad_outer_gain = lax.dynamic_slice_in_dim(packed, base + s, 1, 0)
    grad_outer_bias = lax.dynamic_slice_in_dim(packed, base + 2 + s, 1, 0)
    loss = packed[base + 4, 0] / token_count

    def columns(array):
        return array.astype(F32).reshape(-1, width).T

    grad_qkv = jnp.stack(
        [columns(attn_sum[0, :, 0]), columns(attn_sum[1, :, 0]), columns(attn_sum[0, :, 1])]
    )
    grad_out_mat = attn_sum[1, :, 1].astype(F32).reshape(-1, width)
    grad_up = columns(feed_sum[0])
    grad_down = feed_sum[1].astype(F32).reshape(-1, width)
    return (
        loss,
        embed_sum,
        grad_outer_gain,
        grad_outer_bias,
        mine[0:2][None],
        mine[2:4][None],
        grad_qkv[None],
        grad_qv[None],
        grad_out_mat[None],
        grad_up[None],
        grad_up_bias[None],
        grad_down[None],
        mine[4:6][None],
    )


def solution(mesh):
    return jax.shard_map(
        functools.partial(per_device, dict(mesh.shape)),
        mesh=mesh,
        in_specs=(
            P("dp", None),
            P("dp", None),
            P(),
            P("tensor", None),
            P("section", None),
            P("section", None),
            P("section", None, None),
            P("section", None, None),
            P("section", None, None, "tensor"),
            P("section", None, "tensor"),
            P("section", "tensor", None),
            P("section", None, "tensor"),
            P("section", "tensor"),
            P("section", "tensor", None),
            P("section", None, None),
        ),
        out_specs=(
            P(),
            P("tensor", None),
            P("section", None),
            P("section", None),
            P("section", None, None),
            P("section", None, None),
            P("section", None, None, "tensor"),
            P("section", None, "tensor"),
            P("section", "tensor", None),
            P("section", None, "tensor"),
            P("section", "tensor"),
            P("section", "tensor", None),
            P("section", None, None),
        ),
        check_vma=False,
    )
```

```python
import functools
import math

import jax
import jax.numpy as jnp
from jax import lax
from jax.experimental import pallas as pl
from jax.experimental.pallas import tpu as pltpu
from jax.sharding import PartitionSpec as P

HEADS = 16
HEAD_DIM = 64
EPS = 1e-05
NEG = -1e30
MESH = pl.DeviceIdType.MESH
F32 = jnp.float32
BF16 = jnp.bfloat16


def matmul(former, latter):
    return jnp.dot(former, latter, preferred_element_type=F32)


def matmul_t(former, latter):
    return lax.dot_general(
        former, latter, (((1,), (1,)), ((), ())), preferred_element_type=F32
    )


def outer_sum(former, latter):
    return lax.dot_general(
        former, latter, (((0,), (0,)), ((), ())), preferred_element_type=F32
    )


def layer_norm(inputs, weight, offset):
    centre = inputs - jnp.mean(inputs, axis=-1, keepdims=True)
    spread = jnp.mean(centre * centre, axis=-1, keepdims=True)
    return centre * lax.rsqrt(spread + EPS) * weight + offset


def gelu_tanh(inputs):
    return jax.nn.gelu(inputs, approximate=True)


class Group:
    def __init__(self, axes, sizes, square=False, line=False):
        self.square = square
        self.line = line
        self.axes = axes
        self.sizes = sizes
        self.count = math.prod(sizes)

    def me(self):
        place = 0
        for axis, size in zip(self.axes, self.sizes):
            place = place * size + lax.axis_index(axis)
        return place

    def device(self, place):
        spot = {}
        for axis, size in reversed(list(zip(self.axes, self.sizes))):
            spot[axis] = lax.rem(place, size)
            place = lax.div(place, size)
        return spot

    def peers(self):
        me = self.me()
        return [lax.rem(me + step, self.count) for step in range(1, self.count)]


def greet(groups):
    barrier = pltpu.get_barrier_semaphore()
    total = 0
    for group in groups:
        for peer in group.peers():
            pl.semaphore_signal(
                barrier, inc=1, device_id=group.device(peer), device_id_type=MESH
            )
            total += 1
    pl.semaphore_wait(barrier, total)


def send(group, peer, step, src, dst, send_sem, recv_sem):
    copy = pltpu.make_async_remote_copy(
        src_ref=src,
        dst_ref=dst,
        send_sem=send_sem.at[step],
        recv_sem=recv_sem.at[step],
        device_id=group.device(peer),
        device_id_type=MESH,
    )
    copy.start()
    return copy


def tie(*arrays):
    return lax.optimization_barrier(arrays)


class LineRows:
    def __init__(self, group, x, full, send_sem, recv_sem):
        self.group, self.count, self.me = group, group.count, group.me()
        self.x, self.full, self.sems = x, full, (send_sem, recv_sem)

    def copy(self, up, step):
        place = self.me - step if up else self.me + step
        place = jnp.clip(place, 0, self.count - 1)
        number = step if up else self.count - 1 + step
        src = self.x if step == 0 else self.full.at[place]
        return pltpu.make_async_remote_copy(
            src_ref=src,
            dst_ref=self.full.at[place],
            send_sem=self.sems[0].at[number],
            recv_sem=self.sems[1].at[number],
            device_id=self.group.device(
                jnp.clip(self.me + 1 if up else self.me - 1, 0, self.count - 1)
            ),
            device_id_type=MESH,
        )

    def leaves(self, up, step):
        if up:
            return (self.me - step >= 0) & (self.me < self.count - 1)
        return (self.me + step < self.count) & (self.me > 0)

    def arrives(self, up, step):
        return self.me - 1 - step >= 0 if up else self.me + 1 + step < self.count

    def start(self):
        for up in (True, False):

            @pl.when(self.leaves(up, 0))
            def _(up=up):
                self.copy(up, 0).start()

    def step(self, step):
        for up in (True, False):

            @pl.when(self.arrives(up, step - 1))
            def _(up=up):
                self.copy(up, step - 1).wait_recv()

            if step < self.count - 1:

                @pl.when(self.leaves(up, step))
                def _(up=up):
                    self.copy(up, step).start()

    def wait_sends(self):
        for step in range(self.count - 1):
            for up in (True, False):

                @pl.when(self.leaves(up, step))
                def _(up=up, step=step):
                    self.copy(up, step).wait_send()

    def finish(self):
        for step in range(1, self.count):
            self.step(step)
        self.wait_sends()


class LineSum:
    def __init__(self, group, x, stage, land, send_sem, recv_sem):
        self.group, self.count, self.me = group, group.count, group.me()
        self.x, self.stage, self.land, self.sems = x, stage, land, (send_sem, recv_sem)

    def copy(self, up, step):
        side = 0 if up else 1
        return pltpu.make_async_remote_copy(
            src_ref=self.stage.at[side, step],
            dst_ref=self.land.at[side, step],
            send_sem=self.sems[0].at[side, step],
            recv_sem=self.sems[1].at[side, step],
            device_id=self.group.device(
                jnp.clip(self.me + 1 if up else self.me - 1, 0, self.count - 1)
            ),
            device_id_type=MESH,
        )

    def leaves(self, up, step):
        return self.me < self.count - 1 - step if up else self.me > step

    def behind(self, up):
        return self.me > 0 if up else self.me < self.count - 1

    def first(self, step):
        for up in (True, False):
            place = self.count - 1 - step if up else step
            side = 0 if up else 1

            @pl.when(self.leaves(up, step) & jnp.logical_not(self.behind(up)))
            def _(up=up, place=place, side=side):
                self.stage[side, step] = self.x[place]
                self.copy(up, step).start()

    def rest(self, step, near=None):
        for up in (True, False):
            place = self.count - 1 - step if up else step
            side = 0 if up else 1
            here = self.leaves(up, step) & self.behind(up)
            if near is not None:
                by_end = self.me == (1 if up else self.count - 2)
                here = here & (by_end if near else jnp.logical_not(by_end))

            @pl.when(here)
            def _(up=up, place=place, side=side):
                self.copy(up, step).wait_recv()
                total = self.x[place].astype(F32) + self.land[side, step].astype(F32)
                self.stage[side, step] = total.astype(self.stage.dtype)
                self.copy(up, step).start()

    def finish(self, out):
        out[...] = self.x[self.me].astype(F32)
        for up in (True, False):
            side = 0 if up else 1
            for step in range(self.count - 1):

                @pl.when(self.behind(up) & (self.me == (self.count - 1 - step if up else step)))
                def _(up=up, step=step, side=side):
                    self.copy(up, step).wait_recv()
                    out[...] += self.land[side, step].astype(F32)

        for up in (True, False):
            for step in range(self.count - 1):

                @pl.when(self.leaves(up, step))
                def _(up=up, step=step):
                    self.copy(up, step).wait_send()


class Job:
    def __init__(self, kind, groups, x, axis=0, late=False):
        self.late = late
        self.kind, self.groups, self.x, self.axis = kind, groups, x, axis
        count = groups[0].count
        rest = x.shape[:axis] + x.shape[axis + 1 :]
        dma = pltpu.SemaphoreType.DMA
        self.in_spec = pl.BlockSpec(memory_space=pl.ANY)
        self.out_spec = pl.BlockSpec(memory_space=pl.ANY)
        self.scratch = [dma((count - 1,)), dma((count - 1,)), dma]
        if kind in ("gather", "spread"):
            self.in_spec = pl.BlockSpec(memory_space=pltpu.VMEM)
        if kind == "gather" and groups[0].line:
            self.scratch = [dma((2 * count - 2,)), dma((2 * count - 2,)), dma]
        if kind == "gather":
            self.out = jax.ShapeDtypeStruct((count,) + x.shape, x.dtype)
        elif kind == "spread":
            self.out = jax.ShapeDtypeStruct((groups[1].count, count) + x.shape, x.dtype)
            copies = 7 if groups[0].square else count
            if groups[0].square:
                self.scratch = [dma((6,)), dma((6,)), dma]
            self.scratch += [dma((copies,)), dma((copies,))]
        elif kind == "deal":
            self.out = jax.ShapeDtypeStruct((count - 1,) + rest, x.dtype)
        else:
            self.out = jax.ShapeDtypeStruct(rest, F32)
            self.out_spec = pl.BlockSpec(memory_space=pltpu.VMEM)
            if groups[0].line:
                self.in_spec = pl.BlockSpec(memory_space=pltpu.VMEM)
                self.scratch = [dma((2, count - 1)), dma((2, count - 1)), dma]
                self.scratch += [pltpu.VMEM((2, count - 1) + rest, x.dtype)] * 2
            else:
                self.scratch += [
                    pltpu.VMEM(rest, x.dtype), pltpu.VMEM((count - 1,) + rest, x.dtype)
                ]

    def key(self):
        return (self.kind, tuple(g.axes for g in self.groups), self.x.shape, str(self.x.dtype), self.axis)

    def start(self, x, out, send_sem, recv_sem, own_sem, *more):
        group = self.groups[0]
        me = group.me()
        peers = list(enumerate(group.peers()))

        def block(place):
            return x.at[(slice(None),) * self.axis + (place,)]

        if self.kind == "gather" and group.line:
            line = LineRows(group, x, out, send_sem, recv_sem)
            line.start()
            own = pltpu.make_async_copy(x, out.at[me], own_sem)
            own.start()

            def finish():
                line.finish()
                own.wait()

        elif self.kind == "reduce" and group.line:
            line = LineSum(group, x, *more, send_sem, recv_sem)
            for step in range(group.count - 1):
                line.first(step)

            def finish():
                for step in range(group.count - 1):
                    line.rest(step)
                line.finish(out)

        elif self.kind == "gather":
            copies = [send(group, p, k, x, out.at[me], send_sem, recv_sem) for k, p in peers]
            own = pltpu.make_async_copy(x, out.at[me], own_sem)
            own.start()

            def finish():
                for copy in copies + [own]:
                    copy.wait()

        elif self.kind == "spread" and group.square:
            pair = self.groups[1]
            side = pair.me()
            fw_send, fw_recv = more
            size = self.x.shape[0] // 2
            near = [across(me, 0), across(me, 1)]

            def copy_of(number):
                at = pl.ds(SQUARE_HALF[number] * size, size)
                place = me if number < 4 else near[number - 4]
                dst = out.at[side, place, at]
                src = x.at[at] if number < 4 else dst
                copy = pltpu.make_async_remote_copy(
                    src_ref=src, dst_ref=dst, send_sem=send_sem.at[number],
                    recv_sem=recv_sem.at[number], device_id=group.device(near[SQUARE_STEP[number]]),
                    device_id_type=MESH,
                )
                origin = near[SQUARE_STEP[number]] if number < 4 else across(me, 2)
                return copy, out.at[side, origin, at]

            copies = [copy_of(number) for number in range(6)]
            for number in (0, 2, 1, 3):
                copies[number][0].start()
            passed = [send(pair, 1 - side, 6, x, out.at[side, me], fw_send, fw_recv)]
            own = pltpu.make_async_copy(x, out.at[side, me], own_sem)
            own.start()

            def arrived(number):
                copy, landed = copies[number]
                copy.wait_recv()
                passed.append(send(pair, 1 - side, number, landed, landed, fw_send, fw_recv))

            def middle():
                for number in (0, 2):
                    copies[number][0].wait_recv()
                    copies[4 + number // 2][0].start()
                    landed = copies[number][1]
                    passed.append(send(pair, 1 - side, number, landed, landed, fw_send, fw_recv))

            def finish():
                for number in (1, 3, 4, 5):
                    arrived(number)
                for copy in passed:
                    copy.wait()
                for copy, _ in copies:
                    copy.wait_send()
                own.wait()

            return middle, finish

        elif self.kind == "spread":
            pair = self.groups[1]
            side = pair.me()
            fw_send, fw_recv = more
            home = out.at[side, me]
            copies = [send(group, p, k, x, home, send_sem, recv_sem) for k, p in peers]
            last = group.count - 1
            passed = [send(pair, 1 - side, last, x, home, fw_send, fw_recv)]
            own = pltpu.make_async_copy(x, home, own_sem)
            own.start()

            def finish():
                for k, copy in enumerate(copies):
                    copy.wait_recv()
                    place = out.at[side, lax.rem(me + group.count - 1 - k, group.count)]
                    passed.append(send(pair, 1 - side, k, place, place, fw_send, fw_recv))
                for copy in passed:
                    copy.wait()
                for copy in copies:
                    copy.wait_send()
                own.wait()

        elif self.kind == "deal":
            copies = [send(group, p, k, block(p), out.at[k], send_sem, recv_sem) for k, p in peers]

            def finish():
                for copy in copies:
                    copy.wait()

        else:
            kept, slots = more
            copies = [send(group, p, k, block(p), slots.at[k], send_sem, recv_sem) for k, p in peers]
            own = pltpu.make_async_copy(block(me), kept, own_sem)
            own.start()

            def finish():
                own.wait()
                for copy in copies:
                    copy.wait()
                total = kept[...].astype(F32)
                for k in range(group.count - 1):
                    total = total + slots[k].astype(F32)
                out[...] = total

        return None, finish


def pass_on(ends):
    for middle, _ in ends:
        if middle is not None:
            middle()


def finish_jobs(ends):
    for _, finish in ends:
        finish()


def job_groups(jobs):
    return [group for job in jobs for group in job.groups]


def split_scratch(jobs, scratch):
    parts, at = [], 0
    for job in jobs:
        parts.append(scratch[at : at + len(job.scratch)])
        at += len(job.scratch)
    return parts


def exchange_body(jobs, *refs):
    count = len(jobs)
    greet(job_groups(jobs))
    parts = split_scratch(jobs, refs[2 * count :])
    ends = [
        job.start(refs[n], refs[count + n], *parts[n]) for n, job in enumerate(jobs)
    ]
    pass_on(ends)
    finish_jobs(ends)


class Exchanges:
    def __init__(self):
        self.idents = {}

    def ident(self, key):
        return self.idents.setdefault(key, len(self.idents))

    def __call__(self, *jobs):
        jobs = list(jobs)
        return pl.pallas_call(
            functools.partial(exchange_body, jobs),
            out_shape=tuple(job.out for job in jobs),
            in_specs=[job.in_spec for job in jobs],
            out_specs=tuple(job.out_spec for job in jobs),
            scratch_shapes=[one for job in jobs for one in job.scratch],
            compiler_params=pltpu.CompilerParams(
                collective_id=self.ident(tuple(job.key() for job in jobs)),
                has_side_effects=True,
                vmem_limit_bytes=32 * 2**20,
            ),
        )(*[job.x for job in jobs])


CHUNK = 512


def start_rows(group, x_ref, full, send_sem, recv_sem):
    me = group.me()
    full[me] = x_ref[...]
    return [
        send(group, peer, step, x_ref, full.at[me], send_sem, recv_sem)
        for step, peer in enumerate(group.peers())
    ]


def table_body(
    by_section, by_dp, by_tensor, jobs, g_ref, ids_ref, u_ref, gx_ref, *refs
):
    riders = len(jobs)
    xs, (out_ref, *outs), refs = refs[:riders], refs[riders : 2 * riders + 1], refs[2 * riders + 1 :]
    (g_buf, to_partner, from_partner, to_dp, from_dp, own, result,
    g_sem, ps_send, ps_recv, dp_send, dp_recv, ag_send, ag_recv, fw_send, fw_recv, own_sem,
    ) = refs[:17]
    gx_full, gx_send, gx_recv = refs[17:20]
    s, j = by_section.me(), by_dp.me()
    partner = 1 - s
    peers = by_dp.peers() + [j]
    count = by_dp.count
    block = own.shape[0]
    subs = block // CHUNK
    tokens = u_ref.shape[0]
    greet([by_section, by_dp, by_tensor] + job_groups(jobs))
    gx_copies = start_rows(by_tensor, gx_ref, gx_full, gx_send, gx_recv)
    parts = split_scratch(jobs, refs[20:])
    ends = [job.start(xs[n], outs[n], *parts[n]) for n, job in enumerate(jobs)]

    def chunk(half, place, sub):
        return (half * count + place) * subs + sub

    order = [(number, half) for number in range(count) for half in (0, 1)]

    def fetch(index, sub, slot):
        number, away = order[index]
        half = partner if away == 0 else s
        return pltpu.make_async_copy(
            g_ref.at[chunk(half, peers[number], sub)], g_buf.at[slot], g_sem.at[slot]
        )

    def remote(group, peer, number, sub, src, dst, send_sem, recv_sem):
        return pltpu.make_async_remote_copy(
            src_ref=src,
            dst_ref=dst,
            send_sem=send_sem.at[number, sub],
            recv_sem=recv_sem.at[number, sub],
            device_id=group.device(peer),
            device_id_type=MESH,
        )

    def rows(sub):
        return pl.ds(pl.multiple_of(sub * CHUNK, CHUNK), CHUNK)

    def partner_copy(number, sub):
        return remote(
            by_section, partner, number, sub,
            to_partner.at[number, rows(sub)], from_partner.at[number, rows(sub)],
            ps_send, ps_recv,
        )

    def chip_copy(number, sub):
        return remote(
            by_dp, peers[number], number, sub,
            to_dp.at[number, rows(sub)], from_dp.at[number, rows(sub)], dp_send, dp_recv,
        )

    def spread_copy(number, sub):
        return remote(
            by_dp, peers[number], number, sub,
            result.at[rows(sub)], out_ref.at[chunk(s, j, sub)], ag_send, ag_recv,
        )

    sources = [lax.rem(j + count - 1 - number, count) for number in range(count - 1)] + [j]

    def forward_copy(number, sub):
        target = out_ref.at[chunk(s, sources[number], sub)]
        origin = result.at[rows(sub)] if number == count - 1 else target
        return remote(by_section, partner, number, sub, origin, target, fw_send, fw_recv)

    def own_copy(sub):
        return pltpu.make_async_copy(
            result.at[rows(sub)], out_ref.at[chunk(s, j, sub)], own_sem.at[sub]
        )

    for copy in gx_copies:
        copy.wait()
    fetch(0, 0, 0).start()
    for index, (number, away) in enumerate(order):
        half = partner if away == 0 else s

        def one(sub, carry, index=index, number=number, away=away, half=half):
            slot = lax.rem(sub, 2)
            fetch(index, sub, slot).wait()

            @pl.when(sub + 1 < subs)
            def _():
                fetch(index, sub + 1, 1 - slot).start()

            if index + 1 < len(order):

                @pl.when(sub + 1 == subs)
                def _():
                    fetch(index + 1, 0, 1 - slot).start()

            base = chunk(half, peers[number], sub) * CHUNK
            place = base + lax.broadcasted_iota(jnp.int32, (CHUNK, tokens), 0)
            chosen = jnp.where(place == ids_ref[...], 1.0, 0.0).astype(BF16)
            term = outer_sum(g_buf[slot], u_ref[...]) + matmul(
                chosen, gx_full[...].reshape(tokens, gx_full.shape[2])
            )
            if away == 0:
                to_partner[number, rows(sub), :] = term.astype(BF16)
                partner_copy(number, sub).start()
            else:
                partner_copy(number, sub).wait_recv()
                term = term + from_partner[number, rows(sub), :].astype(F32)
                if number < count - 1:
                    to_dp[number, rows(sub), :] = term.astype(BF16)
                    chip_copy(number, sub).start()
                else:
                    own[rows(sub), :] = term
            return carry

        lax.fori_loop(0, subs, one, 0)

    def finish(sub, carry):
        term = own[rows(sub), :]
        for number in range(count - 1):
            chip_copy(number, sub).wait_recv()
            term = term + from_dp[number, rows(sub), :].astype(F32)
        result[rows(sub), :] = term.astype(BF16)
        for number in range(count - 1):
            spread_copy(number, sub).start()
        forward_copy(count - 1, sub).start()
        own_copy(sub).start()
        return carry

    lax.fori_loop(0, subs, finish, 0)

    def take(sub, carry):
        for number in range(count - 1):
            spread_copy(number, sub).wait_recv()
            forward_copy(number, sub).start()
        return carry

    lax.fori_loop(0, subs, take, 0)

    def drain(sub, carry):
        own_copy(sub).wait()
        for number in range(count):
            partner_copy(number, sub).wait_send()
            forward_copy(number, sub).wait()
        for number in range(count - 1):
            chip_copy(number, sub).wait_send()
            spread_copy(number, sub).wait_send()
        return carry

    lax.fori_loop(0, subs, drain, 0)
    pass_on(ends)
    finish_jobs(ends)


def across(me, step):
    bits = jnp.int32(step + 1)
    x, y = lax.rem(me, 2), lax.div(me, 2)
    return 2 * lax.rem(y + lax.div(bits, 2), 2) + lax.rem(x + lax.rem(bits, 2), 2)


SQUARE_HALF = (0, 1, 1, 0, 0, 1)
SQUARE_STEP = (0, 0, 1, 1, 1, 0)


def table_square_body(by_section, by_dp, by_tensor, jobs, g_ref, ids_ref, u_ref, gx_ref, *refs):
    riders = len(jobs)
    xs, (out_ref, *outs), refs = refs[:riders], refs[riders : 2 * riders + 1], refs[2 * riders + 1 :]
    (
        g_buf, to_partner, from_partner, to_dp, hop_land, from_dp, own, result,
        g_sem, ps_send, ps_recv, hop_send, hop_recv, dp_send, dp_recv, ag_send, ag_recv,
        fw_send, fw_recv, own_sem,
    ) = refs[:20]
    gx_full, gx_send, gx_recv = refs[20:23]
    s, j = by_section.me(), by_dp.me()
    partner = 1 - s
    near_x, near_y, far = (across(j, step) for step in range(3))
    peers = [far, near_y, near_x, j]
    count = 4
    block = own.shape[0]
    subs = block // CHUNK
    half_rows = CHUNK // 2
    tokens = u_ref.shape[0]
    greet([by_section, by_dp, by_tensor] + job_groups(jobs))
    line = LineRows(by_tensor, gx_ref, gx_full, gx_send, gx_recv)
    line.start()
    gx_full[line.me] = gx_ref[...]
    parts = split_scratch(jobs, refs[23:])
    ends = [
        job.start(xs[n], outs[n], *parts[n]) for n, job in enumerate(jobs) if not job.late
    ]

    def chunk(half, place, sub):
        return (half * count + place) * subs + sub

    order = [(number, away) for number in range(count) for away in (0, 1)]

    def fetch(index, sub, slot):
        number, away = order[index]
        half = partner if away == 0 else s
        return pltpu.make_async_copy(
            g_ref.at[chunk(half, peers[number], sub)], g_buf.at[slot], g_sem.at[slot]
        )

    def remote(group, peer, number, sub, src, dst, send_sem, recv_sem):
        return pltpu.make_async_remote_copy(
            src_ref=src,
            dst_ref=dst,
            send_sem=send_sem.at[number, sub],
            recv_sem=recv_sem.at[number, sub],
            device_id=group.device(peer),
            device_id_type=MESH,
        )

    def rows(sub):
        return pl.ds(pl.multiple_of(sub * CHUNK, CHUNK), CHUNK)

    def half_of(sub, which):
        return pl.ds(pl.multiple_of(sub * CHUNK + which * half_rows, half_rows), half_rows)

    def partner_copy(number, sub):
        return remote(
            by_section, partner, number, sub,
            to_partner.at[number, rows(sub)], from_partner.at[number, rows(sub)],
            ps_send, ps_recv,
        )

    def hop_copy(which, sub):
        return remote(
            by_dp, (near_x, near_y)[which], which, sub,
            to_dp.at[0, half_of(sub, which)], hop_land.at[half_of(sub, which)], hop_send, hop_recv,
        )

    def chip_copy(number, sub):
        return remote(
            by_dp, (near_y, near_x)[number], number, sub,
            to_dp.at[number + 1, rows(sub)], from_dp.at[number, rows(sub)], dp_send, dp_recv,
        )

    def spread_copy(number, sub):
        which = SQUARE_HALF[number]
        place = j if number < 4 else (near_x, near_y)[number - 4]
        dst = out_ref.at[chunk(s, place, sub), pl.ds(which * half_rows, half_rows)]
        src = result.at[half_of(sub, which)] if number < 4 else dst
        peer = (near_x, near_y)[SQUARE_STEP[number]]
        return remote(by_dp, peer, number, sub, src, dst, ag_send, ag_recv)

    sources = [near_x, near_y, far, j]

    def forward_copy(number, sub):
        target = out_ref.at[chunk(s, sources[number], sub)]
        origin = result.at[rows(sub)] if number == count - 1 else target
        return remote(by_section, partner, number, sub, origin, target, fw_send, fw_recv)

    def own_copy(sub):
        return pltpu.make_async_copy(
            result.at[rows(sub)], out_ref.at[chunk(s, j, sub)], own_sem.at[sub]
        )

    def slot_of(number, away):
        if away == 0:
            return to_partner.at[number]
        return to_dp.at[number] if number < 3 else own

    fetch(0, 0, 0).start()
    stops = {(step * len(order)) // line.count: step for step in range(1, line.count - 1)}
    for index, (number, away) in enumerate(order):
        if index in stops:
            line.step(stops[index])

        def share(sub, carry, index=index, number=number, away=away):
            slot = lax.rem(sub, 2)
            fetch(index, sub, slot).wait()

            @pl.when(sub + 1 < subs)
            def _():
                fetch(index, sub + 1, 1 - slot).start()

            if index + 1 < len(order):

                @pl.when(sub + 1 == subs)
                def _():
                    fetch(index + 1, 0, 1 - slot).start()

            held = slot_of(number, away)
            held[rows(sub), :] = outer_sum(g_buf[slot], u_ref[...]).astype(held.dtype)
            return carry

        lax.fori_loop(0, subs, share, 0)
    pass_on(ends)
    line.step(line.count - 1)
    line.wait_sends()
    late = [job.start(xs[n], outs[n], *parts[n]) for n, job in enumerate(jobs) if job.late]

    for index, (number, away) in enumerate(order):
        half = partner if away == 0 else s

        def one(sub, carry, number=number, away=away, half=half):
            base = chunk(half, peers[number], sub) * CHUNK
            place = base + lax.broadcasted_iota(jnp.int32, (CHUNK, tokens), 0)
            chosen = jnp.where(place == ids_ref[...], 1.0, 0.0).astype(BF16)
            term = matmul(chosen, gx_full[...].reshape(tokens, gx_full.shape[2]))
            term = term + slot_of(number, away)[rows(sub), :].astype(F32)
            if away == 0:
                to_partner[number, rows(sub), :] = term.astype(BF16)
                partner_copy(number, sub).start()
                return carry
            partner_copy(number, sub).wait_recv()
            term = term + from_partner[number, rows(sub), :].astype(F32)
            if number == 0:
                to_dp[0, rows(sub), :] = term.astype(BF16)
                for which in range(2):
                    hop_copy(which, sub).start()
            elif number < 3:
                which = number - 1
                hop_copy(which, sub).wait_recv()
                mine = slice(which * half_rows, (which + 1) * half_rows)
                rest = slice((1 - which) * half_rows, (2 - which) * half_rows)
                to_dp[number, half_of(sub, which), :] = (
                    term[mine] + hop_land[half_of(sub, which), :].astype(F32)
                ).astype(BF16)
                to_dp[number, half_of(sub, 1 - which), :] = term[rest].astype(BF16)
                chip_copy(which, sub).start()
            else:
                own[rows(sub), :] = term
            return carry

        lax.fori_loop(0, subs, one, 0)

    def finish(sub, carry):
        term = own[rows(sub), :]
        for number in range(2):
            chip_copy(number, sub).wait_recv()
            term = term + from_dp[number, rows(sub), :].astype(F32)
        result[rows(sub), :] = term.astype(BF16)
        for number in (0, 2, 1, 3):
            spread_copy(number, sub).start()
        forward_copy(count - 1, sub).start()
        own_copy(sub).start()
        return carry

    lax.fori_loop(0, subs, finish, 0)

    def pass_chunk(sub, carry):
        for number in (0, 2):
            spread_copy(number, sub).wait_recv()
            spread_copy(4 + number // 2, sub).start()
        for number in (0, 1):
            spread_copy(2 * number + 1, sub).wait_recv()
            forward_copy(number, sub).start()
        return carry

    lax.fori_loop(0, subs, pass_chunk, 0)

    def last(sub, carry):
        for number in (4, 5):
            spread_copy(number, sub).wait_recv()
        forward_copy(2, sub).start()
        return carry

    lax.fori_loop(0, subs, last, 0)

    def drain(sub, carry):
        own_copy(sub).wait()
        for number in range(count):
            partner_copy(number, sub).wait_send()
            forward_copy(number, sub).wait()
        for number in range(2):
            hop_copy(number, sub).wait_send()
            chip_copy(number, sub).wait_send()
        for number in range(6):
            spread_copy(number, sub).wait_send()
        return carry

    lax.fori_loop(0, subs, drain, 0)
    finish_jobs(ends)
    pass_on(late)
    finish_jobs(late)


def table_sum(by_section, by_dp, by_tensor, jobs, grads, ids, final, grad_rows, ident):
    chunks, tokens, _ = grads.shape
    width = final.shape[1]
    count = by_dp.count
    subs = chunks // (2 * count)
    block = subs * CHUNK
    assert subs % 2 == 0
    dma = pltpu.SemaphoreType.DMA
    low = functools.partial(pltpu.VMEM, dtype=BF16)
    square = by_dp.square
    scratch = [
        low((2, tokens, CHUNK)),
        low((count, block, width)),
        low((count, block, width)),
        low((count - 1, block, width)),
    ]
    scratch += [low((block, width)), low((2, block, width))] if square else [
        low((count - 1, block, width))
    ]
    scratch += [pltpu.VMEM((block, width), F32), low((block, width)), dma((2,))]
    copies = (count, 2, 2, 6, count) if square else (count, count - 1, count - 1, count)
    scratch += [dma((copy, subs)) for copy in copies for _ in range(2)] + [dma((subs,))]
    scratch += [low((by_tensor.count,) + grad_rows.shape)]
    scratch += [dma(((by_tensor.count - 1) * (2 if square else 1),))] * 2
    vmem = pl.BlockSpec(memory_space=pltpu.VMEM)
    hbm = pl.BlockSpec(memory_space=pl.ANY)
    return pl.pallas_call(
        functools.partial(
            table_square_body if by_dp.square else table_body, by_section, by_dp, by_tensor, jobs
        ),
        out_shape=(jax.ShapeDtypeStruct((chunks, CHUNK, width), BF16),)
        + tuple(job.out for job in jobs),
        in_specs=[hbm, vmem, vmem, vmem] + [job.in_spec for job in jobs],
        out_specs=(hbm,) + tuple(job.out_spec for job in jobs),
        scratch_shapes=scratch + [one for job in jobs for one in job.scratch],
        compiler_params=pltpu.CompilerParams(
            collective_id=ident, has_side_effects=True, vmem_limit_bytes=56 * 2**20
        ),
    )(grads, ids, final, grad_rows, *[job.x for job in jobs])


LANES = 128


def head_logits_body(u_ref, e_ref, ids_ref, logits_ref, top_ref, total_ref, pick_ref):
    step = pl.program_id(0)
    tokens, tile = logits_ref.shape[1:]

    @pl.when(step == 0)
    def _():
        top_ref[...] = jnp.full_like(top_ref, NEG)
        total_ref[...] = jnp.zeros_like(total_ref)
        pick_ref[...] = jnp.zeros_like(pick_ref)

    logits = matmul_t(u_ref[...], e_ref[...])
    logits_ref[0] = logits
    place = step * tile + lax.broadcasted_iota(jnp.int32, (tokens, tile), 1)
    picked = jnp.where(place == ids_ref[...], logits, 0.0)
    pieces = [logits[:, at : at + LANES] for at in range(0, tile, LANES)]
    before = top_ref[...]
    top = functools.reduce(jnp.maximum, pieces, before)
    total = total_ref[...] * jnp.exp(before - top)
    pick = pick_ref[...]
    for number, piece in enumerate(pieces):
        total = total + jnp.exp(piece - top)
        pick = pick + picked[:, number * LANES : (number + 1) * LANES]
    top_ref[...] = top
    total_ref[...] = total
    pick_ref[...] = pick


def head_logits(final, embedding, ids):
    tokens, width = final.shape
    vocab = embedding.shape[0]
    fixed = pl.BlockSpec((tokens, LANES), lambda step: (0, 0))
    stat = jax.ShapeDtypeStruct((tokens, LANES), F32)
    return pl.pallas_call(
        head_logits_body,
        grid=(vocab // CHUNK,),
        out_shape=(
            jax.ShapeDtypeStruct((vocab // CHUNK, tokens, CHUNK), F32), stat, stat, stat
        ),
        in_specs=[
            pl.BlockSpec((tokens, width), lambda step: (0, 0)),
            pl.BlockSpec((CHUNK, width), lambda step: (step, 0)),
            pl.BlockSpec((tokens, 1), lambda step: (0, 0)),
        ],
        out_specs=(
            pl.BlockSpec((1, tokens, CHUNK), lambda step: (step, 0, 0)), fixed, fixed, fixed
        ),
        compiler_params=pltpu.CompilerParams(vmem_limit_bytes=40 * 2**20),
        cost_estimate=pl.CostEstimate(
            flops=2 * tokens * vocab * width,
            bytes_accessed=4 * tokens * vocab + 2 * vocab * width,
            transcendentals=tokens * vocab,
        ),
    )(final, embedding, ids)


def head_grads_body(logits_ref, e_ref, ids_ref, norm_ref, weight_ref, grads_ref, back_ref, acc):
    step = pl.program_id(0)
    tokens, tile = grads_ref.shape[1:]

    @pl.when(step == 0)
    def _():
        acc[...] = jnp.zeros_like(acc)

    place = step * tile + lax.broadcasted_iota(jnp.int32, (tokens, tile), 1)
    probs = jnp.exp(logits_ref[0] - norm_ref[...])
    grads = (jnp.where(place == ids_ref[...], probs - 1.0, probs) * weight_ref[...]).astype(BF16)
    grads_ref[0] = grads
    acc[...] += matmul(grads, e_ref[...])

    @pl.when(step == pl.num_programs(0) - 1)
    def _():
        back_ref[...] = acc[...].astype(BF16)


def head_grads(logits, embedding, ids, norm, weight):
    chunks, tokens, _ = logits.shape
    vocab, width = embedding.shape
    column = pl.BlockSpec((tokens, 1), lambda step: (0, 0))
    tile = pl.BlockSpec((1, tokens, CHUNK), lambda step: (step, 0, 0))
    return pl.pallas_call(
        head_grads_body,
        grid=(chunks,),
        out_shape=(
            jax.ShapeDtypeStruct(logits.shape, BF16),
            jax.ShapeDtypeStruct((tokens, width), BF16),
        ),
        in_specs=[
            tile, pl.BlockSpec((CHUNK, width), lambda step: (step, 0)), column, column, column
        ],
        out_specs=(tile, pl.BlockSpec((tokens, width), lambda step: (0, 0))),
        scratch_shapes=[pltpu.VMEM((tokens, width), F32)],
        compiler_params=pltpu.CompilerParams(vmem_limit_bytes=40 * 2**20),
        cost_estimate=pl.CostEstimate(
            flops=2 * tokens * vocab * width,
            bytes_accessed=6 * tokens * vocab + 2 * vocab * width,
            transcendentals=tokens * vocab,
        ),
    )(logits, embedding, ids, norm, weight)


BLOCK = 256


def masked_scores(queries, keys, slope, length, first):
    rows, cols = queries.shape[0], keys.shape[0]
    raw = matmul_t(queries, keys)
    i = first + lax.broadcasted_iota(jnp.int32, (rows, cols), 0)
    j = lax.broadcasted_iota(jnp.int32, (rows, cols), 1)
    scores = raw * HEAD_DIM ** (-0.5) - slope * (i - j).astype(F32)
    return jnp.where((j <= i) & (j < length), scores, NEG)


SMEM = pl.BlockSpec(memory_space=pltpu.SMEM)
VMEM = pl.BlockSpec(memory_space=pltpu.VMEM)


class TeamRows:
    def __init__(self, team, x_ref, full, stage, slots, own, ag_send, ag_recv, rs_send, rs_recv):
        self.team, self.count, self.me = team, team.count, team.me()
        self.x_ref, self.full, self.stage, self.slots, self.own = x_ref, full, stage, slots, own
        self.ag_sems, self.rs_sems = (ag_send, ag_recv), (rs_send, rs_recv)

    def shifted(self, step):
        return across(self.me, step)

    def peer(self, step):
        if self.team.square:
            return self.shifted(step)
        return lax.rem(self.me + 1 + step, self.count)

    def source(self, step):
        if self.team.square:
            return self.shifted(step)
        return lax.rem(self.me + self.count - 1 - step, self.count)

    def back_step(self, place):
        if self.team.square:
            flip_x = lax.rem(lax.rem(self.me, 2) + lax.rem(place, 2), 2)
            flip_y = lax.rem(lax.div(self.me, 2) + lax.div(place, 2), 2)
            return 2 * flip_y + flip_x - 1
        return lax.rem(place + self.count - 1 - self.me, self.count)

    def remote(self, number, peer, src, dst, sems):
        return pltpu.make_async_remote_copy(
            src_ref=src,
            dst_ref=dst,
            send_sem=sems[0].at[number],
            recv_sem=sems[1].at[number],
            device_id=self.team.device(peer),
            device_id_type=MESH,
        )

    def ag(self, number):
        if not self.team.square:
            return self.remote(
                number, self.peer(number), self.x_ref, self.full.at[self.me], self.ag_sems
            )
        half = self.x_ref.shape[0] // 2
        which = SQUARE_HALF[number]
        rows = pl.ds(which * half, half)
        peer = self.shifted(SQUARE_STEP[number])
        if number < 4:
            src, place = self.x_ref.at[rows], self.me
        else:
            place = self.shifted(number - 4)
            src = self.full.at[place, rows]
        return self.remote(number, peer, src, self.full.at[place, rows], self.ag_sems)

    def rs(self, step):
        return self.remote(
            step, self.peer(step), self.stage.at[self.peer(step)], self.slots.at[step], self.rs_sems
        )

    def send_rows(self):
        for number in (0, 2, 1, 3) if self.team.square else range(self.count - 1):
            self.ag(number).start()
        self.full[self.me] = self.x_ref[...]

    def pass_on(self):
        if self.team.square:
            for number in (0, 2):
                self.ag(number).wait_recv()
                self.ag(4 + number // 2).start()

    def wait_rows(self, step):
        if not self.team.square:
            self.ag(step).wait_recv()
            return
        for number, these in enumerate(((1,), (3,), (4, 5))):

            @pl.when(step == number)
            def _(these=these):
                for one in these:
                    self.ag(one).wait_recv()

    def each_arrival(self, work):
        work(self.me)
        self.pass_on()

        def one(step, carry):
            self.wait_rows(step)
            work(self.source(step))
            return carry

        lax.fori_loop(0, self.count - 1, one, 0)

    def each_arrival_and_back(self, term):
        self.own[...] = term(self.me)
        self.pass_on()

        def one(step, carry):
            self.wait_rows(step)
            place = self.source(step)
            self.stage[place] = term(place).astype(BF16)
            self.rs(self.back_step(place)).start()
            return carry

        lax.fori_loop(0, self.count - 1, one, 0)

    def finish(self, total_ref):
        pass_on(self.ends)
        finish_jobs(self.ends)
        for step in range(self.count - 1):
            self.rs(step).wait()
        total = self.own[...]
        for step in range(self.count - 1):
            total = total + self.slots[step].astype(F32)
        total_ref[...] = total
        for number in range(6 if self.team.square else self.count - 1):
            self.ag(number).wait_send()


def team_scratch(team, part, model):
    count = team.count
    dma = pltpu.SemaphoreType.DMA
    copies = 6 if team.square else count - 1
    return [
        pltpu.VMEM((count, part, model), BF16),
        pltpu.VMEM((count, part, model), BF16),
        pltpu.VMEM((count - 1, part, model), BF16),
        pltpu.VMEM((part, model), F32),
        dma((copies,)),
        dma((copies,)),
        dma((count - 1,)),
        dma((count - 1,)),
    ]


class LateDeal:
    def __init__(self, pair, landing, send_sem, recv_sem):
        self.pair, self.landing, self.sems = pair, landing, (send_sem, recv_sem)

    def other(self):
        return 1 - self.pair.me()

    def start(self, src):
        self.copy = send(self.pair, self.other(), 0, src, self.landing, *self.sems)

    def wait(self):
        self.copy.wait()


def team_call(body, team, ident, jobs, arrays, specs, outs, out_specs, scratch, pair=None, dealt=None, ahead=0):
    if pair is not None:
        outs, out_specs = tuple(outs) + (dealt,), tuple(out_specs) + (HBM,)
        scratch = list(scratch) + [pltpu.SemaphoreType.DMA((1,))] * 2
    part, model = arrays[0].shape
    count_in, count_out, riders = len(arrays), len(outs), len(jobs)
    own_scratch = team_scratch(team, part, model)

    def kernel(*refs):
        ins, refs = refs[:count_in], refs[count_in:]
        xs, refs = refs[:riders], refs[riders:]
        results, refs = refs[:count_out], refs[count_out:]
        landings, refs = refs[:riders], refs[riders:]
        rows = TeamRows(team, ins[0], *refs[: len(own_scratch)])
        refs = refs[len(own_scratch) :]
        mine, refs = refs[: len(scratch)], refs[len(scratch) :]
        greet([team] + job_groups(jobs) + ([] if pair is None else [pair]))
        rows.send_rows()
        parts = split_scratch(jobs, refs)

        def start(numbers):
            return [jobs[n].start(xs[n], landings[n], *parts[n]) for n in numbers]

        rows.landings = landings
        first = start(range(ahead if ahead else riders))
        if ahead:

            def ready():
                pass_on(first)
                finish_jobs(first)
                rows.ends = start(range(ahead, riders))

            rows.ready = ready
        else:
            rows.ends = first
        if pair is None:
            body(rows, ins, results, mine)
        else:
            body(rows, ins, results[:-1], mine[:-2], LateDeal(pair, results[-1], *mine[-2:]))

    out = pl.pallas_call(
        kernel,
        out_shape=tuple(outs) + tuple(job.out for job in jobs),
        in_specs=list(specs) + [job.in_spec for job in jobs],
        out_specs=tuple(out_specs) + tuple(job.out_spec for job in jobs),
        scratch_shapes=own_scratch + list(scratch) + [one for job in jobs for one in job.scratch],
        compiler_params=pltpu.CompilerParams(
            collective_id=ident, has_side_effects=True, vmem_limit_bytes=58 * 2**20
        ),
    )(*arrays, *[job.x for job in jobs])
    return out[:count_out], list(out[count_out:])


def part_rows(place, part):
    return pl.ds(pl.multiple_of(place * part, part), part)


def attend_body(rows, ins, outs, scratch):
    x_ref, length_ref, slope_ref, bias_ref, *weights = ins
    total_ref, full_out, q_ref, k_ref, v_ref, mixed_ref, lse_ref = outs
    full_sem, *buffers = scratch
    if not weights:
        *weights, sems = buffers
        rows.ready()
        copies = [
            pltpu.make_async_copy(rows.landings[n], weights[n], sems.at[n]) for n in range(2)
        ]
        for copy in copies:
            copy.start()
        for copy in copies:
            copy.wait()
    qk_ref, vo_ref = weights

    def weight(ref, n):
        block = ref[n]
        return block.reshape(-1, block.shape[-1])

    part = x_ref.shape[0]
    width = q_ref.shape[1]

    def project(place):
        at = part_rows(place, part)
        block = rows.full[place]
        q_ref[at, :] = (matmul_t(block, weight(qk_ref, 0)) + bias_ref[0:1, :]).astype(BF16)
        k_ref[at, :] = matmul_t(block, weight(qk_ref, 1)).astype(BF16)
        v_ref[at, :] = (matmul_t(block, weight(vo_ref, 0)) + bias_ref[1:2, :]).astype(BF16)

    rows.each_arrival(project)
    keep = pltpu.make_async_copy(rows.full, full_out, full_sem)
    keep.start()

    def one(turn, carry):
        step = lax.rem(2 * rows.count - 2 - turn, rows.count)
        place = rows.peer(step)
        for block in range(rows.count):

            @pl.when(place == block)
            def _(first=block * part, upto=(block + 1) * part):
                for head in range(width // HEAD_DIM):
                    lanes = slice(head * HEAD_DIM, (head + 1) * HEAD_DIM)
                    scores = masked_scores(
                        q_ref[first:upto, lanes], k_ref[:upto, lanes], slope_ref[head],
                        length_ref[0], first,
                    )
                    highest = jnp.max(scores, axis=-1, keepdims=True)
                    powers = jnp.exp(scores - highest)
                    total = jnp.sum(powers, axis=-1, keepdims=True)
                    probs = (powers * (1.0 / total)).astype(BF16)
                    mixed_ref[first:upto, lanes] = matmul(probs, v_ref[:upto, lanes]).astype(BF16)
                    lse_ref[head, first:upto, :] = highest + jnp.log(total)

        term = matmul(mixed_ref[part_rows(place, part), :], weight(vo_ref, 1))

        @pl.when(step < rows.count - 1)
        def _():
            rows.stage[place] = term.astype(BF16)
            rows.rs(step).start()

        @pl.when(step == rows.count - 1)
        def _():
            rows.own[...] = term

        return carry

    lax.fori_loop(0, rows.count, one, 0)
    rows.finish(total_ref)
    keep.wait()


HBM = pl.BlockSpec(memory_space=pl.ANY)


def attend(team, ident, jobs, x, length, slopes, bias, weights):
    part, model = x.shape
    seq = part * team.count
    width = bias.shape[1]
    scratch = [pltpu.SemaphoreType.DMA]
    if not weights:
        scratch += [pltpu.VMEM(job.out.shape, BF16) for job in jobs[:2]]
        scratch.append(pltpu.SemaphoreType.DMA((2,)))
    low = jax.ShapeDtypeStruct((seq, width), BF16)
    return team_call(
        attend_body, team, ident, jobs,
        [x, length, slopes, bias] + weights,
        [VMEM, SMEM, SMEM, VMEM] + [VMEM] * len(weights),
        (
            jax.ShapeDtypeStruct((part, model), F32),
            jax.ShapeDtypeStruct((team.count, part, model), BF16),
            low, low, low, low,
            jax.ShapeDtypeStruct((width // HEAD_DIM, seq, 1), F32),
        ),
        (VMEM, HBM, VMEM, VMEM, VMEM, VMEM, VMEM),
        scratch,
        ahead=0 if weights else 2,
    )


def attend_back_body(rows, ins, outs, scratch, late=None):
    gy_ref, length_ref, slope_ref, a_ref, qk_ref, vo_ref, q_ref, k_ref, v_ref, mixed_ref, lse_ref = ins
    total_ref, grads_ref, sums_ref = outs
    go, gq, gk, gv, gk_sum, gv_sum = scratch
    part = gy_ref.shape[0]
    seq, width = q_ref.shape
    heads = width // HEAD_DIM
    gk_sum[...] = jnp.zeros_like(gk_sum)
    gv_sum[...] = jnp.zeros_like(gv_sum)
    sums_ref[...] = jnp.zeros_like(sums_ref)

    def open_block(place):
        go[part_rows(place, part), :] = matmul_t(rows.full[place], vo_ref[1]).astype(BF16)

    rows.each_arrival(open_block)
    for block in reversed(range(rows.count)):
        first, upto = block * part, (block + 1) * part
        for head in range(heads):
            lanes = slice(head * HEAD_DIM, (head + 1) * HEAD_DIM)
            queries, grads = q_ref[first:upto, lanes], go[first:upto, lanes]
            keys, values = k_ref[:upto, lanes], v_ref[:upto, lanes]
            scores = masked_scores(queries, keys, slope_ref[head], length_ref[0], first)
            probs = jnp.exp(scores - lse_ref[head, first:upto, :])
            grad_probs = matmul_t(grads, values)
            inner = jnp.sum(probs * grad_probs, axis=-1, keepdims=True)
            grad_scores = (probs * (grad_probs - inner) * HEAD_DIM ** (-0.5)).astype(BF16)
            piece = matmul(grad_scores, keys)
            sums_ref[0:1, lanes] += jnp.sum(piece, axis=0, keepdims=True)
            gq[first:upto, lanes] = piece.astype(BF16)
            gk_sum[:upto, lanes] += outer_sum(grad_scores, queries)
            gv_sum[:upto, lanes] += outer_sum(probs.astype(BF16), grads)
        gk[first:upto, :] = gk_sum[first:upto, :].astype(BF16)
        gv[first:upto, :] = gv_sum[first:upto, :].astype(BF16)
        term = (
            matmul(gq[first:upto, :], qk_ref[0]) + matmul(gk[first:upto, :], qk_ref[1])
            + matmul(gv[first:upto, :], vo_ref[0])
        )

        @pl.when(rows.me != block)
        def _(block=block, term=term):
            rows.stage[block] = term.astype(BF16)
            rows.rs(rows.back_step(block)).start()

        @pl.when(rows.me == block)
        def _(term=term):
            rows.own[...] = term

    sums_ref[1:2, :] = jnp.sum(gv_sum[...], axis=0, keepdims=True)
    model = gy_ref.shape[1]
    grads_ref[3] = outer_sum(mixed_ref[...], rows.full[...].reshape(seq, model))
    grads_ref[0] = outer_sum(gq[...], a_ref[...])
    grads_ref[1] = outer_sum(gv[...], a_ref[...])
    grads_ref[2] = outer_sum(gk[...], a_ref[...])
    if late is not None:
        late.start(grads_ref.at[pl.ds(2 * late.other(), 2)])
    rows.finish(total_ref)
    if late is not None:
        late.wait()


def attend_back(team, ident, jobs, pair, gy, length, slopes, a, qk, vo, q, k, v, mixed, lse):
    part, model = gy.shape
    seq, width = q.shape
    return team_call(
        attend_back_body, team, ident, jobs,
        [gy, length, slopes, a, qk, vo, q, k, v, mixed, lse],
        [VMEM, SMEM, SMEM] + [VMEM] * 8,
        (
            jax.ShapeDtypeStruct((part, model), F32),
            jax.ShapeDtypeStruct((4, width, model), F32),
            jax.ShapeDtypeStruct((2, width), F32),
        ),
        (VMEM,) * 3,
        [pltpu.VMEM((seq, width), BF16)] * 4 + [pltpu.VMEM((seq, width), F32)] * 2,
        pair,
        jax.ShapeDtypeStruct((2, width, model), F32),
    )


GELU_A = 0.7978845608028654
GELU_B = 0.044715


def strip_rows(strips, which, first, size):
    length = strips[0].shape[1]
    return strips[first // length][which, first % length : first % length + size, :]


def feed_body(rows, ins, outs, scratch):
    x_ref, bias_ref, *strips = ins
    total_ref, full_out, before_ref = outs
    (full_sem,) = scratch
    part = x_ref.shape[0]
    units = bias_ref.shape[1]
    tile = min(units, BLOCK)

    def term(place):
        at = part_rows(place, part)
        block = rows.full[place]
        total = None
        for first in range(0, units, tile):
            lanes = slice(first, first + tile)
            before = matmul_t(block, strip_rows(strips, 0, first, tile)) + bias_ref[:, lanes]
            before_ref[at, lanes] = before
            bend = jnp.tanh(GELU_A * (before + GELU_B * before * before * before))
            active = (0.5 * before * (1.0 + bend)).astype(BF16)
            piece = matmul(active, strip_rows(strips, 1, first, tile))
            total = piece if total is None else total + piece
        return total

    rows.each_arrival_and_back(term)
    keep = pltpu.make_async_copy(rows.full, full_out, full_sem)
    keep.start()
    rows.finish(total_ref)
    keep.wait()


def feed(team, ident, jobs, x, strips, bias):
    part, model = x.shape
    units = bias.shape[1]
    return team_call(
        feed_body, team, ident, jobs,
        [x, bias] + strips,
        [VMEM] * (2 + len(strips)),
        (
            jax.ShapeDtypeStruct((part, model), F32),
            jax.ShapeDtypeStruct((team.count, part, model), BF16),
            jax.ShapeDtypeStruct((part * team.count, units), F32),
        ),
        (VMEM, HBM, VMEM),
        [pltpu.SemaphoreType.DMA],
    )


def feed_back_body(rows, ins, outs, scratch, late=None):
    gz_ref, c_ref, before_ref, *strips = ins
    total_ref, grads_ref, sums_ref = outs
    active, low = scratch
    part, model = gz_ref.shape
    seq = part * rows.count
    units = before_ref.shape[1]
    tile = min(units, BLOCK)
    sums_ref[...] = jnp.zeros_like(sums_ref)

    def term(place):
        at = part_rows(place, part)
        gz = rows.full[place]
        for first in range(0, units, tile):
            lanes = slice(first, first + tile)
            before = before_ref[at, lanes]
            square = before * before
            bend = jnp.tanh(GELU_A * before * (1.0 + GELU_B * square))
            half = 0.5 * (1.0 + bend)
            slope = half + 0.5 * before * (1.0 - bend * bend) * (
                GELU_A * (1.0 + 3.0 * GELU_B * square)
            )
            grad = matmul_t(gz, strip_rows(strips, 1, first, tile)) * slope
            sums_ref[:, lanes] += jnp.sum(grad, axis=0, keepdims=True)
            active[at, lanes] = (before * half).astype(BF16)
            low[at, lanes] = grad.astype(BF16)
        length = strips[0].shape[1]
        return sum(
            matmul(low[at, n * length : (n + 1) * length], strip[0])
            for n, strip in enumerate(strips)
        )

    rows.each_arrival_and_back(term)
    for first in range(0, units, tile):
        lanes = slice(first, first + tile)
        grads_ref[0, lanes, :] = outer_sum(low[:, lanes], c_ref[...])
        grads_ref[1, lanes, :] = outer_sum(active[:, lanes], rows.full[...].reshape(seq, model))
    if late is not None:
        late.start(grads_ref.at[late.other()])
    rows.finish(total_ref)
    if late is not None:
        late.wait()


def feed_back(team, ident, jobs, pair, gz, c, before, strips):
    part, model = gz.shape
    seq = part * team.count
    units = before.shape[1]
    return team_call(
        feed_back_body, team, ident, jobs,
        [gz, c, before] + strips,
        [VMEM] * (3 + len(strips)),
        (
            jax.ShapeDtypeStruct((part, model), F32),
            jax.ShapeDtypeStruct((2, units, model), F32),
            jax.ShapeDtypeStruct((1, units), F32),
        ),
        (VMEM,) * 3,
        [pltpu.VMEM((seq, units), BF16)] * 2,
        pair,
        jax.ShapeDtypeStruct((units, model), F32),
    )


def line_head_logits_body(
    group, x_ref, e_ref, ids_ref, logits_ref, full_out, stats_out,
    full, table, staged, top, total, pick, stats,
    ag_send, ag_recv, e_sem, out_sem, full_sem, st_send, st_recv,
):
    count, me = group.count, group.me()
    part = x_ref.shape[0]
    tiles = e_ref.shape[0] // CHUNK
    line = LineRows(group, x_ref, full, ag_send, ag_recv)
    greet([group])
    line.start()
    full[me] = x_ref[...]
    top[...] = jnp.full_like(top, NEG)
    total[...] = jnp.zeros_like(total)
    pick[...] = jnp.zeros_like(pick)

    def rows_of(tile):
        return pl.ds(pl.multiple_of(tile * CHUNK, CHUNK), CHUNK)

    def load(tile):
        return pltpu.make_async_copy(
            e_ref.at[rows_of(tile)], table.at[rows_of(tile)], e_sem.at[tile]
        )

    def leave(tile, place, slot):
        return pltpu.make_async_copy(
            staged.at[slot], logits_ref.at[tile, part_rows(place, part)], out_sem.at[slot]
        )

    for tile in range(tiles):
        load(tile).start()

    def work(place, first):
        at = part_rows(place, part)
        ids = ids_ref[at, :]

        def one(pair, carry):
            for slot in range(2):
                tile = 2 * pair + slot
                if first:
                    load(tile).wait()

                    @pl.when(pair > 0)
                    def _(slot=slot, tile=tile):
                        leave(tile, place, slot).wait()

                else:
                    leave(tile, place, slot).wait()
                logits = matmul_t(full[place], table[rows_of(tile), :])
                staged[slot] = logits
                leave(tile, place, slot).start()
                column = tile * CHUNK + lax.broadcasted_iota(jnp.int32, (part, CHUNK), 1)
                picked = jnp.where(column == ids, logits, 0.0)
                pieces = [logits[:, at : at + LANES] for at in range(0, CHUNK, LANES)]
                before = top[at, :]
                high = functools.reduce(jnp.maximum, pieces, before)
                sums = total[at, :] * jnp.exp(before - high)
                found = pick[at, :]
                for number, piece in enumerate(pieces):
                    sums = sums + jnp.exp(piece - high)
                    found = found + picked[:, number * LANES : (number + 1) * LANES]
                top[at, :] = high
                total[at, :] = sums
                pick[at, :] = found
            return carry

        lax.fori_loop(0, tiles // 2, one, 0)

    work(me, True)
    for step in range(1, count):
        line.step(step)

        @pl.when(me >= step)
        def _(step=step):
            work(me - step, False)

        @pl.when(me + step < count)
        def _(step=step):
            work(me + step, False)

    keep = pltpu.make_async_copy(full, full_out, full_sem)
    keep.start()
    tall = top[...].T
    high = jnp.max(tall, axis=0, keepdims=True)
    stats[me] = jnp.zeros(stats.shape[1:], F32)
    stats[me, 0:1, :] = high
    stats[me, 1:2, :] = jnp.sum(total[...].T * jnp.exp(tall - high), axis=0, keepdims=True)
    stats[me, 2:3, :] = jnp.sum(pick[...].T, axis=0, keepdims=True)
    copies = [
        send(group, peer, step, stats.at[me], stats.at[me], st_send, st_recv)
        for step, peer in enumerate(group.peers())
    ]
    for slot in range(2):
        leave(0, me, slot).wait()
    line.wait_sends()
    for copy in copies:
        copy.wait()
    stats_out[...] = stats[...]
    keep.wait()


def line_head_logits(group, ident, x, embedding, ids):
    part, width = x.shape
    vocab = embedding.shape[0]
    count = group.count
    tokens = part * count
    tiles = vocab // CHUNK
    assert tiles % 2 == 0
    dma = pltpu.SemaphoreType.DMA
    return pl.pallas_call(
        functools.partial(line_head_logits_body, group),
        out_shape=(
            jax.ShapeDtypeStruct((tiles, tokens, CHUNK), F32),
            jax.ShapeDtypeStruct((count, part, width), BF16),
            jax.ShapeDtypeStruct((count, 8, tokens), F32),
        ),
        in_specs=[VMEM, HBM, VMEM],
        out_specs=(HBM, HBM, VMEM),
        scratch_shapes=[
            pltpu.VMEM((count, part, width), BF16),
            pltpu.VMEM((vocab, width), BF16),
            pltpu.VMEM((2, part, CHUNK), F32),
            pltpu.VMEM((tokens, LANES), F32),
            pltpu.VMEM((tokens, LANES), F32),
            pltpu.VMEM((tokens, LANES), F32),
            pltpu.VMEM((count, 8, tokens), F32),
            dma((2 * count - 2,)),
            dma((2 * count - 2,)),
            dma((tiles,)),
            dma((2,)),
            dma,
            dma((count - 1,)),
            dma((count - 1,)),
        ],
        compiler_params=pltpu.CompilerParams(
            collective_id=ident, has_side_effects=True, vmem_limit_bytes=56 * 2**20
        ),
    )(x, embedding, ids)


def line_head_grads_body(
    group, logits_ref, e_ref, ids_ref, norm_ref, weight_ref, grads_ref, total_ref,
    terms, stage, land, table, staged, low, acc,
    rs_send, rs_recv, e_sem, in_sem, out_sem,
):
    count, me = group.count, group.me()
    part = terms.shape[1]
    tiles = e_ref.shape[0] // CHUNK
    line = LineSum(group, terms, stage, land, rs_send, rs_recv)
    greet([group])

    def rows_of(tile):
        return pl.ds(pl.multiple_of(tile * CHUNK, CHUNK), CHUNK)

    def load(tile):
        return pltpu.make_async_copy(
            e_ref.at[rows_of(tile)], table.at[rows_of(tile)], e_sem.at[tile]
        )

    def enter(tile, place, slot):
        return pltpu.make_async_copy(
            logits_ref.at[tile, part_rows(place, part)], staged.at[slot], in_sem.at[slot]
        )

    def leave(tile, place, slot):
        return pltpu.make_async_copy(
            low.at[:, pl.ds(slot * CHUNK, CHUNK)],
            grads_ref.at[tile, part_rows(place, part)],
            out_sem.at[slot],
        )

    for tile in range(tiles):
        load(tile).start()

    def work(place, fresh=False):
        at = part_rows(place, part)
        ids, norm, weight = ids_ref[at, :], norm_ref[at, :], weight_ref[at, :]
        for slot in range(2):
            enter(slot, place, slot).start()
        acc[...] = jnp.zeros_like(acc)

        def one(pair, carry):
            for slot in range(2):
                tile = 2 * pair + slot
                enter(tile, place, slot).wait()
                if fresh:
                    load(tile).wait()
                column = tile * CHUNK + lax.broadcasted_iota(jnp.int32, (part, CHUNK), 1)
                probs = jnp.exp(staged[slot] - norm)
                grads = (jnp.where(column == ids, probs - 1.0, probs) * weight).astype(BF16)

                @pl.when(pair > 0)
                def _(slot=slot, tile=tile):
                    leave(tile, place, slot).wait()

                low[:, slot * CHUNK : (slot + 1) * CHUNK] = grads
                leave(tile, place, slot).start()

                @pl.when(pair + 1 < tiles // 2)
                def _(slot=slot, tile=tile):
                    enter(tile + 2, place, slot).start()

            rows = pl.ds(pl.multiple_of(pair * 2 * CHUNK, 2 * CHUNK), 2 * CHUNK)
            acc[...] += matmul(low[...], table[rows, :])
            return carry

        lax.fori_loop(0, tiles // 2, one, 0)
        for slot in range(2):
            leave(0, place, slot).wait()
        terms[place] = acc[...].astype(BF16)

    for step in range(count - 1):

        @pl.when(me < count - 1 - step)
        def _(step=step):
            work(count - 1 - step, fresh=step == 0)

        if step == 0:

            @pl.when(me == count - 1)
            def _():
                work(0, fresh=True)

        @pl.when((me > step) & ((me < count - 1) | (step > 0)))
        def _(step=step):
            work(step)

        line.first(step)
        if step == 1:
            line.rest(0, near=True)
    work(me)
    line.rest(0, near=False)
    for step in range(1, count - 1):
        line.rest(step)
    line.finish(total_ref)


def line_head_grads(group, ident, logits, embedding, ids, norm, weight):
    tiles, tokens, _ = logits.shape
    vocab, width = embedding.shape
    count = group.count
    part = tokens // count
    dma = pltpu.SemaphoreType.DMA
    return pl.pallas_call(
        functools.partial(line_head_grads_body, group),
        out_shape=(
            jax.ShapeDtypeStruct(logits.shape, BF16),
            jax.ShapeDtypeStruct((part, width), F32),
        ),
        in_specs=[HBM, HBM, VMEM, VMEM, VMEM],
        out_specs=(HBM, VMEM),
        scratch_shapes=[
            pltpu.VMEM((count, part, width), BF16),
            pltpu.VMEM((2, count - 1, part, width), BF16),
            pltpu.VMEM((2, count - 1, part, width), BF16),
            pltpu.VMEM((vocab, width), BF16),
            pltpu.VMEM((2, part, CHUNK), F32),
            pltpu.VMEM((part, 2 * CHUNK), BF16),
            pltpu.VMEM((part, width), F32),
            dma((2, count - 1)),
            dma((2, count - 1)),
            dma((tiles,)),
            dma((2,)),
            dma((2,)),
        ],
        compiler_params=pltpu.CompilerParams(
            collective_id=ident, has_side_effects=True, vmem_limit_bytes=56 * 2**20
        ),
    )(logits, embedding, ids, norm, weight)


def per_device(
    mesh_shape,
    token_ids,
    target_ids,
    lengths,
    embedding,
    outer_gain,
    outer_bias,
    norm_gain,
    norm_bias,
    qkv_weight,
    qv_bias,
    out_weight,
    up_weight,
    up_bias,
    down_weight,
    row_bias,
):
    sections, groups, shards = (mesh_shape[name] for name in ("section", "dp", "tensor"))
    s, j, z = (lax.axis_index(name) for name in ("section", "dp", "tensor"))
    by_section = Group(("section",), (sections,))
    by_dp = Group(("dp",), (groups,))
    by_tensor = Group(("tensor",), (shards,))
    exchange = Exchanges()
    layers = sections
    vocab, width = embedding.shape
    seq = token_ids.shape[1]
    rows = token_ids.shape[0] * groups
    local_cols = qkv_weight.shape[-1]
    planes = rows == sections * shards and local_cols % (groups * HEAD_DIM) == 0
    by_dp.square = planes and groups == 4
    by_tensor.line = planes
    team = by_dp if planes else by_tensor
    cut = groups if planes else 1
    fan = shards if planes else 1
    halves = 2 if planes else 1
    part = seq // team.count
    cols = local_cols // cut
    hidden = up_weight.shape[-1] // cut
    strip = hidden // halves
    cut_index = j if planes else 0
    my_row = z * sections + s if planes else j * sections + s
    length = lax.dynamic_slice(lengths, (my_row,), (1,))
    token_count = jnp.sum(lengths).astype(F32)
    vocab_start = z * vocab

    def chosen_cols(array, size):
        return lax.dynamic_slice_in_dim(array, cut_index * size, size, array.ndim - 1).T

    def chosen_rows(array, size):
        return lax.dynamic_slice_in_dim(array, cut_index * size, size, 0)

    def pad_rows(array, count):
        return jnp.pad(array, ((0, count - array.shape[0]), (0, width - array.shape[1])))

    sides = jnp.stack(
        [
            jnp.concatenate(
                [
                    chosen_cols(qkv_weight[0, 0], cols),
                    chosen_cols(qkv_weight[0, 2], cols),
                    chosen_cols(up_weight[0], hidden),
                ]
            ),
            jnp.concatenate(
                [
                    chosen_cols(qkv_weight[0, 1], cols),
                    chosen_rows(out_weight[0], cols),
                    chosen_rows(down_weight[0], hidden),
                ]
            ),
        ]
    )
    qv_piece = lax.dynamic_slice_in_dim(qv_bias[0], cut_index * cols, cols, 1)
    up_piece = lax.dynamic_slice_in_dim(up_bias[0], cut_index * hidden, hidden, 0)
    small = jnp.concatenate(
        [outer_gain, outer_bias, norm_gain[0], norm_bias[0], row_bias[0]]
    )
    bias_piece = jnp.concatenate([qv_piece[0], qv_piece[1], up_piece])
    bias_piece = jnp.pad(bias_piece, (0, -bias_piece.shape[0] % 1024)).reshape(-1, 128)

    def gather(group, x):
        return Job("gather", [group], x)

    def deal(group, x, axis=0):
        return Job("deal", [group], x, axis)

    def own_and_dealt(x, dealt, place, axis=0):
        own = lax.dynamic_index_in_dim(x, place, axis, keepdims=False).astype(F32)
        return own + jnp.sum(dealt.astype(F32), axis=0)

    if planes:
        other, both, small_all, bias_all = exchange(
            deal(by_section, sides),
            gather(by_dp, jnp.stack([token_ids, target_ids])),
            gather(by_section, small),
            gather(Group(("section", "tensor"), (sections, shards)), bias_piece),
        )
        bias_all = bias_all.reshape(sections, shards, -1)
        own_side = lax.dynamic_index_in_dim(sides, s, 0, keepdims=False)
        side = [jnp.where(s == l, own_side, other[0]) for l in range(layers)]
        both = jnp.swapaxes(both, 0, 1).reshape(2, shards, sections, groups, part)
        both = lax.dynamic_index_in_dim(
            lax.dynamic_index_in_dim(both, s, 2, keepdims=False), j, 2, keepdims=False
        )
        ids, targets = both[0].reshape(-1), both[1].reshape(-1)
        group_lengths = lax.dynamic_index_in_dim(
            lengths.reshape(shards, sections), s, 1, keepdims=False
        )
        places = jnp.broadcast_to(j * part + jnp.arange(part), (shards, part))
        valid = (places < group_lengths[:, None]).reshape(-1)
    else:
        sides_all, small_all, bias_all = exchange(
            gather(by_section, sides), gather(by_section, small), gather(by_section, bias_piece)
        )
        bias_all = bias_all.reshape(sections, 1, -1)
        ids, targets = token_ids[s], target_ids[s]
        valid = jnp.arange(seq) < lengths[my_row]

    outer_gains = [small_all[l, 0] for l in range(layers)]
    outer_offsets = [small_all[l, 1] for l in range(layers)]
    params = []
    for l in range(layers):
        biases = [bias_all[l, :, n * cols : (n + 1) * cols].reshape(-1) for n in range(2)]
        units = bias_all[l, :, 2 * cols : 2 * cols + hidden].reshape(fan, halves, strip)
        params.append(
            dict(
                gains=small_all[l, 2:4],
                offsets=small_all[l, 4:6],
                row_bias=small_all[l, 6:8],
                bias=jnp.stack(biases),
                up_bias=jnp.swapaxes(units, 0, 1).reshape(1, -1),
            )
        )
        if not planes:
            block = sides_all[l]
            params[l].update(
                qk=block[:, :cols],
                vo=block[:, cols : 2 * cols],
                strips=[block[:, 2 * cols :]],
            )
    head_number = (
        (jnp.arange(fan)[:, None] if planes else z) * (local_cols // HEAD_DIM)
        + cut_index * (cols // HEAD_DIM)
        + jnp.arange(cols // HEAD_DIM)
    ).reshape(-1)
    slopes = jnp.exp2(-8.0 * (head_number + 1).astype(F32) / HEADS)

    def attn_jobs(l):
        if not planes or l >= layers:
            return []
        return [
            Job("spread", [by_tensor, by_section], side[l][first : first + cols])
            for first in (0, cols)
        ]

    def feed_jobs(l, n):
        if not planes or l >= layers:
            return []
        first = 2 * cols + n * strip
        return [Job("spread", [by_tensor, by_section], side[l][first : first + strip])]

    def take_attn(l, got):
        if got:
            params[l]["qk"], params[l]["vo"] = (
                one.reshape(2, fan * cols, width) for one in got
            )

    def take_feed(l, got):
        if got:
            params[l]["strips"] = [one.reshape(2, fan * strip, width) for one in got]

    def ident(kind, jobs):
        return exchange.ident((kind,) + tuple(job.key() for job in jobs))

    local_ids = ids - vocab_start
    inside = (local_ids >= 0) & (local_ids < vocab)
    looked = jnp.where(
        inside[:, None], jnp.take(embedding, jnp.clip(local_ids, 0, vocab - 1), axis=0), 0
    )
    group_part = looked.shape[0] // shards
    (x,) = exchange(Job("reduce", [by_tensor], looked.reshape(shards, group_part, width)))
    h = layer_norm(x, outer_gains[0], outer_offsets[0])

    kept = []
    for l, p in enumerate(params):
        jobs = (attn_jobs(l) if l == 0 else []) + feed_jobs(l, 0) + feed_jobs(l, 1)
        normed = layer_norm(h, p["gains"][0], p["offsets"][0]).astype(BF16)
        (total, normed, q, k, v, mixed, lse), got = attend(
            team, ident("attend", jobs), jobs, normed, length, slopes, p["bias"],
            [p["qk"], p["vo"]] if "qk" in p else [],
        )
        if "qk" not in p:
            take_attn(l, got[:2])
            got = got[2:]
        take_feed(l, got)
        middle = h + total + p["row_bias"][0]
        jobs = attn_jobs(l + 1)
        second = layer_norm(middle, p["gains"][1], p["offsets"][1]).astype(BF16)
        (total, second, before), got = feed(
            team, ident("feed", jobs), jobs, second, p["strips"], p["up_bias"]
        )
        take_attn(l + 1, got)
        kept.append((h, normed.reshape(seq, width), q, k, v, mixed, lse, middle, second, before))
        h = middle + total + p["row_bias"][1]

    final = layer_norm(h, outer_gains[-1], outer_offsets[-1]).astype(BF16)
    columns_of = (targets - vocab_start)[:, None]
    if planes:
        logits, final, stats = line_head_logits(
            by_tensor, exchange.ident("head logits"), final, embedding, columns_of
        )
        final = final.reshape(-1, width)
    else:
        (final,) = exchange(gather(by_tensor, final))
        final = final.reshape(-1, width)
        logits, tops, totals, picks = head_logits(final, embedding, columns_of)
        top = jnp.max(tops, axis=1)
        total = jnp.sum(totals * jnp.exp(tops - top[:, None]), axis=1)
        pick = jnp.sum(picks, axis=1)
        (stats,) = exchange(
            gather(by_tensor, jnp.pad(jnp.stack([top, total, pick]), ((0, 5), (0, 0))))
        )
    tokens = final.shape[0]
    top_all = jnp.max(stats[:, 0], axis=0)
    log_norm = top_all + jnp.log(jnp.sum(stats[:, 1] * jnp.exp(stats[:, 0] - top_all), axis=0))
    terms = jnp.where(valid, log_norm - jnp.sum(stats[:, 2], axis=0), 0.0)
    loss_part = jnp.sum(
        lax.dynamic_index_in_dim(terms.reshape(shards, -1), z, 0, keepdims=False)
    )
    row_weight = jnp.where(valid, 1.0 / token_count, 0.0)
    if planes:
        grad_logits, grad_final = line_head_grads(
            by_tensor, exchange.ident("head grads"), logits, embedding, columns_of,
            log_norm[:, None], row_weight[:, None],
        )
    else:
        grad_logits, back = head_grads(
            logits, embedding, columns_of, log_norm[:, None], row_weight[:, None]
        )
        (grad_final,) = exchange(
            Job("reduce", [by_tensor], back.reshape(shards, group_part, width))
        )
    _, final_back = jax.vjp(layer_norm, h, outer_gains[-1], outer_offsets[-1])
    grad, final_gain, final_offset = final_back(grad_final)

    def section_sums(pair, got):
        out = []
        for one, dealt in zip(pair, got):
            low = own_and_dealt(one, dealt, s).astype(BF16)
            if one.ndim == 4:
                out.append(low.reshape(low.shape[0], fan, cols, width))
            else:
                out.append(low.reshape(halves, fan, strip, width))
        return out

    def tensor_jobs(lows):
        return [deal(by_tensor, low, 1) for low in lows]

    def tensor_sums(lows, got):
        return [
            own_and_dealt(low, dealt, z, 1).astype(BF16) for low, dealt in zip(lows, got)
        ]

    def spread_jobs(pieces):
        return [Job("spread", [by_dp, by_section], piece) for piece in pieces]

    small_rows = [None] * layers
    pairs = [None] * layers
    attn_low, attn_done, feed_done = ([None] * layers for _ in range(3))
    for l in reversed(range(layers)):
        p = params[l]
        section_in, normed, q, k, v, mixed, lse, middle, second, before = kept[l]
        pair = by_section if planes else None
        late = planes and l + 1 < layers
        jobs = tensor_jobs(attn_low[l + 1]) if late else []
        (total, g_feed, up_sum, *dealt), got = feed_back(
            team, ident("feed back", jobs), jobs, pair, grad.astype(BF16),
            second.reshape(seq, width), before, p["strips"],
        )
        if late:
            attn_done[l + 1] = tensor_sums(attn_low[l + 1], got)
        if planes:
            feed_low = section_sums([g_feed], [one[None] for one in dealt])
        _, norm_back = jax.vjp(layer_norm, middle, p["gains"][1], p["offsets"][1])
        grad_mid, gain_two, offset_two = norm_back(total)
        grad_mid = grad_mid + grad
        jobs = tensor_jobs(feed_low) if planes else []
        (total, g_attn, qv_sum, *dealt), got = attend_back(
            team, ident("attend back", jobs), jobs, pair, grad_mid.astype(BF16), length, slopes,
            normed, p["qk"], p["vo"], q, k, v, mixed, lse,
        )
        g_attn = g_attn.reshape((2, 2) + g_attn.shape[1:])
        if planes:
            feed_done[l] = tensor_sums(feed_low, got)
            attn_low[l] = section_sums([g_attn], [one[None] for one in dealt])
        _, norm_back = jax.vjp(layer_norm, section_in, p["gains"][0], p["offsets"][0])
        grad_in, gain_one, offset_one = norm_back(total)
        bias_two = jnp.sum(grad, axis=0)
        grad = grad_in + grad_mid
        pairs[l] = (g_attn, g_feed)

        def placed(values, size):
            out = jnp.zeros((fan if planes else shards, cut, size), F32)
            at = (0, j, 0) if planes else (z, 0, 0)
            return lax.dynamic_update_slice(out, values.reshape(fan, 1, size), at).reshape(
                -1, width
            )

        units = jnp.swapaxes(up_sum.reshape(halves, fan, strip), 0, 1)
        small_rows[l] = [
            gain_one[None],
            gain_two[None],
            offset_one[None],
            offset_two[None],
            jnp.sum(grad_mid, axis=0)[None],
            bias_two[None],
            placed(qv_sum[0], cols),
            placed(qv_sum[1], cols),
            placed(units, hidden),
        ]

    _, embed_back = jax.vjp(layer_norm, x, outer_gains[0], outer_offsets[0])
    grad_rows, embed_gain, embed_offset = embed_back(grad)
    packed = jnp.concatenate(
        [row for l in range(layers) for row in small_rows[l]]
        + [embed_gain[None], final_gain[None], embed_offset[None], final_offset[None]]
        + [jnp.broadcast_to(loss_part, (1, width))]
    )
    used = packed.shape[0]
    packed = jnp.pad(packed, ((0, -used % 8), (0, 0)))
    jobs = [Job("gather", [Group(("section", "tensor"), (sections, shards))], packed, late=True)]
    if planes:
        jobs += spread_jobs(attn_done[1] + feed_done[1] + feed_done[0])
        jobs += [Job("deal", [by_tensor], low, 1, late=True) for low in attn_low[0]]
    embed_sum, packed, *got = table_sum(
        by_section, by_dp, by_tensor, jobs, grad_logits, ids[None, :] - vocab_start, final,
        grad_rows.astype(BF16), exchange.ident("table"),
    )
    packed = jnp.sum(packed, axis=0)
    jobs = [gather(by_dp, packed)]
    if planes:
        spread_one = got[:2]
        jobs += spread_jobs(tensor_sums(attn_low[0], got[3:]))
    packed, *spread_zero = exchange(*jobs)
    packed = jnp.sum(packed, axis=0)
    if planes:
        spread_zero.append(got[2])
        attn_sum, feed_sum = (
            jnp.where(s == 0, zero, one) for zero, one in zip(spread_zero, spread_one)
        )
    else:
        chosen = [
            lax.dynamic_index_in_dim(
                lax.psum(jnp.stack([pair[n] for pair in pairs]), ("section", "dp")),
                s, 0, keepdims=False,
            )
            for n in range(2)
        ]
        attn_sum = chosen[0][:, None]
        feed_sum = chosen[1][:, None, None]
    embed_sum = embed_sum.reshape(vocab, width).astype(F32)
    per_layer = (used - 5) // layers
    mine = lax.dynamic_slice_in_dim(packed, s * per_layer, per_layer, 0)
    qv_rows = mine[6:8].reshape(2, -1)
    ff_row = mine[8:].reshape(-1)
    grad_qv = lax.dynamic_slice_in_dim(qv_rows, z * local_cols, local_cols, 1)
    grad_up_bias = lax.dynamic_slice_in_dim(ff_row, z * hidden * cut, hidden * cut, 0)
    base = per_layer * layers
    grad_outer_gain = lax.dynamic_slice_in_dim(packed, base + s, 1, 0)
    grad_outer_bias = lax.dynamic_slice_in_dim(packed, base + 2 + s, 1, 0)
    loss = packed[base + 4, 0] / token_count

    def columns(array):
        return array.reshape(-1, width).T.astype(F32)

    grad_qkv = jnp.stack(
        [columns(attn_sum[0, :, 0]), columns(attn_sum[1, :, 0]), columns(attn_sum[0, :, 1])]
    )
    grad_out_mat = attn_sum[1, :, 1].astype(F32).reshape(-1, width)
    grad_up = columns(feed_sum[0])
    grad_down = feed_sum[1].astype(F32).reshape(-1, width)
    return (
        loss,
        embed_sum,
        grad_outer_gain,
        grad_outer_bias,
        mine[0:2][None],
        mine[2:4][None],
        grad_qkv[None],
        grad_qv[None],
        grad_out_mat[None],
        grad_up[None],
        grad_up_bias[None],
        grad_down[None],
        mine[4:6][None],
    )


def solution(mesh):
    return jax.shard_map(
        functools.partial(per_device, dict(mesh.shape)),
        mesh=mesh,
        in_specs=(
            P("dp", None),
            P("dp", None),
            P(),
            P("tensor", None),
            P("section", None),
            P("section", None),
            P("section", None, None),
            P("section", None, None),
            P("section", None, None, "tensor"),
            P("section", None, "tensor"),
            P("section", "tensor", None),
            P("section", None, "tensor"),
            P("section", "tensor"),
            P("section", "tensor", None),
            P("section", None, None),
        ),
        out_specs=(
            P(),
            P("tensor", None),
            P("section", None),
            P("section", None),
            P("section", None, None),
            P("section", None, None),
            P("section", None, None, "tensor"),
            P("section", None, "tensor"),
            P("section", "tensor", None),
            P("section", None, "tensor"),
            P("section", "tensor"),
            P("section", "tensor", None),
            P("section", None, None),
        ),
        check_vma=False,
    )
```

```python
import functools
import math

import jax
import jax.numpy as jnp
from jax import lax
from jax.experimental import pallas as pl
from jax.experimental.pallas import tpu as pltpu
from jax.sharding import PartitionSpec as P

HEADS = 16
HEAD_DIM = 64
EPS = 1e-05
NEG = -1e30
MESH = pl.DeviceIdType.MESH
F32 = jnp.float32
BF16 = jnp.bfloat16


def matmul(former, latter):
    return jnp.dot(former, latter, preferred_element_type=F32)


def matmul_t(former, latter):
    return lax.dot_general(
        former, latter, (((1,), (1,)), ((), ())), preferred_element_type=F32
    )


def outer_sum(former, latter):
    return lax.dot_general(
        former, latter, (((0,), (0,)), ((), ())), preferred_element_type=F32
    )


def layer_norm(inputs, weight, offset):
    centre = inputs - jnp.mean(inputs, axis=-1, keepdims=True)
    spread = jnp.mean(centre * centre, axis=-1, keepdims=True)
    return centre * lax.rsqrt(spread + EPS) * weight + offset


def gelu_tanh(inputs):
    return jax.nn.gelu(inputs, approximate=True)


class Group:
    def __init__(self, axes, sizes, square=False, line=False):
        self.square = square
        self.line = line
        self.axes = axes
        self.sizes = sizes
        self.count = math.prod(sizes)

    def me(self):
        place = 0
        for axis, size in zip(self.axes, self.sizes):
            place = place * size + lax.axis_index(axis)
        return place

    def device(self, place):
        spot = {}
        for axis, size in reversed(list(zip(self.axes, self.sizes))):
            spot[axis] = lax.rem(place, size)
            place = lax.div(place, size)
        return spot

    def peers(self):
        me = self.me()
        return [lax.rem(me + step, self.count) for step in range(1, self.count)]


def greet(groups):
    barrier = pltpu.get_barrier_semaphore()
    total = 0
    for group in groups:
        for peer in group.peers():
            pl.semaphore_signal(
                barrier, inc=1, device_id=group.device(peer), device_id_type=MESH
            )
            total += 1
    pl.semaphore_wait(barrier, total)


def send(group, peer, step, src, dst, send_sem, recv_sem):
    copy = pltpu.make_async_remote_copy(
        src_ref=src,
        dst_ref=dst,
        send_sem=send_sem.at[step],
        recv_sem=recv_sem.at[step],
        device_id=group.device(peer),
        device_id_type=MESH,
    )
    copy.start()
    return copy


def tie(*arrays):
    return lax.optimization_barrier(arrays)


class LineRows:
    def __init__(self, group, x, full, send_sem, recv_sem):
        self.group, self.count, self.me = group, group.count, group.me()
        self.x, self.full, self.sems = x, full, (send_sem, recv_sem)

    def copy(self, up, step):
        place = self.me - step if up else self.me + step
        place = jnp.clip(place, 0, self.count - 1)
        number = step if up else self.count - 1 + step
        src = self.x if step == 0 else self.full.at[place]
        return pltpu.make_async_remote_copy(
            src_ref=src,
            dst_ref=self.full.at[place],
            send_sem=self.sems[0].at[number],
            recv_sem=self.sems[1].at[number],
            device_id=self.group.device(
                jnp.clip(self.me + 1 if up else self.me - 1, 0, self.count - 1)
            ),
            device_id_type=MESH,
        )

    def leaves(self, up, step):
        if up:
            return (self.me - step >= 0) & (self.me < self.count - 1)
        return (self.me + step < self.count) & (self.me > 0)

    def arrives(self, up, step):
        return self.me - 1 - step >= 0 if up else self.me + 1 + step < self.count

    def start(self):
        for up in (True, False):

            @pl.when(self.leaves(up, 0))
            def _(up=up):
                self.copy(up, 0).start()

    def step(self, step):
        for up in (True, False):

            @pl.when(self.arrives(up, step - 1))
            def _(up=up):
                self.copy(up, step - 1).wait_recv()

            if step < self.count - 1:

                @pl.when(self.leaves(up, step))
                def _(up=up):
                    self.copy(up, step).start()

    def wait_sends(self):
        for step in range(self.count - 1):
            for up in (True, False):

                @pl.when(self.leaves(up, step))
                def _(up=up, step=step):
                    self.copy(up, step).wait_send()

    def finish(self):
        for step in range(1, self.count):
            self.step(step)
        self.wait_sends()


class LineSum:
    def __init__(self, group, x, stage, land, send_sem, recv_sem):
        self.group, self.count, self.me = group, group.count, group.me()
        self.x, self.stage, self.land, self.sems = x, stage, land, (send_sem, recv_sem)

    def copy(self, up, step):
        side = 0 if up else 1
        return pltpu.make_async_remote_copy(
            src_ref=self.stage.at[side, step],
            dst_ref=self.land.at[side, step],
            send_sem=self.sems[0].at[side, step],
            recv_sem=self.sems[1].at[side, step],
            device_id=self.group.device(
                jnp.clip(self.me + 1 if up else self.me - 1, 0, self.count - 1)
            ),
            device_id_type=MESH,
        )

    def leaves(self, up, step):
        return self.me < self.count - 1 - step if up else self.me > step

    def behind(self, up):
        return self.me > 0 if up else self.me < self.count - 1

    def first(self, step):
        for up in (True, False):
            place = self.count - 1 - step if up else step
            side = 0 if up else 1

            @pl.when(self.leaves(up, step) & jnp.logical_not(self.behind(up)))
            def _(up=up, place=place, side=side):
                self.stage[side, step] = self.x[place]
                self.copy(up, step).start()

    def rest(self, step, near=None):
        for up in (True, False):
            place = self.count - 1 - step if up else step
            side = 0 if up else 1
            here = self.leaves(up, step) & self.behind(up)
            if near is not None:
                by_end = self.me == (1 if up else self.count - 2)
                here = here & (by_end if near else jnp.logical_not(by_end))

            @pl.when(here)
            def _(up=up, place=place, side=side):
                self.copy(up, step).wait_recv()
                total = self.x[place].astype(F32) + self.land[side, step].astype(F32)
                self.stage[side, step] = total.astype(self.stage.dtype)
                self.copy(up, step).start()

    def finish(self, out):
        out[...] = self.x[self.me].astype(F32)
        for up in (True, False):
            side = 0 if up else 1
            for step in range(self.count - 1):

                @pl.when(self.behind(up) & (self.me == (self.count - 1 - step if up else step)))
                def _(up=up, step=step, side=side):
                    self.copy(up, step).wait_recv()
                    out[...] += self.land[side, step].astype(F32)

        for up in (True, False):
            for step in range(self.count - 1):

                @pl.when(self.leaves(up, step))
                def _(up=up, step=step):
                    self.copy(up, step).wait_send()


class Job:
    def __init__(self, kind, groups, x, axis=0, late=False):
        self.late = late
        self.kind, self.groups, self.x, self.axis = kind, groups, x, axis
        count = groups[0].count
        rest = x.shape[:axis] + x.shape[axis + 1 :]
        dma = pltpu.SemaphoreType.DMA
        self.in_spec = pl.BlockSpec(memory_space=pl.ANY)
        self.out_spec = pl.BlockSpec(memory_space=pl.ANY)
        self.scratch = [dma((count - 1,)), dma((count - 1,)), dma]
        if kind in ("gather", "spread"):
            self.in_spec = pl.BlockSpec(memory_space=pltpu.VMEM)
        if kind == "gather" and groups[0].line:
            self.scratch = [dma((2 * count - 2,)), dma((2 * count - 2,)), dma]
        if kind == "gather":
            self.out = jax.ShapeDtypeStruct((count,) + x.shape, x.dtype)
        elif kind == "spread":
            self.out = jax.ShapeDtypeStruct((groups[1].count, count) + x.shape, x.dtype)
            copies = 7 if groups[0].square else count
            if groups[0].square:
                self.scratch = [dma((6,)), dma((6,)), dma]
            self.scratch += [dma((copies,)), dma((copies,))]
        elif kind == "deal":
            self.out = jax.ShapeDtypeStruct((count - 1,) + rest, x.dtype)
        else:
            self.out = jax.ShapeDtypeStruct(rest, F32)
            self.out_spec = pl.BlockSpec(memory_space=pltpu.VMEM)
            if groups[0].line:
                self.in_spec = pl.BlockSpec(memory_space=pltpu.VMEM)
                self.scratch = [dma((2, count - 1)), dma((2, count - 1)), dma]
                self.scratch += [pltpu.VMEM((2, count - 1) + rest, x.dtype)] * 2
            else:
                self.scratch += [
                    pltpu.VMEM(rest, x.dtype), pltpu.VMEM((count - 1,) + rest, x.dtype)
                ]

    def key(self):
        return (self.kind, tuple(g.axes for g in self.groups), self.x.shape, str(self.x.dtype), self.axis)

    def start(self, x, out, send_sem, recv_sem, own_sem, *more):
        group = self.groups[0]
        me = group.me()
        peers = list(enumerate(group.peers()))

        def block(place):
            return x.at[(slice(None),) * self.axis + (place,)]

        if self.kind == "gather" and group.line:
            line = LineRows(group, x, out, send_sem, recv_sem)
            line.start()
            own = pltpu.make_async_copy(x, out.at[me], own_sem)
            own.start()

            def finish():
                line.finish()
                own.wait()

        elif self.kind == "reduce" and group.line:
            line = LineSum(group, x, *more, send_sem, recv_sem)
            for step in range(group.count - 1):
                line.first(step)

            def finish():
                for step in range(group.count - 1):
                    line.rest(step)
                line.finish(out)

        elif self.kind == "gather":
            copies = [send(group, p, k, x, out.at[me], send_sem, recv_sem) for k, p in peers]
            own = pltpu.make_async_copy(x, out.at[me], own_sem)
            own.start()

            def finish():
                for copy in copies + [own]:
                    copy.wait()

        elif self.kind == "spread" and group.square:
            pair = self.groups[1]
            side = pair.me()
            fw_send, fw_recv = more
            size = self.x.shape[0] // 2
            near = [across(me, 0), across(me, 1)]

            def copy_of(number):
                at = pl.ds(SQUARE_HALF[number] * size, size)
                place = me if number < 4 else near[number - 4]
                dst = out.at[side, place, at]
                src = x.at[at] if number < 4 else dst
                copy = pltpu.make_async_remote_copy(
                    src_ref=src, dst_ref=dst, send_sem=send_sem.at[number],
                    recv_sem=recv_sem.at[number], device_id=group.device(near[SQUARE_STEP[number]]),
                    device_id_type=MESH,
                )
                origin = near[SQUARE_STEP[number]] if number < 4 else across(me, 2)
                return copy, out.at[side, origin, at]

            copies = [copy_of(number) for number in range(6)]
            for number in (0, 2, 1, 3):
                copies[number][0].start()
            passed = [send(pair, 1 - side, 6, x, out.at[side, me], fw_send, fw_recv)]
            own = pltpu.make_async_copy(x, out.at[side, me], own_sem)
            own.start()

            def arrived(number):
                copy, landed = copies[number]
                copy.wait_recv()
                passed.append(send(pair, 1 - side, number, landed, landed, fw_send, fw_recv))

            def middle():
                for number in (0, 2):
                    copies[number][0].wait_recv()
                    copies[4 + number // 2][0].start()
                    landed = copies[number][1]
                    passed.append(send(pair, 1 - side, number, landed, landed, fw_send, fw_recv))

            def finish():
                for number in (1, 3, 4, 5):
                    arrived(number)
                for copy in passed:
                    copy.wait()
                for copy, _ in copies:
                    copy.wait_send()
                own.wait()

            return middle, finish

        elif self.kind == "spread":
            pair = self.groups[1]
            side = pair.me()
            fw_send, fw_recv = more
            home = out.at[side, me]
            copies = [send(group, p, k, x, home, send_sem, recv_sem) for k, p in peers]
            last = group.count - 1
            passed = [send(pair, 1 - side, last, x, home, fw_send, fw_recv)]
            own = pltpu.make_async_copy(x, home, own_sem)
            own.start()

            def finish():
                for k, copy in enumerate(copies):
                    copy.wait_recv()
                    place = out.at[side, lax.rem(me + group.count - 1 - k, group.count)]
                    passed.append(send(pair, 1 - side, k, place, place, fw_send, fw_recv))
                for copy in passed:
                    copy.wait()
                for copy in copies:
                    copy.wait_send()
                own.wait()

        elif self.kind == "deal":
            copies = [send(group, p, k, block(p), out.at[k], send_sem, recv_sem) for k, p in peers]

            def finish():
                for copy in copies:
                    copy.wait()

        else:
            kept, slots = more
            copies = [send(group, p, k, block(p), slots.at[k], send_sem, recv_sem) for k, p in peers]
            own = pltpu.make_async_copy(block(me), kept, own_sem)
            own.start()

            def finish():
                own.wait()
                for copy in copies:
                    copy.wait()
                total = kept[...].astype(F32)
                for k in range(group.count - 1):
                    total = total + slots[k].astype(F32)
                out[...] = total

        return None, finish


def pass_on(ends):
    for middle, _ in ends:
        if middle is not None:
            middle()


def finish_jobs(ends):
    for _, finish in ends:
        finish()


def job_groups(jobs):
    return [group for job in jobs for group in job.groups]


def split_scratch(jobs, scratch):
    parts, at = [], 0
    for job in jobs:
        parts.append(scratch[at : at + len(job.scratch)])
        at += len(job.scratch)
    return parts


def exchange_body(jobs, *refs):
    count = len(jobs)
    greet(job_groups(jobs))
    parts = split_scratch(jobs, refs[2 * count :])
    ends = [
        job.start(refs[n], refs[count + n], *parts[n]) for n, job in enumerate(jobs)
    ]
    pass_on(ends)
    finish_jobs(ends)


class Exchanges:
    def __init__(self):
        self.idents = {}

    def ident(self, key):
        return self.idents.setdefault(key, len(self.idents))

    def __call__(self, *jobs):
        jobs = list(jobs)
        return pl.pallas_call(
            functools.partial(exchange_body, jobs),
            out_shape=tuple(job.out for job in jobs),
            in_specs=[job.in_spec for job in jobs],
            out_specs=tuple(job.out_spec for job in jobs),
            scratch_shapes=[one for job in jobs for one in job.scratch],
            compiler_params=pltpu.CompilerParams(
                collective_id=self.ident(tuple(job.key() for job in jobs)),
                has_side_effects=True,
                vmem_limit_bytes=32 * 2**20,
            ),
        )(*[job.x for job in jobs])


CHUNK = 512


def start_rows(group, x_ref, full, send_sem, recv_sem):
    me = group.me()
    full[me] = x_ref[...]
    return [
        send(group, peer, step, x_ref, full.at[me], send_sem, recv_sem)
        for step, peer in enumerate(group.peers())
    ]


def table_body(
    by_section, by_dp, by_tensor, jobs, g_ref, ids_ref, u_ref, gx_ref, *refs
):
    riders = len(jobs)
    xs, (out_ref, *outs), refs = refs[:riders], refs[riders : 2 * riders + 1], refs[2 * riders + 1 :]
    (g_buf, to_partner, from_partner, to_dp, from_dp, own, result,
    g_sem, ps_send, ps_recv, dp_send, dp_recv, ag_send, ag_recv, fw_send, fw_recv, own_sem,
    ) = refs[:17]
    gx_full, gx_send, gx_recv = refs[17:20]
    s, j = by_section.me(), by_dp.me()
    partner = 1 - s
    peers = by_dp.peers() + [j]
    count = by_dp.count
    block = own.shape[0]
    subs = block // CHUNK
    tokens = u_ref.shape[0]
    greet([by_section, by_dp, by_tensor] + job_groups(jobs))
    gx_copies = start_rows(by_tensor, gx_ref, gx_full, gx_send, gx_recv)
    parts = split_scratch(jobs, refs[20:])
    ends = [job.start(xs[n], outs[n], *parts[n]) for n, job in enumerate(jobs)]

    def chunk(half, place, sub):
        return (half * count + place) * subs + sub

    order = [(number, half) for number in range(count) for half in (0, 1)]

    def fetch(index, sub, slot):
        number, away = order[index]
        half = partner if away == 0 else s
        return pltpu.make_async_copy(
            g_ref.at[chunk(half, peers[number], sub)], g_buf.at[slot], g_sem.at[slot]
        )

    def remote(group, peer, number, sub, src, dst, send_sem, recv_sem):
        return pltpu.make_async_remote_copy(
            src_ref=src,
            dst_ref=dst,
            send_sem=send_sem.at[number, sub],
            recv_sem=recv_sem.at[number, sub],
            device_id=group.device(peer),
            device_id_type=MESH,
        )

    def rows(sub):
        return pl.ds(pl.multiple_of(sub * CHUNK, CHUNK), CHUNK)

    def partner_copy(number, sub):
        return remote(
            by_section, partner, number, sub,
            to_partner.at[number, rows(sub)], from_partner.at[number, rows(sub)],
            ps_send, ps_recv,
        )

    def chip_copy(number, sub):
        return remote(
            by_dp, peers[number], number, sub,
            to_dp.at[number, rows(sub)], from_dp.at[number, rows(sub)], dp_send, dp_recv,
        )

    def spread_copy(number, sub):
        return remote(
            by_dp, peers[number], number, sub,
            result.at[rows(sub)], out_ref.at[chunk(s, j, sub)], ag_send, ag_recv,
        )

    sources = [lax.rem(j + count - 1 - number, count) for number in range(count - 1)] + [j]

    def forward_copy(number, sub):
        target = out_ref.at[chunk(s, sources[number], sub)]
        origin = result.at[rows(sub)] if number == count - 1 else target
        return remote(by_section, partner, number, sub, origin, target, fw_send, fw_recv)

    def own_copy(sub):
        return pltpu.make_async_copy(
            result.at[rows(sub)], out_ref.at[chunk(s, j, sub)], own_sem.at[sub]
        )

    for copy in gx_copies:
        copy.wait()
    fetch(0, 0, 0).start()
    for index, (number, away) in enumerate(order):
        half = partner if away == 0 else s

        def one(sub, carry, index=index, number=number, away=away, half=half):
            slot = lax.rem(sub, 2)
            fetch(index, sub, slot).wait()

            @pl.when(sub + 1 < subs)
            def _():
                fetch(index, sub + 1, 1 - slot).start()

            if index + 1 < len(order):

                @pl.when(sub + 1 == subs)
                def _():
                    fetch(index + 1, 0, 1 - slot).start()

            base = chunk(half, peers[number], sub) * CHUNK
            place = base + lax.broadcasted_iota(jnp.int32, (CHUNK, tokens), 0)
            chosen = jnp.where(place == ids_ref[...], 1.0, 0.0).astype(BF16)
            term = outer_sum(g_buf[slot], u_ref[...]) + matmul(
                chosen, gx_full[...].reshape(tokens, gx_full.shape[2])
            )
            if away == 0:
                to_partner[number, rows(sub), :] = term.astype(BF16)
                partner_copy(number, sub).start()
            else:
                partner_copy(number, sub).wait_recv()
                term = term + from_partner[number, rows(sub), :].astype(F32)
                if number < count - 1:
                    to_dp[number, rows(sub), :] = term.astype(BF16)
                    chip_copy(number, sub).start()
                else:
                    own[rows(sub), :] = term
            return carry

        lax.fori_loop(0, subs, one, 0)

    def finish(sub, carry):
        term = own[rows(sub), :]
        for number in range(count - 1):
            chip_copy(number, sub).wait_recv()
            term = term + from_dp[number, rows(sub), :].astype(F32)
        result[rows(sub), :] = term.astype(BF16)
        for number in range(count - 1):
            spread_copy(number, sub).start()
        forward_copy(count - 1, sub).start()
        own_copy(sub).start()
        return carry

    lax.fori_loop(0, subs, finish, 0)

    def take(sub, carry):
        for number in range(count - 1):
            spread_copy(number, sub).wait_recv()
            forward_copy(number, sub).start()
        return carry

    lax.fori_loop(0, subs, take, 0)

    def drain(sub, carry):
        own_copy(sub).wait()
        for number in range(count):
            partner_copy(number, sub).wait_send()
            forward_copy(number, sub).wait()
        for number in range(count - 1):
            chip_copy(number, sub).wait_send()
            spread_copy(number, sub).wait_send()
        return carry

    lax.fori_loop(0, subs, drain, 0)
    pass_on(ends)
    finish_jobs(ends)


def across(me, step):
    bits = jnp.int32(step + 1)
    x, y = lax.rem(me, 2), lax.div(me, 2)
    return 2 * lax.rem(y + lax.div(bits, 2), 2) + lax.rem(x + lax.rem(bits, 2), 2)


SQUARE_HALF = (0, 1, 1, 0, 0, 1)
SQUARE_STEP = (0, 0, 1, 1, 1, 0)


def table_square_body(by_section, by_dp, by_tensor, jobs, g_ref, ids_ref, u_ref, gx_ref, *refs):
    riders = len(jobs)
    xs, (out_ref, *outs), refs = refs[:riders], refs[riders : 2 * riders + 1], refs[2 * riders + 1 :]
    (
        g_buf, to_partner, from_partner, to_dp, hop_land, from_dp, own, result,
        g_sem, ps_send, ps_recv, hop_send, hop_recv, dp_send, dp_recv, ag_send, ag_recv,
        fw_send, fw_recv, own_sem,
    ) = refs[:20]
    gx_full, gx_send, gx_recv = refs[20:23]
    s, j = by_section.me(), by_dp.me()
    partner = 1 - s
    near_x, near_y, far = (across(j, step) for step in range(3))
    peers = [far, near_y, near_x, j]
    count = 4
    block = own.shape[0]
    subs = block // CHUNK
    half_rows = CHUNK // 2
    tokens = u_ref.shape[0]
    greet([by_section, by_dp, by_tensor] + job_groups(jobs))
    line = LineRows(by_tensor, gx_ref, gx_full, gx_send, gx_recv)
    line.start()
    gx_full[line.me] = gx_ref[...]
    parts = split_scratch(jobs, refs[23:])
    ends = [
        job.start(xs[n], outs[n], *parts[n]) for n, job in enumerate(jobs) if not job.late
    ]

    def chunk(half, place, sub):
        return (half * count + place) * subs + sub

    order = [(number, away) for number in range(count) for away in (0, 1)]

    def fetch(index, sub, slot):
        number, away = order[index]
        half = partner if away == 0 else s
        return pltpu.make_async_copy(
            g_ref.at[chunk(half, peers[number], sub)], g_buf.at[slot], g_sem.at[slot]
        )

    def remote(group, peer, number, sub, src, dst, send_sem, recv_sem):
        return pltpu.make_async_remote_copy(
            src_ref=src,
            dst_ref=dst,
            send_sem=send_sem.at[number, sub],
            recv_sem=recv_sem.at[number, sub],
            device_id=group.device(peer),
            device_id_type=MESH,
        )

    def rows(sub):
        return pl.ds(pl.multiple_of(sub * CHUNK, CHUNK), CHUNK)

    def half_of(sub, which):
        return pl.ds(pl.multiple_of(sub * CHUNK + which * half_rows, half_rows), half_rows)

    def partner_copy(number, sub):
        return remote(
            by_section, partner, number, sub,
            to_partner.at[number, rows(sub)], from_partner.at[number, rows(sub)],
            ps_send, ps_recv,
        )

    def hop_copy(which, sub):
        return remote(
            by_dp, (near_x, near_y)[which], which, sub,
            to_dp.at[0, half_of(sub, which)], hop_land.at[half_of(sub, which)], hop_send, hop_recv,
        )

    def chip_copy(number, sub):
        return remote(
            by_dp, (near_y, near_x)[number], number, sub,
            to_dp.at[number + 1, rows(sub)], from_dp.at[number, rows(sub)], dp_send, dp_recv,
        )

    def spread_copy(number, sub):
        which = SQUARE_HALF[number]
        place = j if number < 4 else (near_x, near_y)[number - 4]
        dst = out_ref.at[chunk(s, place, sub), pl.ds(which * half_rows, half_rows)]
        src = result.at[half_of(sub, which)] if number < 4 else dst
        peer = (near_x, near_y)[SQUARE_STEP[number]]
        return remote(by_dp, peer, number, sub, src, dst, ag_send, ag_recv)

    sources = [near_x, near_y, far, j]

    def forward_copy(number, sub):
        target = out_ref.at[chunk(s, sources[number], sub)]
        origin = result.at[rows(sub)] if number == count - 1 else target
        return remote(by_section, partner, number, sub, origin, target, fw_send, fw_recv)

    def own_copy(sub):
        return pltpu.make_async_copy(
            result.at[rows(sub)], out_ref.at[chunk(s, j, sub)], own_sem.at[sub]
        )

    def slot_of(number, away):
        if away == 0:
            return to_partner.at[number]
        return to_dp.at[number] if number < 3 else own

    fetch(0, 0, 0).start()
    stops = {(step * len(order)) // line.count: step for step in range(1, line.count - 1)}
    for index, (number, away) in enumerate(order):
        if index in stops:
            line.step(stops[index])

        def share(sub, carry, index=index, number=number, away=away):
            slot = lax.rem(sub, 2)
            fetch(index, sub, slot).wait()

            @pl.when(sub + 1 < subs)
            def _():
                fetch(index, sub + 1, 1 - slot).start()

            if index + 1 < len(order):

                @pl.when(sub + 1 == subs)
                def _():
                    fetch(index + 1, 0, 1 - slot).start()

            held = slot_of(number, away)
            held[rows(sub), :] = outer_sum(g_buf[slot], u_ref[...]).astype(held.dtype)
            return carry

        lax.fori_loop(0, subs, share, 0)
    pass_on(ends)
    line.step(line.count - 1)
    line.wait_sends()
    late = [job.start(xs[n], outs[n], *parts[n]) for n, job in enumerate(jobs) if job.late]

    for index, (number, away) in enumerate(order):
        half = partner if away == 0 else s

        def one(sub, carry, number=number, away=away, half=half):
            base = chunk(half, peers[number], sub) * CHUNK
            place = base + lax.broadcasted_iota(jnp.int32, (CHUNK, tokens), 0)
            chosen = jnp.where(place == ids_ref[...], 1.0, 0.0).astype(BF16)
            term = matmul(chosen, gx_full[...].reshape(tokens, gx_full.shape[2]))
            term = term + slot_of(number, away)[rows(sub), :].astype(F32)
            if away == 0:
                to_partner[number, rows(sub), :] = term.astype(BF16)
                partner_copy(number, sub).start()
                return carry
            partner_copy(number, sub).wait_recv()
            term = term + from_partner[number, rows(sub), :].astype(F32)
            if number == 0:
                to_dp[0, rows(sub), :] = term.astype(BF16)
                for which in range(2):
                    hop_copy(which, sub).start()
            elif number < 3:
                which = number - 1
                hop_copy(which, sub).wait_recv()
                mine = slice(which * half_rows, (which + 1) * half_rows)
                rest = slice((1 - which) * half_rows, (2 - which) * half_rows)
                to_dp[number, half_of(sub, which), :] = (
                    term[mine] + hop_land[half_of(sub, which), :].astype(F32)
                ).astype(BF16)
                to_dp[number, half_of(sub, 1 - which), :] = term[rest].astype(BF16)
                chip_copy(which, sub).start()
            else:
                own[rows(sub), :] = term
            return carry

        lax.fori_loop(0, subs, one, 0)

    def finish(sub, carry):
        term = own[rows(sub), :]
        for number in range(2):
            chip_copy(number, sub).wait_recv()
            term = term + from_dp[number, rows(sub), :].astype(F32)
        result[rows(sub), :] = term.astype(BF16)
        for number in (0, 2, 1, 3):
            spread_copy(number, sub).start()
        forward_copy(count - 1, sub).start()
        own_copy(sub).start()
        return carry

    lax.fori_loop(0, subs, finish, 0)

    def pass_chunk(sub, carry):
        for number in (0, 2):
            spread_copy(number, sub).wait_recv()
            spread_copy(4 + number // 2, sub).start()
        for number in (0, 1):
            spread_copy(2 * number + 1, sub).wait_recv()
            forward_copy(number, sub).start()
        return carry

    lax.fori_loop(0, subs, pass_chunk, 0)

    def last(sub, carry):
        for number in (4, 5):
            spread_copy(number, sub).wait_recv()
        forward_copy(2, sub).start()
        return carry

    lax.fori_loop(0, subs, last, 0)

    def drain(sub, carry):
        own_copy(sub).wait()
        for number in range(count):
            partner_copy(number, sub).wait_send()
            forward_copy(number, sub).wait()
        for number in range(2):
            hop_copy(number, sub).wait_send()
            chip_copy(number, sub).wait_send()
        for number in range(6):
            spread_copy(number, sub).wait_send()
        return carry

    lax.fori_loop(0, subs, drain, 0)
    finish_jobs(ends)
    pass_on(late)
    finish_jobs(late)


def table_sum(by_section, by_dp, by_tensor, jobs, grads, ids, final, grad_rows, ident):
    chunks, tokens, _ = grads.shape
    width = final.shape[1]
    count = by_dp.count
    subs = chunks // (2 * count)
    block = subs * CHUNK
    assert subs % 2 == 0
    dma = pltpu.SemaphoreType.DMA
    low = functools.partial(pltpu.VMEM, dtype=BF16)
    square = by_dp.square
    scratch = [
        low((2, tokens, CHUNK)),
        low((count, block, width)),
        low((count, block, width)),
        low((count - 1, block, width)),
    ]
    scratch += [low((block, width)), low((2, block, width))] if square else [
        low((count - 1, block, width))
    ]
    scratch += [pltpu.VMEM((block, width), F32), low((block, width)), dma((2,))]
    copies = (count, 2, 2, 6, count) if square else (count, count - 1, count - 1, count)
    scratch += [dma((copy, subs)) for copy in copies for _ in range(2)] + [dma((subs,))]
    scratch += [low((by_tensor.count,) + grad_rows.shape)]
    scratch += [dma(((by_tensor.count - 1) * (2 if square else 1),))] * 2
    vmem = pl.BlockSpec(memory_space=pltpu.VMEM)
    hbm = pl.BlockSpec(memory_space=pl.ANY)
    return pl.pallas_call(
        functools.partial(
            table_square_body if by_dp.square else table_body, by_section, by_dp, by_tensor, jobs
        ),
        out_shape=(jax.ShapeDtypeStruct((chunks, CHUNK, width), BF16),)
        + tuple(job.out for job in jobs),
        in_specs=[hbm, vmem, vmem, vmem] + [job.in_spec for job in jobs],
        out_specs=(hbm,) + tuple(job.out_spec for job in jobs),
        scratch_shapes=scratch + [one for job in jobs for one in job.scratch],
        compiler_params=pltpu.CompilerParams(
            collective_id=ident, has_side_effects=True, vmem_limit_bytes=56 * 2**20
        ),
    )(grads, ids, final, grad_rows, *[job.x for job in jobs])


LANES = 128


def head_logits_body(u_ref, e_ref, ids_ref, logits_ref, top_ref, total_ref, pick_ref):
    step = pl.program_id(0)
    tokens, tile = logits_ref.shape[1:]

    @pl.when(step == 0)
    def _():
        top_ref[...] = jnp.full_like(top_ref, NEG)
        total_ref[...] = jnp.zeros_like(total_ref)
        pick_ref[...] = jnp.zeros_like(pick_ref)

    logits = matmul_t(u_ref[...], e_ref[...])
    logits_ref[0] = logits
    place = step * tile + lax.broadcasted_iota(jnp.int32, (tokens, tile), 1)
    picked = jnp.where(place == ids_ref[...], logits, 0.0)
    pieces = [logits[:, at : at + LANES] for at in range(0, tile, LANES)]
    before = top_ref[...]
    top = functools.reduce(jnp.maximum, pieces, before)
    total = total_ref[...] * jnp.exp(before - top)
    pick = pick_ref[...]
    for number, piece in enumerate(pieces):
        total = total + jnp.exp(piece - top)
        pick = pick + picked[:, number * LANES : (number + 1) * LANES]
    top_ref[...] = top
    total_ref[...] = total
    pick_ref[...] = pick


def head_logits(final, embedding, ids):
    tokens, width = final.shape
    vocab = embedding.shape[0]
    fixed = pl.BlockSpec((tokens, LANES), lambda step: (0, 0))
    stat = jax.ShapeDtypeStruct((tokens, LANES), F32)
    return pl.pallas_call(
        head_logits_body,
        grid=(vocab // CHUNK,),
        out_shape=(
            jax.ShapeDtypeStruct((vocab // CHUNK, tokens, CHUNK), F32), stat, stat, stat
        ),
        in_specs=[
            pl.BlockSpec((tokens, width), lambda step: (0, 0)),
            pl.BlockSpec((CHUNK, width), lambda step: (step, 0)),
            pl.BlockSpec((tokens, 1), lambda step: (0, 0)),
        ],
        out_specs=(
            pl.BlockSpec((1, tokens, CHUNK), lambda step: (step, 0, 0)), fixed, fixed, fixed
        ),
        compiler_params=pltpu.CompilerParams(vmem_limit_bytes=40 * 2**20),
        cost_estimate=pl.CostEstimate(
            flops=2 * tokens * vocab * width,
            bytes_accessed=4 * tokens * vocab + 2 * vocab * width,
            transcendentals=tokens * vocab,
        ),
    )(final, embedding, ids)


def head_grads_body(logits_ref, e_ref, ids_ref, norm_ref, weight_ref, grads_ref, back_ref, acc):
    step = pl.program_id(0)
    tokens, tile = grads_ref.shape[1:]

    @pl.when(step == 0)
    def _():
        acc[...] = jnp.zeros_like(acc)

    place = step * tile + lax.broadcasted_iota(jnp.int32, (tokens, tile), 1)
    probs = jnp.exp(logits_ref[0] - norm_ref[...])
    grads = (jnp.where(place == ids_ref[...], probs - 1.0, probs) * weight_ref[...]).astype(BF16)
    grads_ref[0] = grads
    acc[...] += matmul(grads, e_ref[...])

    @pl.when(step == pl.num_programs(0) - 1)
    def _():
        back_ref[...] = acc[...].astype(BF16)


def head_grads(logits, embedding, ids, norm, weight):
    chunks, tokens, _ = logits.shape
    vocab, width = embedding.shape
    column = pl.BlockSpec((tokens, 1), lambda step: (0, 0))
    tile = pl.BlockSpec((1, tokens, CHUNK), lambda step: (step, 0, 0))
    return pl.pallas_call(
        head_grads_body,
        grid=(chunks,),
        out_shape=(
            jax.ShapeDtypeStruct(logits.shape, BF16),
            jax.ShapeDtypeStruct((tokens, width), BF16),
        ),
        in_specs=[
            tile, pl.BlockSpec((CHUNK, width), lambda step: (step, 0)), column, column, column
        ],
        out_specs=(tile, pl.BlockSpec((tokens, width), lambda step: (0, 0))),
        scratch_shapes=[pltpu.VMEM((tokens, width), F32)],
        compiler_params=pltpu.CompilerParams(vmem_limit_bytes=40 * 2**20),
        cost_estimate=pl.CostEstimate(
            flops=2 * tokens * vocab * width,
            bytes_accessed=6 * tokens * vocab + 2 * vocab * width,
            transcendentals=tokens * vocab,
        ),
    )(logits, embedding, ids, norm, weight)


BLOCK = 256


def masked_scores(queries, keys, slope, length, first):
    rows, cols = queries.shape[0], keys.shape[0]
    raw = matmul_t(queries, keys)
    i = first + lax.broadcasted_iota(jnp.int32, (rows, cols), 0)
    j = lax.broadcasted_iota(jnp.int32, (rows, cols), 1)
    scores = raw * HEAD_DIM ** (-0.5) - slope * (i - j).astype(F32)
    return jnp.where((j <= i) & (j < length), scores, NEG)


SMEM = pl.BlockSpec(memory_space=pltpu.SMEM)
VMEM = pl.BlockSpec(memory_space=pltpu.VMEM)


class TeamRows:
    def __init__(self, team, x_ref, full, stage, slots, own, ag_send, ag_recv, rs_send, rs_recv):
        self.team, self.count, self.me = team, team.count, team.me()
        self.x_ref, self.full, self.stage, self.slots, self.own = x_ref, full, stage, slots, own
        self.ag_sems, self.rs_sems = (ag_send, ag_recv), (rs_send, rs_recv)

    def shifted(self, step):
        return across(self.me, step)

    def peer(self, step):
        if self.team.square:
            return self.shifted(step)
        return lax.rem(self.me + 1 + step, self.count)

    def source(self, step):
        if self.team.square:
            return self.shifted(step)
        return lax.rem(self.me + self.count - 1 - step, self.count)

    def back_step(self, place):
        if self.team.square:
            flip_x = lax.rem(lax.rem(self.me, 2) + lax.rem(place, 2), 2)
            flip_y = lax.rem(lax.div(self.me, 2) + lax.div(place, 2), 2)
            return 2 * flip_y + flip_x - 1
        return lax.rem(place + self.count - 1 - self.me, self.count)

    def remote(self, number, peer, src, dst, sems):
        return pltpu.make_async_remote_copy(
            src_ref=src,
            dst_ref=dst,
            send_sem=sems[0].at[number],
            recv_sem=sems[1].at[number],
            device_id=self.team.device(peer),
            device_id_type=MESH,
        )

    def ag(self, number):
        if not self.team.square:
            return self.remote(
                number, self.peer(number), self.x_ref, self.full.at[self.me], self.ag_sems
            )
        half = self.x_ref.shape[0] // 2
        which = SQUARE_HALF[number]
        rows = pl.ds(which * half, half)
        peer = self.shifted(SQUARE_STEP[number])
        if number < 4:
            src, place = self.x_ref.at[rows], self.me
        else:
            place = self.shifted(number - 4)
            src = self.full.at[place, rows]
        return self.remote(number, peer, src, self.full.at[place, rows], self.ag_sems)

    def rs(self, step):
        return self.remote(
            step, self.peer(step), self.stage.at[self.peer(step)], self.slots.at[step], self.rs_sems
        )

    def send_rows(self):
        for number in (0, 2, 1, 3) if self.team.square else range(self.count - 1):
            self.ag(number).start()
        self.full[self.me] = self.x_ref[...]

    def pass_on(self):
        if self.team.square:
            for number in (0, 2):
                self.ag(number).wait_recv()
                self.ag(4 + number // 2).start()

    def wait_rows(self, step):
        if not self.team.square:
            self.ag(step).wait_recv()
            return
        for number, these in enumerate(((1,), (3,), (4, 5))):

            @pl.when(step == number)
            def _(these=these):
                for one in these:
                    self.ag(one).wait_recv()

    def each_arrival(self, work):
        work(self.me)
        self.pass_on()

        def one(step, carry):
            self.wait_rows(step)
            work(self.source(step))
            return carry

        lax.fori_loop(0, self.count - 1, one, 0)

    def each_arrival_and_back(self, term):
        self.own[...] = term(self.me)
        self.pass_on()

        def one(step, carry):
            self.wait_rows(step)
            place = self.source(step)
            self.stage[place] = term(place).astype(BF16)
            self.rs(self.back_step(place)).start()
            return carry

        lax.fori_loop(0, self.count - 1, one, 0)

    def finish(self, total_ref):
        pass_on(self.ends)
        finish_jobs(self.ends)
        for step in range(self.count - 1):
            self.rs(step).wait()
        total = self.own[...]
        for step in range(self.count - 1):
            total = total + self.slots[step].astype(F32)
        total_ref[...] = total
        for number in range(6 if self.team.square else self.count - 1):
            self.ag(number).wait_send()


def team_scratch(team, part, model):
    count = team.count
    dma = pltpu.SemaphoreType.DMA
    copies = 6 if team.square else count - 1
    return [
        pltpu.VMEM((count, part, model), BF16),
        pltpu.VMEM((count, part, model), BF16),
        pltpu.VMEM((count - 1, part, model), BF16),
        pltpu.VMEM((part, model), F32),
        dma((copies,)),
        dma((copies,)),
        dma((count - 1,)),
        dma((count - 1,)),
    ]


class LateDeal:
    def __init__(self, pair, landing, send_sem, recv_sem):
        self.pair, self.landing, self.sems = pair, landing, (send_sem, recv_sem)

    def other(self):
        return 1 - self.pair.me()

    def start(self, src):
        self.copy = send(self.pair, self.other(), 0, src, self.landing, *self.sems)

    def wait(self):
        self.copy.wait()


def team_call(body, team, ident, jobs, arrays, specs, outs, out_specs, scratch, pair=None, dealt=None, ahead=0):
    if pair is not None:
        outs, out_specs = tuple(outs) + (dealt,), tuple(out_specs) + (HBM,)
        scratch = list(scratch) + [pltpu.SemaphoreType.DMA((1,))] * 2
    part, model = arrays[0].shape
    count_in, count_out, riders = len(arrays), len(outs), len(jobs)
    own_scratch = team_scratch(team, part, model)

    def kernel(*refs):
        ins, refs = refs[:count_in], refs[count_in:]
        xs, refs = refs[:riders], refs[riders:]
        results, refs = refs[:count_out], refs[count_out:]
        landings, refs = refs[:riders], refs[riders:]
        rows = TeamRows(team, ins[0], *refs[: len(own_scratch)])
        refs = refs[len(own_scratch) :]
        mine, refs = refs[: len(scratch)], refs[len(scratch) :]
        greet([team] + job_groups(jobs) + ([] if pair is None else [pair]))
        rows.send_rows()
        parts = split_scratch(jobs, refs)

        def start(numbers):
            return [jobs[n].start(xs[n], landings[n], *parts[n]) for n in numbers]

        rows.landings = landings
        first = start(range(ahead if ahead else riders))
        if ahead:

            def ready():
                pass_on(first)
                finish_jobs(first)
                rows.ends = start(range(ahead, riders))

            rows.ready = ready
        else:
            rows.ends = first
        if pair is None:
            body(rows, ins, results, mine)
        else:
            body(rows, ins, results[:-1], mine[:-2], LateDeal(pair, results[-1], *mine[-2:]))

    out = pl.pallas_call(
        kernel,
        out_shape=tuple(outs) + tuple(job.out for job in jobs),
        in_specs=list(specs) + [job.in_spec for job in jobs],
        out_specs=tuple(out_specs) + tuple(job.out_spec for job in jobs),
        scratch_shapes=own_scratch + list(scratch) + [one for job in jobs for one in job.scratch],
        compiler_params=pltpu.CompilerParams(
            collective_id=ident, has_side_effects=True, vmem_limit_bytes=58 * 2**20
        ),
    )(*arrays, *[job.x for job in jobs])
    return out[:count_out], list(out[count_out:])


def part_rows(place, part):
    return pl.ds(pl.multiple_of(place * part, part), part)


def attend_body(rows, ins, outs, scratch):
    x_ref, length_ref, slope_ref, bias_ref, *weights = ins
    total_ref, full_out, q_ref, k_ref, v_ref, mixed_ref, lse_ref = outs
    full_sem, *buffers = scratch
    if not weights:
        *weights, sems = buffers
        rows.ready()
        copies = [
            pltpu.make_async_copy(rows.landings[n], weights[n], sems.at[n]) for n in range(2)
        ]
        for copy in copies:
            copy.start()
        for copy in copies:
            copy.wait()
    qk_ref, vo_ref = weights

    def weight(ref, n):
        block = ref[n]
        return block.reshape(-1, block.shape[-1])

    part = x_ref.shape[0]
    width = q_ref.shape[1]

    def project(place):
        at = part_rows(place, part)
        block = rows.full[place]
        q_ref[at, :] = (matmul_t(block, weight(qk_ref, 0)) + bias_ref[0:1, :]).astype(BF16)
        k_ref[at, :] = matmul_t(block, weight(qk_ref, 1)).astype(BF16)
        v_ref[at, :] = (matmul_t(block, weight(vo_ref, 0)) + bias_ref[1:2, :]).astype(BF16)

    rows.each_arrival(project)
    keep = pltpu.make_async_copy(rows.full, full_out, full_sem)
    keep.start()

    def one(turn, carry):
        step = lax.rem(2 * rows.count - 2 - turn, rows.count)
        place = rows.peer(step)
        for block in range(rows.count):

            @pl.when(place == block)
            def _(first=block * part, upto=(block + 1) * part):
                for head in range(width // HEAD_DIM):
                    lanes = slice(head * HEAD_DIM, (head + 1) * HEAD_DIM)
                    scores = masked_scores(
                        q_ref[first:upto, lanes], k_ref[:upto, lanes], slope_ref[head],
                        length_ref[0], first,
                    )
                    highest = jnp.max(scores, axis=-1, keepdims=True)
                    powers = jnp.exp(scores - highest)
                    total = jnp.sum(powers, axis=-1, keepdims=True)
                    probs = (powers * (1.0 / total)).astype(BF16)
                    mixed_ref[first:upto, lanes] = matmul(probs, v_ref[:upto, lanes]).astype(BF16)
                    lse_ref[head, first:upto, :] = highest + jnp.log(total)

        term = matmul(mixed_ref[part_rows(place, part), :], weight(vo_ref, 1))

        @pl.when(step < rows.count - 1)
        def _():
            rows.stage[place] = term.astype(BF16)
            rows.rs(step).start()

        @pl.when(step == rows.count - 1)
        def _():
            rows.own[...] = term

        return carry

    lax.fori_loop(0, rows.count, one, 0)
    rows.finish(total_ref)
    keep.wait()


HBM = pl.BlockSpec(memory_space=pl.ANY)


def attend(team, ident, jobs, x, length, slopes, bias, weights):
    part, model = x.shape
    seq = part * team.count
    width = bias.shape[1]
    scratch = [pltpu.SemaphoreType.DMA]
    if not weights:
        scratch += [pltpu.VMEM(job.out.shape, BF16) for job in jobs[:2]]
        scratch.append(pltpu.SemaphoreType.DMA((2,)))
    low = jax.ShapeDtypeStruct((seq, width), BF16)
    return team_call(
        attend_body, team, ident, jobs,
        [x, length, slopes, bias] + weights,
        [VMEM, SMEM, SMEM, VMEM] + [VMEM] * len(weights),
        (
            jax.ShapeDtypeStruct((part, model), F32),
            jax.ShapeDtypeStruct((team.count, part, model), BF16),
            low, low, low, low,
            jax.ShapeDtypeStruct((width // HEAD_DIM, seq, 1), F32),
        ),
        (VMEM, HBM, VMEM, VMEM, VMEM, VMEM, VMEM),
        scratch,
        ahead=0 if weights else 2,
    )


def attend_back_body(rows, ins, outs, scratch, late=None):
    gy_ref, length_ref, slope_ref, a_ref, qk_ref, vo_ref, q_ref, k_ref, v_ref, mixed_ref, lse_ref = ins
    total_ref, grads_ref, sums_ref = outs
    go, gq, gk, gv, gk_sum, gv_sum = scratch
    part = gy_ref.shape[0]
    seq, width = q_ref.shape
    heads = width // HEAD_DIM
    gk_sum[...] = jnp.zeros_like(gk_sum)
    gv_sum[...] = jnp.zeros_like(gv_sum)
    sums_ref[...] = jnp.zeros_like(sums_ref)

    def open_block(place):
        go[part_rows(place, part), :] = matmul_t(rows.full[place], vo_ref[1]).astype(BF16)

    rows.each_arrival(open_block)
    for block in reversed(range(rows.count)):
        first, upto = block * part, (block + 1) * part
        for head in range(heads):
            lanes = slice(head * HEAD_DIM, (head + 1) * HEAD_DIM)
            queries, grads = q_ref[first:upto, lanes], go[first:upto, lanes]
            keys, values = k_ref[:upto, lanes], v_ref[:upto, lanes]
            scores = masked_scores(queries, keys, slope_ref[head], length_ref[0], first)
            probs = jnp.exp(scores - lse_ref[head, first:upto, :])
            grad_probs = matmul_t(grads, values)
            inner = jnp.sum(probs * grad_probs, axis=-1, keepdims=True)
            grad_scores = (probs * (grad_probs - inner) * HEAD_DIM ** (-0.5)).astype(BF16)
            piece = matmul(grad_scores, keys)
            sums_ref[0:1, lanes] += jnp.sum(piece, axis=0, keepdims=True)
            gq[first:upto, lanes] = piece.astype(BF16)
            gk_sum[:upto, lanes] += outer_sum(grad_scores, queries)
            gv_sum[:upto, lanes] += outer_sum(probs.astype(BF16), grads)
        gk[first:upto, :] = gk_sum[first:upto, :].astype(BF16)
        gv[first:upto, :] = gv_sum[first:upto, :].astype(BF16)
        term = (
            matmul(gq[first:upto, :], qk_ref[0]) + matmul(gk[first:upto, :], qk_ref[1])
            + matmul(gv[first:upto, :], vo_ref[0])
        )

        @pl.when(rows.me != block)
        def _(block=block, term=term):
            rows.stage[block] = term.astype(BF16)
            rows.rs(rows.back_step(block)).start()

        @pl.when(rows.me == block)
        def _(term=term):
            rows.own[...] = term

    sums_ref[1:2, :] = jnp.sum(gv_sum[...], axis=0, keepdims=True)
    model = gy_ref.shape[1]
    grads_ref[3] = outer_sum(mixed_ref[...], rows.full[...].reshape(seq, model))
    grads_ref[0] = outer_sum(gq[...], a_ref[...])
    grads_ref[1] = outer_sum(gv[...], a_ref[...])
    grads_ref[2] = outer_sum(gk[...], a_ref[...])
    if late is not None:
        late.start(grads_ref.at[pl.ds(2 * late.other(), 2)])
    rows.finish(total_ref)
    if late is not None:
        late.wait()


def attend_back(team, ident, jobs, pair, gy, length, slopes, a, qk, vo, q, k, v, mixed, lse):
    part, model = gy.shape
    seq, width = q.shape
    return team_call(
        attend_back_body, team, ident, jobs,
        [gy, length, slopes, a, qk, vo, q, k, v, mixed, lse],
        [VMEM, SMEM, SMEM] + [VMEM] * 8,
        (
            jax.ShapeDtypeStruct((part, model), F32),
            jax.ShapeDtypeStruct((4, width, model), F32),
            jax.ShapeDtypeStruct((2, width), F32),
        ),
        (VMEM,) * 3,
        [pltpu.VMEM((seq, width), BF16)] * 4 + [pltpu.VMEM((seq, width), F32)] * 2,
        pair,
        jax.ShapeDtypeStruct((2, width, model), F32),
    )


GELU_A = 0.7978845608028654
GELU_B = 0.044715


def strip_rows(strips, which, first, size):
    length = strips[0].shape[1]
    return strips[first // length][which, first % length : first % length + size, :]


def feed_body(rows, ins, outs, scratch):
    x_ref, bias_ref, *strips = ins
    total_ref, full_out, before_ref = outs
    (full_sem,) = scratch
    part = x_ref.shape[0]
    units = bias_ref.shape[1]
    tile = min(units, BLOCK)

    def term(place):
        at = part_rows(place, part)
        block = rows.full[place]
        total = None
        for first in range(0, units, tile):
            lanes = slice(first, first + tile)
            before = matmul_t(block, strip_rows(strips, 0, first, tile)) + bias_ref[:, lanes]
            before_ref[at, lanes] = before
            bend = jnp.tanh(GELU_A * (before + GELU_B * before * before * before))
            active = (0.5 * before * (1.0 + bend)).astype(BF16)
            piece = matmul(active, strip_rows(strips, 1, first, tile))
            total = piece if total is None else total + piece
        return total

    rows.each_arrival_and_back(term)
    keep = pltpu.make_async_copy(rows.full, full_out, full_sem)
    keep.start()
    rows.finish(total_ref)
    keep.wait()


def feed(team, ident, jobs, x, strips, bias):
    part, model = x.shape
    units = bias.shape[1]
    return team_call(
        feed_body, team, ident, jobs,
        [x, bias] + strips,
        [VMEM] * (2 + len(strips)),
        (
            jax.ShapeDtypeStruct((part, model), F32),
            jax.ShapeDtypeStruct((team.count, part, model), BF16),
            jax.ShapeDtypeStruct((part * team.count, units), F32),
        ),
        (VMEM, HBM, VMEM),
        [pltpu.SemaphoreType.DMA],
    )


def feed_back_body(rows, ins, outs, scratch, late=None):
    gz_ref, c_ref, before_ref, *strips = ins
    total_ref, grads_ref, sums_ref = outs
    active, low = scratch
    part, model = gz_ref.shape
    seq = part * rows.count
    units = before_ref.shape[1]
    tile = min(units, BLOCK)
    sums_ref[...] = jnp.zeros_like(sums_ref)

    def term(place):
        at = part_rows(place, part)
        gz = rows.full[place]
        for first in range(0, units, tile):
            lanes = slice(first, first + tile)
            before = before_ref[at, lanes]
            square = before * before
            bend = jnp.tanh(GELU_A * before * (1.0 + GELU_B * square))
            half = 0.5 * (1.0 + bend)
            slope = half + 0.5 * before * (1.0 - bend * bend) * (
                GELU_A * (1.0 + 3.0 * GELU_B * square)
            )
            grad = matmul_t(gz, strip_rows(strips, 1, first, tile)) * slope
            sums_ref[:, lanes] += jnp.sum(grad, axis=0, keepdims=True)
            active[at, lanes] = (before * half).astype(BF16)
            low[at, lanes] = grad.astype(BF16)
        length = strips[0].shape[1]
        return sum(
            matmul(low[at, n * length : (n + 1) * length], strip[0])
            for n, strip in enumerate(strips)
        )

    rows.each_arrival_and_back(term)
    for first in range(0, units, tile):
        lanes = slice(first, first + tile)
        grads_ref[0, lanes, :] = outer_sum(low[:, lanes], c_ref[...])
        grads_ref[1, lanes, :] = outer_sum(active[:, lanes], rows.full[...].reshape(seq, model))
    if late is not None:
        late.start(grads_ref.at[late.other()])
    rows.finish(total_ref)
    if late is not None:
        late.wait()


def feed_back(team, ident, jobs, pair, gz, c, before, strips):
    part, model = gz.shape
    seq = part * team.count
    units = before.shape[1]
    return team_call(
        feed_back_body, team, ident, jobs,
        [gz, c, before] + strips,
        [VMEM] * (3 + len(strips)),
        (
            jax.ShapeDtypeStruct((part, model), F32),
            jax.ShapeDtypeStruct((2, units, model), F32),
            jax.ShapeDtypeStruct((1, units), F32),
        ),
        (VMEM,) * 3,
        [pltpu.VMEM((seq, units), BF16)] * 2,
        pair,
        jax.ShapeDtypeStruct((units, model), F32),
    )


def line_head_logits_body(
    group, x_ref, e_ref, ids_ref, logits_ref, full_out, stats_out,
    full, table, staged, top, total, pick, stats,
    ag_send, ag_recv, e_sem, out_sem, full_sem, st_send, st_recv,
):
    count, me = group.count, group.me()
    part = x_ref.shape[0]
    tiles = e_ref.shape[0] // CHUNK
    line = LineRows(group, x_ref, full, ag_send, ag_recv)
    greet([group])
    line.start()
    full[me] = x_ref[...]
    top[...] = jnp.full_like(top, NEG)
    total[...] = jnp.zeros_like(total)
    pick[...] = jnp.zeros_like(pick)

    def rows_of(tile):
        return pl.ds(pl.multiple_of(tile * CHUNK, CHUNK), CHUNK)

    def load(tile):
        return pltpu.make_async_copy(
            e_ref.at[rows_of(tile)], table.at[rows_of(tile)], e_sem.at[tile]
        )

    def leave(tile, place, slot):
        return pltpu.make_async_copy(
            staged.at[slot], logits_ref.at[tile, part_rows(place, part)], out_sem.at[slot]
        )

    for tile in range(tiles):
        load(tile).start()

    def work(place, first):
        at = part_rows(place, part)
        ids = ids_ref[at, :]

        def one(pair, carry):
            for slot in range(2):
                tile = 2 * pair + slot
                if first:
                    load(tile).wait()

                    @pl.when(pair > 0)
                    def _(slot=slot, tile=tile):
                        leave(tile, place, slot).wait()

                else:
                    leave(tile, place, slot).wait()
                logits = matmul_t(full[place], table[rows_of(tile), :])
                staged[slot] = logits
                leave(tile, place, slot).start()
                column = lax.broadcasted_iota(jnp.int32, (part, CHUNK), 1)
                wanted = ids - tile * CHUNK
                picked = jnp.where(column == wanted, logits, 0.0)
                pieces = [logits[:, at : at + LANES] for at in range(0, CHUNK, LANES)]
                before = top[at, :]
                high = functools.reduce(jnp.maximum, pieces, before)
                sums = total[at, :] * jnp.exp(before - high)
                found = pick[at, :]
                for number, piece in enumerate(pieces):
                    sums = sums + jnp.exp(piece - high)
                    found = found + picked[:, number * LANES : (number + 1) * LANES]
                top[at, :] = high
                total[at, :] = sums
                pick[at, :] = found
            return carry

        lax.fori_loop(0, tiles // 2, one, 0)

    work(me, True)
    for step in range(1, count):
        line.step(step)

        @pl.when(me >= step)
        def _(step=step):
            work(me - step, False)

        @pl.when(me + step < count)
        def _(step=step):
            work(me + step, False)

    keep = pltpu.make_async_copy(full, full_out, full_sem)
    keep.start()
    tall = top[...].T
    high = jnp.max(tall, axis=0, keepdims=True)
    stats[me] = jnp.zeros(stats.shape[1:], F32)
    stats[me, 0:1, :] = high
    stats[me, 1:2, :] = jnp.sum(total[...].T * jnp.exp(tall - high), axis=0, keepdims=True)
    stats[me, 2:3, :] = jnp.sum(pick[...].T, axis=0, keepdims=True)
    copies = [
        send(group, peer, step, stats.at[me], stats.at[me], st_send, st_recv)
        for step, peer in enumerate(group.peers())
    ]
    for slot in range(2):
        leave(0, me, slot).wait()
    line.wait_sends()
    for copy in copies:
        copy.wait()
    stats_out[...] = stats[...]
    keep.wait()


def line_head_logits(group, ident, x, embedding, ids):
    part, width = x.shape
    vocab = embedding.shape[0]
    count = group.count
    tokens = part * count
    tiles = vocab // CHUNK
    assert tiles % 2 == 0
    dma = pltpu.SemaphoreType.DMA
    return pl.pallas_call(
        functools.partial(line_head_logits_body, group),
        out_shape=(
            jax.ShapeDtypeStruct((tiles, tokens, CHUNK), F32),
            jax.ShapeDtypeStruct((count, part, width), BF16),
            jax.ShapeDtypeStruct((count, 8, tokens), F32),
        ),
        in_specs=[VMEM, HBM, VMEM],
        out_specs=(HBM, HBM, VMEM),
        scratch_shapes=[
            pltpu.VMEM((count, part, width), BF16),
            pltpu.VMEM((vocab, width), BF16),
            pltpu.VMEM((2, part, CHUNK), F32),
            pltpu.VMEM((tokens, LANES), F32),
            pltpu.VMEM((tokens, LANES), F32),
            pltpu.VMEM((tokens, LANES), F32),
            pltpu.VMEM((count, 8, tokens), F32),
            dma((2 * count - 2,)),
            dma((2 * count - 2,)),
            dma((tiles,)),
            dma((2,)),
            dma,
            dma((count - 1,)),
            dma((count - 1,)),
        ],
        compiler_params=pltpu.CompilerParams(
            collective_id=ident, has_side_effects=True, vmem_limit_bytes=56 * 2**20
        ),
    )(x, embedding, ids)


def line_head_grads_body(
    group, logits_ref, e_ref, ids_ref, norm_ref, weight_ref, grads_ref, total_ref,
    terms, stage, land, table, staged, low, acc,
    rs_send, rs_recv, e_sem, in_sem, out_sem,
):
    count, me = group.count, group.me()
    part = terms.shape[1]
    tiles = e_ref.shape[0] // CHUNK
    line = LineSum(group, terms, stage, land, rs_send, rs_recv)
    greet([group])

    def rows_of(tile):
        return pl.ds(pl.multiple_of(tile * CHUNK, CHUNK), CHUNK)

    def load(tile):
        return pltpu.make_async_copy(
            e_ref.at[rows_of(tile)], table.at[rows_of(tile)], e_sem.at[tile]
        )

    def enter(tile, place, slot):
        return pltpu.make_async_copy(
            logits_ref.at[tile, part_rows(place, part)], staged.at[slot], in_sem.at[slot]
        )

    def leave(tile, place, slot):
        return pltpu.make_async_copy(
            low.at[:, pl.ds(slot * CHUNK, CHUNK)],
            grads_ref.at[tile, part_rows(place, part)],
            out_sem.at[slot],
        )

    for tile in range(tiles):
        load(tile).start()

    def work(place, fresh=False):
        at = part_rows(place, part)
        ids, norm, weight = ids_ref[at, :], norm_ref[at, :], weight_ref[at, :]
        for slot in range(2):
            enter(slot, place, slot).start()
        acc[...] = jnp.zeros_like(acc)

        def one(pair, carry):
            for slot in range(2):
                tile = 2 * pair + slot
                enter(tile, place, slot).wait()
                if fresh:
                    load(tile).wait()
                column = lax.broadcasted_iota(jnp.int32, (part, CHUNK), 1)
                wanted = ids - tile * CHUNK
                probs = jnp.exp(staged[slot] - norm)
                grads = (jnp.where(column == wanted, probs - 1.0, probs) * weight).astype(BF16)

                @pl.when(pair > 0)
                def _(slot=slot, tile=tile):
                    leave(tile, place, slot).wait()

                low[:, slot * CHUNK : (slot + 1) * CHUNK] = grads
                leave(tile, place, slot).start()

                @pl.when(pair + 1 < tiles // 2)
                def _(slot=slot, tile=tile):
                    enter(tile + 2, place, slot).start()

            rows = pl.ds(pl.multiple_of(pair * 2 * CHUNK, 2 * CHUNK), 2 * CHUNK)
            acc[...] += matmul(low[...], table[rows, :])
            return carry

        lax.fori_loop(0, tiles // 2, one, 0)
        for slot in range(2):
            leave(0, place, slot).wait()
        terms[place] = acc[...].astype(BF16)

    for step in range(count - 1):

        @pl.when(me < count - 1 - step)
        def _(step=step):
            work(count - 1 - step, fresh=step == 0)

        if step == 0:

            @pl.when(me == count - 1)
            def _():
                work(0, fresh=True)

        @pl.when((me > step) & ((me < count - 1) | (step > 0)))
        def _(step=step):
            work(step)

        line.first(step)
        if step == 1:
            line.rest(0, near=True)
    work(me)
    line.rest(0, near=False)
    for step in range(1, count - 1):
        line.rest(step)
    line.finish(total_ref)


def line_head_grads(group, ident, logits, embedding, ids, norm, weight):
    tiles, tokens, _ = logits.shape
    vocab, width = embedding.shape
    count = group.count
    part = tokens // count
    dma = pltpu.SemaphoreType.DMA
    return pl.pallas_call(
        functools.partial(line_head_grads_body, group),
        out_shape=(
            jax.ShapeDtypeStruct(logits.shape, BF16),
            jax.ShapeDtypeStruct((part, width), F32),
        ),
        in_specs=[HBM, HBM, VMEM, VMEM, VMEM],
        out_specs=(HBM, VMEM),
        scratch_shapes=[
            pltpu.VMEM((count, part, width), BF16),
            pltpu.VMEM((2, count - 1, part, width), BF16),
            pltpu.VMEM((2, count - 1, part, width), BF16),
            pltpu.VMEM((vocab, width), BF16),
            pltpu.VMEM((2, part, CHUNK), F32),
            pltpu.VMEM((part, 2 * CHUNK), BF16),
            pltpu.VMEM((part, width), F32),
            dma((2, count - 1)),
            dma((2, count - 1)),
            dma((tiles,)),
            dma((2,)),
            dma((2,)),
        ],
        compiler_params=pltpu.CompilerParams(
            collective_id=ident, has_side_effects=True, vmem_limit_bytes=56 * 2**20
        ),
    )(logits, embedding, ids, norm, weight)


def per_device(
    mesh_shape,
    token_ids,
    target_ids,
    lengths,
    embedding,
    outer_gain,
    outer_bias,
    norm_gain,
    norm_bias,
    qkv_weight,
    qv_bias,
    out_weight,
    up_weight,
    up_bias,
    down_weight,
    row_bias,
):
    sections, groups, shards = (mesh_shape[name] for name in ("section", "dp", "tensor"))
    s, j, z = (lax.axis_index(name) for name in ("section", "dp", "tensor"))
    by_section = Group(("section",), (sections,))
    by_dp = Group(("dp",), (groups,))
    by_tensor = Group(("tensor",), (shards,))
    exchange = Exchanges()
    layers = sections
    vocab, width = embedding.shape
    seq = token_ids.shape[1]
    rows = token_ids.shape[0] * groups
    local_cols = qkv_weight.shape[-1]
    planes = rows == sections * shards and local_cols % (groups * HEAD_DIM) == 0
    by_dp.square = planes and groups == 4
    by_tensor.line = planes
    team = by_dp if planes else by_tensor
    cut = groups if planes else 1
    fan = shards if planes else 1
    halves = 2 if planes else 1
    part = seq // team.count
    cols = local_cols // cut
    hidden = up_weight.shape[-1] // cut
    strip = hidden // halves
    cut_index = j if planes else 0
    my_row = z * sections + s if planes else j * sections + s
    length = lax.dynamic_slice(lengths, (my_row,), (1,))
    token_count = jnp.sum(lengths).astype(F32)
    vocab_start = z * vocab

    def chosen_cols(array, size):
        return lax.dynamic_slice_in_dim(array, cut_index * size, size, array.ndim - 1).T

    def chosen_rows(array, size):
        return lax.dynamic_slice_in_dim(array, cut_index * size, size, 0)

    def pad_rows(array, count):
        return jnp.pad(array, ((0, count - array.shape[0]), (0, width - array.shape[1])))

    sides = jnp.stack(
        [
            jnp.concatenate(
                [
                    chosen_cols(qkv_weight[0, 0], cols),
                    chosen_cols(qkv_weight[0, 2], cols),
                    chosen_cols(up_weight[0], hidden),
                ]
            ),
            jnp.concatenate(
                [
                    chosen_cols(qkv_weight[0, 1], cols),
                    chosen_rows(out_weight[0], cols),
                    chosen_rows(down_weight[0], hidden),
                ]
            ),
        ]
    )
    qv_piece = lax.dynamic_slice_in_dim(qv_bias[0], cut_index * cols, cols, 1)
    up_piece = lax.dynamic_slice_in_dim(up_bias[0], cut_index * hidden, hidden, 0)
    small = jnp.concatenate(
        [outer_gain, outer_bias, norm_gain[0], norm_bias[0], row_bias[0]]
    )
    bias_piece = jnp.concatenate([qv_piece[0], qv_piece[1], up_piece])
    bias_piece = jnp.pad(bias_piece, (0, -bias_piece.shape[0] % 1024)).reshape(-1, 128)

    def gather(group, x):
        return Job("gather", [group], x)

    def deal(group, x, axis=0):
        return Job("deal", [group], x, axis)

    def own_and_dealt(x, dealt, place, axis=0):
        own = lax.dynamic_index_in_dim(x, place, axis, keepdims=False).astype(F32)
        return own + jnp.sum(dealt.astype(F32), axis=0)

    if planes:
        other, both, small_all, bias_all = exchange(
            deal(by_section, sides),
            gather(by_dp, jnp.stack([token_ids, target_ids])),
            gather(by_section, small),
            gather(Group(("section", "tensor"), (sections, shards)), bias_piece),
        )
        bias_all = bias_all.reshape(sections, shards, -1)
        own_side = lax.dynamic_index_in_dim(sides, s, 0, keepdims=False)
        side = [jnp.where(s == l, own_side, other[0]) for l in range(layers)]
        both = jnp.swapaxes(both, 0, 1).reshape(2, shards, sections, groups, part)
        both = lax.dynamic_index_in_dim(
            lax.dynamic_index_in_dim(both, s, 2, keepdims=False), j, 2, keepdims=False
        )
        ids, targets = both[0].reshape(-1), both[1].reshape(-1)
        group_lengths = lax.dynamic_index_in_dim(
            lengths.reshape(shards, sections), s, 1, keepdims=False
        )
        places = jnp.broadcast_to(j * part + jnp.arange(part), (shards, part))
        valid = (places < group_lengths[:, None]).reshape(-1)
    else:
        sides_all, small_all, bias_all = exchange(
            gather(by_section, sides), gather(by_section, small), gather(by_section, bias_piece)
        )
        bias_all = bias_all.reshape(sections, 1, -1)
        ids, targets = token_ids[s], target_ids[s]
        valid = jnp.arange(seq) < lengths[my_row]

    outer_gains = [small_all[l, 0] for l in range(layers)]
    outer_offsets = [small_all[l, 1] for l in range(layers)]
    params = []
    for l in range(layers):
        biases = [bias_all[l, :, n * cols : (n + 1) * cols].reshape(-1) for n in range(2)]
        units = bias_all[l, :, 2 * cols : 2 * cols + hidden].reshape(fan, halves, strip)
        params.append(
            dict(
                gains=small_all[l, 2:4],
                offsets=small_all[l, 4:6],
                row_bias=small_all[l, 6:8],
                bias=jnp.stack(biases),
                up_bias=jnp.swapaxes(units, 0, 1).reshape(1, -1),
            )
        )
        if not planes:
            block = sides_all[l]
            params[l].update(
                qk=block[:, :cols],
                vo=block[:, cols : 2 * cols],
                strips=[block[:, 2 * cols :]],
            )
    head_number = (
        (jnp.arange(fan)[:, None] if planes else z) * (local_cols // HEAD_DIM)
        + cut_index * (cols // HEAD_DIM)
        + jnp.arange(cols // HEAD_DIM)
    ).reshape(-1)
    slopes = jnp.exp2(-8.0 * (head_number + 1).astype(F32) / HEADS)

    def attn_jobs(l):
        if not planes or l >= layers:
            return []
        return [
            Job("spread", [by_tensor, by_section], side[l][first : first + cols])
            for first in (0, cols)
        ]

    def feed_jobs(l, n):
        if not planes or l >= layers:
            return []
        first = 2 * cols + n * strip
        return [Job("spread", [by_tensor, by_section], side[l][first : first + strip])]

    def take_attn(l, got):
        if got:
            params[l]["qk"], params[l]["vo"] = (
                one.reshape(2, fan * cols, width) for one in got
            )

    def take_feed(l, got):
        if got:
            params[l]["strips"] = [one.reshape(2, fan * strip, width) for one in got]

    def ident(kind, jobs):
        return exchange.ident((kind,) + tuple(job.key() for job in jobs))

    local_ids = ids - vocab_start
    inside = (local_ids >= 0) & (local_ids < vocab)
    looked = jnp.where(
        inside[:, None], jnp.take(embedding, jnp.clip(local_ids, 0, vocab - 1), axis=0), 0
    )
    group_part = looked.shape[0] // shards
    (x,) = exchange(Job("reduce", [by_tensor], looked.reshape(shards, group_part, width)))
    h = layer_norm(x, outer_gains[0], outer_offsets[0])

    kept = []
    for l, p in enumerate(params):
        jobs = (attn_jobs(l) if l == 0 else []) + feed_jobs(l, 0) + feed_jobs(l, 1)
        normed = layer_norm(h, p["gains"][0], p["offsets"][0]).astype(BF16)
        (total, normed, q, k, v, mixed, lse), got = attend(
            team, ident("attend", jobs), jobs, normed, length, slopes, p["bias"],
            [p["qk"], p["vo"]] if "qk" in p else [],
        )
        if "qk" not in p:
            take_attn(l, got[:2])
            got = got[2:]
        take_feed(l, got)
        middle = h + total + p["row_bias"][0]
        jobs = attn_jobs(l + 1)
        second = layer_norm(middle, p["gains"][1], p["offsets"][1]).astype(BF16)
        (total, second, before), got = feed(
            team, ident("feed", jobs), jobs, second, p["strips"], p["up_bias"]
        )
        take_attn(l + 1, got)
        kept.append((h, normed.reshape(seq, width), q, k, v, mixed, lse, middle, second, before))
        h = middle + total + p["row_bias"][1]

    final = layer_norm(h, outer_gains[-1], outer_offsets[-1]).astype(BF16)
    columns_of = (targets - vocab_start)[:, None]
    if planes:
        logits, final, stats = line_head_logits(
            by_tensor, exchange.ident("head logits"), final, embedding, columns_of
        )
        final = final.reshape(-1, width)
    else:
        (final,) = exchange(gather(by_tensor, final))
        final = final.reshape(-1, width)
        logits, tops, totals, picks = head_logits(final, embedding, columns_of)
        top = jnp.max(tops, axis=1)
        total = jnp.sum(totals * jnp.exp(tops - top[:, None]), axis=1)
        pick = jnp.sum(picks, axis=1)
        (stats,) = exchange(
            gather(by_tensor, jnp.pad(jnp.stack([top, total, pick]), ((0, 5), (0, 0))))
        )
    tokens = final.shape[0]
    top_all = jnp.max(stats[:, 0], axis=0)
    log_norm = top_all + jnp.log(jnp.sum(stats[:, 1] * jnp.exp(stats[:, 0] - top_all), axis=0))
    terms = jnp.where(valid, log_norm - jnp.sum(stats[:, 2], axis=0), 0.0)
    loss_part = jnp.sum(
        lax.dynamic_index_in_dim(terms.reshape(shards, -1), z, 0, keepdims=False)
    )
    row_weight = jnp.where(valid, 1.0 / token_count, 0.0)
    if planes:
        grad_logits, grad_final = line_head_grads(
            by_tensor, exchange.ident("head grads"), logits, embedding, columns_of,
            log_norm[:, None], row_weight[:, None],
        )
    else:
        grad_logits, back = head_grads(
            logits, embedding, columns_of, log_norm[:, None], row_weight[:, None]
        )
        (grad_final,) = exchange(
            Job("reduce", [by_tensor], back.reshape(shards, group_part, width))
        )
    _, final_back = jax.vjp(layer_norm, h, outer_gains[-1], outer_offsets[-1])
    grad, final_gain, final_offset = final_back(grad_final)

    def section_sums(pair, got):
        out = []
        for one, dealt in zip(pair, got):
            low = own_and_dealt(one, dealt, s).astype(BF16)
            if one.ndim == 4:
                out.append(low.reshape(low.shape[0], fan, cols, width))
            else:
                out.append(low.reshape(halves, fan, strip, width))
        return out

    def tensor_jobs(lows):
        return [deal(by_tensor, low, 1) for low in lows]

    def tensor_sums(lows, got):
        return [
            own_and_dealt(low, dealt, z, 1).astype(BF16) for low, dealt in zip(lows, got)
        ]

    def spread_jobs(pieces):
        return [Job("spread", [by_dp, by_section], piece) for piece in pieces]

    small_rows = [None] * layers
    pairs = [None] * layers
    attn_low, attn_done, feed_done = ([None] * layers for _ in range(3))
    for l in reversed(range(layers)):
        p = params[l]
        section_in, normed, q, k, v, mixed, lse, middle, second, before = kept[l]
        pair = by_section if planes else None
        late = planes and l + 1 < layers
        jobs = tensor_jobs(attn_low[l + 1]) if late else []
        (total, g_feed, up_sum, *dealt), got = feed_back(
            team, ident("feed back", jobs), jobs, pair, grad.astype(BF16),
            second.reshape(seq, width), before, p["strips"],
        )
        if late:
            attn_done[l + 1] = tensor_sums(attn_low[l + 1], got)
        if planes:
            feed_low = section_sums([g_feed], [one[None] for one in dealt])
        _, norm_back = jax.vjp(layer_norm, middle, p["gains"][1], p["offsets"][1])
        grad_mid, gain_two, offset_two = norm_back(total)
        grad_mid = grad_mid + grad
        jobs = tensor_jobs(feed_low) if planes else []
        (total, g_attn, qv_sum, *dealt), got = attend_back(
            team, ident("attend back", jobs), jobs, pair, grad_mid.astype(BF16), length, slopes,
            normed, p["qk"], p["vo"], q, k, v, mixed, lse,
        )
        g_attn = g_attn.reshape((2, 2) + g_attn.shape[1:])
        if planes:
            feed_done[l] = tensor_sums(feed_low, got)
            attn_low[l] = section_sums([g_attn], [one[None] for one in dealt])
        _, norm_back = jax.vjp(layer_norm, section_in, p["gains"][0], p["offsets"][0])
        grad_in, gain_one, offset_one = norm_back(total)
        bias_two = jnp.sum(grad, axis=0)
        grad = grad_in + grad_mid
        pairs[l] = (g_attn, g_feed)

        def placed(values, size):
            out = jnp.zeros((fan if planes else shards, cut, size), F32)
            at = (0, j, 0) if planes else (z, 0, 0)
            return lax.dynamic_update_slice(out, values.reshape(fan, 1, size), at).reshape(
                -1, width
            )

        units = jnp.swapaxes(up_sum.reshape(halves, fan, strip), 0, 1)
        small_rows[l] = [
            gain_one[None],
            gain_two[None],
            offset_one[None],
            offset_two[None],
            jnp.sum(grad_mid, axis=0)[None],
            bias_two[None],
            placed(qv_sum[0], cols),
            placed(qv_sum[1], cols),
            placed(units, hidden),
        ]

    _, embed_back = jax.vjp(layer_norm, x, outer_gains[0], outer_offsets[0])
    grad_rows, embed_gain, embed_offset = embed_back(grad)
    packed = jnp.concatenate(
        [row for l in range(layers) for row in small_rows[l]]
        + [embed_gain[None], final_gain[None], embed_offset[None], final_offset[None]]
        + [jnp.broadcast_to(loss_part, (1, width))]
    )
    used = packed.shape[0]
    packed = jnp.pad(packed, ((0, -used % 8), (0, 0)))
    jobs = [Job("gather", [Group(("section", "tensor"), (sections, shards))], packed, late=True)]
    if planes:
        jobs += spread_jobs(attn_done[1] + feed_done[1] + feed_done[0])
        jobs += [Job("deal", [by_tensor], low, 1, late=True) for low in attn_low[0]]
    embed_sum, packed, *got = table_sum(
        by_section, by_dp, by_tensor, jobs, grad_logits, ids[None, :] - vocab_start, final,
        grad_rows.astype(BF16), exchange.ident("table"),
    )
    packed = jnp.sum(packed, axis=0)
    jobs = [gather(by_dp, packed)]
    if planes:
        spread_one = got[:2]
        jobs += spread_jobs(tensor_sums(attn_low[0], got[3:]))
    packed, *spread_zero = exchange(*jobs)
    packed = jnp.sum(packed, axis=0)
    if planes:
        spread_zero.append(got[2])
        attn_sum, feed_sum = (
            jnp.where(s == 0, zero, one) for zero, one in zip(spread_zero, spread_one)
        )
    else:
        chosen = [
            lax.dynamic_index_in_dim(
                lax.psum(jnp.stack([pair[n] for pair in pairs]), ("section", "dp")),
                s, 0, keepdims=False,
            )
            for n in range(2)
        ]
        attn_sum = chosen[0][:, None]
        feed_sum = chosen[1][:, None, None]
    embed_sum = embed_sum.reshape(vocab, width).astype(F32)
    per_layer = (used - 5) // layers
    mine = lax.dynamic_slice_in_dim(packed, s * per_layer, per_layer, 0)
    qv_rows = mine[6:8].reshape(2, -1)
    ff_row = mine[8:].reshape(-1)
    grad_qv = lax.dynamic_slice_in_dim(qv_rows, z * local_cols, local_cols, 1)
    grad_up_bias = lax.dynamic_slice_in_dim(ff_row, z * hidden * cut, hidden * cut, 0)
    base = per_layer * layers
    grad_outer_gain = lax.dynamic_slice_in_dim(packed, base + s, 1, 0)
    grad_outer_bias = lax.dynamic_slice_in_dim(packed, base + 2 + s, 1, 0)
    loss = packed[base + 4, 0] / token_count

    def columns(array):
        return array.reshape(-1, width).T.astype(F32)

    grad_qkv = jnp.stack(
        [columns(attn_sum[0, :, 0]), columns(attn_sum[1, :, 0]), columns(attn_sum[0, :, 1])]
    )
    grad_out_mat = attn_sum[1, :, 1].astype(F32).reshape(-1, width)
    grad_up = columns(feed_sum[0])
    grad_down = feed_sum[1].astype(F32).reshape(-1, width)
    return (
        loss,
        embed_sum,
        grad_outer_gain,
        grad_outer_bias,
        mine[0:2][None],
        mine[2:4][None],
        grad_qkv[None],
        grad_qv[None],
        grad_out_mat[None],
        grad_up[None],
        grad_up_bias[None],
        grad_down[None],
        mine[4:6][None],
    )


def solution(mesh):
    return jax.shard_map(
        functools.partial(per_device, dict(mesh.shape)),
        mesh=mesh,
        in_specs=(
            P("dp", None),
            P("dp", None),
            P(),
            P("tensor", None),
            P("section", None),
            P("section", None),
            P("section", None, None),
            P("section", None, None),
            P("section", None, None, "tensor"),
            P("section", None, "tensor"),
            P("section", "tensor", None),
            P("section", None, "tensor"),
            P("section", "tensor"),
            P("section", "tensor", None),
            P("section", None, None),
        ),
        out_specs=(
            P(),
            P("tensor", None),
            P("section", None),
            P("section", None),
            P("section", None, None),
            P("section", None, None),
            P("section", None, None, "tensor"),
            P("section", None, "tensor"),
            P("section", "tensor", None),
            P("section", None, "tensor"),
            P("section", "tensor"),
            P("section", "tensor", None),
            P("section", None, None),
        ),
        check_vma=False,
    )
```
